128 devices in a mesh: shard: 2 (over x_hi), blk: 4 (over x_lo, core), aa: 16 (over z, y).
Axes of the slice: x: 4 (x_hi: 2, x_lo: 2; x = x_hi * 2 + x_lo), y: 4, z: 4, core: 2. Of those that a mesh axis runs over, the one named last changes fastest.
Arguments:
- tokens: bfloat16 [2, 8192, 1024], P('shard', ('blk', 'aa')), may hold values from -16 to 16
- segments: int32 [2, 8192], P('shard'), may hold values from 0 to 34, as said below
- valid: int32 [2, 8192], P('shard'), may hold values from 0 to 1, as said below
- w_query: bfloat16 [1024, 1024], P('shard'), may hold values from -0.1875 to 0.1875
- w_key: bfloat16 [1024, 1024], P('shard'), may hold values from -0.1875 to 0.1875
- w_value: bfloat16 [1024, 1024], P('shard'), may hold values from -0.1875 to 0.1875
- w_out: bfloat16 [1024, 1024], P('shard'), may hold values from -6 to 6
- norm1_gain: bfloat16 [1024], P('shard'), may hold values from 0.5 to 1.5
- norm1_bias: bfloat16 [1024], P('shard'), may hold values from -3 to 3
- w_in: bfloat16 [1024, 4096], P('shard'), may hold values from -0.1875 to 0.1875
- w_down: bfloat16 [4096, 1024], P('shard'), may hold values from -0.09375 to 0.09375
- norm2_gain: bfloat16 [1024], P('shard'), may hold values from 0.5 to 1.5
- norm2_bias: bfloat16 [1024], P('shard'), may hold values from -3 to 3
- cotangent: bfloat16 [2, 8192, 1024], P('shard', ('blk', 'aa')), may hold values from -6 to 6
Outputs:
- output: bfloat16 [2, 8192, 1024], P('shard', ('blk', 'aa'))
- grad_tokens: bfloat16 [2, 8192, 1024], P('shard', ('blk', 'aa'))
- grad_w_query: float32 [1024, 1024], P('shard')
- grad_w_key: float32 [1024, 1024], P('shard')
- grad_w_value: float32 [1024, 1024], P('shard')
- grad_w_out: float32 [1024, 1024], P('shard')
- grad_norm1_gain: float32 [1024], P('shard')
- grad_norm1_bias: float32 [1024], P('shard')
- grad_w_in: float32 [1024, 4096], P('shard')
- grad_w_down: float32 [4096, 1024], P('shard')
- grad_norm2_gain: float32 [1024], P('shard')
- grad_norm2_bias: float32 [1024], P('shard')
The draws below stay inside these ranges and needn't reach their ends.
Inputs may be any that keep to these rules, and one draw needn't show every extreme that they name: `segments`: segment numbers never fall along a sequence and start at 0. In each sequence one document begins in the first quarter and ends in the last quarter of the sequence; every other document holds at most 2048 tokens. Padding positions all carry the number 34. `valid`: each sequence is 1 on a prefix and 0 on a tail of at least 256 tokens and fewer than 1024.
All inputs are finite; a program needn't handle non-finite values.
Results may differ from the reference program's by a relative error of at most 0.035.
Values may be sent and summed in bfloat16 or wider, within the bound.
A program may use at most 256 MiB of HBM per device.

```python
import jax
import jax.numpy as jnp
from jax import lax

D = 1024
HEADS = 16
HEAD = 64
FF = 4096
SEQS = 2
LENGTH = 8192


def document_layout(key):

    def one_sequence(seq_key):
        parts = jax.random.split(seq_key, 5)
        start = jax.random.randint(parts[0], (), LENGTH // 8, LENGTH // 4)
        finish = jax.random.randint(parts[1], (), 13 * LENGTH // 16, 7 * LENGTH // 8)
        padding = jax.random.randint(parts[2], (), LENGTH // 32, LENGTH // 8)
        shortest = max(LENGTH // 40, 1)
        longest = LENGTH // 4 + 1
        head_cuts = jnp.cumsum(jax.random.randint(parts[3], (16,), shortest, longest))
        tail_cuts = finish + jnp.cumsum(jax.random.randint(parts[4], (16,), shortest, longest))
        head_cuts = jnp.where(head_cuts < start, head_cuts, LENGTH)
        tail_cuts = jnp.where(tail_cuts < LENGTH, tail_cuts, LENGTH)
        cuts = jnp.concatenate([head_cuts, tail_cuts, jnp.stack([start, finish])]).astype(jnp.int32)
        places = jnp.arange(LENGTH, dtype=jnp.int32)
        numbers = jnp.sum((cuts[None, :] <= places[:, None]).astype(jnp.int32), axis=1)
        kept = (places < LENGTH - padding).astype(jnp.int32)
        numbers = jnp.where(kept == 1, numbers, 34)
        return (numbers.astype(jnp.int32), kept)
    return jax.vmap(one_sequence)(jax.random.split(key, SEQS))


def draw_segments(key, part):
    return document_layout(key)[0]


def draw_valid(key, part):
    return document_layout(key)[1]


def raised(values, key, source, target, blocks, factor):
    owner, partner = [(jnp.arange(values.shape[axis_at]) // (values.shape[axis_at] // blocks)).reshape([-1 if axis == axis_at else 1 for axis in range(values.ndim)]) for axis_at in (source, target)]
    chosen = jax.random.permutation(key, blocks)[partner]
    strong = (owner == chosen) | (owner == (partner + blocks // 2) % blocks)
    return jnp.where(strong, factor * values, values)


def levels(key, shape, pieces, smallest, largest):
    gain = 1.0
    for axis_at, blocks in pieces:
        heights = jax.random.uniform(jax.random.fold_in(jax.random.fold_in(key, 6), axis_at), (blocks,), jnp.float32, smallest / len(pieces), largest / len(pieces))
        gain = gain * jnp.repeat(jnp.exp(heights), shape[axis_at] // blocks).reshape((-1,) + (1,) * (len(shape) - 1 - axis_at))
    return gain


def gaussian(own_key, extent, deviation, most, cuts=(), held_as=jnp.bfloat16):
    drawn = jax.random.normal(own_key, extent, jnp.float32) * deviation
    if len(cuts) > 0:
        drawn = levels(own_key, extent, cuts, -0.22, 0.18) * drawn
    return jnp.clip(drawn, min=-most, max=most).astype(held_as)


def gaussian_with(own_key, extent, width, most, shards, heavy, held_as=jnp.bfloat16):
    values = width * jax.random.normal(own_key, extent, jnp.float32)
    if shards:
        values = values * levels(own_key, extent, shards, -0.22, 0.18)
    return jnp.clip(raised(values, jax.random.fold_in(own_key, 3), *heavy), -most, most).astype(held_as)


def setup_inputs(seed: int = 0) -> dict:
    seeds = jax.random.split(jax.random.key(seed), 15)
    tokens = gaussian_with(seeds[0], (SEQS, LENGTH, D), 1.0, 16.0, ((0, 2), (1, 64)), (1, 2, 64, 4.0))
    segments = draw_segments(jax.random.fold_in(seeds[14], 71), 0)
    valid = draw_valid(jax.random.fold_in(seeds[14], 71), 0)
    w_query = gaussian(seeds[3], (D, D), D ** -0.5, 0.1875, ((0, 2),))
    w_key = gaussian(seeds[4], (D, D), D ** -0.5, 0.1875, ((0, 2),))
    w_value = gaussian(seeds[5], (D, D), D ** -0.5, 0.1875, ((0, 2),))
    w_out = gaussian(seeds[6], (D, D), (max(D // 1024, 1)) ** -0.5, 6.0, ((0, 2),))
    norm1_gain = jnp.clip(1.0 + 0.1 * jax.random.normal(seeds[7], (D,), jnp.float32), 0.5, 1.5).astype(jnp.bfloat16)
    norm1_bias = gaussian(seeds[8], (D,), 0.5, 3.0, ((0, 2),))
    w_in = gaussian(seeds[9], (D, FF), D ** -0.5, 0.1875, ((0, 2),))
    w_down = gaussian(seeds[10], (FF, D), FF ** -0.5, 0.09375, ((0, 2),))
    norm2_gain = jnp.clip(1.0 + 0.1 * jax.random.normal(seeds[11], (D,), jnp.float32), 0.5, 1.5).astype(jnp.bfloat16)
    norm2_bias = gaussian(seeds[12], (D,), 0.5, 3.0, ((0, 2),))
    cotangent = gaussian(seeds[13], (SEQS, LENGTH, D), 1.0, 6.0, ((0, 2), (1, 64)))
    return {"tokens": tokens, "segments": segments, "valid": valid, "w_query": w_query, "w_key": w_key, "w_value": w_value, "w_out": w_out, "norm1_gain": norm1_gain, "norm1_bias": norm1_bias, "w_in": w_in, "w_down": w_down, "norm2_gain": norm2_gain, "norm2_bias": norm2_bias, "cotangent": cotangent}


@jax.custom_vjp
def low(v):
    return lax.optimization_barrier(v.astype(jnp.bfloat16)).astype(jnp.float32)

@jax.custom_vjp
def low_back(v):
    return v

def low_keep(v):
    return (low(v), None)

def low_pass(kept, grad):
    return (grad,)

def back_keep(v):
    return (v, None)

def back_low(kept, grad):
    return (low(grad),)
low.defvjp(low_keep, low_pass)
low_back.defvjp(back_keep, back_low)
EXACT = lax.Precision.HIGHEST
MASKED_SCORE = -1e+30
NORM_EPSILON = 1e-05

def matmul(left, right):
    return jnp.dot(left, right, precision=EXACT, preferred_element_type=jnp.float32)

def layer_norm(summed_in, norm_gain, norm_bias):
    row_mean = lax.optimization_barrier(jnp.mean(summed_in, axis=-1, keepdims=True))
    centred = summed_in - row_mean
    variance = lax.optimization_barrier(jnp.mean(centred * centred, axis=-1, keepdims=True))
    return centred * lax.rsqrt(variance + NORM_EPSILON) * norm_gain + norm_bias

def attend_head(queries, keys, values, allowed):
    scores = low_back(matmul(queries, keys.T) * HEAD ** (-0.5))
    scores = jnp.where(allowed, scores, MASKED_SCORE)
    probs = low(jax.nn.softmax(scores, axis=-1))
    return matmul(probs, values)

def to_heads(matrix):
    return matrix.reshape(matrix.shape[0], HEADS, HEAD).transpose(1, 0, 2)

def forward(inputs, segments, valid, w_query, w_key, w_value, w_out, norm1_gain, norm1_bias, w_in, w_down, norm2_gain, norm2_bias):
    length = inputs.shape[0]
    places = jnp.arange(length, dtype=jnp.int32)
    allowed = (segments[:, None] == segments[None, :]) & (valid[None, :] == 1) | (places[:, None] == places[None, :])
    queries = low_back(low(matmul(inputs, w_query)))
    keys = low_back(low(matmul(inputs, w_key)))
    values = low_back(low(matmul(inputs, w_value)))

    def one_head(triple):
        return attend_head(triple[0], triple[1], triple[2], allowed)
    heads = lax.map(jax.checkpoint(one_head), (to_heads(queries), to_heads(keys), to_heads(values)))
    mixed = low_back(low(heads.transpose(1, 0, 2).reshape(length, HEADS * HEAD)))
    attn = low_back(matmul(mixed, w_out))
    first = layer_norm(inputs + attn, norm1_gain, norm1_bias)
    pre = low_back(matmul(low(first), w_in))
    hidden = low(jax.nn.gelu(pre, approximate=False))
    ff_out = low_back(matmul(hidden, w_down))
    return layer_norm(first + ff_out, norm2_gain, norm2_bias)

def reference(tokens, segments, valid, w_query, w_key, w_value, w_out, norm1_gain, norm1_bias, w_in, w_down, norm2_gain, norm2_bias, cotangent):
    params = tuple((item.astype(jnp.float32) for item in (w_query, w_key, w_value, w_out, norm1_gain, norm1_bias, w_in, w_down, norm2_gain, norm2_bias)))

    def one_sequence(running, inputs):
        seq_tokens, seq_segments, seq_valid, seq_cot = inputs

        def apply_layer(layer_in, *weights):
            return forward(layer_in, seq_segments, seq_valid, *weights)
        result, pull = jax.vjp(apply_layer, seq_tokens.astype(jnp.float32), *params)
        gradients = pull(seq_cot.astype(jnp.float32))
        running = tuple((old + new for old, new in zip(running, gradients[1:])))
        return (running, (result.astype(jnp.bfloat16), gradients[0].astype(jnp.bfloat16)))
    zeros = tuple((jnp.zeros(item.shape, jnp.float32) for item in params))
    totals, (result_all, input_grads) = lax.scan(one_sequence, zeros, (tokens, segments, valid, cotangent))
    return (result_all, input_grads, totals[0], totals[1], totals[2], totals[3], totals[4], totals[5], totals[6], totals[7], totals[8], totals[9])
```

```python
import functools
import math

import jax
import jax.numpy as jnp
from jax import lax
from jax.experimental import pallas as pl
from jax.experimental.pallas import tpu as pltpu
from jax.sharding import PartitionSpec as P

HEADS = 16
HEAD = 64
QBLK = 512


MASKED_SCORE = -1e30
NORM_EPSILON = 1e-05


def from_behind(value, axis, by):
    devices = lax.axis_size(axis)
    return lax.ppermute(value, axis, [(i, (i + by) % devices) for i in range(devices)])


MESH = pl.DeviceIdType.MESH
ROWS = 512
REDUCE_DIMS = ("xa", "ya", "za", "yb", "zb")
GATHER_DIMS = ("ya", "za", "yb", "zb")


def place():
    shard = lax.axis_index("shard")
    blk = lax.axis_index("blk")
    aa = lax.axis_index("aa")
    return (shard, blk // 2, blk % 2, aa // 4, aa % 4)


def flipped(i):
    return i + 1 - 2 * (i % 2)


def partner(dim):
    shard, x_lo, core, z, y = place()
    if dim == "core":
        core = 1 - core
    elif dim == "xa":
        x_lo = 1 - x_lo
    elif dim == "xb":
        shard, x_lo = 1 - shard, 1 - x_lo
    elif dim == "ya":
        y = flipped(y)
    elif dim == "yb":
        y = 3 - y
    elif dim == "za":
        z = flipped(z)
    else:
        z = 3 - z
    return (shard, x_lo * 2 + core, z * 4 + y)


def ring_bit(dim):
    shard, x_lo, _, z, y = place()
    if dim == "xa":
        return (shard * 2 + x_lo + shard) % 2
    if dim == "ya":
        return (y + y // 2) % 2
    if dim == "yb":
        return y // 2
    if dim == "za":
        return (z + z // 2) % 2
    return z // 2


def greet(dims):
    barrier = pltpu.get_barrier_semaphore()
    for dim in dims:
        pl.semaphore_signal(barrier, inc=1, device_id=partner(dim), device_id_type=MESH)
    pl.semaphore_wait(barrier, len(dims))


def remote(src, dst, send_sem, recv_sem, dim):
    return pltpu.make_async_remote_copy(
        src_ref=src,
        dst_ref=dst,
        send_sem=send_sem,
        recv_sem=recv_sem,
        device_id=partner(dim),
        device_id_type=MESH,
    )


def row_starts(dims, rows):
    starts, at, size = ([0], 0, rows)
    for dim in dims:
        size //= 2
        at = at + ring_bit(dim) * size
        starts.append(at)
    return starts


def rotated(dims, by):
    return dims[by:] + dims[:by]


def gather_kernel(shapes, targets, n_out, *refs):
    n = len(shapes)
    ins, outs = (refs[:n], refs[n : n + n_out])
    send, recv, own = refs[n + n_out :]
    shard, _, core, _, _ = place()
    greet(("xb", "core") + GATHER_DIMS)
    sent = []

    def start(copy):
        copy.start()
        sent.append(copy)

    locals_ = []
    for i, (rows, cols) in enumerate(shapes):
        out, off = targets[i]
        copy = pltpu.make_async_copy(
            ins[i],
            outs[out].at[pl.ds(pl.multiple_of(shard * rows, rows), rows), pl.ds(off, cols)],
            own.at[i],
        )
        copy.start()
        locals_.append(copy)

    def block(i, part, base, at, size, inner=False):
        rows, cols = shapes[i]
        out, off = targets[i]
        width = cols // 8
        col = pl.multiple_of(core * (cols // 2) + part * width, 128)
        if inner:
            return ins[i].at[pl.ds(pl.multiple_of(at, 16), size), pl.ds(col, width)]
        col = pl.multiple_of(core * (cols // 2) + (off + part * width), 128)
        at = pl.multiple_of(base * rows + at, 16)
        return outs[out].at[pl.ds(at, size), pl.ds(col, width)]

    other = 1 - shard
    plan = {}
    for i, (rows, _) in enumerate(shapes):
        for part in range(4):
            order = rotated(GATHER_DIMS, part)
            starts = row_starts(order, rows)
            piece = rows // 16
            copy = remote(
                block(i, part, 0, starts[4], piece, inner=True),
                block(i, part, shard, starts[4], piece),
                send.at[i, part, 0],
                recv.at[i, part, 0],
                "xb",
            )
            start(copy)
            plan[i, part] = (order, starts, copy)
    siblings = []
    for stage in range(1, 6):
        for i, (rows, _) in enumerate(shapes):
            for part in range(4):
                order, starts, copy = plan[i, part]
                copy.wait_recv()
                if stage < 5:
                    k = 4 - stage
                    size = rows >> (k + 1)
                    mine = block(i, part, other, starts[k + 1], size)
                    copy = remote(
                        mine, mine, send.at[i, part, stage], recv.at[i, part, stage], order[k]
                    )
                    start(copy)
                    plan[i, part] = (order, starts, copy)
                if stage >= 4:
                    size = rows // 2
                    at = starts[1] if stage == 4 else size - starts[1]
                    mine = block(i, part, other, at, size)
                    copy = remote(
                        mine, mine, send.at[i, part, stage + 1], recv.at[i, part, stage + 1], "core"
                    )
                    start(copy)
                    siblings.append(copy)
    for copy in siblings:
        copy.wait_recv()
    for copy in sent:
        copy.wait_send()
    for copy in locals_:
        copy.wait()


def gather_weights(arrays, targets, out_shapes, collective_id):
    shapes = [a.shape for a in arrays]
    n = len(shapes)
    return pl.pallas_call(
        functools.partial(gather_kernel, shapes, targets, len(out_shapes)),
        out_shape=[jax.ShapeDtypeStruct(shape, jnp.bfloat16) for shape in out_shapes],
        in_specs=[pl.BlockSpec(memory_space=pl.ANY)] * n,
        out_specs=[pl.BlockSpec(memory_space=pl.ANY)] * len(out_shapes),
        scratch_shapes=[
            pltpu.SemaphoreType.DMA((n, 4, 7)),
            pltpu.SemaphoreType.DMA((n, 4, 7)),
            pltpu.SemaphoreType.DMA((n,)),
        ],
        compiler_params=pltpu.CompilerParams(collective_id=collective_id, has_side_effects=True),
    )(*arrays)


def reduce_kernel(n_left, dots, widths, with_norm, *refs):
    refs = list(refs)

    def take(count):
        taken = refs[:count]
        del refs[:count]
        return taken

    n_right = len(dots_rights(dots))
    lefts, rights = (take(n_left), take(n_right))
    norm_in = take(1)[0] if with_norm else None
    out = take(1)[0]
    norm_out = take(1)[0] if with_norm else None
    left_all, right_all = (take(n_left), take(n_right))
    partial = take(1)[0]
    landed = take(6)
    norm_held, norm_landed = take(2) if with_norm else (None, None)
    act_send, act_recv, red_send, red_recv, gat_send, gat_recv, nrm_send, nrm_recv = refs
    shard, _, core, _, _ = place()
    greet(("core", "xa", "xb", "ya", "yb", "za", "zb"))
    sent = []

    def start(copy):
        copy.start()
        sent.append(copy)
        return copy

    half_tokens = lefts[0].shape[0]
    acts = []
    for i, (src, dst) in enumerate(zip(lefts, left_all)):
        acts.append(
            start(
                remote(
                    src,
                    dst.at[pl.ds(half_tokens, half_tokens)],
                    act_send.at[i],
                    act_recv.at[i],
                    "core",
                )
            )
        )
    for i, (src, dst) in enumerate(zip(rights, right_all)):
        half = src.shape[1] // 2
        theirs = pl.ds(pl.multiple_of((1 - core) * half, half), half)
        acts.append(
            start(
                remote(
                    src.at[:, theirs],
                    dst.at[pl.ds(half_tokens, half_tokens)],
                    act_send.at[n_left + i],
                    act_recv.at[n_left + i],
                    "core",
                )
            )
        )
    norm_dims = ("core",) + REDUCE_DIMS + ("xb",)
    norm_copies = []

    def norm_start(k):
        if not with_norm:
            return
        if k < 6:
            src, dst = (norm_held.at[k], norm_landed.at[k])
        else:
            src, dst = (norm_held.at[6, pl.ds(1 - shard, 1)], norm_landed.at[6, pl.ds(0, 1)])
        norm_copies.append(
            start(remote(src, dst, nrm_send.at[k], nrm_recv.at[k], norm_dims[k]))
        )

    def norm_finish(k):
        if not with_norm:
            return
        norm_copies[k].wait_recv()
        if k < 6:
            norm_held[k + 1] = norm_held[k] + norm_landed[k]
        else:
            norm_out[...] = norm_held[6, shard] + norm_landed[6, 0]

    if with_norm:
        norm_held[0] = norm_in[...]
    norm_start(0)
    for src, dst in zip(lefts, left_all):
        dst[pl.ds(0, half_tokens)] = src[...]
    for src, dst in zip(rights, right_all):
        half = src.shape[1] // 2
        dst[pl.ds(0, half_tokens)] = src[:, pl.ds(pl.multiple_of(core * half, half), half)]
    for copy in acts:
        copy.wait_recv()
    norm_finish(0)
    norm_start(1)
    edges = [0]
    for width in widths:
        edges.append(edges[-1] + width)
    parts = range(len(widths))
    cols = [pl.ds(edges[p], widths[p]) for p in parts]
    orders = [rotated(REDUCE_DIMS, p) for p in parts]
    starts = [row_starts(orders[p], ROWS) for p in parts]
    moving = {}

    def reduce_start(p, k):
        if k < 5:
            half = ROWS >> (k + 1)
            away = pl.multiple_of(starts[p][k] + (half - (starts[p][k + 1] - starts[p][k])), 16)
            src = partial.at[:, pl.ds(away, half), cols[p]]
            dst = landed[k].at[:, :, cols[p]]
            dim = orders[p][k]
        else:
            at = pl.multiple_of(starts[p][5], 16)
            src = partial.at[1 - shard, pl.ds(at, 16), cols[p]]
            dst = landed[5].at[:, cols[p]]
            dim = "xb"
        moving[p] = start(remote(src, dst, red_send.at[p, k], red_recv.at[p, k], dim))

    def reduce_add(p, k):
        moving[p].wait_recv()
        if k < 5:
            half = ROWS >> (k + 1)
            step = min(half, 32)

            def add(i, carry):
                here = pl.ds(pl.multiple_of(i * step, step), step)
                there = pl.ds(pl.multiple_of(starts[p][k + 1] + i * step, 16), step)
                total = partial[:, there, cols[p]].astype(jnp.float32)
                total = total + landed[k][:, here, cols[p]].astype(jnp.float32)
                partial[:, there, cols[p]] = total.astype(jnp.bfloat16)
                return carry

            lax.fori_loop(0, half // step, add, 0)
        else:
            here = pl.ds(pl.multiple_of(starts[p][5], 16), 16)
            total = partial[shard, here, cols[p]].astype(jnp.float32)
            total = total + landed[5][:, cols[p]].astype(jnp.float32)
            out[core, here, cols[p]] = total.astype(jnp.bfloat16)

    ready = 0
    for at, (left, left_step, left_off, right, right_off) in enumerate(dots):
        for s in range(2):
            product = lax.dot_general(
                left_all[left][:, pl.ds(s * left_step + left_off, ROWS)],
                right_all[right][:, pl.ds(right_off, 512)],
                (((0,), (0,)), ((), ())),
                preferred_element_type=jnp.float32,
            )
            partial[s, :, pl.ds(at * 512, 512)] = product.astype(jnp.bfloat16)
        while ready < len(widths) and edges[ready + 1] <= (at + 1) * 512:
            reduce_start(ready, 0)
            ready += 1
    for k in range(6):
        norm_finish(k + 1)
        if k < 5:
            norm_start(k + 2)
        for p in parts:
            reduce_add(p, k)
            if k < 5:
                reduce_start(p, k + 1)

    def range_of(p, at, size):
        return out.at[core, pl.ds(pl.multiple_of(at, 16), size), cols[p]]

    def gather_start(p, k):
        mine = range_of(p, starts[p][k + 1], ROWS >> (k + 1))
        moving[p] = start(
            remote(mine, mine, gat_send.at[p, k], gat_recv.at[p, k], orders[p][k])
        )

    shared = []

    def share(p, slot, at):
        mine = range_of(p, at, ROWS // 2)
        shared.append(
            start(remote(mine, mine, gat_send.at[p, 5 + slot], gat_recv.at[p, 5 + slot], "core"))
        )

    for p in parts:
        gather_start(p, 4)
    for k in range(4, -1, -1):
        for p in parts:
            moving[p].wait_recv()
            if k > 0:
                gather_start(p, k - 1)
            if k == 1:
                share(p, 0, starts[p][1])
            if k == 0:
                share(p, 1, ROWS // 2 - starts[p][1])
    for copy in shared:
        copy.wait_recv()
    for copy in sent:
        copy.wait_send()


def dots_rights(dots):
    return sorted({d[3] for d in dots})


def reduce_gradients(lefts, rights, dots, widths, norm, collective_id):
    tokens = lefts[0].shape[0]
    total = sum(widths)
    out_shape = [jax.ShapeDtypeStruct((2, ROWS, total), jnp.bfloat16)]
    scratch = [pltpu.VMEM((2 * tokens, a.shape[1]), jnp.bfloat16) for a in lefts]
    scratch += [pltpu.VMEM((2 * tokens, a.shape[1] // 2), jnp.bfloat16) for a in rights]
    scratch += [pltpu.VMEM((2, ROWS, total), jnp.bfloat16)]
    scratch += [pltpu.VMEM((2, ROWS >> (k + 1), total), jnp.bfloat16) for k in range(5)]
    scratch += [pltpu.VMEM((16, total), jnp.bfloat16)]
    operands = [*lefts, *rights]
    if norm is not None:
        operands.append(norm)
        out_shape.append(jax.ShapeDtypeStruct(norm.shape[1:], jnp.float32))
        scratch += [
            pltpu.VMEM((7, *norm.shape), jnp.float32),
            pltpu.VMEM((7, *norm.shape), jnp.float32),
        ]
    n_act, parts = (len(lefts) + len(rights), len(widths))
    scratch += [pltpu.SemaphoreType.DMA((n_act,))] * 2
    scratch += [pltpu.SemaphoreType.DMA((parts, 6))] * 2
    scratch += [pltpu.SemaphoreType.DMA((parts, 7))] * 2
    scratch += [pltpu.SemaphoreType.DMA((7,))] * 2
    return pl.pallas_call(
        functools.partial(reduce_kernel, len(lefts), dots, widths, norm is not None),
        out_shape=out_shape,
        in_specs=[pl.BlockSpec(memory_space=pltpu.VMEM)] * len(operands),
        out_specs=[pl.BlockSpec(memory_space=pltpu.VMEM)] * len(out_shape),
        scratch_shapes=scratch,
        compiler_params=pltpu.CompilerParams(
            collective_id=collective_id, has_side_effects=True, vmem_limit_bytes=60 * 2**20
        ),
    )(*operands)


FF_DOTS = tuple(
    [(0, 512, 0, 0, j * 512) for j in range(4)]
    + [(1, 2048, q * 512, 1, 0) for q in range(4)]
    + [(2, 512, 0, 2, 0)]
)
FF_WIDTHS = (1024, 896, 896, 896, 896)
QKV_DOTS = ((0, 512, 0, 0, 0), (0, 512, 0, 1, 0), (0, 512, 0, 2, 0))
QKV_WIDTHS = (384, 384, 256, 256, 256)


def cast_kernel(x_ref, o_ref):
    o_ref[...] = x_ref[0].astype(jnp.float32)


def cast_out(gathered, shape, grid, index_in, index_out):
    return pl.pallas_call(
        cast_kernel,
        out_shape=jax.ShapeDtypeStruct(shape, jnp.float32),
        grid=grid,
        in_specs=[pl.BlockSpec((1, ROWS, 512), index_in)],
        out_specs=pl.BlockSpec((ROWS, 512), index_out),
    )(gathered)


def square_out(gathered, slot):
    return cast_out(gathered, (ROWS, 1024), (2,), lambda c: (c, 0, slot), lambda c: (0, c))


def ff_grads_out(gathered):
    grad_in = cast_out(
        gathered, (ROWS, 4096), (2, 4), lambda c, j: (c, 0, j), lambda c, j: (0, c * 4 + j)
    )
    grad_down = cast_out(
        gathered, (2048, 1024), (4, 2), lambda q, c: (c, 0, 4 + q), lambda q, c: (q, c)
    )
    return (grad_in, grad_down, square_out(gathered, 8))


def normalize(summed_in, norm_gain, norm_bias):
    row_mean = jnp.mean(summed_in, axis=-1, keepdims=True)
    centred = summed_in - row_mean
    inv_std = lax.rsqrt(jnp.mean(centred * centred, axis=-1, keepdims=True) + NORM_EPSILON)
    scaled = centred * inv_std
    return (scaled * norm_gain + norm_bias, scaled, inv_std)


def normalize_back(upstream, scaled, inv_std, norm_gain):
    weighted = upstream * norm_gain
    centred = weighted - jnp.mean(weighted, axis=-1, keepdims=True)
    result = inv_std * (centred - scaled * jnp.mean(weighted * scaled, axis=-1, keepdims=True))
    return (result, jnp.sum(upstream * scaled, axis=0), jnp.sum(upstream, axis=0))


def exact_gelu(values):
    return jax.nn.gelu(values, approximate=False)


def allowed_mask(segments, valid, query_start, key_start, query_count, key_count):
    seg_query = lax.dynamic_slice_in_dim(segments, query_start, query_count)
    seg_key = lax.dynamic_slice_in_dim(segments, key_start, key_count)
    live_key = lax.dynamic_slice_in_dim(valid, key_start, key_count)
    place_query = query_start + jnp.arange(query_count, dtype=jnp.int32)
    place_key = key_start + jnp.arange(key_count, dtype=jnp.int32)
    same_doc = (seg_query[:, None] == seg_key[None, :]) & (live_key[None, :] == 1)
    return same_doc | (place_query[:, None] == place_key[None, :])


def pass_keys(kv_pair):
    return from_behind(kv_pair, "blk", 1)


def pass_grads(grad_pair):
    return from_behind(grad_pair.astype(jnp.bfloat16), "blk", 1).astype(grad_pair.dtype)


def shards(
    tokens,
    segments,
    valid,
    w_query,
    w_key,
    w_value,
    w_out,
    norm1_gain,
    norm1_bias,
    w_in,
    w_down,
    norm2_gain,
    norm2_bias,
    cotangent,
):
    packed = jnp.zeros((16, 512), jnp.bfloat16).at[:4].set(
        jnp.stack([norm1_gain, norm1_bias, norm2_gain, norm2_bias])
    )
    full_qkv, full_out, full_in, full_down = gather_weights(
        [w_query, w_key, w_value, w_out, w_in, w_down],
        [(0, 0), (0, 1024), (0, 2048), (1, 0), (2, 0), (3, 0)],
        [(1024, 3072), (1024, 1024), (1024, 4096), (4096, 1024)],
        0,
    )
    full_query, full_key, full_value = jnp.split(full_qkv, 3, axis=1)
    norms = lax.all_gather(packed, "shard", axis=1, tiled=True)[:4]
    gain_one, bias_one, gain_two, bias_two = norms
    gain_one = gain_one.astype(jnp.float32)
    bias_one = bias_one.astype(jnp.float32)
    gain_two = gain_two.astype(jnp.float32)
    bias_two = bias_two.astype(jnp.float32)
    token_rows = tokens[0]
    seq_segments = segments[0]
    seq_valid = valid[0]
    tok_rows, width = token_rows.shape
    groups = lax.axis_size("aa")
    head_local = HEADS // groups
    group_width = head_local * HEAD
    block_len = groups * tok_rows
    block_count = block_len // QBLK
    score_scale = HEAD ** (-0.5)
    cycle_size = lax.axis_size("blk")
    cycle_index = lax.axis_index("blk")
    query_base = cycle_index * block_len
    block_ids = jnp.arange(block_count, dtype=jnp.int32)
    projected = [
        jnp.dot(token_rows, matrix, preferred_element_type=jnp.float32)
        .astype(jnp.bfloat16)
        .reshape(tok_rows, groups, group_width)
        for matrix in (full_query, full_key, full_value)
    ]
    heads_all = lax.all_to_all(
        jnp.concatenate(projected, axis=2), "aa", split_axis=1, concat_axis=0, tiled=True
    )
    heads_all = heads_all.reshape(block_len, 3, head_local, HEAD)
    q_blocks = heads_all[:, 0].reshape(block_count, QBLK, head_local, HEAD)
    kv_pair = heads_all[:, 1:]
    state = (
        jnp.full((block_count, head_local, QBLK), MASKED_SCORE, jnp.float32),
        jnp.zeros((block_count, head_local, QBLK), jnp.float32),
        jnp.zeros((block_count, QBLK, head_local, HEAD), jnp.float32),
    )
    kept_pairs = []
    for cycle_step in range(cycle_size):
        if cycle_step > 0:
            kv_pair = pass_keys(kv_pair)
        kept_pairs.append(kv_pair)
        key_start = (cycle_index - cycle_step) % cycle_size * block_len
        attend_key_heads = kv_pair[:, 0]
        attend_value_heads = kv_pair[:, 1]

        def attend_visit(inputs):
            block_index, query_block, running_max, running_sum, summed = inputs
            allowed = allowed_mask(
                seq_segments, seq_valid, query_base + block_index * QBLK, key_start, QBLK, block_len
            )
            scores = (
                jnp.einsum(
                    "qhd,khd->hqk",
                    query_block,
                    attend_key_heads,
                    preferred_element_type=jnp.float32,
                )
                * score_scale
            )
            scores = jnp.where(allowed[None], scores, MASKED_SCORE)
            new_max = jnp.maximum(running_max, jnp.max(scores, axis=-1))
            factor = jnp.exp(running_max - new_max)
            weights_new = jnp.exp(scores - new_max[..., None])
            new_sum = running_sum * factor + jnp.sum(weights_new, axis=-1)
            new_summed = summed * jnp.transpose(factor)[..., None] + jnp.einsum(
                "hqk,khd->qhd",
                weights_new.astype(jnp.bfloat16),
                attend_value_heads,
                preferred_element_type=jnp.float32,
            )
            return (new_max, new_sum, new_summed)

        state = lax.map(attend_visit, (block_ids, q_blocks) + state)
    running_max, running_sum, summed = state
    attn_heads = summed / jnp.transpose(running_sum, (0, 2, 1))[..., None]
    log_total = running_max + jnp.log(running_sum)
    mixed = lax.all_to_all(
        attn_heads.astype(jnp.bfloat16).reshape(block_len, 1, group_width),
        "aa",
        split_axis=0,
        concat_axis=1,
        tiled=True,
    ).reshape(tok_rows, width)
    attn = jnp.dot(mixed, full_out, preferred_element_type=jnp.float32)
    first, scaled_one, inv_one = normalize(
        token_rows.astype(jnp.float32) + attn, gain_one, bias_one
    )
    first_low = first.astype(jnp.bfloat16)
    pre = jnp.dot(first_low, full_in, preferred_element_type=jnp.float32)
    hidden = exact_gelu(pre).astype(jnp.bfloat16)
    ff_out = jnp.dot(hidden, full_down, preferred_element_type=jnp.float32)
    result, scaled_two, inv_two = normalize(first + ff_out, gain_two, bias_two)
    upstream = cotangent[0].astype(jnp.float32)
    grad_two, grad_gain_two, grad_bias_two = normalize_back(upstream, scaled_two, inv_two, gain_two)
    ff_grad = grad_two.astype(jnp.bfloat16)
    hidden_grad = jnp.einsum("td,fd->tf", ff_grad, full_down, preferred_element_type=jnp.float32)
    gelu_pull = jax.vjp(exact_gelu, pre)[1]
    pre_grad = gelu_pull(hidden_grad)[0].astype(jnp.bfloat16)
    first_grad = grad_two + jnp.einsum(
        "tf,df->td", pre_grad, full_in, preferred_element_type=jnp.float32
    )
    grad_one, grad_gain_one, grad_bias_one = normalize_back(
        first_grad, scaled_one, inv_one, gain_one
    )
    attn_grad = grad_one.astype(jnp.bfloat16)
    norm_sums = jnp.stack([grad_gain_one, grad_bias_one, grad_gain_two, grad_bias_two])
    norm_sums = jnp.pad(norm_sums.reshape(4, 2, 512).transpose(1, 0, 2), ((0, 0), (0, 4), (0, 0)))
    ff_summed, norm_total = reduce_gradients(
        [first_low, hidden, mixed],
        [pre_grad, ff_grad, attn_grad],
        FF_DOTS,
        FF_WIDTHS,
        norm_sums,
        1,
    )
    grad_in, grad_down, grad_out_weight = ff_grads_out(ff_summed)
    mixed_grad = jnp.einsum(
        "td,cd->tc", attn_grad, full_out, preferred_element_type=jnp.float32
    ).astype(jnp.bfloat16)
    grad_blocks = lax.all_to_all(
        mixed_grad.reshape(tok_rows, groups, group_width),
        "aa",
        split_axis=1,
        concat_axis=0,
        tiled=True,
    )
    grad_blocks = grad_blocks.reshape(block_count, QBLK, head_local, HEAD)
    delta = jnp.transpose(jnp.sum(grad_blocks.astype(jnp.float32) * attn_heads, axis=-1), (0, 2, 1))
    grad_pair = jnp.zeros((block_len, 2, head_local, HEAD), jnp.float32)
    query_grad = jnp.zeros((block_count, QBLK, head_local, HEAD), jnp.float32)
    for cycle_step in range(cycle_size):
        if cycle_step > 0:
            grad_pair = pass_grads(grad_pair)
        key_start = (cycle_index - cycle_step) % cycle_size * block_len
        current_pair = kept_pairs[cycle_step]
        key_heads = current_pair[:, 0]
        value_heads = current_pair[:, 1]

        def visit(carry, inputs):
            block_index, query_block, grad_block, log_block, delta_block = inputs
            allowed = allowed_mask(
                seq_segments, seq_valid, query_base + block_index * QBLK, key_start, QBLK, block_len
            )
            scores = (
                jnp.einsum(
                    "qhd,khd->hqk", query_block, key_heads, preferred_element_type=jnp.float32
                )
                * score_scale
            )
            scores = jnp.where(allowed[None], scores, MASKED_SCORE)
            probs = jnp.exp(scores - log_block[..., None])
            value_part = jnp.einsum(
                "hqk,qhd->khd",
                probs.astype(jnp.bfloat16),
                grad_block,
                preferred_element_type=jnp.float32,
            )
            prob_grad = jnp.einsum(
                "qhd,khd->hqk", grad_block, value_heads, preferred_element_type=jnp.float32
            )
            score_grad = (probs * (prob_grad - delta_block[..., None])).astype(jnp.bfloat16)
            query_part = (
                jnp.einsum(
                    "hqk,khd->qhd", score_grad, key_heads, preferred_element_type=jnp.float32
                )
                * score_scale
            )
            key_part = (
                jnp.einsum(
                    "hqk,qhd->khd", score_grad, query_block, preferred_element_type=jnp.float32
                )
                * score_scale
            )
            return (carry + jnp.stack([key_part, value_part], axis=1), query_part)

        grad_pair, query_part = lax.scan(
            visit, grad_pair, (block_ids, q_blocks, grad_blocks, log_total, delta)
        )
        query_grad = query_grad + query_part
    grad_pair = pass_grads(grad_pair)
    head_grads = jnp.concatenate(
        [query_grad.reshape(block_len, 1, head_local, HEAD), grad_pair], axis=1
    ).astype(jnp.bfloat16)
    token_grads = lax.all_to_all(
        head_grads.reshape(block_len, 1, 3 * group_width),
        "aa",
        split_axis=0,
        concat_axis=1,
        tiled=True,
    )
    token_grads = token_grads.reshape(tok_rows, groups, 3, group_width)
    query_tok = token_grads[:, :, 0].reshape(tok_rows, width)
    key_tok = token_grads[:, :, 1].reshape(tok_rows, width)
    value_tok = token_grads[:, :, 2].reshape(tok_rows, width)
    input_grad = grad_one
    input_grad = input_grad + jnp.einsum(
        "td,cd->tc", query_tok, full_query, preferred_element_type=jnp.float32
    )
    input_grad = input_grad + jnp.einsum(
        "td,cd->tc", key_tok, full_key, preferred_element_type=jnp.float32
    )
    input_grad = input_grad + jnp.einsum(
        "td,cd->tc", value_tok, full_value, preferred_element_type=jnp.float32
    )
    qkv_summed = reduce_gradients(
        [token_rows], [query_tok, key_tok, value_tok], QKV_DOTS, QKV_WIDTHS, None, 2
    )[0]
    return (
        result.astype(jnp.bfloat16)[None],
        input_grad.astype(jnp.bfloat16)[None],
        square_out(qkv_summed, 0),
        square_out(qkv_summed, 1),
        square_out(qkv_summed, 2),
        grad_out_weight,
        norm_total[0],
        norm_total[1],
        grad_in,
        grad_down,
        norm_total[2],
        norm_total[3],
    )


def solution(mesh):
    return jax.shard_map(
        shards,
        mesh=mesh,
        in_specs=(
            P("shard", ("blk", "aa"), None),
            P("shard", None),
            P("shard", None),
            P("shard", None),
            P("shard", None),
            P("shard", None),
            P("shard", None),
            P("shard"),
            P("shard"),
            P("shard", None),
            P("shard", None),
            P("shard"),
            P("shard"),
            P("shard", ("blk", "aa"), None),
        ),
        out_specs=(
            P("shard", ("blk", "aa"), None),
            P("shard", ("blk", "aa"), None),
            P("shard", None),
            P("shard", None),
            P("shard", None),
            P("shard", None),
            P("shard"),
            P("shard"),
            P("shard", None),
            P("shard", None),
            P("shard"),
            P("shard"),
        ),
        check_vma=False,
    )
```

```python
import functools

import jax
import jax.numpy as jnp
from jax import lax
from jax.experimental import pallas as pl
from jax.experimental.pallas import tpu as pltpu
from jax.sharding import PartitionSpec as P

HEADS = 16
HEAD = 64
MASKED_SCORE = -1e30
NORM_EPSILON = 1e-05
QUERY_BLOCK = 512
PARTS = 1
BLOCK_LEN = 2048
KEY_BLOCK = 1024


def spans(segments, valid):
    numbers = jnp.arange(36, dtype=jnp.int32)
    before = jnp.sum((segments[None, :] < numbers[:, None]).astype(jnp.int32), axis=1)
    live = jnp.sum(valid)
    picked = segments[:, None] == numbers[None, :35]
    first = jnp.sum(jnp.where(picked, before[None, :35], 0), axis=1)
    last = jnp.sum(jnp.where(picked, before[None, 1:], 0), axis=1)
    return (first, last, jnp.minimum(last, live))


def block_plan(first, last, live, query_start, count):
    mine = [lax.dynamic_slice_in_dim(a, query_start, count) for a in (first, last, live)]
    low = mine[0].reshape(-1, QUERY_BLOCK)
    high = mine[1].reshape(-1, QUERY_BLOCK)
    end = mine[2].reshape(-1, QUERY_BLOCK)
    begin = low[:, 0] // KEY_BLOCK
    stop = -(-high[:, -1] // KEY_BLOCK)
    single = low[:, 0] == low[:, -1]
    full_from = -(-low[:, 0] // KEY_BLOCK)
    full_to = end[:, 0] // KEY_BLOCK
    some = single & (full_to > full_from)
    full_from = jnp.where(some, full_from, stop)
    full_to = jnp.where(some, full_to, stop)
    return (jnp.stack([begin, full_from, full_to, stop]), mine[0], mine[2])


def slot_of(j, blk):
    per = BLOCK_LEN // KEY_BLOCK
    at = ((j // per) ^ blk) * per + j % per
    return pl.ds(pl.multiple_of(at * KEY_BLOCK, KEY_BLOCK), KEY_BLOCK)


def attend_kernel(plan_ref, start_ref, q_ref, kv_ref, kvt_ref, low_ref, end_ref, o_ref, lse_ref):
    i = pl.program_id(0)
    low, end = (low_ref[0:1], end_ref[0:1])
    place_q = start_ref[0] + i * QUERY_BLOCK + lax.broadcasted_iota(jnp.int32, (1, QUERY_BLOCK), 1)
    split = QUERY_BLOCK // PARTS

    def step(j, carry, masked):
        here = slot_of(j, start_ref[1])
        keys = kv_ref[here]
        keys_t = kvt_ref[:, here]
        done = []
        for part, (top, total, summed) in enumerate(carry):
            cols = slice(part * split, (part + 1) * split)
            scores = lax.dot_general(
                keys, q_ref[cols], (((1,), (1,)), ((), ())), preferred_element_type=jnp.float32
            )
            if masked:
                place_k = j * KEY_BLOCK + lax.broadcasted_iota(jnp.int32, scores.shape, 0)
                allowed = (place_k >= low[:, cols]) & (place_k < end[:, cols])
                allowed = allowed | (place_k == place_q[:, cols])
                scores = jnp.where(allowed, scores, MASKED_SCORE)
            new_top = jnp.maximum(top, jnp.max(scores, axis=0, keepdims=True))
            weights = jnp.exp(scores - new_top)
            factor = jnp.exp(top - new_top)
            total = total * factor + jnp.sum(weights, axis=0, keepdims=True)
            summed = summed * factor + jnp.dot(
                keys_t, weights.astype(jnp.bfloat16), preferred_element_type=jnp.float32
            )
            done.append((new_top, total, summed))
        return tuple(done)

    carry = tuple(
        (
            jnp.full((1, split), MASKED_SCORE, jnp.float32),
            jnp.zeros((1, split), jnp.float32),
            jnp.zeros((128, split), jnp.float32),
        )
        for _ in range(PARTS)
    )
    masked_step = functools.partial(step, masked=True)
    carry = lax.fori_loop(plan_ref[0, i], plan_ref[1, i], masked_step, carry)
    carry = lax.fori_loop(
        plan_ref[1, i], plan_ref[2, i], functools.partial(step, masked=False), carry
    )
    carry = lax.fori_loop(plan_ref[2, i], plan_ref[3, i], masked_step, carry)
    for part, (top, total, summed) in enumerate(carry):
        cols = slice(part * split, (part + 1) * split)
        o_ref[cols] = jnp.transpose(summed / total)
        lse_ref[:, cols] = jnp.broadcast_to(top + jnp.log(total), (8, split))


def attend(plan, query_start, queries, pairs, low, end):
    count = queries.shape[0]
    blocks = count // QUERY_BLOCK
    row = pl.BlockSpec((8, QUERY_BLOCK), lambda i, *_: (0, i))
    return pl.pallas_call(
        attend_kernel,
        out_shape=[
            jax.ShapeDtypeStruct((count, 128), jnp.float32),
            jax.ShapeDtypeStruct((8, count), jnp.float32),
        ],
        grid_spec=pltpu.PrefetchScalarGridSpec(
            num_scalar_prefetch=2,
            grid=(blocks,),
            in_specs=[
                pl.BlockSpec((QUERY_BLOCK, 128), lambda i, *_: (i, 0)),
                pl.BlockSpec(pairs.shape, lambda i, *_: (0, 0)),
                pl.BlockSpec(pairs.shape[::-1], lambda i, *_: (0, 0)),
                row,
                row,
            ],
            out_specs=[pl.BlockSpec((QUERY_BLOCK, 128), lambda i, *_: (i, 0)), row],
        ),
        compiler_params=pltpu.CompilerParams(vmem_limit_bytes=56 * 2**20),
    )(
        plan,
        query_start,
        queries,
        pairs,
        pairs.T,
        jnp.broadcast_to(low[None], (8, count)),
        jnp.broadcast_to(end[None], (8, count)),
    )


def attend_back_kernel(
    plan_ref, start_ref, q_ref, g_ref, kv_ref, kvt_ref, low_ref, end_ref, lse_ref, delta_ref, dq_ref, dkv_ref
):
    i = pl.program_id(0)

    @pl.when(i == 0)
    def _():
        dkv_ref[...] = jnp.zeros_like(dkv_ref)

    queries, upstream = (q_ref[...], g_ref[...])
    low, end = (low_ref[0:1], end_ref[0:1])
    lse, delta = (lse_ref[0:1], delta_ref[0:1])
    place_q = start_ref[0] + i * QUERY_BLOCK + lax.broadcasted_iota(jnp.int32, (1, QUERY_BLOCK), 1)

    def step(j, query_grad, masked):
        here = slot_of(j, start_ref[1])
        keys = kv_ref[here]
        scores = lax.dot_general(
            keys, queries, (((1,), (1,)), ((), ())), preferred_element_type=jnp.float32
        )
        if masked:
            place_k = j * KEY_BLOCK + lax.broadcasted_iota(jnp.int32, scores.shape, 0)
            allowed = ((place_k >= low) & (place_k < end)) | (place_k == place_q)
            scores = jnp.where(allowed, scores, MASKED_SCORE)
        probs = jnp.exp(scores - lse)
        prob_grad = lax.dot_general(
            keys, upstream, (((1,), (1,)), ((), ())), preferred_element_type=jnp.float32
        )
        score_grad = (probs * (prob_grad - delta)).astype(jnp.bfloat16)
        dkv_ref[here] += jnp.dot(
            score_grad, queries, preferred_element_type=jnp.float32
        ) + jnp.dot(probs.astype(jnp.bfloat16), upstream, preferred_element_type=jnp.float32)
        return query_grad + jnp.dot(
            kvt_ref[:, here], score_grad, preferred_element_type=jnp.float32
        )

    masked_step = functools.partial(step, masked=True)
    grad = jnp.zeros((128, QUERY_BLOCK), jnp.float32)
    grad = lax.fori_loop(plan_ref[0, i], plan_ref[1, i], masked_step, grad)
    grad = lax.fori_loop(
        plan_ref[1, i], plan_ref[2, i], functools.partial(step, masked=False), grad
    )
    grad = lax.fori_loop(plan_ref[2, i], plan_ref[3, i], masked_step, grad)
    dq_ref[...] = jnp.transpose(grad)


def attend_back(plan, query_start, queries, upstream, pairs, low, end, lse, delta):
    count = queries.shape[0]
    blocks = count // QUERY_BLOCK
    rows = [
        jnp.broadcast_to(low[None], (8, count)),
        jnp.broadcast_to(end[None], (8, count)),
        lse,
        jnp.broadcast_to(delta[None], (8, count)),
    ]
    wide = pl.BlockSpec((QUERY_BLOCK, 128), lambda i, *_: (i, 0))
    row = pl.BlockSpec((8, QUERY_BLOCK), lambda i, *_: (0, i))
    whole = pl.BlockSpec(pairs.shape, lambda i, *_: (0, 0))
    flat = pl.BlockSpec(pairs.shape[::-1], lambda i, *_: (0, 0))
    return pl.pallas_call(
        attend_back_kernel,
        out_shape=[
            jax.ShapeDtypeStruct((count, 128), jnp.float32),
            jax.ShapeDtypeStruct(pairs.shape, jnp.float32),
        ],
        grid_spec=pltpu.PrefetchScalarGridSpec(
            num_scalar_prefetch=2,
            grid=(blocks,),
            in_specs=[wide, wide, whole, flat, row, row, row, row],
            out_specs=[wide, whole],
        ),
        compiler_params=pltpu.CompilerParams(vmem_limit_bytes=56 * 2**20),
    )(plan, query_start, queries, upstream, pairs, pairs.T, *rows)


MESH = pl.DeviceIdType.MESH
ROWS = 512
REDUCE_DIMS = ("xa", "ya", "za", "yb", "zb")
GATHER_DIMS = ("ya", "za", "yb", "zb")


def place():
    shard = lax.axis_index("shard")
    blk = lax.axis_index("blk")
    aa = lax.axis_index("aa")
    return (shard, blk // 2, blk % 2, aa // 4, aa % 4)


def flipped(i):
    return i + 1 - 2 * (i % 2)


def partner(dim):
    shard, x_lo, core, z, y = place()
    if dim == "core":
        core = 1 - core
    elif dim == "xa":
        x_lo = 1 - x_lo
    elif dim == "xb":
        shard, x_lo = 1 - shard, 1 - x_lo
    elif dim == "ya":
        y = flipped(y)
    elif dim == "yb":
        y = 3 - y
    elif dim == "za":
        z = flipped(z)
    else:
        z = 3 - z
    return (shard, x_lo * 2 + core, z * 4 + y)


def ring_bit(dim):
    shard, x_lo, _, z, y = place()
    if dim == "xa":
        return (shard * 2 + x_lo + shard) % 2
    if dim == "ya":
        return (y + y // 2) % 2
    if dim == "yb":
        return y // 2
    if dim == "za":
        return (z + z // 2) % 2
    return z // 2


def greet(dims):
    barrier = pltpu.get_barrier_semaphore()
    for dim in dims:
        pl.semaphore_signal(barrier, inc=1, device_id=partner(dim), device_id_type=MESH)
    pl.semaphore_wait(barrier, len(dims))


def remote(src, dst, send_sem, recv_sem, dim):
    return pltpu.make_async_remote_copy(
        src_ref=src,
        dst_ref=dst,
        send_sem=send_sem,
        recv_sem=recv_sem,
        device_id=partner(dim),
        device_id_type=MESH,
    )


def row_starts(dims, rows):
    starts, at, size = ([0], 0, rows)
    for dim in dims:
        size //= 2
        at = at + ring_bit(dim) * size
        starts.append(at)
    return starts


def rotated(dims, by):
    return dims[by:] + dims[:by]


def gather_kernel(shapes, targets, n_out, *refs):
    n = len(shapes)
    ins, outs = (refs[:n], refs[n : n + n_out])
    send, recv, own_in, own_out = refs[n + n_out : n + n_out + 4]
    bounce = refs[n + n_out + 4 :]
    shard, _, core, _, _ = place()
    greet(("xb", "core") + GATHER_DIMS)
    sent = []

    def start(copy):
        copy.start()
        sent.append(copy)

    locals_ = []
    for i, (rows, cols) in enumerate(shapes):
        out, off = targets[i]
        inward = pltpu.make_async_copy(ins[i], bounce[i], own_in.at[i])
        inward.start()
        outward = pltpu.make_async_copy(
            bounce[i],
            outs[out].at[pl.ds(pl.multiple_of(shard * rows, rows), rows), pl.ds(off, cols)],
            own_out.at[i],
        )
        locals_.append((inward, outward))

    def block(i, part, base, at, size, inner=False):
        rows, cols = shapes[i]
        out, off = targets[i]
        width = cols // 8
        col = pl.multiple_of(core * (cols // 2) + part * width, 128)
        if inner:
            return ins[i].at[pl.ds(pl.multiple_of(at, 16), size), pl.ds(col, width)]
        col = pl.multiple_of(core * (cols // 2) + (off + part * width), 128)
        at = pl.multiple_of(base * rows + at, 16)
        return outs[out].at[pl.ds(at, size), pl.ds(col, width)]

    other = 1 - shard
    plan = {}
    for i, (rows, _) in enumerate(shapes):
        for part in range(4):
            order = rotated(GATHER_DIMS, part)
            starts = row_starts(order, rows)
            piece = rows // 16
            copy = remote(
                block(i, part, 0, starts[4], piece, inner=True),
                block(i, part, shard, starts[4], piece),
                send.at[i, part, 0],
                recv.at[i, part, 0],
                "xb",
            )
            start(copy)
            plan[i, part] = (order, starts, copy)
    for inward, outward in locals_:
        inward.wait()
        outward.start()
    siblings = []
    for stage in range(1, 6):
        for i, (rows, _) in enumerate(shapes):
            for part in range(4):
                order, starts, copy = plan[i, part]
                copy.wait_recv()
                if stage < 5:
                    k = 4 - stage
                    size = rows >> (k + 1)
                    mine = block(i, part, other, starts[k + 1], size)
                    copy = remote(
                        mine, mine, send.at[i, part, stage], recv.at[i, part, stage], order[k]
                    )
                    start(copy)
                    plan[i, part] = (order, starts, copy)
                if stage >= 4:
                    size = rows // 2
                    at = starts[1] if stage == 4 else size - starts[1]
                    mine = block(i, part, other, at, size)
                    copy = remote(
                        mine, mine, send.at[i, part, stage + 1], recv.at[i, part, stage + 1], "core"
                    )
                    start(copy)
                    siblings.append(copy)
    for copy in siblings:
        copy.wait_recv()
    for copy in sent:
        copy.wait_send()
    for _, outward in locals_:
        outward.wait()


def gather_weights(arrays, targets, out_shapes, collective_id):
    shapes = [a.shape for a in arrays]
    n = len(shapes)
    return pl.pallas_call(
        functools.partial(gather_kernel, shapes, targets, len(out_shapes)),
        out_shape=[jax.ShapeDtypeStruct(shape, jnp.bfloat16) for shape in out_shapes],
        in_specs=[pl.BlockSpec(memory_space=pl.ANY)] * n,
        out_specs=[pl.BlockSpec(memory_space=pl.ANY)] * len(out_shapes),
        scratch_shapes=[
            pltpu.SemaphoreType.DMA((n, 4, 7)),
            pltpu.SemaphoreType.DMA((n, 4, 7)),
            pltpu.SemaphoreType.DMA((n,)),
            pltpu.SemaphoreType.DMA((n,)),
            *[pltpu.VMEM(shape, jnp.bfloat16) for shape in shapes],
        ],
        compiler_params=pltpu.CompilerParams(
            collective_id=collective_id, has_side_effects=True, vmem_limit_bytes=40 * 2**20
        ),
    )(*arrays)


def reduce_kernel(n_left, dots, widths, with_norm, *refs):
    refs = list(refs)

    def take(count):
        taken = refs[:count]
        del refs[:count]
        return taken

    n_right = len(dots_rights(dots))
    lefts, rights = (take(n_left), take(n_right))
    norm_in = take(1)[0] if with_norm else None
    out = take(1)[0]
    norm_out = take(1)[0] if with_norm else None
    left_all, right_all = (take(n_left), take(n_right))
    partial = take(1)[0]
    landed = take(6)
    norm_held, norm_landed = take(2) if with_norm else (None, None)
    act_send, act_recv, red_send, red_recv, gat_send, gat_recv, nrm_send, nrm_recv = refs
    shard, _, core, _, _ = place()
    greet(("core", "xa", "xb", "ya", "yb", "za", "zb"))
    sent = []

    def start(copy):
        copy.start()
        sent.append(copy)
        return copy

    half_tokens = lefts[0].shape[0]
    acts = []
    for i, (src, dst) in enumerate(zip(lefts, left_all)):
        acts.append(
            start(
                remote(
                    src,
                    dst.at[pl.ds(half_tokens, half_tokens)],
                    act_send.at[i],
                    act_recv.at[i],
                    "core",
                )
            )
        )
    for i, (src, dst) in enumerate(zip(rights, right_all)):
        half = src.shape[1] // 2
        theirs = pl.ds(pl.multiple_of((1 - core) * half, half), half)
        acts.append(
            start(
                remote(
                    src.at[:, theirs],
                    dst.at[pl.ds(half_tokens, half_tokens)],
                    act_send.at[n_left + i],
                    act_recv.at[n_left + i],
                    "core",
                )
            )
        )
    norm_dims = ("core",) + REDUCE_DIMS + ("xb",)
    norm_copies = []

    def norm_start(k):
        if not with_norm:
            return
        if k < 6:
            src, dst = (norm_held.at[k], norm_landed.at[k])
        else:
            src, dst = (norm_held.at[6, pl.ds(1 - shard, 1)], norm_landed.at[6, pl.ds(0, 1)])
        norm_copies.append(
            start(remote(src, dst, nrm_send.at[k], nrm_recv.at[k], norm_dims[k]))
        )

    def norm_finish(k):
        if not with_norm:
            return
        norm_copies[k].wait_recv()
        if k < 6:
            norm_held[k + 1] = norm_held[k] + norm_landed[k]
        else:
            norm_out[...] = norm_held[6, shard] + norm_landed[6, 0]

    if with_norm:
        norm_held[0] = norm_in[...]
    norm_start(0)
    for src, dst in zip(lefts, left_all):
        dst[pl.ds(0, half_tokens)] = src[...]
    for src, dst in zip(rights, right_all):
        half = src.shape[1] // 2
        dst[pl.ds(0, half_tokens)] = src[:, pl.ds(pl.multiple_of(core * half, half), half)]
    for copy in acts:
        copy.wait_recv()
    norm_finish(0)
    norm_start(1)
    edges = [0]
    for width in widths:
        edges.append(edges[-1] + width)
    parts = range(len(widths))
    cols = [pl.ds(edges[p], widths[p]) for p in parts]
    orders = [rotated(REDUCE_DIMS, p) for p in parts]
    starts = [row_starts(orders[p], ROWS) for p in parts]
    moving = {}

    def reduce_start(p, k):
        if k < 5:
            half = ROWS >> (k + 1)
            away = pl.multiple_of(starts[p][k] + (half - (starts[p][k + 1] - starts[p][k])), 16)
            src = partial.at[:, pl.ds(away, half), cols[p]]
            dst = landed[k].at[:, :, cols[p]]
            dim = orders[p][k]
        else:
            at = pl.multiple_of(starts[p][5], 16)
            src = partial.at[1 - shard, pl.ds(at, 16), cols[p]]
            dst = landed[5].at[:, cols[p]]
            dim = "xb"
        moving[p] = start(remote(src, dst, red_send.at[p, k], red_recv.at[p, k], dim))

    def reduce_add(p, k):
        moving[p].wait_recv()
        if k < 5:
            half = ROWS >> (k + 1)
            step = min(half, 32)

            def add(i, carry):
                here = pl.ds(pl.multiple_of(i * step, step), step)
                there = pl.ds(pl.multiple_of(starts[p][k + 1] + i * step, 16), step)
                total = partial[:, there, cols[p]].astype(jnp.float32)
                total = total + landed[k][:, here, cols[p]].astype(jnp.float32)
                partial[:, there, cols[p]] = total.astype(jnp.bfloat16)
                return carry

            lax.fori_loop(0, half // step, add, 0)
        else:
            here = pl.ds(pl.multiple_of(starts[p][5], 16), 16)
            total = partial[shard, here, cols[p]].astype(jnp.float32)
            total = total + landed[5][:, cols[p]].astype(jnp.float32)
            out[core, here, cols[p]] = total.astype(jnp.bfloat16)

    ready = 0
    for at, (left, left_step, left_off, right, right_off) in enumerate(dots):
        for s in range(2):
            product = lax.dot_general(
                left_all[left][:, pl.ds(s * left_step + left_off, ROWS)],
                right_all[right][:, pl.ds(right_off, 512)],
                (((0,), (0,)), ((), ())),
                preferred_element_type=jnp.float32,
            )
            partial[s, :, pl.ds(at * 512, 512)] = product.astype(jnp.bfloat16)
        while ready < len(widths) and edges[ready + 1] <= (at + 1) * 512:
            reduce_start(ready, 0)
            ready += 1
    for k in range(6):
        norm_finish(k + 1)
        if k < 5:
            norm_start(k + 2)
        for p in parts:
            reduce_add(p, k)
            if k < 5:
                reduce_start(p, k + 1)

    def range_of(p, at, size):
        return out.at[core, pl.ds(pl.multiple_of(at, 16), size), cols[p]]

    def gather_start(p, k):
        mine = range_of(p, starts[p][k + 1], ROWS >> (k + 1))
        moving[p] = start(
            remote(mine, mine, gat_send.at[p, k], gat_recv.at[p, k], orders[p][k])
        )

    shared = []

    def share(p, slot, at):
        mine = range_of(p, at, ROWS // 2)
        shared.append(
            start(remote(mine, mine, gat_send.at[p, 5 + slot], gat_recv.at[p, 5 + slot], "core"))
        )

    for p in parts:
        gather_start(p, 4)
    for k in range(4, -1, -1):
        for p in parts:
            moving[p].wait_recv()
            if k > 0:
                gather_start(p, k - 1)
            if k == 1:
                share(p, 0, starts[p][1])
            if k == 0:
                share(p, 1, ROWS // 2 - starts[p][1])
    for copy in shared:
        copy.wait_recv()
    for copy in sent:
        copy.wait_send()


def dots_rights(dots):
    return sorted({d[3] for d in dots})


def reduce_gradients(lefts, rights, dots, widths, norm, collective_id):
    tokens = lefts[0].shape[0]
    total = sum(widths)
    out_shape = [jax.ShapeDtypeStruct((2, ROWS, total), jnp.bfloat16)]
    scratch = [pltpu.VMEM((2 * tokens, a.shape[1]), jnp.bfloat16) for a in lefts]
    scratch += [pltpu.VMEM((2 * tokens, a.shape[1] // 2), jnp.bfloat16) for a in rights]
    scratch += [pltpu.VMEM((2, ROWS, total), jnp.bfloat16)]
    scratch += [pltpu.VMEM((2, ROWS >> (k + 1), total), jnp.bfloat16) for k in range(5)]
    scratch += [pltpu.VMEM((16, total), jnp.bfloat16)]
    operands = [*lefts, *rights]
    if norm is not None:
        operands.append(norm)
        out_shape.append(jax.ShapeDtypeStruct(norm.shape[1:], jnp.float32))
        scratch += [
            pltpu.VMEM((7, *norm.shape), jnp.float32),
            pltpu.VMEM((7, *norm.shape), jnp.float32),
        ]
    n_act, parts = (len(lefts) + len(rights), len(widths))
    scratch += [pltpu.SemaphoreType.DMA((n_act,))] * 2
    scratch += [pltpu.SemaphoreType.DMA((parts, 6))] * 2
    scratch += [pltpu.SemaphoreType.DMA((parts, 7))] * 2
    scratch += [pltpu.SemaphoreType.DMA((7,))] * 2
    return pl.pallas_call(
        functools.partial(reduce_kernel, len(lefts), dots, widths, norm is not None),
        out_shape=out_shape,
        in_specs=[pl.BlockSpec(memory_space=pltpu.VMEM)] * len(operands),
        out_specs=[pl.BlockSpec(memory_space=pltpu.VMEM)] * len(out_shape),
        scratch_shapes=scratch,
        compiler_params=pltpu.CompilerParams(
            collective_id=collective_id, has_side_effects=True, vmem_limit_bytes=60 * 2**20
        ),
    )(*operands)


FF_DOTS = tuple(
    [(0, 512, 0, 0, j * 512) for j in range(4)]
    + [(1, 2048, q * 512, 1, 0) for q in range(4)]
    + [(2, 512, 0, 2, 0)]
)
FF_WIDTHS = (1024, 896, 896, 896, 896)
QKV_DOTS = ((0, 512, 0, 0, 0), (0, 512, 0, 1, 0), (0, 512, 0, 2, 0))
QKV_WIDTHS = (384, 384, 256, 256, 256)


def cast_kernel(x_ref, o_ref):
    o_ref[...] = x_ref[0].astype(jnp.float32)


def cast_out(gathered, shape, grid, index_in, index_out):
    return pl.pallas_call(
        cast_kernel,
        out_shape=jax.ShapeDtypeStruct(shape, jnp.float32),
        grid=grid,
        in_specs=[pl.BlockSpec((1, ROWS, 512), index_in)],
        out_specs=pl.BlockSpec((ROWS, 512), index_out),
    )(gathered)


def square_out(gathered, slot):
    return cast_out(gathered, (ROWS, 1024), (2,), lambda c: (c, 0, slot), lambda c: (0, c))


def ff_grads_out(gathered):
    grad_in = cast_out(
        gathered, (ROWS, 4096), (2, 4), lambda c, j: (c, 0, j), lambda c, j: (0, c * 4 + j)
    )
    grad_down = cast_out(
        gathered, (2048, 1024), (4, 2), lambda q, c: (c, 0, 4 + q), lambda q, c: (q, c)
    )
    return (grad_in, grad_down, square_out(gathered, 8))


def normalize(summed_in, norm_gain, norm_bias):
    row_mean = jnp.mean(summed_in, axis=-1, keepdims=True)
    centred = summed_in - row_mean
    inv_std = lax.rsqrt(jnp.mean(centred * centred, axis=-1, keepdims=True) + NORM_EPSILON)
    scaled = centred * inv_std
    return (scaled * norm_gain + norm_bias, scaled, inv_std)


def normalize_back(upstream, scaled, inv_std, norm_gain):
    weighted = upstream * norm_gain
    centred = weighted - jnp.mean(weighted, axis=-1, keepdims=True)
    result = inv_std * (centred - scaled * jnp.mean(weighted * scaled, axis=-1, keepdims=True))
    return (result, jnp.sum(upstream * scaled, axis=0), jnp.sum(upstream, axis=0))


def exact_gelu(values):
    return jax.nn.gelu(values, approximate=False)


def neighbour(value, bit):
    flips = [(i, i ^ bit) for i in range(4)]
    return lax.ppermute(value, "blk", flips)


def project_kernel(x_ref, w_ref, o_ref):
    for piece in range(2):
        cols = pl.ds(piece * 512, 512)
        q, k, v = [
            jnp.dot(
                x_ref[...],
                w_ref[:, pl.ds(which * 1024 + piece * 512, 512)],
                preferred_element_type=jnp.float32,
            )
            for which in range(3)
        ]
        q = (q.astype(jnp.bfloat16).astype(jnp.float32) * HEAD ** (-0.5)).astype(jnp.bfloat16)
        k, v = (k.astype(jnp.bfloat16), v.astype(jnp.bfloat16))
        for h in range(8):
            at = slice(h * HEAD, (h + 1) * HEAD)
            head = piece * 8 + h
            o_ref[head, 0:128] = jnp.concatenate([k[:, at], v[:, at]], axis=1)
            o_ref[head, 128:192] = jnp.concatenate([q[0:64, at], q[64:128, at]], axis=1)


def project(token_rows, full_qkv):
    return pl.pallas_call(
        project_kernel,
        out_shape=jax.ShapeDtypeStruct((HEADS, 192, 128), jnp.bfloat16),
        compiler_params=pltpu.CompilerParams(vmem_limit_bytes=32 * 2**20),
    )(token_rows, full_qkv)


def unfold(packed):
    n = packed.shape[0]
    return packed.reshape(n, 64, 2, HEAD).transpose(0, 2, 1, 3).reshape(n * 128, HEAD)


def fold(rows):
    n = rows.shape[0] // 128
    return rows.reshape(n, 2, 64, HEAD).transpose(0, 2, 1, 3).reshape(n, 64, 2 * HEAD)


def to_tokens(packed):
    return packed.reshape(HEADS, 64, 2, HEAD).transpose(2, 1, 0, 3).reshape(128, HEADS * HEAD)


def to_heads(rows):
    return rows.reshape(2, 64, HEADS, HEAD).transpose(2, 1, 0, 3).reshape(HEADS, 64, 2 * HEAD)


def swap(packed):
    return lax.all_to_all(packed, "aa", split_axis=0, concat_axis=0, tiled=True)


def shards(
    tokens,
    segments,
    valid,
    w_query,
    w_key,
    w_value,
    w_out,
    norm1_gain,
    norm1_bias,
    w_in,
    w_down,
    norm2_gain,
    norm2_bias,
    cotangent,
):
    packed = jnp.zeros((16, 512), jnp.bfloat16).at[:4].set(
        jnp.stack([norm1_gain, norm1_bias, norm2_gain, norm2_bias])
    )
    full_qkv, full_out, full_in, full_down = gather_weights(
        [w_query, w_key, w_value, w_out, w_in, w_down],
        [(0, 0), (0, 1024), (0, 2048), (1, 0), (2, 0), (3, 0)],
        [(1024, 3072), (1024, 1024), (1024, 4096), (4096, 1024)],
        0,
    )
    norms = lax.all_gather(packed, "shard", axis=1, tiled=True)[:4].astype(jnp.float32)
    gain_one, bias_one, gain_two, bias_two = norms
    token_rows = tokens[0]
    blk = lax.axis_index("blk")
    query_start = blk * BLOCK_LEN
    place = jnp.stack([query_start, blk]).astype(jnp.int32)
    plan, low, end = block_plan(*spans(segments[0], valid[0]), query_start, BLOCK_LEN)

    heads_all = swap(project(token_rows, full_qkv))
    own_pair = heads_all[:, 0:128].reshape(BLOCK_LEN, 128)
    queries = jnp.pad(unfold(heads_all[:, 128:192]), ((0, 0), (0, HEAD)))
    far_pair = neighbour(own_pair, 2)
    pairs = jnp.concatenate([own_pair, neighbour(own_pair, 1), far_pair, neighbour(far_pair, 1)])
    summed, lse = attend(plan, place, queries, pairs, low, end)
    attn_heads = summed[:, HEAD:]
    mixed = to_tokens(swap(fold(attn_heads.astype(jnp.bfloat16))))

    attn = jnp.dot(mixed, full_out, preferred_element_type=jnp.float32)
    first, scaled_one, inv_one = normalize(
        token_rows.astype(jnp.float32) + attn, gain_one, bias_one
    )
    first_low = first.astype(jnp.bfloat16)
    pre = jnp.dot(first_low, full_in, preferred_element_type=jnp.float32)
    hidden = exact_gelu(pre).astype(jnp.bfloat16)
    ff_out = jnp.dot(hidden, full_down, preferred_element_type=jnp.float32)
    result, scaled_two, inv_two = normalize(first + ff_out, gain_two, bias_two)
    upstream = cotangent[0].astype(jnp.float32)
    grad_two, grad_gain_two, grad_bias_two = normalize_back(upstream, scaled_two, inv_two, gain_two)
    ff_grad = grad_two.astype(jnp.bfloat16)
    hidden_grad = jnp.einsum("td,fd->tf", ff_grad, full_down, preferred_element_type=jnp.float32)
    gelu_pull = jax.vjp(exact_gelu, pre)[1]
    pre_grad = gelu_pull(hidden_grad)[0].astype(jnp.bfloat16)
    first_grad = grad_two + jnp.einsum(
        "tf,df->td", pre_grad, full_in, preferred_element_type=jnp.float32
    )
    grad_one, grad_gain_one, grad_bias_one = normalize_back(
        first_grad, scaled_one, inv_one, gain_one
    )
    attn_grad = grad_one.astype(jnp.bfloat16)
    mixed_grad = jnp.einsum(
        "td,cd->tc", attn_grad, full_out, preferred_element_type=jnp.float32
    ).astype(jnp.bfloat16)
    norm_sums = jnp.stack([grad_gain_one, grad_bias_one, grad_gain_two, grad_bias_two])
    norm_sums = jnp.pad(norm_sums.reshape(4, 2, 512).transpose(1, 0, 2), ((0, 0), (0, 4), (0, 0)))

    head_grads = unfold(swap(to_heads(mixed_grad)))
    delta = jnp.sum(head_grads.astype(jnp.float32) * attn_heads, axis=-1)
    wide_grads = jnp.pad(head_grads, ((0, 0), (HEAD, 0)))
    query_grad, pair_grads = attend_back(
        plan, place, queries, wide_grads, pairs, low, end, lse, delta
    )
    pair_grads = pair_grads.reshape(4, BLOCK_LEN, 128)
    theirs = neighbour(pair_grads[1::2].astype(jnp.bfloat16), 1).astype(jnp.float32)
    near = pair_grads[0::2] + theirs
    own_grad = near[0] + neighbour(near[1].astype(jnp.bfloat16), 2).astype(jnp.float32)
    query_grad = fold((query_grad[:, :HEAD] * HEAD ** (-0.5)).astype(jnp.bfloat16))
    own_grad = own_grad.astype(jnp.bfloat16).reshape(16, 128, 128)
    token_grads = swap(jnp.concatenate([own_grad, query_grad], axis=1))
    query_tok = to_tokens(token_grads[:, 128:192])
    key_tok = token_grads[:, 0:128, :HEAD].transpose(1, 0, 2).reshape(128, 1024)
    value_tok = token_grads[:, 0:128, HEAD:].transpose(1, 0, 2).reshape(128, 1024)

    ff_summed, norm_total = reduce_gradients(
        [first_low, hidden, mixed],
        [pre_grad, ff_grad, attn_grad],
        FF_DOTS,
        FF_WIDTHS,
        norm_sums,
        1,
    )
    grad_in, grad_down, grad_out = ff_grads_out(ff_summed)
    all_tok = jnp.concatenate([query_tok, key_tok, value_tok], axis=1)
    input_grad = grad_one + jnp.einsum(
        "td,cd->tc", all_tok, full_qkv, preferred_element_type=jnp.float32
    )
    qkv_summed = reduce_gradients(
        [token_rows], [query_tok, key_tok, value_tok], QKV_DOTS, QKV_WIDTHS, None, 2
    )[0]
    return (
        result.astype(jnp.bfloat16)[None],
        input_grad.astype(jnp.bfloat16)[None],
        square_out(qkv_summed, 0),
        square_out(qkv_summed, 1),
        square_out(qkv_summed, 2),
        grad_out,
        norm_total[0],
        norm_total[1],
        grad_in,
        grad_down,
        norm_total[2],
        norm_total[3],
    )


def solution(mesh):
    return jax.shard_map(
        shards,
        mesh=mesh,
        in_specs=(
            P("shard", ("blk", "aa"), None),
            P("shard", None),
            P("shard", None),
            P("shard", None),
            P("shard", None),
            P("shard", None),
            P("shard", None),
            P("shard"),
            P("shard"),
            P("shard", None),
            P("shard", None),
            P("shard"),
            P("shard"),
            P("shard", ("blk", "aa"), None),
        ),
        out_specs=(
            P("shard", ("blk", "aa"), None),
            P("shard", ("blk", "aa"), None),
            P("shard", None),
            P("shard", None),
            P("shard", None),
            P("shard", None),
            P("shard"),
            P("shard"),
            P("shard", None),
            P("shard", None),
            P("shard"),
            P("shard"),
        ),
        check_vma=False,
    )
```

```python
import functools

import jax
import jax.numpy as jnp
from jax import lax
from jax.experimental import pallas as pl
from jax.experimental.pallas import tpu as pltpu
from jax.sharding import PartitionSpec as P

HEADS = 16
HEAD = 64
MASKED_SCORE = -1e30
NORM_EPSILON = 1e-05
QUERY_BLOCK = 512
PARTS = 1
BLOCK_LEN = 2048
KEY_BLOCK = 1024


def spans(segments, valid):
    numbers = jnp.arange(36, dtype=jnp.int32)
    before = jnp.sum((segments[None, :] < numbers[:, None]).astype(jnp.int32), axis=1)
    live = jnp.sum(valid)
    picked = segments[:, None] == numbers[None, :35]
    first = jnp.sum(jnp.where(picked, before[None, :35], 0), axis=1)
    last = jnp.sum(jnp.where(picked, before[None, 1:], 0), axis=1)
    return (first, last, jnp.minimum(last, live))


def block_plan(first, last, live, query_start, count):
    mine = [lax.dynamic_slice_in_dim(a, query_start, count) for a in (first, last, live)]
    low = mine[0].reshape(-1, QUERY_BLOCK)
    high = mine[1].reshape(-1, QUERY_BLOCK)
    end = mine[2].reshape(-1, QUERY_BLOCK)
    begin = low[:, 0] // KEY_BLOCK
    stop = -(-high[:, -1] // KEY_BLOCK)
    single = low[:, 0] == low[:, -1]
    full_from = -(-low[:, 0] // KEY_BLOCK)
    full_to = end[:, 0] // KEY_BLOCK
    some = single & (full_to > full_from)
    full_from = jnp.where(some, full_from, stop)
    full_to = jnp.where(some, full_to, stop)
    return (jnp.stack([begin, full_from, full_to, stop]), mine[0], mine[2])


def slot_of(j, blk):
    per = BLOCK_LEN // KEY_BLOCK
    at = ((j // per) ^ blk) * per + j % per
    return pl.ds(pl.multiple_of(at * KEY_BLOCK, KEY_BLOCK), KEY_BLOCK)


def attend_kernel(plan_ref, start_ref, q_ref, kv_ref, kvt_ref, low_ref, end_ref, o_ref, lse_ref, folded_ref):
    i = pl.program_id(0)
    low, end = (low_ref[0:1], end_ref[0:1])
    place_q = start_ref[0] + i * QUERY_BLOCK + lax.broadcasted_iota(jnp.int32, (1, QUERY_BLOCK), 1)
    split = QUERY_BLOCK // PARTS

    def step(j, carry, masked):
        here = slot_of(j, start_ref[1])
        keys = kv_ref[here]
        keys_t = kvt_ref[:, here]
        done = []
        for part, (top, total, summed) in enumerate(carry):
            cols = slice(part * split, (part + 1) * split)
            scores = lax.dot_general(
                keys, q_ref[cols], (((1,), (1,)), ((), ())), preferred_element_type=jnp.float32
            )
            if masked:
                place_k = j * KEY_BLOCK + lax.broadcasted_iota(jnp.int32, scores.shape, 0)
                allowed = (place_k >= low[:, cols]) & (place_k < end[:, cols])
                allowed = allowed | (place_k == place_q[:, cols])
                scores = jnp.where(allowed, scores, MASKED_SCORE)
            new_top = jnp.maximum(top, jnp.max(scores, axis=0, keepdims=True))
            weights = jnp.exp(scores - new_top)
            factor = jnp.exp(top - new_top)
            total = total * factor + jnp.sum(weights, axis=0, keepdims=True)
            summed = summed * factor + jnp.dot(
                keys_t, weights.astype(jnp.bfloat16), preferred_element_type=jnp.float32
            )
            done.append((new_top, total, summed))
        return tuple(done)

    carry = tuple(
        (
            jnp.full((1, split), MASKED_SCORE, jnp.float32),
            jnp.zeros((1, split), jnp.float32),
            jnp.zeros((128, split), jnp.float32),
        )
        for _ in range(PARTS)
    )
    masked_step = functools.partial(step, masked=True)
    carry = lax.fori_loop(plan_ref[0, i], plan_ref[1, i], masked_step, carry)
    carry = lax.fori_loop(
        plan_ref[1, i], plan_ref[2, i], functools.partial(step, masked=False), carry
    )
    carry = lax.fori_loop(plan_ref[2, i], plan_ref[3, i], masked_step, carry)
    for part, (top, total, summed) in enumerate(carry):
        cols = slice(part * split, (part + 1) * split)
        summed = summed / total
        o_ref[:, cols] = summed
        for c in range(split // 128):
            block = jnp.transpose(summed[:, c * 128 : (c + 1) * 128])
            folded = jnp.concatenate([block[0:64, HEAD:], block[64:128, HEAD:]], axis=1)
            folded_ref[part * (split // 128) + c] = folded.astype(jnp.bfloat16)
        lse_ref[:, cols] = jnp.broadcast_to(top + jnp.log(total), (8, split))


def attend(plan, query_start, queries, pairs, low, end):
    count = queries.shape[0]
    blocks = count // QUERY_BLOCK
    row = pl.BlockSpec((8, QUERY_BLOCK), lambda i, *_: (0, i))
    return pl.pallas_call(
        attend_kernel,
        out_shape=[
            jax.ShapeDtypeStruct((128, count), jnp.float32),
            jax.ShapeDtypeStruct((8, count), jnp.float32),
            jax.ShapeDtypeStruct((count // 128, 64, 128), jnp.bfloat16),
        ],
        grid_spec=pltpu.PrefetchScalarGridSpec(
            num_scalar_prefetch=2,
            grid=(blocks,),
            in_specs=[
                pl.BlockSpec((QUERY_BLOCK, 128), lambda i, *_: (i, 0)),
                pl.BlockSpec(pairs.shape, lambda i, *_: (0, 0)),
                pl.BlockSpec(pairs.shape[::-1], lambda i, *_: (0, 0)),
                row,
                row,
            ],
            out_specs=[
                pl.BlockSpec((128, QUERY_BLOCK), lambda i, *_: (0, i)),
                row,
                pl.BlockSpec((QUERY_BLOCK // 128, 64, 128), lambda i, *_: (i, 0, 0)),
            ],
        ),
        compiler_params=pltpu.CompilerParams(vmem_limit_bytes=56 * 2**20),
    )(
        plan,
        query_start,
        queries,
        pairs,
        pairs.T,
        jnp.broadcast_to(low[None], (8, count)),
        jnp.broadcast_to(end[None], (8, count)),
    )


MESH = pl.DeviceIdType.MESH
ROWS = 512
REDUCE_DIMS = ("xa", "ya", "za", "yb", "zb")
GATHER_DIMS = ("ya", "za", "yb", "zb")


def place():
    shard = lax.axis_index("shard")
    blk = lax.axis_index("blk")
    aa = lax.axis_index("aa")
    return (shard, blk // 2, blk % 2, aa // 4, aa % 4)


def flipped(i):
    return i + 1 - 2 * (i % 2)


def partner(dim):
    shard, x_lo, core, z, y = place()
    if dim == "core":
        core = 1 - core
    elif dim == "xa":
        x_lo = 1 - x_lo
    elif dim == "xb":
        shard, x_lo = 1 - shard, 1 - x_lo
    elif dim == "ya":
        y = flipped(y)
    elif dim == "yb":
        y = 3 - y
    elif dim == "za":
        z = flipped(z)
    else:
        z = 3 - z
    return (shard, x_lo * 2 + core, z * 4 + y)


def ring_bit(dim):
    shard, x_lo, _, z, y = place()
    if dim == "xa":
        return (shard * 2 + x_lo + shard) % 2
    if dim == "ya":
        return (y + y // 2) % 2
    if dim == "yb":
        return y // 2
    if dim == "za":
        return (z + z // 2) % 2
    return z // 2


def greet(dims):
    barrier = pltpu.get_barrier_semaphore()
    for dim in dims:
        pl.semaphore_signal(barrier, inc=1, device_id=partner(dim), device_id_type=MESH)
    pl.semaphore_wait(barrier, len(dims))


def remote(src, dst, send_sem, recv_sem, dim):
    return pltpu.make_async_remote_copy(
        src_ref=src,
        dst_ref=dst,
        send_sem=send_sem,
        recv_sem=recv_sem,
        device_id=partner(dim),
        device_id_type=MESH,
    )


def row_starts(dims, rows):
    starts, at, size = ([0], 0, rows)
    for dim in dims:
        size //= 2
        at = at + ring_bit(dim) * size
        starts.append(at)
    return starts


def rotated(dims, by):
    return dims[by:] + dims[:by]


def gather_kernel(shapes, targets, n_out, *refs):
    n = len(shapes)
    ins, outs = (refs[:n], refs[n : n + n_out])
    send, recv, own_in, own_out = refs[n + n_out : n + n_out + 4]
    bounce = refs[n + n_out + 4 :]
    shard, _, core, _, _ = place()
    greet(("xb", "core") + GATHER_DIMS)
    sent = []

    def start(copy):
        copy.start()
        sent.append(copy)

    locals_ = []
    for i, (rows, cols) in enumerate(shapes):
        out, off = targets[i]
        inward = pltpu.make_async_copy(ins[i], bounce[i], own_in.at[i])
        inward.start()
        outward = pltpu.make_async_copy(
            bounce[i],
            outs[out].at[pl.ds(pl.multiple_of(shard * rows, rows), rows), pl.ds(off, cols)],
            own_out.at[i],
        )
        locals_.append((inward, outward))

    def block(i, part, base, at, size, inner=False):
        rows, cols = shapes[i]
        out, off = targets[i]
        width = cols // 8
        col = pl.multiple_of(core * (cols // 2) + part * width, 128)
        if inner:
            return ins[i].at[pl.ds(pl.multiple_of(at, 16), size), pl.ds(col, width)]
        col = pl.multiple_of(core * (cols // 2) + (off + part * width), 128)
        at = pl.multiple_of(base * rows + at, 16)
        return outs[out].at[pl.ds(at, size), pl.ds(col, width)]

    other = 1 - shard
    plan = {}
    for i, (rows, _) in enumerate(shapes):
        for part in range(4):
            order = rotated(GATHER_DIMS, part)
            starts = row_starts(order, rows)
            piece = rows // 16
            copy = remote(
                block(i, part, 0, starts[4], piece, inner=True),
                block(i, part, shard, starts[4], piece),
                send.at[i, part, 0],
                recv.at[i, part, 0],
                "xb",
            )
            start(copy)
            plan[i, part] = (order, starts, copy)
    for inward, outward in locals_:
        inward.wait()
        outward.start()
    siblings = []
    for stage in range(1, 6):
        for i, (rows, _) in enumerate(shapes):
            for part in range(4):
                order, starts, copy = plan[i, part]
                copy.wait_recv()
                if stage < 5:
                    k = 4 - stage
                    size = rows >> (k + 1)
                    mine = block(i, part, other, starts[k + 1], size)
                    copy = remote(
                        mine, mine, send.at[i, part, stage], recv.at[i, part, stage], order[k]
                    )
                    start(copy)
                    plan[i, part] = (order, starts, copy)
                if stage >= 4:
                    size = rows // 2
                    at = starts[1] if stage == 4 else size - starts[1]
                    mine = block(i, part, other, at, size)
                    copy = remote(
                        mine, mine, send.at[i, part, stage + 1], recv.at[i, part, stage + 1], "core"
                    )
                    start(copy)
                    siblings.append(copy)
    for copy in siblings:
        copy.wait_recv()
    for copy in sent:
        copy.wait_send()
    for _, outward in locals_:
        outward.wait()


def gather_weights(arrays, targets, out_shapes, collective_id):
    shapes = [a.shape for a in arrays]
    n = len(shapes)
    return pl.pallas_call(
        functools.partial(gather_kernel, shapes, targets, len(out_shapes)),
        out_shape=[jax.ShapeDtypeStruct(shape, jnp.bfloat16) for shape in out_shapes],
        in_specs=[pl.BlockSpec(memory_space=pl.ANY)] * n,
        out_specs=[pl.BlockSpec(memory_space=pl.ANY)] * len(out_shapes),
        scratch_shapes=[
            pltpu.SemaphoreType.DMA((n, 4, 7)),
            pltpu.SemaphoreType.DMA((n, 4, 7)),
            pltpu.SemaphoreType.DMA((n,)),
            pltpu.SemaphoreType.DMA((n,)),
            *[pltpu.VMEM(shape, jnp.bfloat16) for shape in shapes],
        ],
        compiler_params=pltpu.CompilerParams(
            collective_id=collective_id, has_side_effects=True, vmem_limit_bytes=40 * 2**20
        ),
    )(*arrays)


BACK_ACTS = 6
BACK_REDUCE = (26, 36, 42, 46, 48, 50)
BACK_GATHER = (64, 60, 55, 53, 51)
UNITS = 64
SLOT_UNITS = 16
BACK_BLOCK = 512


def back_scratch():
    return [
        pltpu.VMEM((BLOCK_LEN, 128), jnp.bfloat16),
        pltpu.VMEM((128, 4 * BLOCK_LEN), jnp.bfloat16),
        pltpu.VMEM((8, BLOCK_LEN), jnp.float32),
        pltpu.VMEM((128, BLOCK_LEN), jnp.float32),
        pltpu.VMEM((4 * BLOCK_LEN, 128), jnp.float32),
        pltpu.VMEM((3, BLOCK_LEN, 128), jnp.bfloat16),
        pltpu.VMEM((3, BLOCK_LEN, 128), jnp.bfloat16),
        pltpu.SemaphoreType.DMA((3,)),
        pltpu.SemaphoreType.DMA((3,)),
    ]


class AttendBack:
    def __init__(self, ins, out, scratch, start):
        self.q, self.packed, self.pairs, self.low, self.end, self.lse, self.o_t = ins
        self.out = out
        self.g, self.pairs_t, self.delta, self.dq, self.dkv = scratch[:5]
        self.away, self.landed, self.send, self.recv = scratch[5:9]
        self.start = start
        self.copies = {}
        self.events = [
            (0, self.begin),
            (SLOT_UNITS, lambda: self.give(3, 0, None, "core")),
            (2 * SLOT_UNITS + 2, lambda: self.give(2, 1, 0, "xa")),
            (3 * SLOT_UNITS, lambda: self.give(1, 2, None, "core")),
        ]

    def begin(self):
        lane = lax.broadcasted_iota(jnp.int32, (64, 128), 1)
        self.delta[...] = jnp.zeros_like(self.delta)
        self.dq[...] = jnp.zeros_like(self.dq)
        self.dkv[...] = jnp.zeros_like(self.dkv)

        def chunk(c, carry):
            block = self.packed[c].astype(jnp.float32)
            moved = jnp.concatenate([block[:, HEAD:], block[:, :HEAD]], axis=1)
            upper = jnp.where(lane >= HEAD, moved, 0.0)
            lower = jnp.where(lane >= HEAD, block, 0.0)
            both = jnp.concatenate([upper, lower], axis=0)
            here = pl.ds(pl.multiple_of(c * 128, 128), 128)
            self.g[here] = both.astype(jnp.bfloat16)
            products = jnp.transpose(both) * self.o_t[:, here]
            total = jnp.sum(products, axis=0, keepdims=True)
            self.delta[:, here] = jnp.broadcast_to(total, (8, 128))
            return carry

        lax.fori_loop(0, 16, chunk, 0)

        def turn(c, carry):
            here = pl.ds(pl.multiple_of(c * 512, 512), 512)
            self.pairs_t[:, here] = jnp.transpose(self.pairs[here])
            return carry

        lax.fori_loop(0, 16, turn, 0)

    def run(self, first, last):
        edge = 3 * SLOT_UNITS
        if first < edge:
            lax.fori_loop(first, min(last, edge), functools.partial(self.unit, own=False), 0)
        if last > edge:
            lax.fori_loop(max(first, edge), last, functools.partial(self.unit, own=True), 0)

    def unit(self, n, carry, own):
        _, x_lo, core, _, _ = place()
        chunk, block = (n // 4, n % 4)
        slot = 3 - chunk // 4
        owner = (slot // 2 + x_lo) % 2 * 2 + (slot % 2 + core) % 2
        key_start = owner * BLOCK_LEN + chunk % 4 * BACK_BLOCK
        here = slot * BLOCK_LEN + chunk % 4 * BACK_BLOCK
        here = pl.ds(pl.multiple_of(here, BACK_BLOCK), BACK_BLOCK)
        mine = pl.ds(pl.multiple_of(block * BACK_BLOCK, BACK_BLOCK), BACK_BLOCK)
        keys = self.pairs[here]
        queries, upstream = (self.q[mine], self.g[mine])
        scores = lax.dot_general(
            keys, queries, (((1,), (1,)), ((), ())), preferred_element_type=jnp.float32
        )
        place_k = lax.broadcasted_iota(jnp.int32, scores.shape, 0)
        low, end = (self.low[0:1, mine] - key_start, self.end[0:1, mine] - key_start)
        allowed = (place_k >= low) & (place_k < end)
        if own:
            place_q = lax.broadcasted_iota(jnp.int32, (1, BACK_BLOCK), 1)
            place_q = place_q + (block - chunk % 4) * BACK_BLOCK
            allowed = allowed | (place_k == place_q)
        scores = jnp.where(allowed, scores, MASKED_SCORE)
        probs = jnp.exp(scores - self.lse[0:1, mine])
        prob_grad = lax.dot_general(
            keys, upstream, (((1,), (1,)), ((), ())), preferred_element_type=jnp.float32
        )
        score_grad = (probs * (prob_grad - self.delta[0:1, mine])).astype(jnp.bfloat16)
        self.dkv[here] += jnp.dot(
            score_grad, queries, preferred_element_type=jnp.float32
        ) + jnp.dot(probs.astype(jnp.bfloat16), upstream, preferred_element_type=jnp.float32)
        self.dq[:, mine] += jnp.dot(
            self.pairs_t[:, here], score_grad, preferred_element_type=jnp.float32
        )
        return carry

    def give(self, slot, index, add, dim):
        if add is not None:
            self.copies[add].wait_recv()

        def chunk(c, carry):
            here = pl.ds(pl.multiple_of(c * 256, 256), 256)
            there = pl.ds(pl.multiple_of(slot * BLOCK_LEN + c * 256, 256), 256)
            total = self.dkv[there]
            if add is not None:
                total = total + self.landed[add, here].astype(jnp.float32)
            self.away[index, here] = total.astype(jnp.bfloat16)
            return carry

        lax.fori_loop(0, BLOCK_LEN // 256, chunk, 0)
        self.copies[index] = self.start(
            remote(
                self.away.at[index],
                self.landed.at[index],
                self.send.at[index],
                self.recv.at[index],
                dim,
            )
        )

    def finish(self):
        self.copies[1].wait_recv()
        self.copies[2].wait_recv()

        def chunk(c, carry):
            here = pl.ds(pl.multiple_of(c * 128, 128), 128)
            total = self.dkv[here] + self.landed[1, here].astype(jnp.float32)
            total = total + self.landed[2, here].astype(jnp.float32)
            self.out[c, 0:128] = total.astype(jnp.bfloat16)
            grad = jnp.transpose(self.dq[:, here]) * HEAD ** (-0.5)
            folded = jnp.concatenate([grad[0:64, :HEAD], grad[64:128, :HEAD]], axis=1)
            self.out[c, 128:192] = folded.astype(jnp.bfloat16)
            return carry

        lax.fori_loop(0, 16, chunk, 0)


def reduce_kernel(n_left, dots, widths, with_norm, with_attention, *refs):
    refs = list(refs)

    def take(count):
        taken = refs[:count]
        del refs[:count]
        return taken

    n_right = len(dots_rights(dots))
    lefts, rights = (take(n_left), take(n_right))
    norm_in = take(1)[0] if with_norm else None
    attention_in = take(7) if with_attention else None
    out = take(1)[0]
    norm_out = take(1)[0] if with_norm else None
    head_out = take(1)[0] if with_attention else None
    left_all, right_all = (take(n_left), take(n_right))
    partial = take(1)[0]
    landed = take(6)
    norm_held, norm_landed = take(2) if with_norm else (None, None)
    attention_scratch = take(9) if with_attention else None
    act_send, act_recv, red_send, red_recv, gat_send, gat_recv, nrm_send, nrm_recv = refs
    shard, _, core, _, _ = place()
    greet(("core", "xa", "xb", "ya", "yb", "za", "zb"))
    sent = []

    def start(copy):
        copy.start()
        sent.append(copy)
        return copy

    half_tokens = lefts[0].shape[0]
    acts = []
    for i, (src, dst) in enumerate(zip(lefts, left_all)):
        acts.append(
            start(
                remote(
                    src,
                    dst.at[pl.ds(half_tokens, half_tokens)],
                    act_send.at[i],
                    act_recv.at[i],
                    "core",
                )
            )
        )
    for i, (src, dst) in enumerate(zip(rights, right_all)):
        half = src.shape[1] // 2
        theirs = pl.ds(pl.multiple_of((1 - core) * half, half), half)
        acts.append(
            start(
                remote(
                    src.at[:, theirs],
                    dst.at[pl.ds(half_tokens, half_tokens)],
                    act_send.at[n_left + i],
                    act_recv.at[n_left + i],
                    "core",
                )
            )
        )
    norm_dims = ("core",) + REDUCE_DIMS + ("xb",)
    norm_copies = []

    def norm_start(k):
        if not with_norm:
            return
        if k < 6:
            src, dst = (norm_held.at[k], norm_landed.at[k])
        else:
            src, dst = (norm_held.at[6, pl.ds(1 - shard, 1)], norm_landed.at[6, pl.ds(0, 1)])
        norm_copies.append(
            start(remote(src, dst, nrm_send.at[k], nrm_recv.at[k], norm_dims[k]))
        )

    def norm_finish(k):
        if not with_norm:
            return
        norm_copies[k].wait_recv()
        if k < 6:
            norm_held[k + 1] = norm_held[k] + norm_landed[k]
        else:
            norm_out[...] = norm_held[6, shard] + norm_landed[6, 0]

    if with_norm:
        norm_held[0] = norm_in[...]
    norm_start(0)
    for src, dst in zip(lefts, left_all):
        dst[pl.ds(0, half_tokens)] = src[...]
    for src, dst in zip(rights, right_all):
        half = src.shape[1] // 2
        dst[pl.ds(0, half_tokens)] = src[:, pl.ds(pl.multiple_of(core * half, half), half)]
    edges = [0]
    for width in widths:
        edges.append(edges[-1] + width)
    parts = range(len(widths))
    cols = [pl.ds(edges[p], widths[p]) for p in parts]
    orders = [rotated(REDUCE_DIMS, p) for p in parts]
    starts = [row_starts(orders[p], ROWS) for p in parts]
    moving = {}

    def reduce_start(p, k):
        if k < 5:
            half = ROWS >> (k + 1)
            away = pl.multiple_of(starts[p][k] + (half - (starts[p][k + 1] - starts[p][k])), 16)
            src = partial.at[:, pl.ds(away, half), cols[p]]
            dst = landed[k].at[:, :, cols[p]]
            dim = orders[p][k]
        else:
            at = pl.multiple_of(starts[p][5], 16)
            src = partial.at[1 - shard, pl.ds(at, 16), cols[p]]
            dst = landed[5].at[:, cols[p]]
            dim = "xb"
        moving[p] = start(remote(src, dst, red_send.at[p, k], red_recv.at[p, k], dim))

    def reduce_add(p, k):
        moving[p].wait_recv()
        if k < 5:
            half = ROWS >> (k + 1)
            step = min(half, 32)

            def add(i, carry):
                here = pl.ds(pl.multiple_of(i * step, step), step)
                there = pl.ds(pl.multiple_of(starts[p][k + 1] + i * step, 16), step)
                total = partial[:, there, cols[p]].astype(jnp.float32)
                total = total + landed[k][:, here, cols[p]].astype(jnp.float32)
                partial[:, there, cols[p]] = total.astype(jnp.bfloat16)
                return carry

            lax.fori_loop(0, half // step, add, 0)
        else:
            here = pl.ds(pl.multiple_of(starts[p][5], 16), 16)
            total = partial[shard, here, cols[p]].astype(jnp.float32)
            total = total + landed[5][:, cols[p]].astype(jnp.float32)
            out[core, here, cols[p]] = total.astype(jnp.bfloat16)

    def acts_arrive():
        for copy in acts:
            copy.wait_recv()
        norm_finish(0)
        norm_start(1)

    def multiply(at):
        left, left_step, left_off, right, right_off = dots[at]
        for s in range(2):
            product = lax.dot_general(
                left_all[left][:, pl.ds(s * left_step + left_off, ROWS)],
                right_all[right][:, pl.ds(right_off, 512)],
                (((0,), (0,)), ((), ())),
                preferred_element_type=jnp.float32,
            )
            partial[s, :, pl.ds(at * 512, 512)] = product.astype(jnp.bfloat16)
        for p in parts:
            if at * 512 < edges[p + 1] <= (at + 1) * 512:
                reduce_start(p, 0)

    def reduce_step(p, k):
        if p == 0:
            norm_finish(k + 1)
            if k < 5:
                norm_start(k + 2)
        reduce_add(p, k)
        if k < 5:
            reduce_start(p, k + 1)
        else:
            gather_start(p, 4)

    def gather_step(p, k):
        moving[p].wait_recv()
        if k > 0:
            gather_start(p, k - 1)
        if k == 1:
            share(p, 0, starts[p][1])
        if k == 0:
            share(p, 1, ROWS // 2 - starts[p][1])

    def range_of(p, at, size):
        return out.at[core, pl.ds(pl.multiple_of(at, 16), size), cols[p]]

    def gather_start(p, k):
        mine = range_of(p, starts[p][k + 1], ROWS >> (k + 1))
        moving[p] = start(
            remote(mine, mine, gat_send.at[p, k], gat_recv.at[p, k], orders[p][k])
        )

    shared = []

    def share(p, slot, at):
        mine = range_of(p, at, ROWS // 2)
        shared.append(
            start(remote(mine, mine, gat_send.at[p, 5 + slot], gat_recv.at[p, 5 + slot], "core"))
        )

    events = [(BACK_ACTS, acts_arrive)]
    events += [(BACK_ACTS, functools.partial(multiply, at)) for at in range(len(dots))]
    for k in range(6):
        events += [(BACK_REDUCE[k], functools.partial(reduce_step, p, k)) for p in parts]
    for k in range(4, -1, -1):
        events += [(BACK_GATHER[k], functools.partial(gather_step, p, k)) for p in parts]
    if with_attention:
        attention = AttendBack(attention_in, head_out, attention_scratch, start)
        events += attention.events
        events.sort(key=lambda e: e[0])
        done = 0
        for at, act in events:
            if at > done:
                attention.run(done, at)
                done = at
            act()
        attention.finish()
    else:
        for _, act in events:
            act()
    for copy in shared:
        copy.wait_recv()
    for copy in sent:
        copy.wait_send()


def dots_rights(dots):
    return sorted({d[3] for d in dots})


def reduce_gradients(lefts, rights, dots, widths, norm, attention, collective_id):
    tokens = lefts[0].shape[0]
    total = sum(widths)
    out_shape = [jax.ShapeDtypeStruct((2, ROWS, total), jnp.bfloat16)]
    scratch = [pltpu.VMEM((2 * tokens, a.shape[1]), jnp.bfloat16) for a in lefts]
    scratch += [pltpu.VMEM((2 * tokens, a.shape[1] // 2), jnp.bfloat16) for a in rights]
    scratch += [pltpu.VMEM((2, ROWS, total), jnp.bfloat16)]
    scratch += [pltpu.VMEM((2, ROWS >> (k + 1), total), jnp.bfloat16) for k in range(5)]
    scratch += [pltpu.VMEM((16, total), jnp.bfloat16)]
    operands = [*lefts, *rights]
    if norm is not None:
        operands.append(norm)
        out_shape.append(jax.ShapeDtypeStruct(norm.shape[1:], jnp.float32))
        scratch += [
            pltpu.VMEM((7, *norm.shape), jnp.float32),
            pltpu.VMEM((7, *norm.shape), jnp.float32),
        ]
    if attention is not None:
        operands += attention
        out_shape.append(jax.ShapeDtypeStruct((HEADS, 192, 128), jnp.bfloat16))
        scratch += back_scratch()
    n_act, parts = (len(lefts) + len(rights), len(widths))
    scratch += [pltpu.SemaphoreType.DMA((n_act,))] * 2
    scratch += [pltpu.SemaphoreType.DMA((parts, 6))] * 2
    scratch += [pltpu.SemaphoreType.DMA((parts, 7))] * 2
    scratch += [pltpu.SemaphoreType.DMA((7,))] * 2
    return pl.pallas_call(
        functools.partial(
            reduce_kernel, len(lefts), dots, widths, norm is not None, attention is not None
        ),
        out_shape=out_shape,
        in_specs=[pl.BlockSpec(memory_space=pltpu.VMEM)] * len(operands),
        out_specs=[pl.BlockSpec(memory_space=pltpu.VMEM)] * len(out_shape),
        scratch_shapes=scratch,
        compiler_params=pltpu.CompilerParams(
            collective_id=collective_id, has_side_effects=True, vmem_limit_bytes=60 * 2**20
        ),
    )(*operands)


FF_DOTS = tuple(
    [(0, 512, 0, 0, j * 512) for j in range(4)]
    + [(1, 2048, q * 512, 1, 0) for q in range(4)]
    + [(2, 512, 0, 2, 0)]
)
FF_WIDTHS = (1024, 896, 896, 896, 896)
QKV_DOTS = ((0, 512, 0, 0, 0), (0, 512, 0, 1, 0), (0, 512, 0, 2, 0))
QKV_WIDTHS = (384, 384, 256, 256, 256)


def cast_kernel(x_ref, o_ref):
    o_ref[...] = x_ref[0].astype(jnp.float32)


def cast_out(gathered, shape, grid, index_in, index_out):
    return pl.pallas_call(
        cast_kernel,
        out_shape=jax.ShapeDtypeStruct(shape, jnp.float32),
        grid=grid,
        in_specs=[pl.BlockSpec((1, ROWS, 512), index_in)],
        out_specs=pl.BlockSpec((ROWS, 512), index_out),
    )(gathered)


def square_out(gathered, slot):
    return cast_out(gathered, (ROWS, 1024), (2,), lambda c: (c, 0, slot), lambda c: (0, c))


def ff_grads_out(gathered):
    grad_in = cast_out(
        gathered, (ROWS, 4096), (2, 4), lambda c, j: (c, 0, j), lambda c, j: (0, c * 4 + j)
    )
    grad_down = cast_out(
        gathered, (2048, 1024), (4, 2), lambda q, c: (c, 0, 4 + q), lambda q, c: (q, c)
    )
    return (grad_in, grad_down, square_out(gathered, 8))


def normalize(summed_in, norm_gain, norm_bias):
    row_mean = jnp.mean(summed_in, axis=-1, keepdims=True)
    centred = summed_in - row_mean
    inv_std = lax.rsqrt(jnp.mean(centred * centred, axis=-1, keepdims=True) + NORM_EPSILON)
    scaled = centred * inv_std
    return (scaled * norm_gain + norm_bias, scaled, inv_std)


def normalize_back(upstream, scaled, inv_std, norm_gain):
    weighted = upstream * norm_gain
    centred = weighted - jnp.mean(weighted, axis=-1, keepdims=True)
    result = inv_std * (centred - scaled * jnp.mean(weighted * scaled, axis=-1, keepdims=True))
    return (result, jnp.sum(upstream * scaled, axis=0), jnp.sum(upstream, axis=0))


def exact_gelu(values):
    return jax.nn.gelu(values, approximate=False)


def neighbour(value, bit):
    flips = [(i, i ^ bit) for i in range(4)]
    return lax.ppermute(value, "blk", flips)


def project_kernel(x_ref, w_ref, o_ref):
    for piece in range(2):
        cols = pl.ds(piece * 512, 512)
        q, k, v = [
            jnp.dot(
                x_ref[...],
                w_ref[:, pl.ds(which * 1024 + piece * 512, 512)],
                preferred_element_type=jnp.float32,
            )
            for which in range(3)
        ]
        q = (q.astype(jnp.bfloat16).astype(jnp.float32) * HEAD ** (-0.5)).astype(jnp.bfloat16)
        k, v = (k.astype(jnp.bfloat16), v.astype(jnp.bfloat16))
        for h in range(8):
            at = slice(h * HEAD, (h + 1) * HEAD)
            head = piece * 8 + h
            o_ref[head, 0:128] = jnp.concatenate([k[:, at], v[:, at]], axis=1)
            o_ref[head, 128:192] = jnp.concatenate([q[0:64, at], q[64:128, at]], axis=1)


def project(token_rows, full_qkv):
    return pl.pallas_call(
        project_kernel,
        out_shape=jax.ShapeDtypeStruct((HEADS, 192, 128), jnp.bfloat16),
        compiler_params=pltpu.CompilerParams(vmem_limit_bytes=32 * 2**20),
    )(token_rows, full_qkv)


def unfold(packed):
    n = packed.shape[0]
    return packed.reshape(n, 64, 2, HEAD).transpose(0, 2, 1, 3).reshape(n * 128, HEAD)


def fold(rows):
    n = rows.shape[0] // 128
    return rows.reshape(n, 2, 64, HEAD).transpose(0, 2, 1, 3).reshape(n, 64, 2 * HEAD)


def to_tokens(packed):
    return packed.reshape(HEADS, 64, 2, HEAD).transpose(2, 1, 0, 3).reshape(128, HEADS * HEAD)


def to_heads(rows):
    return rows.reshape(2, 64, HEADS, HEAD).transpose(2, 1, 0, 3).reshape(HEADS, 64, 2 * HEAD)


def swap(packed):
    return lax.all_to_all(packed, "aa", split_axis=0, concat_axis=0, tiled=True)


def shards(
    tokens,
    segments,
    valid,
    w_query,
    w_key,
    w_value,
    w_out,
    norm1_gain,
    norm1_bias,
    w_in,
    w_down,
    norm2_gain,
    norm2_bias,
    cotangent,
):
    packed = jnp.zeros((16, 512), jnp.bfloat16).at[:4].set(
        jnp.stack([norm1_gain, norm1_bias, norm2_gain, norm2_bias])
    )
    full_qkv, full_out, full_in, full_down = gather_weights(
        [w_query, w_key, w_value, w_out, w_in, w_down],
        [(0, 0), (0, 1024), (0, 2048), (1, 0), (2, 0), (3, 0)],
        [(1024, 3072), (1024, 1024), (1024, 4096), (4096, 1024)],
        0,
    )
    norms = lax.all_gather(packed, "shard", axis=1, tiled=True)[:4].astype(jnp.float32)
    gain_one, bias_one, gain_two, bias_two = norms
    token_rows = tokens[0]
    blk = lax.axis_index("blk")
    query_start = blk * BLOCK_LEN
    place = jnp.stack([query_start, blk]).astype(jnp.int32)
    plan, low, end = block_plan(*spans(segments[0], valid[0]), query_start, BLOCK_LEN)

    heads_all = swap(project(token_rows, full_qkv))
    own_pair = heads_all[:, 0:128].reshape(BLOCK_LEN, 128)
    queries = jnp.pad(unfold(heads_all[:, 128:192]), ((0, 0), (0, HEAD)))
    far_pair = neighbour(own_pair, 2)
    pairs = jnp.concatenate([own_pair, neighbour(own_pair, 1), far_pair, neighbour(far_pair, 1)])
    summed, lse, folded = attend(plan, place, queries, pairs, low, end)
    mixed = to_tokens(swap(folded))

    attn = jnp.dot(mixed, full_out, preferred_element_type=jnp.float32)
    first, scaled_one, inv_one = normalize(
        token_rows.astype(jnp.float32) + attn, gain_one, bias_one
    )
    first_low = first.astype(jnp.bfloat16)
    pre = jnp.dot(first_low, full_in, preferred_element_type=jnp.float32)
    hidden = exact_gelu(pre).astype(jnp.bfloat16)
    ff_out = jnp.dot(hidden, full_down, preferred_element_type=jnp.float32)
    result, scaled_two, inv_two = normalize(first + ff_out, gain_two, bias_two)
    upstream = cotangent[0].astype(jnp.float32)
    grad_two, grad_gain_two, grad_bias_two = normalize_back(upstream, scaled_two, inv_two, gain_two)
    ff_grad = grad_two.astype(jnp.bfloat16)
    hidden_grad = jnp.einsum("td,fd->tf", ff_grad, full_down, preferred_element_type=jnp.float32)
    gelu_pull = jax.vjp(exact_gelu, pre)[1]
    pre_grad = gelu_pull(hidden_grad)[0].astype(jnp.bfloat16)
    first_grad = grad_two + jnp.einsum(
        "tf,df->td", pre_grad, full_in, preferred_element_type=jnp.float32
    )
    grad_one, grad_gain_one, grad_bias_one = normalize_back(
        first_grad, scaled_one, inv_one, gain_one
    )
    attn_grad = grad_one.astype(jnp.bfloat16)
    mixed_grad = jnp.einsum(
        "td,cd->tc", attn_grad, full_out, preferred_element_type=jnp.float32
    ).astype(jnp.bfloat16)
    norm_sums = jnp.stack([grad_gain_one, grad_bias_one, grad_gain_two, grad_bias_two])
    norm_sums = jnp.pad(norm_sums.reshape(4, 2, 512).transpose(1, 0, 2), ((0, 0), (0, 4), (0, 0)))

    ff_summed, norm_total, head_grads = reduce_gradients(
        [first_low, hidden, mixed],
        [pre_grad, ff_grad, attn_grad],
        FF_DOTS,
        FF_WIDTHS,
        norm_sums,
        [
            queries,
            swap(to_heads(mixed_grad)),
            pairs,
            jnp.broadcast_to(low[None], (8, BLOCK_LEN)),
            jnp.broadcast_to(end[None], (8, BLOCK_LEN)),
            lse,
            summed,
        ],
        1,
    )
    grad_in, grad_down, grad_out = ff_grads_out(ff_summed)
    token_grads = swap(head_grads)
    query_tok = to_tokens(token_grads[:, 128:192])
    key_tok = token_grads[:, 0:128, :HEAD].transpose(1, 0, 2).reshape(128, 1024)
    value_tok = token_grads[:, 0:128, HEAD:].transpose(1, 0, 2).reshape(128, 1024)
    all_tok = jnp.concatenate([query_tok, key_tok, value_tok], axis=1)
    input_grad = grad_one + jnp.einsum(
        "td,cd->tc", all_tok, full_qkv, preferred_element_type=jnp.float32
    )
    qkv_summed = reduce_gradients(
        [token_rows], [query_tok, key_tok, value_tok], QKV_DOTS, QKV_WIDTHS, None, None, 2
    )[0]
    return (
        result.astype(jnp.bfloat16)[None],
        input_grad.astype(jnp.bfloat16)[None],
        square_out(qkv_summed, 0),
        square_out(qkv_summed, 1),
        square_out(qkv_summed, 2),
        grad_out,
        norm_total[0],
        norm_total[1],
        grad_in,
        grad_down,
        norm_total[2],
        norm_total[3],
    )


def solution(mesh):
    return jax.shard_map(
        shards,
        mesh=mesh,
        in_specs=(
            P("shard", ("blk", "aa"), None),
            P("shard", None),
            P("shard", None),
            P("shard", None),
            P("shard", None),
            P("shard", None),
            P("shard", None),
            P("shard"),
            P("shard"),
            P("shard", None),
            P("shard", None),
            P("shard"),
            P("shard"),
            P("shard", ("blk", "aa"), None),
        ),
        out_specs=(
            P("shard", ("blk", "aa"), None),
            P("shard", ("blk", "aa"), None),
            P("shard", None),
            P("shard", None),
            P("shard", None),
            P("shard", None),
            P("shard"),
            P("shard"),
            P("shard", None),
            P("shard", None),
            P("shard"),
            P("shard"),
        ),
        check_vma=False,
    )
```

```python
import functools

import jax
import jax.numpy as jnp
from jax import lax
from jax.experimental import pallas as pl
from jax.experimental.pallas import tpu as pltpu
from jax.sharding import PartitionSpec as P

HEADS = 16
HEAD = 64
MASKED_SCORE = -1e30
NORM_EPSILON = 1e-05
BLOCK_LEN = 2048


def query_spans(segments, valid, query_start):
    numbers = jnp.arange(36, dtype=jnp.int32)
    before = jnp.sum((segments[None, :] < numbers[:, None]).astype(jnp.int32), axis=1)
    mine = lax.dynamic_slice_in_dim(segments, query_start, BLOCK_LEN)
    picked = numbers[:35, None] == mine[None, :]
    low = jnp.sum(jnp.where(picked, before[:35, None], 0), axis=0)
    end = jnp.sum(jnp.where(picked, before[1:, None], 0), axis=0)
    end = jnp.minimum(end, jnp.sum(valid))
    return [jnp.broadcast_to(a[None], (8, BLOCK_LEN)) for a in (low, end)]


MESH = pl.DeviceIdType.MESH
ROWS = 512
REDUCE_DIMS = ("xa", "ya", "za", "yb", "zb")
GATHER_DIMS = ("ya", "za", "yb", "zb")


def place():
    shard = lax.axis_index("shard")
    blk = lax.axis_index("blk")
    aa = lax.axis_index("aa")
    return (shard, blk // 2, blk % 2, aa // 4, aa % 4)


def flipped(i):
    return i + 1 - 2 * (i % 2)


def partner(dim):
    shard, x_lo, core, z, y = place()
    if dim == "core":
        core = 1 - core
    elif dim == "xa":
        x_lo = 1 - x_lo
    elif dim == "xb":
        shard, x_lo = 1 - shard, 1 - x_lo
    elif dim == "ya":
        y = flipped(y)
    elif dim == "yb":
        y = 3 - y
    elif dim == "za":
        z = flipped(z)
    else:
        z = 3 - z
    return (shard, x_lo * 2 + core, z * 4 + y)


def ring_bit(dim):
    shard, x_lo, _, z, y = place()
    if dim == "xa":
        return (shard * 2 + x_lo + shard) % 2
    if dim == "ya":
        return (y + y // 2) % 2
    if dim == "yb":
        return y // 2
    if dim == "za":
        return (z + z // 2) % 2
    return z // 2


def greet(dims):
    barrier = pltpu.get_barrier_semaphore()
    for dim in dims:
        pl.semaphore_signal(barrier, inc=1, device_id=partner(dim), device_id_type=MESH)
    pl.semaphore_wait(barrier, len(dims))


def remote(src, dst, send_sem, recv_sem, dim):
    return pltpu.make_async_remote_copy(
        src_ref=src,
        dst_ref=dst,
        send_sem=send_sem,
        recv_sem=recv_sem,
        device_id=partner(dim),
        device_id_type=MESH,
    )


def row_starts(dims, rows):
    starts, at, size = ([0], 0, rows)
    for dim in dims:
        size //= 2
        at = at + ring_bit(dim) * size
        starts.append(at)
    return starts


def rotated(dims, by):
    return dims[by:] + dims[:by]


class Gather:
    def __init__(self, sources, places, send, recv, start):
        self.sources, self.places = (sources, places)
        self.send, self.recv, self.start = (send, recv, start)
        self.shard, _, self.core, _, _ = place()
        self.orders = [rotated(GATHER_DIMS, part) for part in range(4)]
        self.moving, self.siblings = ({}, [])

    def columns(self, i, part, off):
        cols = self.sources[i].shape[1]
        col = pl.multiple_of(self.core * (cols // 2) + (off + part * (cols // 8)), 128)
        return pl.ds(col, cols // 8)

    def block(self, i, part, shard, at, size):
        target, off = self.places[i]
        rows = self.sources[i].shape[0]
        at = pl.multiple_of(shard * rows + at, 16)
        return target.at[pl.ds(at, size), self.columns(i, part, off)]

    def own(self, i):
        target, off = self.places[i]
        rows, cols = self.sources[i].shape
        return target.at[pl.ds(pl.multiple_of(self.shard * rows, rows), rows), pl.ds(off, cols)]

    def begin(self, i):
        rows = self.sources[i].shape[0]
        for part in range(4):
            at = row_starts(self.orders[part], rows)[4]
            mine = pl.ds(pl.multiple_of(at, 16), rows // 16)
            self.moving[i, part] = self.start(
                remote(
                    self.sources[i].at[mine, self.columns(i, part, 0)],
                    self.block(i, part, self.shard, at, rows // 16),
                    self.send.at[i, part, 0],
                    self.recv.at[i, part, 0],
                    "xb",
                )
            )

    def stage(self, i, stage):
        rows = self.sources[i].shape[0]
        for part in range(4):
            self.moving[i, part].wait_recv()
            starts = row_starts(self.orders[part], rows)
            if stage < 5:
                k = 4 - stage
                mine = self.block(i, part, 1 - self.shard, starts[k + 1], rows >> (k + 1))
                self.moving[i, part] = self.start(
                    remote(
                        mine,
                        mine,
                        self.send.at[i, part, stage],
                        self.recv.at[i, part, stage],
                        self.orders[part][k],
                    )
                )
            if stage >= 4:
                at = starts[1] if stage == 4 else rows // 2 - starts[1]
                mine = self.block(i, part, 1 - self.shard, at, rows // 2)
                self.siblings.append(
                    self.start(
                        remote(
                            mine,
                            mine,
                            self.send.at[i, part, stage + 1],
                            self.recv.at[i, part, stage + 1],
                            "core",
                        )
                    )
                )

    def finish(self):
        for copy in self.siblings:
            copy.wait_recv()
        self.siblings = []


def plane_peer(step):
    shard, x_lo, core, z, y = place()
    return (shard, x_lo * 2 + core, (z * 4 + y + step) % 16)


class Exchange:
    def __init__(self, outgoing, incoming, send, recv, start):
        self.outgoing, self.incoming = (outgoing, incoming)
        self.send, self.recv, self.start = (send, recv, start)
        self.copies = []

    def begin(self):
        me = lax.axis_index("aa")
        for step in (1, 3, 4, 12, 15, 13, 5, 11, 2, 8, 14, 6, 10, 7, 9):
            self.copies.append(
                self.start(
                    pltpu.make_async_remote_copy(
                        src_ref=self.outgoing.at[(me + step) % 16],
                        dst_ref=self.incoming.at[me],
                        send_sem=self.send.at[step],
                        recv_sem=self.recv.at[step],
                        device_id=plane_peer(step),
                        device_id_type=MESH,
                    )
                )
            )
        self.incoming[me] = self.outgoing[me]

    def finish(self):
        for copy in self.copies:
            copy.wait_recv()


def greet_all(dims):
    barrier = pltpu.get_barrier_semaphore()
    for dim in dims:
        pl.semaphore_signal(barrier, inc=1, device_id=partner(dim), device_id_type=MESH)
    for step in range(1, 16):
        pl.semaphore_signal(barrier, inc=1, device_id=plane_peer(step), device_id_type=MESH)
    pl.semaphore_wait(barrier, len(dims) + 15)


def unfolded(block, side):
    lane = lax.broadcasted_iota(jnp.int32, (64, 128), 1)
    keep = (lane >= HEAD) if side else (lane < HEAD)
    block = block.astype(jnp.float32)
    moved = jnp.concatenate([block[:, HEAD:], block[:, :HEAD]], axis=1)
    first, second = (moved, block) if side else (block, moved)
    both = jnp.concatenate([jnp.where(keep, first, 0.0), jnp.where(keep, second, 0.0)], axis=0)
    return both.astype(jnp.bfloat16)


LEAST = -(2**31)
FRONT_BLOCK = 512


def visible(place_k, low, end, start):
    size = jnp.maximum(end - low, 0) + LEAST
    return (place_k - (low - start - LEAST)) < size


def front_kernel(
    x_ref,
    wq_ref,
    wk_ref,
    wv_ref,
    wo_ref,
    wi_ref,
    wd_ref,
    norm_ref,
    low_ref,
    end_ref,
    qkv_out,
    out_out,
    in_out,
    down_out,
    norm_out,
    q_out,
    pairs_out,
    o_out,
    lse_out,
    mixed_out,
    wqkv,
    staged,
    heads_in,
    folded,
    pairs_t,
    top_s,
    send,
    recv,
    own_in,
    own_out,
    hop_send,
    hop_recv,
    swap_send,
    swap_recv,
    back_send,
    back_recv,
    *bounce,
):
    shard, _, _, _, _ = place()
    sent = []

    def start(copy):
        copy.start()
        sent.append(copy)
        return copy

    gather = Gather(
        [wq_ref, wk_ref, wv_ref, wo_ref, wi_ref, wd_ref],
        [(wqkv, 0), (wqkv, 1024), (wqkv, 2048), (out_out, 0), (in_out, 0), (down_out, 0)],
        send,
        recv,
        start,
    )
    inward = []
    for i in range(6):
        target = gather.own(i) if i < 3 else bounce[i - 3]
        inward.append(pltpu.make_async_copy(gather.sources[i], target, own_in.at[i]))
        inward[i].start()
    greet_all(("core", "xa", "xb"))
    norms = start(
        remote(norm_ref, norm_out.at[shard], hop_send.at[3], hop_recv.at[3], "xb")
    )
    norm_out[shard] = norm_ref[...]
    for i in range(6):
        gather.begin(i)
    for i in range(3):
        gather.stage(i, 1)
    outward = []
    for i in range(3, 6):
        inward[i].wait()
        outward.append(pltpu.make_async_copy(bounce[i - 3], gather.own(i), own_out.at[i - 3]))
        outward[-1].start()
    for stage in range(2, 6):
        for i in range(3):
            gather.stage(i, stage)
        if stage == 3:
            for i in range(3, 6):
                gather.stage(i, 1)
    for i in range(3):
        inward[i].wait()
    gather.finish()
    keep = pltpu.make_async_copy(wqkv, qkv_out, own_out.at[3])
    keep.start()

    def project(piece, carry):
        q, k, v = [
            jnp.dot(
                x_ref[...],
                wqkv[:, pl.ds(pl.multiple_of(which * 1024 + piece * 256, 256), 256)],
                preferred_element_type=jnp.float32,
            )
            for which in range(3)
        ]
        q = (q.astype(jnp.bfloat16).astype(jnp.float32) * HEAD ** (-0.5)).astype(jnp.bfloat16)
        k, v = (k.astype(jnp.bfloat16), v.astype(jnp.bfloat16))
        for h in range(4):
            at = slice(h * HEAD, (h + 1) * HEAD)
            staged[piece * 4 + h, 0:128] = jnp.concatenate([k[:, at], v[:, at]], axis=1)
            staged[piece * 4 + h, 128:192] = jnp.concatenate([q[0:64, at], q[64:128, at]], axis=1)
        return carry

    lax.fori_loop(0, 4, project, 0)
    heads = Exchange(staged, heads_in, swap_send, swap_recv, start)
    heads.begin()
    for i in range(3, 6):
        gather.stage(i, 2)
    heads.finish()

    def spread(c, carry):
        here = pl.ds(pl.multiple_of(c * 128, 128), 128)
        pairs_out[here] = heads_in[c, 0:128]
        q_out[here] = unfolded(heads_in[c, 128:192], 0)
        return carry

    lax.fori_loop(0, 16, spread, 0)

    def slot_rows(slot):
        return pairs_out.at[pl.ds(slot * BLOCK_LEN, BLOCK_LEN)]

    def hop(index, source, target, dim):
        return start(
            remote(
                slot_rows(source), slot_rows(target), hop_send.at[index], hop_recv.at[index], dim
            )
        )

    hops = {1: hop(0, 0, 1, "core"), 2: hop(1, 0, 2, "xa")}
    top_s[...] = jnp.full_like(top_s, MASKED_SCORE)
    o_out[...] = jnp.zeros_like(o_out)
    first_row = lax.broadcasted_iota(jnp.int32, (128, 512), 0) == 0

    def turn(c, carry):
        here = pl.ds(pl.multiple_of(c * 512, 512), 512)
        turned = jnp.transpose(pairs_out[here].astype(jnp.float32))
        pairs_t[:, here] = jnp.where(first_row, 1.0, turned).astype(jnp.bfloat16)
        return carry

    def slot_step(slot, block):
        _, x_lo, core, _, _ = place()
        owner = (slot // 2 + x_lo) % 2 * 2 + (slot % 2 + core) % 2
        rows = pl.ds(slot * BLOCK_LEN, BLOCK_LEN)
        mine = pl.ds(pl.multiple_of(block * FRONT_BLOCK, FRONT_BLOCK), FRONT_BLOCK)
        scores = lax.dot_general(
            pairs_out[rows],
            q_out[mine],
            (((1,), (1,)), ((), ())),
            preferred_element_type=jnp.float32,
        )
        place_k = lax.broadcasted_iota(jnp.int32, scores.shape, 0)
        allowed = visible(place_k, low_ref[0:1, mine], end_ref[0:1, mine], owner * BLOCK_LEN)
        if slot == 0:
            place_q = lax.broadcasted_iota(jnp.int32, (1, FRONT_BLOCK), 1) + block * FRONT_BLOCK
            allowed = allowed | (place_k == place_q)
        scores = jnp.where(allowed, scores, MASKED_SCORE)
        top = top_s[0:1, mine]
        new_top = jnp.maximum(top, jnp.max(scores, axis=0, keepdims=True))
        weights = jnp.exp(scores - new_top)
        factor = jnp.exp(top - new_top)
        o_out[:, mine] = o_out[:, mine] * factor + jnp.dot(
            pairs_t[:, rows], weights.astype(jnp.bfloat16), preferred_element_type=jnp.float32
        )
        top_s[:, mine] = jnp.broadcast_to(new_top, (8, FRONT_BLOCK))

    events = {
        0: [(i, 3) for i in (3, 4, 5)],
        1: [(i, 4) for i in (3, 4, 5)],
        3: [(i, 5) for i in (3, 4, 5)],
    }
    for slot in range(4):
        if slot:
            hops[slot].wait_recv()
        if slot == 2:
            hops[3] = hop(2, 2, 3, "core")
        lax.fori_loop(slot * 4, slot * 4 + 4, turn, 0)
        for half in range(2):

            def blocks(b, carry):
                slot_step(slot, b)
                return carry

            lax.fori_loop(half * 2, half * 2 + 2, blocks, 0)
            if half == 0:
                for i, stage in events.get(slot, ()):
                    gather.stage(i, stage)

    def close(c, carry):
        here = pl.ds(pl.multiple_of(c * 128, 128), 128)
        total = o_out[0:1, here]
        mixed = o_out[:, here] / total
        o_out[:, here] = mixed
        lse = top_s[0:1, here] + jnp.log(total)
        lse_out[:, here] = jnp.broadcast_to(lse, (8, 128))
        block = jnp.transpose(mixed)
        both = jnp.concatenate([block[0:64, HEAD:], block[64:128, HEAD:]], axis=1)
        folded[c] = both.astype(jnp.bfloat16)
        return carry

    lax.fori_loop(0, 16, close, 0)
    back = Exchange(folded, mixed_out, back_send, back_recv, start)
    back.begin()
    gather.finish()
    norms.wait_recv()
    back.finish()
    for copy in outward:
        copy.wait()
    keep.wait()
    for copy in sent:
        copy.wait_send()


def front(token_rows, weights, packed, low, end):
    bf16, f32 = (jnp.bfloat16, jnp.float32)
    n = len(weights)
    whole, anywhere = (pl.BlockSpec(memory_space=pltpu.VMEM), pl.BlockSpec(memory_space=pl.ANY))
    return pl.pallas_call(
        front_kernel,
        out_shape=[
            jax.ShapeDtypeStruct((1024, 3072), bf16),
            jax.ShapeDtypeStruct((1024, 1024), bf16),
            jax.ShapeDtypeStruct((1024, 4096), bf16),
            jax.ShapeDtypeStruct((4096, 1024), bf16),
            jax.ShapeDtypeStruct((2, 16, 512), bf16),
            jax.ShapeDtypeStruct((BLOCK_LEN, 128), bf16),
            jax.ShapeDtypeStruct((4 * BLOCK_LEN, 128), bf16),
            jax.ShapeDtypeStruct((128, BLOCK_LEN), f32),
            jax.ShapeDtypeStruct((8, BLOCK_LEN), f32),
            jax.ShapeDtypeStruct((16, 64, 128), bf16),
        ],
        in_specs=[whole] + [anywhere] * n + [whole] * 3,
        out_specs=[anywhere] * 4 + [whole] * 6,
        scratch_shapes=[
            pltpu.VMEM((1024, 3072), bf16),
            pltpu.VMEM((16, 192, 128), bf16),
            pltpu.VMEM((16, 192, 128), bf16),
            pltpu.VMEM((16, 64, 128), bf16),
            pltpu.VMEM((128, 4 * BLOCK_LEN), bf16),
            pltpu.VMEM((8, BLOCK_LEN), f32),
            pltpu.SemaphoreType.DMA((n, 4, 7)),
            pltpu.SemaphoreType.DMA((n, 4, 7)),
            pltpu.SemaphoreType.DMA((n,)),
            pltpu.SemaphoreType.DMA((4,)),
            pltpu.SemaphoreType.DMA((4,)),
            pltpu.SemaphoreType.DMA((4,)),
            pltpu.SemaphoreType.DMA((16,)),
            pltpu.SemaphoreType.DMA((16,)),
            pltpu.SemaphoreType.DMA((16,)),
            pltpu.SemaphoreType.DMA((16,)),
            *[pltpu.VMEM(w.shape, bf16) for w in weights[3:]],
        ],
        compiler_params=pltpu.CompilerParams(
            collective_id=0, has_side_effects=True, vmem_limit_bytes=60 * 2**20
        ),
    )(token_rows, *weights, packed, low, end)


BACK_ACTS = 3
BACK_REDUCE = (14, 20, 23, 25, 26, 27)
BACK_GATHER = (32, 32, 30, 29, 28)
SLOT_UNITS = 8
BACK_BLOCK = 512
BACK_KEYS = 1024


def back_scratch():
    return [
        pltpu.VMEM((BLOCK_LEN, 128), jnp.bfloat16),
        pltpu.VMEM((128, 4 * BLOCK_LEN), jnp.bfloat16),
        pltpu.VMEM((8, BLOCK_LEN), jnp.float32),
        pltpu.VMEM((128, BLOCK_LEN), jnp.float32),
        pltpu.VMEM((4 * BLOCK_LEN, 128), jnp.float32),
        pltpu.VMEM((3, BLOCK_LEN, 128), jnp.bfloat16),
        pltpu.VMEM((3, BLOCK_LEN, 128), jnp.bfloat16),
        pltpu.SemaphoreType.DMA((3,)),
        pltpu.SemaphoreType.DMA((3,)),
    ]


class AttendBack:
    def __init__(self, ins, out, scratch, start):
        self.q, self.packed, self.pairs, self.low, self.end, self.lse, self.o_t = ins
        self.out = out
        self.g, self.pairs_t, self.delta, self.dq, self.dkv = scratch[:5]
        self.away, self.landed, self.send, self.recv = scratch[5:9]
        self.start = start
        self.copies = {}
        self.events = [
            (0, self.begin),
            (SLOT_UNITS, lambda: self.give(3, 0, None, "core")),
            (2 * SLOT_UNITS + 1, lambda: self.give(2, 1, 0, "xa")),
            (3 * SLOT_UNITS, lambda: self.give(1, 2, None, "core")),
        ]

    def begin(self):
        self.delta[...] = jnp.zeros_like(self.delta)
        self.dq[...] = jnp.zeros_like(self.dq)
        self.dkv[...] = jnp.zeros_like(self.dkv)

        def chunk(c, carry):
            both = unfolded(self.packed[c], 1)
            here = pl.ds(pl.multiple_of(c * 128, 128), 128)
            self.g[here] = both
            products = jnp.transpose(both.astype(jnp.float32)) * self.o_t[:, here]
            total = jnp.sum(products, axis=0, keepdims=True)
            self.delta[:, here] = jnp.broadcast_to(total, (8, 128))
            return carry

        lax.fori_loop(0, 16, chunk, 0)

        def turn(c, carry):
            here = pl.ds(pl.multiple_of(c * 512, 512), 512)
            self.pairs_t[:, here] = jnp.transpose(self.pairs[here])
            return carry

        lax.fori_loop(0, 16, turn, 0)

    def run(self, first, last):
        edge = 3 * SLOT_UNITS
        if first < edge:
            lax.fori_loop(first, min(last, edge), functools.partial(self.unit, own=False), 0)
        if last > edge:
            lax.fori_loop(max(first, edge), last, functools.partial(self.unit, own=True), 0)

    def unit(self, n, carry, own):
        _, x_lo, core, _, _ = place()
        chunk, block = (n // 4, n % 4)
        slot = 3 - chunk // 2
        owner = (slot // 2 + x_lo) % 2 * 2 + (slot % 2 + core) % 2
        key_start = owner * BLOCK_LEN + chunk % 2 * BACK_KEYS
        here = slot * BLOCK_LEN + chunk % 2 * BACK_KEYS
        here = pl.ds(pl.multiple_of(here, BACK_KEYS), BACK_KEYS)
        mine = pl.ds(pl.multiple_of(block * BACK_BLOCK, BACK_BLOCK), BACK_BLOCK)
        keys = self.pairs[here]
        queries, upstream = (self.q[mine], self.g[mine])
        scores = lax.dot_general(
            keys, queries, (((1,), (1,)), ((), ())), preferred_element_type=jnp.float32
        )
        place_k = lax.broadcasted_iota(jnp.int32, scores.shape, 0)
        allowed = visible(place_k, self.low[0:1, mine], self.end[0:1, mine], key_start)
        if own:
            place_q = lax.broadcasted_iota(jnp.int32, (1, BACK_BLOCK), 1)
            place_q = place_q + (block * BACK_BLOCK - chunk % 2 * BACK_KEYS)
            allowed = allowed | (place_k == place_q)
        scores = jnp.where(allowed, scores, MASKED_SCORE)
        probs = jnp.exp(scores - self.lse[0:1, mine])
        prob_grad = lax.dot_general(
            keys, upstream, (((1,), (1,)), ((), ())), preferred_element_type=jnp.float32
        )
        score_grad = (probs * (prob_grad - self.delta[0:1, mine])).astype(jnp.bfloat16)
        self.dkv[here] += jnp.dot(
            score_grad, queries, preferred_element_type=jnp.float32
        ) + jnp.dot(probs.astype(jnp.bfloat16), upstream, preferred_element_type=jnp.float32)
        self.dq[:, mine] += jnp.dot(
            self.pairs_t[:, here], score_grad, preferred_element_type=jnp.float32
        )
        return carry

    def give(self, slot, index, add, dim):
        if add is not None:
            self.copies[add].wait_recv()

        def chunk(c, carry):
            here = pl.ds(pl.multiple_of(c * 256, 256), 256)
            there = pl.ds(pl.multiple_of(slot * BLOCK_LEN + c * 256, 256), 256)
            total = self.dkv[there]
            if add is not None:
                total = total + self.landed[add, here].astype(jnp.float32)
            self.away[index, here] = total.astype(jnp.bfloat16)
            return carry

        lax.fori_loop(0, BLOCK_LEN // 256, chunk, 0)
        self.copies[index] = self.start(
            remote(
                self.away.at[index],
                self.landed.at[index],
                self.send.at[index],
                self.recv.at[index],
                dim,
            )
        )

    def finish(self):
        self.copies[1].wait_recv()
        self.copies[2].wait_recv()

        def chunk(c, carry):
            here = pl.ds(pl.multiple_of(c * 128, 128), 128)
            total = self.dkv[here] + self.landed[1, here].astype(jnp.float32)
            total = total + self.landed[2, here].astype(jnp.float32)
            self.out[c, 0:128] = total.astype(jnp.bfloat16)
            grad = jnp.transpose(self.dq[:, here]) * HEAD ** (-0.5)
            folded = jnp.concatenate([grad[0:64, :HEAD], grad[64:128, :HEAD]], axis=1)
            self.out[c, 128:192] = folded.astype(jnp.bfloat16)
            return carry

        lax.fori_loop(0, 16, chunk, 0)


def reduce_kernel(n_left, dots, widths, with_norm, with_attention, *refs):
    refs = list(refs)

    def take(count):
        taken = refs[:count]
        del refs[:count]
        return taken

    n_right = len(dots_rights(dots))
    lefts, rights = (take(n_left), take(n_right))
    norm_in = take(1)[0] if with_norm else None
    attention_in = take(7) if with_attention else None
    out = take(1)[0]
    norm_out = take(1)[0] if with_norm else None
    head_out = take(1)[0] if with_attention else None
    left_all, right_all = (take(n_left), take(n_right))
    partial = take(1)[0]
    landed = take(6)
    norm_held, norm_landed = take(2) if with_norm else (None, None)
    attention_scratch = take(9) if with_attention else None
    act_send, act_recv, red_send, red_recv, gat_send, gat_recv, nrm_send, nrm_recv = refs
    shard, _, core, _, _ = place()
    greet(("core", "xa", "xb", "ya", "yb", "za", "zb"))
    sent = []

    def start(copy):
        copy.start()
        sent.append(copy)
        return copy

    half_tokens = lefts[0].shape[0]
    acts = []
    for i, (src, dst) in enumerate(zip(lefts, left_all)):
        acts.append(
            start(
                remote(
                    src,
                    dst.at[pl.ds(half_tokens, half_tokens)],
                    act_send.at[i],
                    act_recv.at[i],
                    "core",
                )
            )
        )
    for i, (src, dst) in enumerate(zip(rights, right_all)):
        half = src.shape[1] // 2
        theirs = pl.ds(pl.multiple_of((1 - core) * half, half), half)
        acts.append(
            start(
                remote(
                    src.at[:, theirs],
                    dst.at[pl.ds(half_tokens, half_tokens)],
                    act_send.at[n_left + i],
                    act_recv.at[n_left + i],
                    "core",
                )
            )
        )
    norm_dims = ("core",) + REDUCE_DIMS + ("xb",)
    norm_copies = []

    def norm_start(k):
        if not with_norm:
            return
        if k < 6:
            src, dst = (norm_held.at[k], norm_landed.at[k])
        else:
            src, dst = (norm_held.at[6, pl.ds(1 - shard, 1)], norm_landed.at[6, pl.ds(0, 1)])
        norm_copies.append(
            start(remote(src, dst, nrm_send.at[k], nrm_recv.at[k], norm_dims[k]))
        )

    def norm_finish(k):
        if not with_norm:
            return
        norm_copies[k].wait_recv()
        if k < 6:
            norm_held[k + 1] = norm_held[k] + norm_landed[k]
        else:
            norm_out[...] = norm_held[6, shard] + norm_landed[6, 0]

    if with_norm:
        norm_held[0] = norm_in[...]
    norm_start(0)
    for src, dst in zip(lefts, left_all):
        dst[pl.ds(0, half_tokens)] = src[...]
    for src, dst in zip(rights, right_all):
        half = src.shape[1] // 2
        dst[pl.ds(0, half_tokens)] = src[:, pl.ds(pl.multiple_of(core * half, half), half)]
    edges = [0]
    for width in widths:
        edges.append(edges[-1] + width)
    parts = range(len(widths))
    cols = [pl.ds(edges[p], widths[p]) for p in parts]
    orders = [rotated(REDUCE_DIMS, p) for p in parts]
    starts = [row_starts(orders[p], ROWS) for p in parts]
    moving = {}

    def reduce_start(p, k):
        if k < 5:
            half = ROWS >> (k + 1)
            away = pl.multiple_of(starts[p][k] + (half - (starts[p][k + 1] - starts[p][k])), 16)
            src = partial.at[:, pl.ds(away, half), cols[p]]
            dst = landed[k].at[:, :, cols[p]]
            dim = orders[p][k]
        else:
            at = pl.multiple_of(starts[p][5], 16)
            src = partial.at[1 - shard, pl.ds(at, 16), cols[p]]
            dst = landed[5].at[:, cols[p]]
            dim = "xb"
        moving[p] = start(remote(src, dst, red_send.at[p, k], red_recv.at[p, k], dim))

    def reduce_add(p, k):
        moving[p].wait_recv()
        if k < 5:
            half = ROWS >> (k + 1)
            step = min(half, 32)

            def add(i, carry):
                here = pl.ds(pl.multiple_of(i * step, step), step)
                there = pl.ds(pl.multiple_of(starts[p][k + 1] + i * step, 16), step)
                total = partial[:, there, cols[p]].astype(jnp.float32)
                total = total + landed[k][:, here, cols[p]].astype(jnp.float32)
                partial[:, there, cols[p]] = total.astype(jnp.bfloat16)
                return carry

            lax.fori_loop(0, half // step, add, 0)
        else:
            here = pl.ds(pl.multiple_of(starts[p][5], 16), 16)
            total = partial[shard, here, cols[p]].astype(jnp.float32)
            total = total + landed[5][:, cols[p]].astype(jnp.float32)
            out[core, here, cols[p]] = total.astype(jnp.bfloat16)

    def acts_arrive():
        for copy in acts:
            copy.wait_recv()
        norm_finish(0)
        norm_start(1)

    def multiply(at):
        left, left_step, left_off, right, right_off = dots[at]
        for s in range(2):
            product = lax.dot_general(
                left_all[left][:, pl.ds(s * left_step + left_off, ROWS)],
                right_all[right][:, pl.ds(right_off, 512)],
                (((0,), (0,)), ((), ())),
                preferred_element_type=jnp.float32,
            )
            partial[s, :, pl.ds(at * 512, 512)] = product.astype(jnp.bfloat16)
        for p in parts:
            if at * 512 < edges[p + 1] <= (at + 1) * 512:
                reduce_start(p, 0)

    def reduce_step(p, k):
        if p == 0:
            norm_finish(k + 1)
            if k < 5:
                norm_start(k + 2)
        reduce_add(p, k)
        if k < 5:
            reduce_start(p, k + 1)
        else:
            gather_start(p, 4)

    def gather_step(p, k):
        moving[p].wait_recv()
        if k > 0:
            gather_start(p, k - 1)
        if k == 1:
            share(p, 0, starts[p][1])
        if k == 0:
            share(p, 1, ROWS // 2 - starts[p][1])

    def range_of(p, at, size):
        return out.at[core, pl.ds(pl.multiple_of(at, 16), size), cols[p]]

    def gather_start(p, k):
        mine = range_of(p, starts[p][k + 1], ROWS >> (k + 1))
        moving[p] = start(
            remote(mine, mine, gat_send.at[p, k], gat_recv.at[p, k], orders[p][k])
        )

    shared = []

    def share(p, slot, at):
        mine = range_of(p, at, ROWS // 2)
        shared.append(
            start(remote(mine, mine, gat_send.at[p, 5 + slot], gat_recv.at[p, 5 + slot], "core"))
        )

    events = [(BACK_ACTS, acts_arrive)]
    events += [(BACK_ACTS, functools.partial(multiply, at)) for at in range(len(dots))]
    for k in range(6):
        events += [(BACK_REDUCE[k], functools.partial(reduce_step, p, k)) for p in parts]
    for k in range(4, -1, -1):
        events += [(BACK_GATHER[k], functools.partial(gather_step, p, k)) for p in parts]
    if with_attention:
        attention = AttendBack(attention_in, head_out, attention_scratch, start)
        events += attention.events
        events.sort(key=lambda e: e[0])
        done = 0
        for at, act in events:
            if at > done:
                attention.run(done, at)
                done = at
            act()
        attention.finish()
    else:
        for _, act in events:
            act()
    for copy in shared:
        copy.wait_recv()
    for copy in sent:
        copy.wait_send()


def dots_rights(dots):
    return sorted({d[3] for d in dots})


def reduce_gradients(lefts, rights, dots, widths, norm, attention, collective_id):
    tokens = lefts[0].shape[0]
    total = sum(widths)
    out_shape = [jax.ShapeDtypeStruct((2, ROWS, total), jnp.bfloat16)]
    scratch = [pltpu.VMEM((2 * tokens, a.shape[1]), jnp.bfloat16) for a in lefts]
    scratch += [pltpu.VMEM((2 * tokens, a.shape[1] // 2), jnp.bfloat16) for a in rights]
    scratch += [pltpu.VMEM((2, ROWS, total), jnp.bfloat16)]
    scratch += [pltpu.VMEM((2, ROWS >> (k + 1), total), jnp.bfloat16) for k in range(5)]
    scratch += [pltpu.VMEM((16, total), jnp.bfloat16)]
    operands = [*lefts, *rights]
    if norm is not None:
        operands.append(norm)
        out_shape.append(jax.ShapeDtypeStruct(norm.shape[1:], jnp.float32))
        scratch += [
            pltpu.VMEM((7, *norm.shape), jnp.float32),
            pltpu.VMEM((7, *norm.shape), jnp.float32),
        ]
    if attention is not None:
        operands += attention
        out_shape.append(jax.ShapeDtypeStruct((HEADS, 192, 128), jnp.bfloat16))
        scratch += back_scratch()
    n_act, parts = (len(lefts) + len(rights), len(widths))
    scratch += [pltpu.SemaphoreType.DMA((n_act,))] * 2
    scratch += [pltpu.SemaphoreType.DMA((parts, 6))] * 2
    scratch += [pltpu.SemaphoreType.DMA((parts, 7))] * 2
    scratch += [pltpu.SemaphoreType.DMA((7,))] * 2
    return pl.pallas_call(
        functools.partial(
            reduce_kernel, len(lefts), dots, widths, norm is not None, attention is not None
        ),
        out_shape=out_shape,
        in_specs=[pl.BlockSpec(memory_space=pltpu.VMEM)] * len(operands),
        out_specs=[pl.BlockSpec(memory_space=pltpu.VMEM)] * len(out_shape),
        scratch_shapes=scratch,
        compiler_params=pltpu.CompilerParams(
            collective_id=collective_id, has_side_effects=True, vmem_limit_bytes=60 * 2**20
        ),
    )(*operands)


FF_DOTS = tuple(
    [(0, 512, 0, 0, j * 512) for j in range(4)]
    + [(1, 2048, q * 512, 1, 0) for q in range(4)]
    + [(2, 512, 0, 2, 0)]
)
FF_WIDTHS = (1024, 896, 896, 896, 896)
QKV_DOTS = ((0, 512, 0, 0, 0), (0, 512, 0, 1, 0), (0, 512, 0, 2, 0))
QKV_WIDTHS = (384, 384, 256, 256, 256)


def cast_kernel(x_ref, o_ref):
    o_ref[...] = x_ref[0].astype(jnp.float32)


def cast_out(gathered, shape, grid, index_in, index_out):
    return pl.pallas_call(
        cast_kernel,
        out_shape=jax.ShapeDtypeStruct(shape, jnp.float32),
        grid=grid,
        in_specs=[pl.BlockSpec((1, ROWS, 512), index_in)],
        out_specs=pl.BlockSpec((ROWS, 512), index_out),
    )(gathered)


def square_out(gathered, slot):
    return cast_out(gathered, (ROWS, 1024), (2,), lambda c: (c, 0, slot), lambda c: (0, c))


def ff_grads_out(gathered):
    grad_in = cast_out(
        gathered, (ROWS, 4096), (2, 4), lambda c, j: (c, 0, j), lambda c, j: (0, c * 4 + j)
    )
    grad_down = cast_out(
        gathered, (2048, 1024), (4, 2), lambda q, c: (c, 0, 4 + q), lambda q, c: (q, c)
    )
    return (grad_in, grad_down, square_out(gathered, 8))


def normalize(summed_in, norm_gain, norm_bias):
    row_mean = jnp.mean(summed_in, axis=-1, keepdims=True)
    centred = summed_in - row_mean
    inv_std = lax.rsqrt(jnp.mean(centred * centred, axis=-1, keepdims=True) + NORM_EPSILON)
    scaled = centred * inv_std
    return (scaled * norm_gain + norm_bias, scaled, inv_std)


def normalize_back(upstream, scaled, inv_std, norm_gain):
    weighted = upstream * norm_gain
    centred = weighted - jnp.mean(weighted, axis=-1, keepdims=True)
    result = inv_std * (centred - scaled * jnp.mean(weighted * scaled, axis=-1, keepdims=True))
    return (result, jnp.sum(upstream * scaled, axis=0), jnp.sum(upstream, axis=0))


def exact_gelu(values):
    return jax.nn.gelu(values, approximate=False)


def to_tokens(packed):
    return packed.reshape(HEADS, 64, 2, HEAD).transpose(2, 1, 0, 3).reshape(128, HEADS * HEAD)


def to_heads(rows):
    return rows.reshape(2, 64, HEADS, HEAD).transpose(2, 1, 0, 3).reshape(HEADS, 64, 2 * HEAD)


def swap(packed):
    return lax.all_to_all(packed, "aa", split_axis=0, concat_axis=0, tiled=True)


def shards(
    tokens,
    segments,
    valid,
    w_query,
    w_key,
    w_value,
    w_out,
    norm1_gain,
    norm1_bias,
    w_in,
    w_down,
    norm2_gain,
    norm2_bias,
    cotangent,
):
    packed = jnp.zeros((16, 512), jnp.bfloat16).at[:4].set(
        jnp.stack([norm1_gain, norm1_bias, norm2_gain, norm2_bias])
    )
    token_rows = tokens[0]
    low, end = query_spans(segments[0], valid[0], lax.axis_index("blk") * BLOCK_LEN)
    (
        full_qkv,
        full_out,
        full_in,
        full_down,
        norms,
        queries,
        pairs,
        summed,
        lse,
        mixed,
    ) = front(token_rows, [w_query, w_key, w_value, w_out, w_in, w_down], packed, low, end)
    norms = norms[:, :4].transpose(1, 0, 2).reshape(4, 1024).astype(jnp.float32)
    gain_one, bias_one, gain_two, bias_two = norms
    mixed = to_tokens(mixed)

    attn = jnp.dot(mixed, full_out, preferred_element_type=jnp.float32)
    first, scaled_one, inv_one = normalize(
        token_rows.astype(jnp.float32) + attn, gain_one, bias_one
    )
    first_low = first.astype(jnp.bfloat16)
    pre = jnp.dot(first_low, full_in, preferred_element_type=jnp.float32)
    hidden = exact_gelu(pre).astype(jnp.bfloat16)
    ff_out = jnp.dot(hidden, full_down, preferred_element_type=jnp.float32)
    result, scaled_two, inv_two = normalize(first + ff_out, gain_two, bias_two)
    upstream = cotangent[0].astype(jnp.float32)
    grad_two, grad_gain_two, grad_bias_two = normalize_back(upstream, scaled_two, inv_two, gain_two)
    ff_grad = grad_two.astype(jnp.bfloat16)
    hidden_grad = jnp.einsum("td,fd->tf", ff_grad, full_down, preferred_element_type=jnp.float32)
    gelu_pull = jax.vjp(exact_gelu, pre)[1]
    pre_grad = gelu_pull(hidden_grad)[0].astype(jnp.bfloat16)
    first_grad = grad_two + jnp.einsum(
        "tf,df->td", pre_grad, full_in, preferred_element_type=jnp.float32
    )
    grad_one, grad_gain_one, grad_bias_one = normalize_back(
        first_grad, scaled_one, inv_one, gain_one
    )
    attn_grad = grad_one.astype(jnp.bfloat16)
    mixed_grad = jnp.einsum(
        "td,cd->tc", attn_grad, full_out, preferred_element_type=jnp.float32
    ).astype(jnp.bfloat16)
    norm_sums = jnp.stack([grad_gain_one, grad_bias_one, grad_gain_two, grad_bias_two])
    norm_sums = jnp.pad(norm_sums.reshape(4, 2, 512).transpose(1, 0, 2), ((0, 0), (0, 4), (0, 0)))

    ff_summed, norm_total, head_grads = reduce_gradients(
        [first_low, hidden, mixed],
        [pre_grad, ff_grad, attn_grad],
        FF_DOTS,
        FF_WIDTHS,
        norm_sums,
        [
            queries,
            swap(to_heads(mixed_grad)),
            pairs,
            low,
            end,
            lse,
            summed,
        ],
        1,
    )
    grad_in, grad_down, grad_out = ff_grads_out(ff_summed)
    token_grads = swap(head_grads)
    query_tok = to_tokens(token_grads[:, 128:192])
    key_tok = token_grads[:, 0:128, :HEAD].transpose(1, 0, 2).reshape(128, 1024)
    value_tok = token_grads[:, 0:128, HEAD:].transpose(1, 0, 2).reshape(128, 1024)
    all_tok = jnp.concatenate([query_tok, key_tok, value_tok], axis=1)
    input_grad = grad_one + jnp.einsum(
        "td,cd->tc", all_tok, full_qkv, preferred_element_type=jnp.float32
    )
    qkv_summed = reduce_gradients(
        [token_rows], [query_tok, key_tok, value_tok], QKV_DOTS, QKV_WIDTHS, None, None, 2
    )[0]
    return (
        result.astype(jnp.bfloat16)[None],
        input_grad.astype(jnp.bfloat16)[None],
        square_out(qkv_summed, 0),
        square_out(qkv_summed, 1),
        square_out(qkv_summed, 2),
        grad_out,
        norm_total[0],
        norm_total[1],
        grad_in,
        grad_down,
        norm_total[2],
        norm_total[3],
    )


def solution(mesh):
    return jax.shard_map(
        shards,
        mesh=mesh,
        in_specs=(
            P("shard", ("blk", "aa"), None),
            P("shard", None),
            P("shard", None),
            P("shard", None),
            P("shard", None),
            P("shard", None),
            P("shard", None),
            P("shard"),
            P("shard"),
            P("shard", None),
            P("shard", None),
            P("shard"),
            P("shard"),
            P("shard", ("blk", "aa"), None),
        ),
        out_specs=(
            P("shard", ("blk", "aa"), None),
            P("shard", ("blk", "aa"), None),
            P("shard", None),
            P("shard", None),
            P("shard", None),
            P("shard", None),
            P("shard"),
            P("shard"),
            P("shard", None),
            P("shard", None),
            P("shard"),
            P("shard"),
        ),
        check_vma=False,
    )
```

```python
import functools

import jax
import jax.numpy as jnp
from jax import lax
from jax.experimental import pallas as pl
from jax.experimental.pallas import tpu as pltpu
from jax.sharding import PartitionSpec as P

HEADS = 16
HEAD = 64
MASKED_SCORE = -1e30
NORM_EPSILON = 1e-05
BLOCK_LEN = 2048


MESH = pl.DeviceIdType.MESH
ROWS = 512
REDUCE_DIMS = ("xa", "ya", "za", "yb", "zb")
GATHER_DIMS = ("ya", "za", "yb", "zb")


def place():
    shard = lax.axis_index("shard")
    blk = lax.axis_index("blk")
    aa = lax.axis_index("aa")
    return (shard, blk // 2, blk % 2, aa // 4, aa % 4)


def flipped(i):
    return i + 1 - 2 * (i % 2)


def partner(dim):
    shard, x_lo, core, z, y = place()
    if dim == "core":
        core = 1 - core
    elif dim == "xa":
        x_lo = 1 - x_lo
    elif dim == "xb":
        shard, x_lo = 1 - shard, 1 - x_lo
    elif dim == "ya":
        y = flipped(y)
    elif dim == "yb":
        y = 3 - y
    elif dim == "za":
        z = flipped(z)
    else:
        z = 3 - z
    return (shard, x_lo * 2 + core, z * 4 + y)


def ring_bit(dim):
    shard, x_lo, _, z, y = place()
    if dim == "xa":
        return (shard * 2 + x_lo + shard) % 2
    if dim == "ya":
        return (y + y // 2) % 2
    if dim == "yb":
        return y // 2
    if dim == "za":
        return (z + z // 2) % 2
    return z // 2


def remote(src, dst, send_sem, recv_sem, dim):
    return pltpu.make_async_remote_copy(
        src_ref=src,
        dst_ref=dst,
        send_sem=send_sem,
        recv_sem=recv_sem,
        device_id=partner(dim),
        device_id_type=MESH,
    )


def row_starts(dims, rows):
    starts, at, size = ([0], 0, rows)
    for dim in dims:
        size //= 2
        at = at + ring_bit(dim) * size
        starts.append(at)
    return starts


def rotated(dims, by):
    return dims[by:] + dims[:by]


class Gather:
    def __init__(self, sources, places, send, recv, start):
        self.sources, self.places = (sources, places)
        self.send, self.recv, self.start = (send, recv, start)
        self.shard, _, self.core, _, _ = place()
        self.orders = [rotated(GATHER_DIMS, part) for part in range(4)]
        self.moving, self.siblings = ({}, [])

    def columns(self, i, part, off):
        cols = self.sources[i].shape[1]
        col = pl.multiple_of(self.core * (cols // 2) + (off + part * (cols // 8)), 128)
        return pl.ds(col, cols // 8)

    def block(self, i, part, shard, at, size):
        target, off = self.places[i]
        rows = self.sources[i].shape[0]
        at = pl.multiple_of(shard * rows + at, 16)
        return target.at[pl.ds(at, size), self.columns(i, part, off)]

    def own(self, i):
        target, off = self.places[i]
        rows, cols = self.sources[i].shape
        return target.at[pl.ds(pl.multiple_of(self.shard * rows, rows), rows), pl.ds(off, cols)]

    def begin(self, i):
        rows = self.sources[i].shape[0]
        for part in range(4):
            at = row_starts(self.orders[part], rows)[4]
            mine = pl.ds(pl.multiple_of(at, 16), rows // 16)
            self.moving[i, part] = self.start(
                remote(
                    self.sources[i].at[mine, self.columns(i, part, 0)],
                    self.block(i, part, self.shard, at, rows // 16),
                    self.send.at[i, part, 0],
                    self.recv.at[i, part, 0],
                    "xb",
                )
            )

    def stage(self, i, stage):
        rows = self.sources[i].shape[0]
        for part in range(4):
            self.moving[i, part].wait_recv()
            starts = row_starts(self.orders[part], rows)
            if stage < 5:
                k = 4 - stage
                mine = self.block(i, part, 1 - self.shard, starts[k + 1], rows >> (k + 1))
                self.moving[i, part] = self.start(
                    remote(
                        mine,
                        mine,
                        self.send.at[i, part, stage],
                        self.recv.at[i, part, stage],
                        self.orders[part][k],
                    )
                )
            if stage >= 4:
                at = starts[1] if stage == 4 else rows // 2 - starts[1]
                mine = self.block(i, part, 1 - self.shard, at, rows // 2)
                self.siblings.append(
                    self.start(
                        remote(
                            mine,
                            mine,
                            self.send.at[i, part, stage + 1],
                            self.recv.at[i, part, stage + 1],
                            "core",
                        )
                    )
                )

    def finish(self):
        for copy in self.siblings:
            copy.wait_recv()
        self.siblings = []


def plane_peer(step):
    shard, x_lo, core, z, y = place()
    return (shard, x_lo * 2 + core, (z * 4 + y + step) % 16)


class Exchange:
    def __init__(self, outgoing, incoming, send, recv, start):
        self.outgoing, self.incoming = (outgoing, incoming)
        self.send, self.recv, self.start = (send, recv, start)
        self.copies = []

    def begin(self):
        me = lax.axis_index("aa")
        for step in (1, 3, 4, 12, 15, 13, 5, 11, 2, 8, 14, 6, 10, 7, 9):
            self.copies.append(
                self.start(
                    pltpu.make_async_remote_copy(
                        src_ref=self.outgoing.at[(me + step) % 16],
                        dst_ref=self.incoming.at[me],
                        send_sem=self.send.at[step],
                        recv_sem=self.recv.at[step],
                        device_id=plane_peer(step),
                        device_id_type=MESH,
                    )
                )
            )
        self.incoming[me] = self.outgoing[me]

    def finish(self):
        for copy in self.copies:
            copy.wait_recv()


def greet_all(dims):
    barrier = pltpu.get_barrier_semaphore()
    for dim in dims:
        pl.semaphore_signal(barrier, inc=1, device_id=partner(dim), device_id_type=MESH)
    for step in range(1, 16):
        pl.semaphore_signal(barrier, inc=1, device_id=plane_peer(step), device_id_type=MESH)
    pl.semaphore_wait(barrier, len(dims) + 15)


def unfolded(block, side):
    lane = lax.broadcasted_iota(jnp.int32, (64, 128), 1)
    keep = (lane >= HEAD) if side else (lane < HEAD)
    block = block.astype(jnp.float32)
    moved = jnp.concatenate([block[:, HEAD:], block[:, :HEAD]], axis=1)
    first, second = (moved, block) if side else (block, moved)
    both = jnp.concatenate([jnp.where(keep, first, 0.0), jnp.where(keep, second, 0.0)], axis=0)
    return both.astype(jnp.bfloat16)


LEAST = -(2**31)
FRONT_BLOCK = 512


def visible(place_k, low, end, start):
    size = jnp.maximum(end - low, 0) + LEAST
    return (place_k - (low - start - LEAST)) < size


def query_spans(segments_ref, valid_ref, low_ref, end_ref):
    _, x_lo, core, _, _ = place()
    segments = segments_ref[...]
    start = pl.multiple_of((x_lo * 2 + core) * 16, 16)
    mine = segments_ref[pl.ds(start, 16)]
    low, end = (jnp.zeros_like(mine), jnp.zeros_like(mine))
    before = jnp.zeros((1, 1), jnp.int32)
    for number in range(35):
        same = jnp.where(segments == number, 1, 0)
        count = jnp.sum(jnp.sum(same, axis=1, keepdims=True), axis=0, keepdims=True)
        picked = mine == number
        low = jnp.where(picked, before, low)
        before = before + count
        end = jnp.where(picked, before, end)
    live = jnp.sum(jnp.sum(valid_ref[...], axis=1, keepdims=True), axis=0, keepdims=True)
    end = jnp.minimum(end, live)
    for row in range(16):
        here = pl.ds(row * 128, 128)
        low_ref[:, here] = jnp.broadcast_to(low[row : row + 1], (8, 128))
        end_ref[:, here] = jnp.broadcast_to(end[row : row + 1], (8, 128))


def front_kernel(
    x_ref,
    wq_ref,
    wk_ref,
    wv_ref,
    wo_ref,
    wi_ref,
    wd_ref,
    norm_ref,
    segments_ref,
    valid_ref,
    qkv_out,
    out_out,
    in_out,
    down_out,
    norm_out,
    q_out,
    pairs_out,
    o_out,
    lse_out,
    mixed_out,
    low_ref,
    end_ref,
    wqkv,
    staged,
    heads_in,
    folded,
    pairs_t,
    top_s,
    send,
    recv,
    own_in,
    own_out,
    hop_send,
    hop_recv,
    swap_send,
    swap_recv,
    back_send,
    back_recv,
    *bounce,
):
    shard, _, _, _, _ = place()
    sent = []

    def start(copy):
        copy.start()
        sent.append(copy)
        return copy

    gather = Gather(
        [wq_ref, wk_ref, wv_ref, wo_ref, wi_ref, wd_ref],
        [(wqkv, 0), (wqkv, 1024), (wqkv, 2048), (out_out, 0), (in_out, 0), (down_out, 0)],
        send,
        recv,
        start,
    )
    inward = []
    for i in range(6):
        target = gather.own(i) if i < 3 else bounce[i - 3]
        inward.append(pltpu.make_async_copy(gather.sources[i], target, own_in.at[i]))
        inward[i].start()
    greet_all(("core", "xa", "xb"))
    norms = start(
        remote(norm_ref, norm_out.at[shard], hop_send.at[3], hop_recv.at[3], "xb")
    )
    norm_out[shard] = norm_ref[...]
    for i in range(6):
        gather.begin(i)
    query_spans(segments_ref, valid_ref, low_ref, end_ref)
    for i in range(3):
        gather.stage(i, 1)
    outward = []
    for i in range(3, 6):
        inward[i].wait()
        outward.append(pltpu.make_async_copy(bounce[i - 3], gather.own(i), own_out.at[i - 3]))
        outward[-1].start()
    for stage in range(2, 6):
        for i in range(3):
            gather.stage(i, stage)
        if stage == 3:
            for i in range(3, 6):
                gather.stage(i, 1)
    for i in range(3):
        inward[i].wait()
    gather.finish()
    keep = pltpu.make_async_copy(wqkv, qkv_out, own_out.at[3])
    keep.start()

    def project(piece, carry):
        q, k, v = [
            jnp.dot(
                x_ref[...],
                wqkv[:, pl.ds(pl.multiple_of(which * 1024 + piece * 256, 256), 256)],
                preferred_element_type=jnp.float32,
            )
            for which in range(3)
        ]
        q = (q.astype(jnp.bfloat16).astype(jnp.float32) * HEAD ** (-0.5)).astype(jnp.bfloat16)
        k, v = (k.astype(jnp.bfloat16), v.astype(jnp.bfloat16))
        for h in range(4):
            at = slice(h * HEAD, (h + 1) * HEAD)
            staged[piece * 4 + h, 0:128] = jnp.concatenate([k[:, at], v[:, at]], axis=1)
            staged[piece * 4 + h, 128:192] = jnp.concatenate([q[0:64, at], q[64:128, at]], axis=1)
        return carry

    lax.fori_loop(0, 4, project, 0)
    heads = Exchange(staged, heads_in, swap_send, swap_recv, start)
    heads.begin()
    for i in range(3, 6):
        gather.stage(i, 2)
    heads.finish()

    def spread(c, carry):
        here = pl.ds(pl.multiple_of(c * 128, 128), 128)
        pairs_out[here] = heads_in[c, 0:128]
        q_out[here] = unfolded(heads_in[c, 128:192], 0)
        return carry

    lax.fori_loop(0, 16, spread, 0)

    def slot_rows(slot):
        return pairs_out.at[pl.ds(slot * BLOCK_LEN, BLOCK_LEN)]

    def hop(index, source, target, dim):
        return start(
            remote(
                slot_rows(source), slot_rows(target), hop_send.at[index], hop_recv.at[index], dim
            )
        )

    hops = {1: hop(0, 0, 1, "core"), 2: hop(1, 0, 2, "xa")}
    top_s[...] = jnp.full_like(top_s, MASKED_SCORE)
    o_out[...] = jnp.zeros_like(o_out)
    first_row = lax.broadcasted_iota(jnp.int32, (128, 512), 0) == 0

    def turn(c, carry):
        here = pl.ds(pl.multiple_of(c * 512, 512), 512)
        turned = jnp.transpose(pairs_out[here].astype(jnp.float32))
        pairs_t[:, here] = jnp.where(first_row, 1.0, turned).astype(jnp.bfloat16)
        return carry

    def slot_step(slot, block):
        _, x_lo, core, _, _ = place()
        owner = (slot // 2 + x_lo) % 2 * 2 + (slot % 2 + core) % 2
        rows = pl.ds(slot * BLOCK_LEN, BLOCK_LEN)
        mine = pl.ds(pl.multiple_of(block * FRONT_BLOCK, FRONT_BLOCK), FRONT_BLOCK)
        scores = lax.dot_general(
            pairs_out[rows],
            q_out[mine],
            (((1,), (1,)), ((), ())),
            preferred_element_type=jnp.float32,
        )
        place_k = lax.broadcasted_iota(jnp.int32, scores.shape, 0)
        allowed = visible(place_k, low_ref[0:1, mine], end_ref[0:1, mine], owner * BLOCK_LEN)
        if slot == 0:
            place_q = lax.broadcasted_iota(jnp.int32, (1, FRONT_BLOCK), 1) + block * FRONT_BLOCK
            allowed = allowed | (place_k == place_q)
        scores = jnp.where(allowed, scores, MASKED_SCORE)
        top = top_s[0:1, mine]
        new_top = jnp.maximum(top, jnp.max(scores, axis=0, keepdims=True))
        weights = jnp.exp(scores - new_top)
        factor = jnp.exp(top - new_top)
        o_out[:, mine] = o_out[:, mine] * factor + jnp.dot(
            pairs_t[:, rows], weights.astype(jnp.bfloat16), preferred_element_type=jnp.float32
        )
        top_s[:, mine] = jnp.broadcast_to(new_top, (8, FRONT_BLOCK))

    events = {
        0: [(i, 3) for i in (3, 4, 5)],
        1: [(i, 4) for i in (3, 4, 5)],
        3: [(i, 5) for i in (3, 4, 5)],
    }
    for slot in range(4):
        if slot:
            hops[slot].wait_recv()
        if slot == 2:
            hops[3] = hop(2, 2, 3, "core")
        lax.fori_loop(slot * 4, slot * 4 + 4, turn, 0)
        for half in range(2):

            def blocks(b, carry):
                slot_step(slot, b)
                return carry

            lax.fori_loop(half * 2, half * 2 + 2, blocks, 0)
            if half == 0:
                for i, stage in events.get(slot, ()):
                    gather.stage(i, stage)

    def close(c, carry):
        here = pl.ds(pl.multiple_of(c * 128, 128), 128)
        total = o_out[0:1, here]
        mixed = o_out[:, here] / total
        o_out[:, here] = mixed
        lse = top_s[0:1, here] + jnp.log(total)
        lse_out[:, here] = jnp.broadcast_to(lse, (8, 128))
        block = jnp.transpose(mixed)
        both = jnp.concatenate([block[0:64, HEAD:], block[64:128, HEAD:]], axis=1)
        folded[c] = both.astype(jnp.bfloat16)
        return carry

    lax.fori_loop(0, 16, close, 0)
    back = Exchange(folded, mixed_out, back_send, back_recv, start)
    back.begin()
    gather.finish()
    norms.wait_recv()
    back.finish()
    for copy in outward:
        copy.wait()
    keep.wait()
    for copy in sent:
        copy.wait_send()


def front(token_rows, weights, packed, segments, valid):
    bf16, f32 = (jnp.bfloat16, jnp.float32)
    n = len(weights)
    whole, anywhere = (pl.BlockSpec(memory_space=pltpu.VMEM), pl.BlockSpec(memory_space=pl.ANY))
    return pl.pallas_call(
        front_kernel,
        out_shape=[
            jax.ShapeDtypeStruct((1024, 3072), bf16),
            jax.ShapeDtypeStruct((1024, 1024), bf16),
            jax.ShapeDtypeStruct((1024, 4096), bf16),
            jax.ShapeDtypeStruct((4096, 1024), bf16),
            jax.ShapeDtypeStruct((2, 16, 512), bf16),
            jax.ShapeDtypeStruct((BLOCK_LEN, 128), bf16),
            jax.ShapeDtypeStruct((4 * BLOCK_LEN, 128), bf16),
            jax.ShapeDtypeStruct((128, BLOCK_LEN), f32),
            jax.ShapeDtypeStruct((8, BLOCK_LEN), f32),
            jax.ShapeDtypeStruct((16, 64, 128), bf16),
            jax.ShapeDtypeStruct((8, BLOCK_LEN), jnp.int32),
            jax.ShapeDtypeStruct((8, BLOCK_LEN), jnp.int32),
        ],
        in_specs=[whole] + [anywhere] * n + [whole] * 3,
        out_specs=[anywhere] * 4 + [whole] * 8,
        scratch_shapes=[
            pltpu.VMEM((1024, 3072), bf16),
            pltpu.VMEM((16, 192, 128), bf16),
            pltpu.VMEM((16, 192, 128), bf16),
            pltpu.VMEM((16, 64, 128), bf16),
            pltpu.VMEM((128, 4 * BLOCK_LEN), bf16),
            pltpu.VMEM((8, BLOCK_LEN), f32),
            pltpu.SemaphoreType.DMA((n, 4, 7)),
            pltpu.SemaphoreType.DMA((n, 4, 7)),
            pltpu.SemaphoreType.DMA((n,)),
            pltpu.SemaphoreType.DMA((4,)),
            pltpu.SemaphoreType.DMA((4,)),
            pltpu.SemaphoreType.DMA((4,)),
            pltpu.SemaphoreType.DMA((16,)),
            pltpu.SemaphoreType.DMA((16,)),
            pltpu.SemaphoreType.DMA((16,)),
            pltpu.SemaphoreType.DMA((16,)),
            *[pltpu.VMEM(w.shape, bf16) for w in weights[3:]],
        ],
        compiler_params=pltpu.CompilerParams(
            collective_id=0, has_side_effects=True, vmem_limit_bytes=60 * 2**20
        ),
    )(token_rows, *weights, packed, segments.reshape(64, 128), valid.reshape(64, 128))


BACK_REDUCE = (7, 12)
SLOT_UNITS = 4
BACK_BLOCK = 512


def back_scratch():
    return [
        pltpu.VMEM((BLOCK_LEN, 128), jnp.bfloat16),
        pltpu.VMEM((128, 4 * BLOCK_LEN), jnp.bfloat16),
        pltpu.VMEM((8, BLOCK_LEN), jnp.float32),
        pltpu.VMEM((128, BLOCK_LEN), jnp.float32),
        pltpu.VMEM((4 * BLOCK_LEN, 128), jnp.float32),
        pltpu.VMEM((3, BLOCK_LEN, 128), jnp.bfloat16),
        pltpu.VMEM((3, BLOCK_LEN, 128), jnp.bfloat16),
        pltpu.SemaphoreType.DMA((3,)),
        pltpu.SemaphoreType.DMA((3,)),
    ]


class AttendBack:
    def __init__(self, ins, out, scratch, start):
        self.q, self.packed, self.pairs, self.low, self.end, self.lse, self.o_t = ins
        self.out = out
        self.g, self.pairs_t, self.delta, self.dq, self.dkv = scratch[:5]
        self.away, self.landed, self.send, self.recv = scratch[5:9]
        self.start = start
        self.copies = {}
        self.events = [
            (0, self.begin),
            (SLOT_UNITS, lambda: self.give(3, 0, None, "core")),
            (2 * SLOT_UNITS + 1, lambda: self.give(2, 1, 0, "xa")),
            (3 * SLOT_UNITS, lambda: self.give(1, 2, None, "core")),
        ]

    def begin(self):
        self.delta[...] = jnp.zeros_like(self.delta)
        self.dq[...] = jnp.zeros_like(self.dq)
        self.dkv[...] = jnp.zeros_like(self.dkv)

        def chunk(c, carry):
            both = unfolded(self.packed[c], 1)
            here = pl.ds(pl.multiple_of(c * 128, 128), 128)
            self.g[here] = both
            products = jnp.transpose(both.astype(jnp.float32)) * self.o_t[:, here]
            total = jnp.sum(products, axis=0, keepdims=True)
            self.delta[:, here] = jnp.broadcast_to(total, (8, 128))
            return carry

        lax.fori_loop(0, 16, chunk, 0)

        def turn(c, carry):
            here = pl.ds(pl.multiple_of(c * 512, 512), 512)
            self.pairs_t[:, here] = jnp.transpose(self.pairs[here])
            return carry

        lax.fori_loop(0, 16, turn, 0)

    def run(self, first, last):
        edge = 3 * SLOT_UNITS
        if first < edge:
            lax.fori_loop(first, min(last, edge), functools.partial(self.unit, own=False), 0)
        if last > edge:
            lax.fori_loop(max(first, edge), last, functools.partial(self.unit, own=True), 0)

    def unit(self, n, carry, own):
        _, x_lo, core, _, _ = place()
        block = n % 4
        slot = 3 - n // 4
        owner = (slot // 2 + x_lo) % 2 * 2 + (slot % 2 + core) % 2
        key_start = owner * BLOCK_LEN
        here = pl.ds(pl.multiple_of(slot * BLOCK_LEN, BLOCK_LEN), BLOCK_LEN)
        mine = pl.ds(pl.multiple_of(block * BACK_BLOCK, BACK_BLOCK), BACK_BLOCK)
        keys = self.pairs[here]
        queries, upstream = (self.q[mine], self.g[mine])
        scores = lax.dot_general(
            keys, queries, (((1,), (1,)), ((), ())), preferred_element_type=jnp.float32
        )
        place_k = lax.broadcasted_iota(jnp.int32, scores.shape, 0)
        allowed = visible(place_k, self.low[0:1, mine], self.end[0:1, mine], key_start)
        if own:
            place_q = lax.broadcasted_iota(jnp.int32, (1, BACK_BLOCK), 1)
            place_q = place_q + block * BACK_BLOCK
            allowed = allowed | (place_k == place_q)
        scores = jnp.where(allowed, scores, MASKED_SCORE)
        probs = jnp.exp(scores - self.lse[0:1, mine])
        prob_grad = lax.dot_general(
            keys, upstream, (((1,), (1,)), ((), ())), preferred_element_type=jnp.float32
        )
        score_grad = (probs * (prob_grad - self.delta[0:1, mine])).astype(jnp.bfloat16)
        self.dkv[here] += jnp.dot(
            score_grad, queries, preferred_element_type=jnp.float32
        ) + jnp.dot(probs.astype(jnp.bfloat16), upstream, preferred_element_type=jnp.float32)
        self.dq[:, mine] += jnp.dot(
            self.pairs_t[:, here], score_grad, preferred_element_type=jnp.float32
        )
        return carry

    def give(self, slot, index, add, dim):
        if add is not None:
            self.copies[add].wait_recv()

        def chunk(c, carry):
            here = pl.ds(pl.multiple_of(c * 256, 256), 256)
            there = pl.ds(pl.multiple_of(slot * BLOCK_LEN + c * 256, 256), 256)
            total = self.dkv[there]
            if add is not None:
                total = total + self.landed[add, here].astype(jnp.float32)
            self.away[index, here] = total.astype(jnp.bfloat16)
            return carry

        lax.fori_loop(0, BLOCK_LEN // 256, chunk, 0)
        self.copies[index] = self.start(
            remote(
                self.away.at[index],
                self.landed.at[index],
                self.send.at[index],
                self.recv.at[index],
                dim,
            )
        )

    def finish(self):
        self.copies[1].wait_recv()
        self.copies[2].wait_recv()

        def chunk(c, carry):
            here = pl.ds(pl.multiple_of(c * 128, 128), 128)
            total = self.dkv[here] + self.landed[1, here].astype(jnp.float32)
            total = total + self.landed[2, here].astype(jnp.float32)
            self.out[c, 0:128] = total.astype(jnp.bfloat16)
            grad = jnp.transpose(self.dq[:, here]) * HEAD ** (-0.5)
            folded = jnp.concatenate([grad[0:64, :HEAD], grad[64:128, :HEAD]], axis=1)
            self.out[c, 128:192] = folded.astype(jnp.bfloat16)
            return carry

        lax.fori_loop(0, 16, chunk, 0)


class Reducer:
    def __init__(self, acts, dots, widths, refs, start):
        self.acts, self.dots, self.start = (acts, dots, start)
        self.partial, self.landed, self.last, self.out = (refs[0], refs[1:7], refs[7], refs[8])
        self.act_send, self.act_recv, self.red_send, self.red_recv = refs[9:13]
        self.gat_send, self.gat_recv, self.own = refs[13:16]
        self.shard, _, self.core, _, _ = place()
        self.parts = range(len(widths))
        self.edges = [sum(widths[:p]) for p in range(len(widths) + 1)]
        self.cols = [pl.ds(self.edges[p], widths[p]) for p in self.parts]
        self.orders = [rotated(REDUCE_DIMS, p) for p in self.parts]
        self.starts = [row_starts(self.orders[p], ROWS) for p in self.parts]
        self.moving, self.held, self.shared = ({}, {}, [])

    def pool(self, i, src, whole):
        dst = self.acts[i]
        tokens = src.shape[0]
        half = src.shape[1] // 2
        mine, theirs = [
            src if whole else src.at[:, pl.ds(pl.multiple_of(c * half, half), half)]
            for c in (self.core, 1 - self.core)
        ]
        near = pltpu.make_async_copy(mine, dst.at[pl.ds(0, tokens)], self.own.at[i])
        near.start()
        far = remote(
            theirs, dst.at[pl.ds(tokens, tokens)], self.act_send.at[i], self.act_recv.at[i], "core"
        )
        return (near, self.start(far))

    def multiply(self, at):
        left, left_step, left_off, right, right_off = self.dots[at]
        for s in range(2):
            product = lax.dot_general(
                self.acts[left][:, pl.ds(s * left_step + left_off, ROWS)],
                self.acts[right][:, pl.ds(right_off, 512)],
                (((0,), (0,)), ((), ())),
                preferred_element_type=jnp.float32,
            )
            self.partial[s, :, pl.ds(at * 512, 512)] = product.astype(jnp.bfloat16)
        for p in self.parts:
            if at * 512 < self.edges[p + 1] <= (at + 1) * 512:
                self.reduce_start(p, 0)

    def reduce_start(self, p, k):
        starts, cols = (self.starts[p], self.cols[p])
        if k < 5:
            half = ROWS >> (k + 1)
            away = pl.multiple_of(starts[k] + (half - (starts[k + 1] - starts[k])), 16)
            src = self.partial.at[:, pl.ds(away, half), cols]
            dst = self.landed[k].at[:, :, cols]
            dim = self.orders[p][k]
        else:
            src = self.partial.at[1 - self.shard, pl.ds(pl.multiple_of(starts[5], 16), 16), cols]
            dst = self.landed[5].at[:, cols]
            dim = "xb"
        self.moving[p] = self.start(
            remote(src, dst, self.red_send.at[p, k], self.red_recv.at[p, k], dim)
        )

    def reduce_step(self, p, k):
        self.moving[p].wait_recv()
        starts, cols = (self.starts[p], self.cols[p])
        if k < 5:
            half = ROWS >> (k + 1)
            step = min(half, 32)

            def add(i, carry):
                here = pl.ds(pl.multiple_of(i * step, step), step)
                there = pl.ds(pl.multiple_of(starts[k + 1] + i * step, 16), step)
                self.partial[:, there, cols] += self.landed[k][:, here, cols]
                return carry

            lax.fori_loop(0, half // step, add, 0)
            self.reduce_start(p, k + 1)
        else:
            here = pl.ds(pl.multiple_of(starts[5], 16), 16)
            self.last[:, cols] = self.partial[self.shard, here, cols] + self.landed[5][:, cols]
            self.held[p] = pltpu.make_async_copy(
                self.last.at[:, cols], self.rows_out(p, starts[5], 16), self.own.at[8 + p]
            )
            self.held[p].start()
            self.gather_start(p, 4)

    def rows_out(self, p, at, size):
        return self.out.at[self.core, pl.ds(pl.multiple_of(at, 16), size), self.cols[p]]

    def gather_start(self, p, k):
        mine = self.rows_out(p, self.starts[p][k + 1], ROWS >> (k + 1))
        src = self.last.at[:, self.cols[p]] if k == 4 else mine
        self.moving[p] = self.start(
            remote(src, mine, self.gat_send.at[p, k], self.gat_recv.at[p, k], self.orders[p][k])
        )

    def gather_step(self, p, k):
        self.moving[p].wait_recv()
        if k == 4:
            self.held[p].wait()
        if k > 0:
            self.gather_start(p, k - 1)
        if k == 1:
            self.share(p, 0, self.starts[p][1])
        if k == 0:
            self.share(p, 1, ROWS // 2 - self.starts[p][1])

    def share(self, p, slot, at):
        mine = self.rows_out(p, at, ROWS // 2)
        sems = (self.gat_send.at[p, 5 + slot], self.gat_recv.at[p, 5 + slot])
        self.shared.append(self.start(remote(mine, mine, *sems, "core")))

    def finish(self):
        for copy in self.shared:
            copy.wait_recv()


class NormSums:
    def __init__(self, held, landed, out, send, recv, start):
        self.held, self.landed, self.out = (held, landed, out)
        self.send, self.recv, self.start = (send, recv, start)
        self.dims = ("core",) + REDUCE_DIMS + ("xb",)

    def begin(self, k):
        shard, _, _, _, _ = place()
        if k < 6:
            src, dst = (self.held.at[k], self.landed.at[k])
        else:
            src, dst = (self.held.at[6, pl.ds(1 - shard, 1)], self.landed.at[6, pl.ds(0, 1)])
        self.copy = self.start(remote(src, dst, self.send.at[k], self.recv.at[k], self.dims[k]))

    def step(self, k):
        shard, _, _, _, _ = place()
        self.copy.wait_recv()
        if k < 6:
            self.held[k + 1] = self.held[k] + self.landed[k]
            self.begin(k + 1)
        else:
            self.out[...] = self.held[6, shard] + self.landed[6, 0]


def back_kernel(*refs):
    refs = list(refs)

    def take(count):
        taken = refs[:count]
        del refs[:count]
        return taken

    first_ref, hidden_ref, mixed_ref, pre_ref, down_ref, attn_ref, x_ref = take(7)
    norm_ref, mixed_grad, q_ref, pairs_ref, low_ref, end_ref, lse_ref, o_ref = take(8)
    ff_out, qkv_out, norm_out, tok_out = take(4)
    ff_acts, qkv_acts = (take(6), take(4))
    ff_refs = take(8) + [ff_out] + take(7)
    qkv_refs = take(8) + [qkv_out] + take(7)
    norm_refs = take(2) + [norm_out] + take(2)
    staged, heads_in, heads_out, tok_in = take(4)
    swaps = [take(2), take(2)]
    attention_refs = refs
    sent = []

    def start(copy):
        copy.start()
        sent.append(copy)
        return copy

    for pair in range(8):
        both = mixed_grad[:, pair * 128 : (pair + 1) * 128]
        for side in range(2):
            head = both[:, side * HEAD : (side + 1) * HEAD]
            staged[pair * 2 + side] = jnp.concatenate([head[0:64], head[64:128]], axis=1)
    greet_all(("core", "xa", "xb"))
    ff = Reducer(ff_acts, FF_DOTS, FF_WIDTHS, ff_refs, start)
    qkv = Reducer(qkv_acts, QKV_DOTS, QKV_WIDTHS, qkv_refs, start)
    pooled = [
        ff.pool(i, src, i < 3)
        for i, src in enumerate([first_ref, hidden_ref, mixed_ref, pre_ref, down_ref, attn_ref])
    ]
    upstream = Exchange(staged, heads_in, *swaps[0], start)
    upstream.begin()
    sums = NormSums(*norm_refs, start)
    sums.held[0] = norm_ref[...]
    sums.begin(0)
    tokens = qkv.pool(0, x_ref, True)
    for near, far in pooled:
        near.wait()
        far.wait_recv()
    sums.step(0)
    for at in range(len(FF_DOTS)):
        ff.multiply(at)
    upstream.finish()
    attention = AttendBack(
        [q_ref, heads_in, pairs_ref, low_ref, end_ref, lse_ref, o_ref],
        heads_out,
        attention_refs,
        start,
    )
    def ff_reduce(k):
        sums.step(k + 1)
        for p in ff.parts:
            ff.reduce_step(p, k)

    def ff_gather(k):
        for p in ff.parts:
            ff.gather_step(p, k)

    def qkv_reduce(k):
        for p in qkv.parts:
            qkv.reduce_step(p, k)

    def qkv_gather(k):
        for p in qkv.parts:
            qkv.gather_step(p, k)

    events = [(BACK_REDUCE[k], functools.partial(ff_reduce, k)) for k in range(2)]
    events += attention.events
    events.sort(key=lambda e: e[0])
    done = 0
    for at, act in events:
        if at > done:
            attention.run(done, at)
            done = at
        act()
    attention.run(done, 4 * SLOT_UNITS)
    attention.finish()
    downstream = Exchange(heads_out, tok_in, *swaps[1], start)
    downstream.begin()
    ff_reduce(2)
    ff_reduce(3)
    downstream.finish()

    def unpack(i, carry):
        both = [tok_in[i * 2], tok_in[i * 2 + 1]]
        query = [jnp.concatenate([t[128:192, :HEAD], t[128:192, HEAD:]], axis=0) for t in both]
        key = [t[0:128, :HEAD] for t in both]
        value = [t[0:128, HEAD:] for t in both]
        for which, piece in enumerate((query, key, value)):
            here = pl.ds(pl.multiple_of(which * 1024 + i * 128, 128), 128)
            tok_out[:, here] = jnp.concatenate(piece, axis=1)
        return carry

    lax.fori_loop(0, 8, unpack, 0)
    pooled = [
        qkv.pool(1 + which, tok_out.at[:, pl.ds(which * 1024, 1024)], False) for which in range(3)
    ]
    ff_reduce(4)
    for near, far in (tokens, *pooled):
        near.wait()
        far.wait_recv()
    for at in range(len(QKV_DOTS)):
        qkv.multiply(at)
    ff_reduce(5)
    ff_gather(4)
    ff_gather(3)
    qkv_reduce(0)
    ff_gather(2)
    qkv_reduce(1)
    qkv_reduce(2)
    ff_gather(1)
    qkv_reduce(3)
    qkv_reduce(4)
    qkv_reduce(5)
    qkv_gather(4)
    qkv_gather(3)
    ff_gather(0)
    qkv_gather(2)
    qkv_gather(1)
    qkv_gather(0)
    ff.finish()
    qkv.finish()
    for copy in sent:
        copy.wait_send()


FF_DOTS = tuple(
    [(0, 512, 0, 3, j * 512) for j in range(4)]
    + [(1, 2048, q * 512, 4, 0) for q in range(4)]
    + [(2, 512, 0, 5, 0)]
)
FF_WIDTHS = (1024, 896, 896, 896, 896)
QKV_DOTS = ((0, 512, 0, 1, 0), (0, 512, 0, 2, 0), (0, 512, 0, 3, 0))
QKV_WIDTHS = (384, 384, 256, 256, 256)


def reducer_scratch(widths):
    total, parts = (sum(widths), len(widths))
    bf16, dma = (jnp.bfloat16, pltpu.SemaphoreType.DMA)
    return [
        pltpu.VMEM((2, ROWS, total), bf16),
        *[pltpu.VMEM((2, ROWS >> (k + 1), total), bf16) for k in range(5)],
        pltpu.VMEM((16, total), bf16),
        pltpu.VMEM((16, total), bf16),
        dma((8,)),
        dma((8,)),
        dma((parts, 6)),
        dma((parts, 6)),
        dma((parts, 7)),
        dma((parts, 7)),
        dma((8 + parts,)),
    ]


def back(acts, token_rows, norm_sums, mixed_grad, attention):
    bf16, f32, dma = (jnp.bfloat16, jnp.float32, pltpu.SemaphoreType.DMA)
    whole, anywhere = (pl.BlockSpec(memory_space=pltpu.VMEM), pl.BlockSpec(memory_space=pl.ANY))
    ff_total, qkv_total = (sum(FF_WIDTHS), sum(QKV_WIDTHS))
    held = pltpu.VMEM((7, 2, 8, 512), f32)
    return pl.pallas_call(
        back_kernel,
        out_shape=[
            jax.ShapeDtypeStruct((2, ROWS, ff_total), bf16),
            jax.ShapeDtypeStruct((2, ROWS, qkv_total), bf16),
            jax.ShapeDtypeStruct((8, 512), f32),
            jax.ShapeDtypeStruct((128, 3072), bf16),
        ],
        in_specs=[anywhere] * 7 + [whole] * 8,
        out_specs=[anywhere] * 2 + [whole] * 2,
        scratch_shapes=[
            *[pltpu.VMEM((256, width), bf16) for width in (1024, 4096, 1024, 2048, 512, 512)],
            *[pltpu.VMEM((256, width), bf16) for width in (1024, 512, 512, 512)],
            *reducer_scratch(FF_WIDTHS),
            *reducer_scratch(QKV_WIDTHS),
            held,
            held,
            dma((7,)),
            dma((7,)),
            pltpu.VMEM((16, 64, 128), bf16),
            pltpu.VMEM((16, 64, 128), bf16),
            pltpu.VMEM((16, 192, 128), bf16),
            pltpu.VMEM((16, 192, 128), bf16),
            *[dma((16,))] * 4,
            *back_scratch(),
        ],
        compiler_params=pltpu.CompilerParams(
            collective_id=1, has_side_effects=True, vmem_limit_bytes=62 * 2**20
        ),
    )(*acts, token_rows, norm_sums, mixed_grad, *attention)


CHUNK = 512


def cast_kernel(ff_ref, qkv_ref, *refs):
    outs, (narrow, wide, in_sem, out_sem) = (refs[:6], refs[6:])
    grad_in, grad_down, grad_out, *grad_qkv = outs
    chunks = []
    for c in range(2):
        for j in range(9):
            src = ff_ref.at[c, :, pl.ds(j * CHUNK, CHUNK)]
            if j < 4:
                dst = grad_in.at[:, pl.ds((c * 4 + j) * CHUNK, CHUNK)]
            elif j < 8:
                dst = grad_down.at[pl.ds((j - 4) * ROWS, ROWS), pl.ds(c * CHUNK, CHUNK)]
            else:
                dst = grad_out.at[:, pl.ds(c * CHUNK, CHUNK)]
            chunks.append((src, dst))
        for j in range(3):
            src = qkv_ref.at[c, :, pl.ds(j * CHUNK, CHUNK)]
            chunks.append((src, grad_qkv[j].at[:, pl.ds(c * CHUNK, CHUNK)]))
    loads = [
        pltpu.make_async_copy(src, narrow.at[n], in_sem.at[n]) for n, (src, _) in enumerate(chunks)
    ]
    stores = [
        pltpu.make_async_copy(wide.at[n], dst, out_sem.at[n]) for n, (_, dst) in enumerate(chunks)
    ]
    for load in loads:
        load.start()
    for n in range(len(chunks)):
        loads[n].wait()

        def widen(i, carry):
            here = pl.ds(pl.multiple_of(i * 64, 64), 64)
            wide[n, here] = narrow[n, here].astype(jnp.float32)
            return carry

        lax.fori_loop(0, ROWS // 64, widen, 0)
        stores[n].start()
    for store in stores:
        store.wait()


def grads_out(ff_summed, qkv_summed):
    f32 = jnp.float32
    anywhere = pl.BlockSpec(memory_space=pl.ANY)
    square = jax.ShapeDtypeStruct((ROWS, 1024), f32)
    return pl.pallas_call(
        cast_kernel,
        out_shape=[
            jax.ShapeDtypeStruct((ROWS, 4096), f32),
            jax.ShapeDtypeStruct((2048, 1024), f32),
            square,
            square,
            square,
            square,
        ],
        in_specs=[anywhere] * 2,
        out_specs=[anywhere] * 6,
        scratch_shapes=[
            pltpu.VMEM((24, ROWS, CHUNK), jnp.bfloat16),
            pltpu.VMEM((24, ROWS, CHUNK), f32),
            pltpu.SemaphoreType.DMA((24,)),
            pltpu.SemaphoreType.DMA((24,)),
        ],
        compiler_params=pltpu.CompilerParams(vmem_limit_bytes=56 * 2**20),
    )(ff_summed, qkv_summed)


def normalize(summed_in, norm_gain, norm_bias):
    row_mean = jnp.mean(summed_in, axis=-1, keepdims=True)
    centred = summed_in - row_mean
    inv_std = lax.rsqrt(jnp.mean(centred * centred, axis=-1, keepdims=True) + NORM_EPSILON)
    scaled = centred * inv_std
    return (scaled * norm_gain + norm_bias, scaled, inv_std)


def normalize_back(upstream, scaled, inv_std, norm_gain):
    weighted = upstream * norm_gain
    centred = weighted - jnp.mean(weighted, axis=-1, keepdims=True)
    result = inv_std * (centred - scaled * jnp.mean(weighted * scaled, axis=-1, keepdims=True))
    return (result, jnp.sum(upstream * scaled, axis=0), jnp.sum(upstream, axis=0))


def exact_gelu(values):
    return jax.nn.gelu(values, approximate=False)


def to_tokens(packed):
    return packed.reshape(HEADS, 64, 2, HEAD).transpose(2, 1, 0, 3).reshape(128, HEADS * HEAD)


def shards(
    tokens,
    segments,
    valid,
    w_query,
    w_key,
    w_value,
    w_out,
    norm1_gain,
    norm1_bias,
    w_in,
    w_down,
    norm2_gain,
    norm2_bias,
    cotangent,
):
    packed = jnp.zeros((16, 512), jnp.bfloat16).at[:4].set(
        jnp.stack([norm1_gain, norm1_bias, norm2_gain, norm2_bias])
    )
    token_rows = tokens[0]
    (
        full_qkv,
        full_out,
        full_in,
        full_down,
        norms,
        queries,
        pairs,
        summed,
        lse,
        mixed,
        low,
        end,
    ) = front(
        token_rows,
        [w_query, w_key, w_value, w_out, w_in, w_down],
        packed,
        segments[0],
        valid[0],
    )
    norms = norms[:, :4].transpose(1, 0, 2).reshape(4, 1024).astype(jnp.float32)
    gain_one, bias_one, gain_two, bias_two = norms
    mixed = to_tokens(mixed)

    attn = jnp.dot(mixed, full_out, preferred_element_type=jnp.float32)
    first, scaled_one, inv_one = normalize(
        token_rows.astype(jnp.float32) + attn, gain_one, bias_one
    )
    first_low = first.astype(jnp.bfloat16)
    pre = jnp.dot(first_low, full_in, preferred_element_type=jnp.float32)
    hidden = exact_gelu(pre).astype(jnp.bfloat16)
    ff_out = jnp.dot(hidden, full_down, preferred_element_type=jnp.float32)
    result, scaled_two, inv_two = normalize(first + ff_out, gain_two, bias_two)
    upstream = cotangent[0].astype(jnp.float32)
    grad_two, grad_gain_two, grad_bias_two = normalize_back(upstream, scaled_two, inv_two, gain_two)
    ff_grad = grad_two.astype(jnp.bfloat16)
    hidden_grad = jnp.einsum("td,fd->tf", ff_grad, full_down, preferred_element_type=jnp.float32)
    gelu_pull = jax.vjp(exact_gelu, pre)[1]
    pre_grad = gelu_pull(hidden_grad)[0].astype(jnp.bfloat16)
    first_grad = grad_two + jnp.einsum(
        "tf,df->td", pre_grad, full_in, preferred_element_type=jnp.float32
    )
    grad_one, grad_gain_one, grad_bias_one = normalize_back(
        first_grad, scaled_one, inv_one, gain_one
    )
    attn_grad = grad_one.astype(jnp.bfloat16)
    mixed_grad = jnp.einsum(
        "td,cd->tc", attn_grad, full_out, preferred_element_type=jnp.float32
    ).astype(jnp.bfloat16)
    norm_sums = jnp.stack([grad_gain_one, grad_bias_one, grad_gain_two, grad_bias_two])
    norm_sums = jnp.pad(norm_sums.reshape(4, 2, 512).transpose(1, 0, 2), ((0, 0), (0, 4), (0, 0)))

    ff_summed, qkv_summed, norm_total, all_tok = back(
        [first_low, hidden, mixed, pre_grad, ff_grad, attn_grad],
        token_rows,
        norm_sums,
        mixed_grad,
        [queries, pairs, low, end, lse, summed],
    )
    grad_in, grad_down, grad_out, *grad_qkv = grads_out(ff_summed, qkv_summed)
    input_grad = grad_one + jnp.einsum(
        "td,cd->tc", all_tok, full_qkv, preferred_element_type=jnp.float32
    )
    return (
        result.astype(jnp.bfloat16)[None],
        input_grad.astype(jnp.bfloat16)[None],
        *grad_qkv,
        grad_out,
        norm_total[0],
        norm_total[1],
        grad_in,
        grad_down,
        norm_total[2],
        norm_total[3],
    )


def solution(mesh):
    return jax.shard_map(
        shards,
        mesh=mesh,
        in_specs=(
            P("shard", ("blk", "aa"), None),
            P("shard", None),
            P("shard", None),
            P("shard", None),
            P("shard", None),
            P("shard", None),
            P("shard", None),
            P("shard"),
            P("shard"),
            P("shard", None),
            P("shard", None),
            P("shard"),
            P("shard"),
            P("shard", ("blk", "aa"), None),
        ),
        out_specs=(
            P("shard", ("blk", "aa"), None),
            P("shard", ("blk", "aa"), None),
            P("shard", None),
            P("shard", None),
            P("shard", None),
            P("shard", None),
            P("shard"),
            P("shard"),
            P("shard", None),
            P("shard", None),
            P("shard"),
            P("shard"),
        ),
        check_vma=False,
    )
```

```python
import functools
import math

import jax
import jax.numpy as jnp
from jax import lax
from jax.experimental import pallas as pl
from jax.experimental.pallas import tpu as pltpu
from jax.sharding import PartitionSpec as P

HEADS = 16
HEAD = 64
MASKED_SCORE = -1e30
NORM_EPSILON = 1e-05
BLOCK_LEN = 2048


MESH = pl.DeviceIdType.MESH
ROWS = 512
REDUCE_DIMS = ("xa", "ya", "za", "yb", "zb")
GATHER_DIMS = ("ya", "za", "yb", "zb")


def place():
    shard = lax.axis_index("shard")
    blk = lax.axis_index("blk")
    aa = lax.axis_index("aa")
    return (shard, blk // 2, blk % 2, aa // 4, aa % 4)


def flipped(i):
    return i + 1 - 2 * (i % 2)


def partner(dim):
    shard, x_lo, core, z, y = place()
    if dim == "core":
        core = 1 - core
    elif dim == "xa":
        x_lo = 1 - x_lo
    elif dim == "xb":
        shard, x_lo = 1 - shard, 1 - x_lo
    elif dim == "ya":
        y = flipped(y)
    elif dim == "yb":
        y = 3 - y
    elif dim == "za":
        z = flipped(z)
    else:
        z = 3 - z
    return (shard, x_lo * 2 + core, z * 4 + y)


def ring_bit(dim):
    shard, x_lo, _, z, y = place()
    if dim == "xa":
        return (shard * 2 + x_lo + shard) % 2
    if dim == "ya":
        return (y + y // 2) % 2
    if dim == "yb":
        return y // 2
    if dim == "za":
        return (z + z // 2) % 2
    return z // 2


def remote(src, dst, send_sem, recv_sem, dim):
    return pltpu.make_async_remote_copy(
        src_ref=src,
        dst_ref=dst,
        send_sem=send_sem,
        recv_sem=recv_sem,
        device_id=partner(dim),
        device_id_type=MESH,
    )


def row_starts(dims, rows):
    starts, at, size = ([0], 0, rows)
    for dim in dims:
        size //= 2
        at = at + ring_bit(dim) * size
        starts.append(at)
    return starts


def rotated(dims, by):
    return dims[by:] + dims[:by]


class Gather:
    def __init__(self, sources, places, send, recv, start):
        self.sources, self.places = (sources, places)
        self.send, self.recv, self.start = (send, recv, start)
        self.shard, _, self.core, _, _ = place()
        self.orders = [rotated(GATHER_DIMS, part) for part in range(4)]
        self.moving, self.siblings = ({}, [])

    def columns(self, i, part, off):
        cols = self.sources[i].shape[1]
        col = pl.multiple_of(self.core * (cols // 2) + (off + part * (cols // 8)), 128)
        return pl.ds(col, cols // 8)

    def block(self, i, part, shard, at, size):
        target, off = self.places[i]
        rows = self.sources[i].shape[0]
        at = pl.multiple_of(shard * rows + at, 16)
        return target.at[pl.ds(at, size), self.columns(i, part, off)]

    def own(self, i):
        target, off = self.places[i]
        rows, cols = self.sources[i].shape
        return target.at[pl.ds(pl.multiple_of(self.shard * rows, rows), rows), pl.ds(off, cols)]

    def begin(self, i):
        rows = self.sources[i].shape[0]
        for part in range(4):
            at = row_starts(self.orders[part], rows)[4]
            mine = pl.ds(pl.multiple_of(at, 16), rows // 16)
            self.moving[i, part] = self.start(
                remote(
                    self.sources[i].at[mine, self.columns(i, part, 0)],
                    self.block(i, part, self.shard, at, rows // 16),
                    self.send.at[i, part, 0],
                    self.recv.at[i, part, 0],
                    "xb",
                )
            )

    def stage(self, i, stage):
        rows = self.sources[i].shape[0]
        for part in range(4):
            self.moving[i, part].wait_recv()
            starts = row_starts(self.orders[part], rows)
            if stage < 5:
                k = 4 - stage
                mine = self.block(i, part, 1 - self.shard, starts[k + 1], rows >> (k + 1))
                self.moving[i, part] = self.start(
                    remote(
                        mine,
                        mine,
                        self.send.at[i, part, stage],
                        self.recv.at[i, part, stage],
                        self.orders[part][k],
                    )
                )
            if stage >= 4:
                at = starts[1] if stage == 4 else rows // 2 - starts[1]
                mine = self.block(i, part, 1 - self.shard, at, rows // 2)
                self.siblings.append(
                    self.start(
                        remote(
                            mine,
                            mine,
                            self.send.at[i, part, stage + 1],
                            self.recv.at[i, part, stage + 1],
                            "core",
                        )
                    )
                )

    def finish(self):
        for copy in self.siblings:
            copy.wait_recv()
        self.siblings = []


def plane_peer(step):
    shard, x_lo, core, z, y = place()
    return (shard, x_lo * 2 + core, (z * 4 + y + step) % 16)


class Exchange:
    def __init__(self, outgoing, incoming, send, recv, start):
        self.outgoing, self.incoming = (outgoing, incoming)
        self.send, self.recv, self.start = (send, recv, start)
        self.copies = []

    def begin(self):
        me = lax.axis_index("aa")
        for step in (1, 3, 4, 12, 15, 13, 5, 11, 2, 8, 14, 6, 10, 7, 9):
            self.copies.append(
                self.start(
                    pltpu.make_async_remote_copy(
                        src_ref=self.outgoing.at[(me + step) % 16],
                        dst_ref=self.incoming.at[me],
                        send_sem=self.send.at[step],
                        recv_sem=self.recv.at[step],
                        device_id=plane_peer(step),
                        device_id_type=MESH,
                    )
                )
            )
        self.incoming[me] = self.outgoing[me]

    def finish(self):
        for copy in self.copies:
            copy.wait_recv()


def greet_all(dims):
    barrier = pltpu.get_barrier_semaphore()
    for dim in dims:
        pl.semaphore_signal(barrier, inc=1, device_id=partner(dim), device_id_type=MESH)
    for step in range(1, 16):
        pl.semaphore_signal(barrier, inc=1, device_id=plane_peer(step), device_id_type=MESH)
    pl.semaphore_wait(barrier, len(dims) + 15)


def unfolded(block, side):
    lane = lax.broadcasted_iota(jnp.int32, (64, 128), 1)
    keep = (lane >= HEAD) if side else (lane < HEAD)
    block = block.astype(jnp.float32)
    moved = jnp.concatenate([block[:, HEAD:], block[:, :HEAD]], axis=1)
    first, second = (moved, block) if side else (block, moved)
    both = jnp.concatenate([jnp.where(keep, first, 0.0), jnp.where(keep, second, 0.0)], axis=0)
    return both.astype(jnp.bfloat16)


LEAST = -(2**31)
FRONT_BLOCK = 512


def visible(place_k, low, end, start):
    size = jnp.maximum(end - low, 0) + LEAST
    return (place_k - (low - start - LEAST)) < size


def query_spans(segments_ref, valid_ref, low_ref, end_ref):
    _, x_lo, core, _, _ = place()
    segments = segments_ref[...]
    start = pl.multiple_of((x_lo * 2 + core) * 16, 16)
    mine = segments_ref[pl.ds(start, 16)]
    low, end = (jnp.zeros_like(mine), jnp.zeros_like(mine))
    before = jnp.zeros((1, 1), jnp.int32)
    for number in range(35):
        same = jnp.where(segments == number, 1, 0)
        count = jnp.sum(jnp.sum(same, axis=1, keepdims=True), axis=0, keepdims=True)
        picked = mine == number
        low = jnp.where(picked, before, low)
        before = before + count
        end = jnp.where(picked, before, end)
    live = jnp.sum(jnp.sum(valid_ref[...], axis=1, keepdims=True), axis=0, keepdims=True)
    end = jnp.minimum(end, live)
    for row in range(16):
        here = pl.ds(row * 128, 128)
        low_ref[:, here] = jnp.broadcast_to(low[row : row + 1], (8, 128))
        end_ref[:, here] = jnp.broadcast_to(end[row : row + 1], (8, 128))


def normalized(values):
    centred = values - jnp.mean(values, axis=1, keepdims=True)
    inverse = lax.rsqrt(jnp.mean(centred * centred, axis=1, keepdims=True) + NORM_EPSILON)
    return (centred * inverse, inverse)


def normalized_back(upstream, scaled, inverse, gain):
    weighted = upstream * gain
    centred = weighted - jnp.mean(weighted, axis=1, keepdims=True)
    return inverse * (centred - scaled * jnp.mean(weighted * scaled, axis=1, keepdims=True))


def summed_rows(values):
    return jnp.sum(values, axis=0, keepdims=True)


def dense(x_ref, cot_ref, mixed_in, norm_in, weights, scratch, outs, give):
    w_out, w_in, w_down = weights
    slope, pre_ref, down_ref, attn_ref = scratch
    (
        _,
        low_out,
        hidden_out,
        mixed_out,
        pre_out,
        down_out,
        attn_out,
        staged_ref,
        sums_ref,
        grad_ref,
        result_ref,
    ) = outs
    own = pl.ds(0, 128)
    _, _, core, _, _ = place()

    def keep_half(src, dst):
        half = dst.shape[1]
        dst[own] = src[:, pl.ds(pl.multiple_of(core * half, half), half)]

    f32, bf16 = (jnp.float32, jnp.bfloat16)
    gain_one, bias_one, gain_two, bias_two = [
        jnp.concatenate([norm_in[0, i : i + 1], norm_in[1, i : i + 1]], axis=1).astype(f32)
        for i in range(4)
    ]
    for pair in range(8):
        both = [mixed_in[pair * 2], mixed_in[pair * 2 + 1]]
        both = [jnp.concatenate([t[:, :HEAD], t[:, HEAD:]], axis=0) for t in both]
        mixed_out[own, pair * 128 : (pair + 1) * 128] = jnp.concatenate(both, axis=1)
    give(3)
    attn = jnp.dot(mixed_out[own], w_out[...], preferred_element_type=f32)
    scaled_one, inverse_one = normalized(x_ref[...].astype(f32) + attn)
    first = scaled_one * gain_one + bias_one
    low_out[own] = first.astype(bf16)
    give(1)

    def up(c, total):
        here = pl.ds(pl.multiple_of(c * 1024, 1024), 1024)
        pre = jnp.dot(low_out[own], w_in[:, here], preferred_element_type=f32)
        share = 0.5 + 0.5 * lax.erf(pre * 0.5**0.5)
        hidden = (pre * share).astype(bf16)
        hidden_out[own, here] = hidden
        slope[:, here] = share + pre * jnp.exp(pre * pre * -0.5) * (2 * math.pi) ** -0.5
        return total + jnp.dot(hidden, w_down[here], preferred_element_type=f32)

    ff_out = lax.fori_loop(0, 4, up, jnp.zeros((128, 1024), f32), unroll=2)
    give(2)
    scaled_two, inverse_two = normalized(first + ff_out)
    result_ref[...] = (scaled_two * gain_two + bias_two).astype(bf16)
    upstream = cot_ref[...].astype(f32)
    grad_two = normalized_back(upstream, scaled_two, inverse_two, gain_two)
    down_ref[...] = grad_two.astype(bf16)
    give(5)
    keep_half(down_ref, down_out)

    def down(c, total):
        here = pl.ds(pl.multiple_of(c * 1024, 1024), 1024)
        grad = lax.dot_general(
            down_ref[...], w_down[here], (((1,), (1,)), ((), ())), preferred_element_type=f32
        )
        grad = (grad * slope[:, here]).astype(bf16)
        pre_ref[:, here] = grad
        return total + lax.dot_general(
            grad, w_in[:, here], (((1,), (1,)), ((), ())), preferred_element_type=f32
        )

    first_grad = lax.fori_loop(0, 4, down, grad_two, unroll=2)
    give(4)
    keep_half(pre_ref, pre_out)
    grad_one = normalized_back(first_grad, scaled_one, inverse_one, gain_one)
    grad_ref[...] = grad_one
    attn_ref[...] = grad_one.astype(bf16)
    give(6)
    keep_half(attn_ref, attn_out)
    mixed_grad = lax.dot_general(
        attn_ref[...], w_out[...], (((1,), (1,)), ((), ())), preferred_element_type=f32
    ).astype(bf16)
    for head in range(HEADS):
        part = mixed_grad[:, head * HEAD : (head + 1) * HEAD]
        staged_ref[head] = jnp.concatenate([part[0:64], part[64:128]], axis=1)
    sums = [
        summed_rows(first_grad * scaled_one),
        summed_rows(first_grad),
        summed_rows(upstream * scaled_two),
        summed_rows(upstream),
    ]
    for half in range(2):
        cols = slice(half * 512, (half + 1) * 512)
        sums_ref[half] = jnp.concatenate([v[:, cols] for v in sums] + [jnp.zeros((4, 512), f32)])


def front_kernel(
    x_ref,
    wq_ref,
    wk_ref,
    wv_ref,
    wo_ref,
    wi_ref,
    wd_ref,
    norm_ref,
    cot_ref,
    segments_ref,
    valid_ref,
    qkv_out,
    q_out,
    pairs_out,
    o_out,
    lse_out,
    low_ref,
    end_ref,
    *refs,
):
    dense_out, refs = (refs[:11], refs[11:])
    front_body(
        x_ref,
        (wq_ref, wk_ref, wv_ref, wo_ref, wi_ref, wd_ref),
        norm_ref,
        cot_ref,
        (segments_ref, valid_ref),
        qkv_out,
        (q_out, pairs_out, o_out, lse_out, low_ref, end_ref),
        dense_out,
        *refs,
    )


def front_body(
    x_ref,
    weights,
    norm_ref,
    cot_ref,
    documents,
    qkv_out,
    attention_out,
    dense_out,
    wqkv,
    w_out,
    w_in,
    w_down,
    norm_in,
    mixed_in,
    slope,
    pre_full,
    down_full,
    attn_full,
    pool_send,
    pool_recv,
    staged,
    heads_in,
    folded,
    pairs_t,
    top_s,
    send,
    recv,
    own_in,
    own_out,
    hop_send,
    hop_recv,
    swap_send,
    swap_recv,
    back_send,
    back_recv,
):
    shard, _, _, _, _ = place()
    q_out, pairs_out, o_out, lse_out, low_ref, end_ref = attention_out
    sent = []

    def start(copy):
        copy.start()
        sent.append(copy)
        return copy

    gather = Gather(
        weights,
        [(wqkv, 0), (wqkv, 1024), (wqkv, 2048), (w_out, 0), (w_in, 0), (w_down, 0)],
        send,
        recv,
        start,
    )
    inward = []
    for i in range(6):
        inward.append(pltpu.make_async_copy(weights[i], gather.own(i), own_in.at[i]))
        inward[i].start()
    greet_all(("core", "xa", "xb"))
    norms = start(
        remote(norm_ref, norm_in.at[shard], hop_send.at[3], hop_recv.at[3], "xb")
    )
    norm_in[shard] = norm_ref[...]
    for i in range(6):
        gather.begin(i)
    _, _, core, _, _ = place()
    pooled = []

    def give(i):
        dst = dense_out[i]
        src = (x_ref, None, None, None, pre_full, down_full, attn_full)[i]
        if src is None:
            src = dst.at[pl.ds(0, 128)]
        half = src.shape[1] // 2
        if i > 3:
            src = src.at[:, pl.ds(pl.multiple_of((1 - core) * half, half), half)]
        sems = (pool_send.at[i], pool_recv.at[i])
        pooled.append(start(remote(src, dst.at[pl.ds(128, 128)], *sems, "core")))

    give(0)
    dense_out[0][pl.ds(0, 128)] = x_ref[...]
    for i in range(3):
        gather.stage(i, 1)
    for stage in range(2, 6):
        for i in range(3):
            gather.stage(i, stage)
        if stage == 3:
            for i in range(3, 6):
                gather.stage(i, 1)
    for i in range(3):
        inward[i].wait()
    gather.finish()
    keep = pltpu.make_async_copy(wqkv, qkv_out, own_out.at[0])
    keep.start()

    def project(piece, carry):
        q, k, v = [
            jnp.dot(
                x_ref[...],
                wqkv[:, pl.ds(pl.multiple_of(which * 1024 + piece * 256, 256), 256)],
                preferred_element_type=jnp.float32,
            )
            for which in range(3)
        ]
        q = (q.astype(jnp.bfloat16).astype(jnp.float32) * HEAD ** (-0.5)).astype(jnp.bfloat16)
        k, v = (k.astype(jnp.bfloat16), v.astype(jnp.bfloat16))
        for h in range(4):
            at = slice(h * HEAD, (h + 1) * HEAD)
            staged[piece * 4 + h, 0:128] = jnp.concatenate([k[:, at], v[:, at]], axis=1)
            staged[piece * 4 + h, 128:192] = jnp.concatenate([q[0:64, at], q[64:128, at]], axis=1)
        return carry

    lax.fori_loop(0, 4, project, 0)
    heads = Exchange(staged, heads_in, swap_send, swap_recv, start)
    heads.begin()
    for i in range(3, 6):
        gather.stage(i, 2)
    query_spans(*documents, low_ref, end_ref)
    heads.finish()

    def spread(c, carry):
        here = pl.ds(pl.multiple_of(c * 128, 128), 128)
        pairs_out[here] = heads_in[c, 0:128]
        q_out[here] = unfolded(heads_in[c, 128:192], 0)
        return carry

    lax.fori_loop(0, 16, spread, 0)

    def slot_rows(slot):
        return pairs_out.at[pl.ds(slot * BLOCK_LEN, BLOCK_LEN)]

    def hop(index, source, target, dim):
        return start(
            remote(
                slot_rows(source), slot_rows(target), hop_send.at[index], hop_recv.at[index], dim
            )
        )

    hops = {1: hop(0, 0, 1, "core"), 2: hop(1, 0, 2, "xa")}
    top_s[...] = jnp.full_like(top_s, MASKED_SCORE)
    o_out[...] = jnp.zeros_like(o_out)
    first_row = lax.broadcasted_iota(jnp.int32, (128, 512), 0) == 0

    def turn(c, carry):
        here = pl.ds(pl.multiple_of(c * 512, 512), 512)
        turned = jnp.transpose(pairs_out[here].astype(jnp.float32))
        pairs_t[:, here] = jnp.where(first_row, 1.0, turned).astype(jnp.bfloat16)
        return carry

    def slot_step(slot, block):
        _, x_lo, core, _, _ = place()
        owner = (slot // 2 + x_lo) % 2 * 2 + (slot % 2 + core) % 2
        rows = pl.ds(slot * BLOCK_LEN, BLOCK_LEN)
        mine = pl.ds(pl.multiple_of(block * FRONT_BLOCK, FRONT_BLOCK), FRONT_BLOCK)
        scores = lax.dot_general(
            pairs_out[rows],
            q_out[mine],
            (((1,), (1,)), ((), ())),
            preferred_element_type=jnp.float32,
        )
        place_k = lax.broadcasted_iota(jnp.int32, scores.shape, 0)
        allowed = visible(place_k, low_ref[0:1, mine], end_ref[0:1, mine], owner * BLOCK_LEN)
        if slot == 0:
            place_q = lax.broadcasted_iota(jnp.int32, (1, FRONT_BLOCK), 1) + block * FRONT_BLOCK
            allowed = allowed | (place_k == place_q)
        scores = jnp.where(allowed, scores, MASKED_SCORE)
        top = top_s[0:1, mine]
        new_top = jnp.maximum(top, jnp.max(scores, axis=0, keepdims=True))
        weights = jnp.exp(scores - new_top)
        factor = jnp.exp(top - new_top)
        o_out[:, mine] = o_out[:, mine] * factor + jnp.dot(
            pairs_t[:, rows], weights.astype(jnp.bfloat16), preferred_element_type=jnp.float32
        )
        top_s[:, mine] = jnp.broadcast_to(new_top, (8, FRONT_BLOCK))

    events = {
        0: [(i, 3) for i in (3, 4, 5)],
        1: [(i, 4) for i in (3, 4, 5)],
        3: [(i, 5) for i in (3, 4, 5)],
    }
    for slot in range(4):
        if slot:
            hops[slot].wait_recv()
        if slot == 2:
            hops[3] = hop(2, 2, 3, "core")
        lax.fori_loop(slot * 4, slot * 4 + 4, turn, 0)
        for half in range(2):

            def blocks(b, carry):
                slot_step(slot, b)
                return carry

            lax.fori_loop(half * 2, half * 2 + 2, blocks, 0)
            if half == 0:
                for i, stage in events.get(slot, ()):
                    gather.stage(i, stage)

    def close(c, carry):
        here = pl.ds(pl.multiple_of(c * 128, 128), 128)
        total = o_out[0:1, here]
        mixed = o_out[:, here] / total
        o_out[:, here] = mixed
        lse = top_s[0:1, here] + jnp.log(total)
        lse_out[:, here] = jnp.broadcast_to(lse, (8, 128))
        block = jnp.transpose(mixed)
        both = jnp.concatenate([block[0:64, HEAD:], block[64:128, HEAD:]], axis=1)
        folded[c] = both.astype(jnp.bfloat16)
        return carry

    lax.fori_loop(0, 16, close, 0)
    back = Exchange(folded, mixed_in, back_send, back_recv, start)
    back.begin()
    gather.finish()
    norms.wait_recv()
    for i in range(3, 6):
        inward[i].wait()
    back.finish()
    dense(
        x_ref,
        cot_ref,
        mixed_in,
        norm_in,
        (w_out, w_in, w_down),
        (slope, pre_full, down_full, attn_full),
        dense_out,
        give,
    )
    for copy in pooled:
        copy.wait_recv()
    keep.wait()
    for copy in sent:
        copy.wait_send()


def front(token_rows, weights, packed, cotangent, segments, valid):
    bf16, f32, i32, dma = (jnp.bfloat16, jnp.float32, jnp.int32, pltpu.SemaphoreType.DMA)
    n, shape = (len(weights), jax.ShapeDtypeStruct)
    whole, anywhere = (pl.BlockSpec(memory_space=pltpu.VMEM), pl.BlockSpec(memory_space=pl.ANY))
    return pl.pallas_call(
        front_kernel,
        out_shape=[
            shape((1024, 3072), bf16),
            shape((BLOCK_LEN, 128), bf16),
            shape((4 * BLOCK_LEN, 128), bf16),
            shape((128, BLOCK_LEN), f32),
            shape((8, BLOCK_LEN), f32),
            shape((8, BLOCK_LEN), i32),
            shape((8, BLOCK_LEN), i32),
            *[shape((256, width), bf16) for width in (1024, 1024, 4096, 1024, 2048, 512, 512)],
            shape((HEADS, 64, 128), bf16),
            shape((2, 8, 512), f32),
            shape((128, 1024), f32),
            shape((128, 1024), bf16),
        ],
        in_specs=[whole] + [anywhere] * n + [whole] * 4,
        out_specs=[anywhere] + [whole] * 17,
        scratch_shapes=[
            pltpu.VMEM((1024, 3072), bf16),
            pltpu.VMEM((1024, 1024), bf16),
            pltpu.VMEM((1024, 4096), bf16),
            pltpu.VMEM((4096, 1024), bf16),
            pltpu.VMEM((2, 16, 512), bf16),
            pltpu.VMEM((16, 64, 128), bf16),
            pltpu.VMEM((128, 4096), f32),
            pltpu.VMEM((128, 4096), bf16),
            pltpu.VMEM((128, 1024), bf16),
            pltpu.VMEM((128, 1024), bf16),
            dma((7,)),
            dma((7,)),
            pltpu.VMEM((16, 192, 128), bf16),
            pltpu.VMEM((16, 192, 128), bf16),
            pltpu.VMEM((16, 64, 128), bf16),
            pltpu.VMEM((128, 4 * BLOCK_LEN), bf16),
            pltpu.VMEM((8, BLOCK_LEN), f32),
            dma((n, 4, 7)),
            dma((n, 4, 7)),
            dma((n,)),
            dma((1,)),
            dma((4,)),
            dma((4,)),
            *[dma((16,))] * 4,
        ],
        compiler_params=pltpu.CompilerParams(
            collective_id=0, has_side_effects=True, vmem_limit_bytes=62 * 2**20
        ),
    )(
        token_rows,
        *weights,
        packed,
        cotangent,
        segments.reshape(64, 128),
        valid.reshape(64, 128),
    )


BACK_REDUCE = (7, 12)
SLOT_UNITS = 4
BACK_BLOCK = 512


def back_scratch():
    return [
        pltpu.VMEM((BLOCK_LEN, 128), jnp.bfloat16),
        pltpu.VMEM((HEAD, 4 * BLOCK_LEN), jnp.bfloat16),
        pltpu.VMEM((8, BLOCK_LEN), jnp.float32),
        pltpu.VMEM((HEAD, BLOCK_LEN), jnp.float32),
        pltpu.VMEM((4 * BLOCK_LEN, 128), jnp.float32),
        pltpu.VMEM((3, BLOCK_LEN, 128), jnp.bfloat16),
        pltpu.VMEM((3, BLOCK_LEN, 128), jnp.bfloat16),
        pltpu.SemaphoreType.DMA((3,)),
        pltpu.SemaphoreType.DMA((3,)),
    ]


class AttendBack:
    def __init__(self, ins, out, scratch, start):
        self.q, self.packed, self.pairs, self.low, self.end, self.lse, self.o_t = ins
        self.out = out
        self.g, self.pairs_t, self.delta, self.dq, self.dkv = scratch[:5]
        self.away, self.landed, self.send, self.recv = scratch[5:9]
        self.start = start
        self.copies = {}
        self.events = [
            (0, self.begin),
            (SLOT_UNITS, lambda: self.give(3, 0, None, "core")),
            (2 * SLOT_UNITS + 1, lambda: self.give(2, 1, 0, "xa")),
            (3 * SLOT_UNITS, lambda: self.give(1, 2, None, "core")),
        ]

    def begin(self):
        self.delta[...] = jnp.zeros_like(self.delta)
        self.dq[...] = jnp.zeros_like(self.dq)
        self.dkv[...] = jnp.zeros_like(self.dkv)

        def chunk(c, carry):
            both = unfolded(self.packed[c], 1)
            here = pl.ds(pl.multiple_of(c * 128, 128), 128)
            self.g[here] = both
            products = jnp.transpose(both.astype(jnp.float32)) * self.o_t[:, here]
            total = jnp.sum(products, axis=0, keepdims=True)
            self.delta[:, here] = jnp.broadcast_to(total, (8, 128))
            return carry

        lax.fori_loop(0, 16, chunk, 0)

        def turn(c, carry):
            here = pl.ds(pl.multiple_of(c * 512, 512), 512)
            self.pairs_t[:, here] = jnp.transpose(self.pairs[here])[0:HEAD]
            return carry

        lax.fori_loop(0, 16, turn, 0)

    def run(self, first, last):
        edge = 3 * SLOT_UNITS
        if first < edge:
            lax.fori_loop(first, min(last, edge), functools.partial(self.unit, own=False), 0)
        if last > edge:
            lax.fori_loop(max(first, edge), last, functools.partial(self.unit, own=True), 0)

    def unit(self, n, carry, own):
        _, x_lo, core, _, _ = place()
        block = n % 4
        slot = 3 - n // 4
        owner = (slot // 2 + x_lo) % 2 * 2 + (slot % 2 + core) % 2
        key_start = owner * BLOCK_LEN
        here = pl.ds(pl.multiple_of(slot * BLOCK_LEN, BLOCK_LEN), BLOCK_LEN)
        mine = pl.ds(pl.multiple_of(block * BACK_BLOCK, BACK_BLOCK), BACK_BLOCK)
        keys = self.pairs[here]
        queries, upstream = (self.q[mine], self.g[mine])
        scores = lax.dot_general(
            keys, queries, (((1,), (1,)), ((), ())), preferred_element_type=jnp.float32
        )
        place_k = lax.broadcasted_iota(jnp.int32, scores.shape, 0)
        allowed = visible(place_k, self.low[0:1, mine], self.end[0:1, mine], key_start)
        if own:
            place_q = lax.broadcasted_iota(jnp.int32, (1, BACK_BLOCK), 1)
            place_q = place_q + block * BACK_BLOCK
            allowed = allowed | (place_k == place_q)
        scores = jnp.where(allowed, scores, MASKED_SCORE)
        probs = jnp.exp(scores - self.lse[0:1, mine])
        prob_grad = lax.dot_general(
            keys, upstream, (((1,), (1,)), ((), ())), preferred_element_type=jnp.float32
        )
        score_grad = (probs * (prob_grad - self.delta[0:1, mine])).astype(jnp.bfloat16)
        self.dkv[here] += jnp.dot(
            score_grad, queries, preferred_element_type=jnp.float32
        ) + jnp.dot(probs.astype(jnp.bfloat16), upstream, preferred_element_type=jnp.float32)
        self.dq[:, mine] += jnp.dot(
            self.pairs_t[:, here], score_grad, preferred_element_type=jnp.float32
        )
        return carry

    def give(self, slot, index, add, dim):
        if add is not None:
            self.copies[add].wait_recv()

        def chunk(c, carry):
            here = pl.ds(pl.multiple_of(c * 256, 256), 256)
            there = pl.ds(pl.multiple_of(slot * BLOCK_LEN + c * 256, 256), 256)
            total = self.dkv[there]
            if add is not None:
                total = total + self.landed[add, here].astype(jnp.float32)
            self.away[index, here] = total.astype(jnp.bfloat16)
            return carry

        lax.fori_loop(0, BLOCK_LEN // 256, chunk, 0)
        self.copies[index] = self.start(
            remote(
                self.away.at[index],
                self.landed.at[index],
                self.send.at[index],
                self.recv.at[index],
                dim,
            )
        )

    def finish(self):
        self.copies[1].wait_recv()
        self.copies[2].wait_recv()

        def chunk(c, carry):
            here = pl.ds(pl.multiple_of(c * 128, 128), 128)
            total = self.dkv[here] + self.landed[1, here].astype(jnp.float32)
            total = total + self.landed[2, here].astype(jnp.float32)
            self.out[c, 0:128] = total.astype(jnp.bfloat16)
            grad = jnp.transpose(self.dq[:, here]) * HEAD ** (-0.5)
            folded = jnp.concatenate([grad[0:64], grad[64:128]], axis=1)
            self.out[c, 128:192] = folded.astype(jnp.bfloat16)
            return carry

        lax.fori_loop(0, 16, chunk, 0)


class Reducer:
    def __init__(self, acts, dots, widths, refs, start):
        self.acts, self.dots, self.start = (acts, dots, start)
        self.partial, self.landed, self.last, self.out = (refs[0], refs[1:7], refs[7], refs[8])
        self.act_send, self.act_recv, self.red_send, self.red_recv = refs[9:13]
        self.gat_send, self.gat_recv, self.own = refs[13:16]
        self.shard, _, self.core, _, _ = place()
        self.parts = range(len(widths))
        self.edges = [sum(widths[:p]) for p in range(len(widths) + 1)]
        self.cols = [pl.ds(self.edges[p], widths[p]) for p in self.parts]
        self.orders = [rotated(REDUCE_DIMS, p) for p in self.parts]
        self.starts = [row_starts(self.orders[p], ROWS) for p in self.parts]
        self.moving, self.held, self.shared = ({}, {}, [])

    def pool(self, i, src):
        dst = self.acts[i]
        tokens = src.shape[0]
        half = src.shape[1] // 2
        mine, theirs = [
            src.at[:, pl.ds(pl.multiple_of(c * half, half), half)]
            for c in (self.core, 1 - self.core)
        ]
        near = pltpu.make_async_copy(mine, dst.at[pl.ds(0, tokens)], self.own.at[i])
        near.start()
        far = remote(
            theirs, dst.at[pl.ds(tokens, tokens)], self.act_send.at[i], self.act_recv.at[i], "core"
        )
        return (near, self.start(far))

    def multiply(self, at):
        left, left_step, left_off, right, right_off = self.dots[at]
        for s in range(2):
            product = lax.dot_general(
                self.acts[left][:, pl.ds(s * left_step + left_off, ROWS)],
                self.acts[right][:, pl.ds(right_off, 512)],
                (((0,), (0,)), ((), ())),
                preferred_element_type=jnp.float32,
            )
            self.partial[s, :, pl.ds(at * 512, 512)] = product.astype(jnp.bfloat16)
        for p in self.parts:
            if at * 512 < self.edges[p + 1] <= (at + 1) * 512:
                self.reduce_start(p, 0)

    def reduce_start(self, p, k):
        starts, cols = (self.starts[p], self.cols[p])
        if k < 5:
            half = ROWS >> (k + 1)
            away = pl.multiple_of(starts[k] + (half - (starts[k + 1] - starts[k])), 16)
            src = self.partial.at[:, pl.ds(away, half), cols]
            dst = self.landed[k].at[:, :, cols]
            dim = self.orders[p][k]
        else:
            src = self.partial.at[1 - self.shard, pl.ds(pl.multiple_of(starts[5], 16), 16), cols]
            dst = self.landed[5].at[:, cols]
            dim = "xb"
        self.moving[p] = self.start(
            remote(src, dst, self.red_send.at[p, k], self.red_recv.at[p, k], dim)
        )

    def reduce_step(self, p, k):
        self.moving[p].wait_recv()
        starts, cols = (self.starts[p], self.cols[p])
        if k < 5:
            half = ROWS >> (k + 1)
            step = min(half, 32)

            def add(i, carry):
                here = pl.ds(pl.multiple_of(i * step, step), step)
                there = pl.ds(pl.multiple_of(starts[k + 1] + i * step, 16), step)
                self.partial[:, there, cols] += self.landed[k][:, here, cols]
                return carry

            lax.fori_loop(0, half // step, add, 0)
            self.reduce_start(p, k + 1)
        else:
            here = pl.ds(pl.multiple_of(starts[5], 16), 16)
            self.last[:, cols] = self.partial[self.shard, here, cols] + self.landed[5][:, cols]
            self.held[p] = pltpu.make_async_copy(
                self.last.at[:, cols], self.rows_out(p, starts[5], 16), self.own.at[8 + p]
            )
            self.held[p].start()
            self.gather_start(p, 4)

    def rows_out(self, p, at, size):
        return self.out.at[self.core, pl.ds(pl.multiple_of(at, 16), size), self.cols[p]]

    def gather_start(self, p, k):
        mine = self.rows_out(p, self.starts[p][k + 1], ROWS >> (k + 1))
        src = self.last.at[:, self.cols[p]] if k == 4 else mine
        self.moving[p] = self.start(
            remote(src, mine, self.gat_send.at[p, k], self.gat_recv.at[p, k], self.orders[p][k])
        )

    def gather_step(self, p, k):
        self.moving[p].wait_recv()
        if k == 4:
            self.held[p].wait()
        if k > 0:
            self.gather_start(p, k - 1)
        if k == 1:
            self.share(p, 0, self.starts[p][1])
        if k == 0:
            self.share(p, 1, ROWS // 2 - self.starts[p][1])

    def share(self, p, slot, at):
        mine = self.rows_out(p, at, ROWS // 2)
        sems = (self.gat_send.at[p, 5 + slot], self.gat_recv.at[p, 5 + slot])
        self.shared.append(self.start(remote(mine, mine, *sems, "core")))

    def finish(self):
        for copy in self.shared:
            copy.wait_recv()


RINGS = {"y": 4, "z": 4, "xa": 2}
RING_ORDERS = (("y", "z", "xa"), ("z", "y", "xa"), ("xa", "y", "z"))


def ring_position(dim):
    _, _, _, z, y = place()
    return {"y": y, "z": z, "xa": ring_bit("xa")}[dim]


def ring_member(dim, step):
    shard, x_lo, core, z, y = place()
    if dim == "xa":
        return partner("xa")
    if dim == "y":
        y = (y + step) % 4
    else:
        z = (z + step) % 4
    return (shard, x_lo * 2 + core, z * 4 + y)


def copy_to(device, src, dst, send_sem, recv_sem):
    return pltpu.make_async_remote_copy(
        src_ref=src,
        dst_ref=dst,
        send_sem=send_sem,
        recv_sem=recv_sem,
        device_id=device,
        device_id_type=MESH,
    )


class RingReducer(Reducer):
    def __init__(self, acts, dots, width, refs, start):
        self.acts, self.dots, self.start, self.width = (acts, dots, start, width)
        self.partial, self.landed, self.crossed, self.last, self.out = (
            refs[0],
            [refs[1 + p * 3 : 4 + p * 3] for p in range(3)],
            refs[10],
            refs[11],
            refs[12],
        )
        self.act_send, self.act_recv, self.red_send, self.red_recv = refs[13:17]
        self.gat_send, self.gat_recv, self.own = refs[17:20]
        self.shard, _, self.core, _, _ = place()
        self.parts = range(3)
        self.edges = [width * p for p in range(4)]
        self.cols = [pl.ds(width * p, width) for p in self.parts]
        self.sizes, self.starts = ([], [])
        for order in RING_ORDERS:
            sizes, starts = ([ROWS], [0])
            for dim in order:
                sizes.append(sizes[-1] // RINGS[dim])
                starts.append(starts[-1] + ring_position(dim) * sizes[-1])
            self.sizes.append(sizes)
            self.starts.append(starts)
        self.moving, self.held, self.shared = ({}, {}, [])

    def others(self, p, k):
        dim = RING_ORDERS[p][k]
        n, at, size = (RINGS[dim], self.starts[p][k], self.sizes[p][k + 1])
        return [
            (ring_member(dim, d), at + (ring_position(dim) + d) % n * size) for d in range(1, n)
        ]

    def reduce_start(self, p, k):
        if k < 3:
            self.moving[p] = []
            for d, (device, at) in enumerate(self.others(p, k)):
                rows = pl.ds(pl.multiple_of(at, 16), self.sizes[p][k + 1])
                self.moving[p].append(
                    self.start(
                        copy_to(
                            device,
                            self.partial.at[:, rows, self.cols[p]],
                            self.landed[p][k].at[d],
                            self.red_send.at[p, k, d],
                            self.red_recv.at[p, k, d],
                        )
                    )
                )
        else:
            rows = pl.ds(pl.multiple_of(self.starts[p][3], 16), 16)
            sems = (self.red_send.at[p, 3, 0], self.red_recv.at[p, 3, 0])
            src = self.partial.at[1 - self.shard, rows, self.cols[p]]
            dst = self.crossed.at[:, self.cols[p]]
            self.moving[p] = [self.start(remote(src, dst, *sems, "xb"))]

    def reduce_step(self, p, k):
        for copy in self.moving[p]:
            copy.wait_recv()
        cols = self.cols[p]
        if k < 3:
            count, size = (len(self.moving[p]), self.sizes[p][k + 1])

            def add(i, carry):
                here = pl.ds(pl.multiple_of(i * 16, 16), 16)
                there = pl.ds(pl.multiple_of(self.starts[p][k + 1] + i * 16, 16), 16)
                total = self.partial[:, there, cols].astype(jnp.float32)
                for d in range(count):
                    total = total + self.landed[p][k][d, :, here].astype(jnp.float32)
                self.partial[:, there, cols] = total.astype(jnp.bfloat16)
                return carry

            lax.fori_loop(0, size // 16, add, 0)
            self.reduce_start(p, k + 1)
        else:
            here = pl.ds(pl.multiple_of(self.starts[p][3], 16), 16)
            self.last[:, cols] = self.partial[self.shard, here, cols] + self.crossed[:, cols]
            self.held[p] = pltpu.make_async_copy(
                self.last.at[:, cols], self.rows_out(p, self.starts[p][3], 16), self.own.at[8 + p]
            )
            self.held[p].start()
            self.gather_start(p, 2)

    def gather_start(self, p, k):
        mine = self.rows_out(p, self.starts[p][k + 1], self.sizes[p][k + 1])
        src = self.last.at[:, self.cols[p]] if k == 2 else mine
        self.moving[p] = [
            self.start(
                copy_to(device, src, mine, self.gat_send.at[p, k, d], self.gat_recv.at[p, k, d])
            )
            for d, (device, _) in enumerate(self.others(p, k))
        ]

    def gather_step(self, p, k):
        if k == 2:
            self.held[p].wait()
        if k > 0:
            for copy in self.moving[p]:
                copy.wait_recv()
            self.gather_start(p, k - 1)
            if k == 1:
                self.share(p, 0, self.starts[p][1])
        else:
            dim = RING_ORDERS[p][0]
            n, size = (RINGS[dim], self.sizes[p][1])
            for d, copy in enumerate(self.moving[p], 1):
                copy.wait_recv()
                self.share(p, d, (ring_position(dim) + n - d) % n * size)

    def share(self, p, slot, at):
        mine = self.rows_out(p, at, self.sizes[p][1])
        sems = (self.gat_send.at[p, 3, slot], self.gat_recv.at[p, 3, slot])
        self.shared.append(self.start(remote(mine, mine, *sems, "core")))


def ring_scratch(width):
    bf16, dma = (jnp.bfloat16, pltpu.SemaphoreType.DMA)
    landed = []
    for order in RING_ORDERS:
        rows = ROWS
        for dim in order:
            rows //= RINGS[dim]
            landed.append(pltpu.VMEM((RINGS[dim] - 1, 2, rows, width), bf16))
    return [
        pltpu.VMEM((2, ROWS, 3 * width), bf16),
        *landed,
        pltpu.VMEM((16, 3 * width), bf16),
        pltpu.VMEM((16, 3 * width), bf16),
        dma((8,)),
        dma((8,)),
        dma((3, 4, 3)),
        dma((3, 4, 3)),
        dma((3, 4, 4)),
        dma((3, 4, 4)),
        dma((11,)),
    ]


class NormSums:
    def __init__(self, held, landed, out, send, recv, start):
        self.held, self.landed, self.out = (held, landed, out)
        self.send, self.recv, self.start = (send, recv, start)
        self.dims = ("core",) + REDUCE_DIMS + ("xb",)

    def begin(self, k):
        shard, _, _, _, _ = place()
        if k < 6:
            src, dst = (self.held.at[k], self.landed.at[k])
        else:
            src, dst = (self.held.at[6, pl.ds(1 - shard, 1)], self.landed.at[6, pl.ds(0, 1)])
        self.copy = self.start(remote(src, dst, self.send.at[k], self.recv.at[k], self.dims[k]))

    def step(self, k):
        shard, _, _, _, _ = place()
        self.copy.wait_recv()
        if k < 6:
            self.held[k + 1] = self.held[k] + self.landed[k]
            self.begin(k + 1)
        else:
            self.out[...] = self.held[6, shard] + self.landed[6, 0]


def project_back(tok_ref, weight_ref, weight, sem, grad_ref, back_out):
    def fetch(c):
        cols = pl.ds(c * 256, 256)
        return pltpu.make_async_copy(weight_ref.at[:, cols], weight.at[c % 2], sem.at[c % 2])

    fetch(0).start()
    total = grad_ref[...]
    for c in range(12):
        if c < 11:
            fetch(c + 1).start()
        fetch(c).wait()
        total = total + lax.dot_general(
            tok_ref[:, c * 256 : (c + 1) * 256],
            weight[c % 2],
            (((1,), (1,)), ((), ())),
            preferred_element_type=jnp.float32,
        )
    back_out[...] = total.astype(jnp.bfloat16)


def back_kernel(*refs):
    refs = list(refs)

    def take(count):
        taken = refs[:count]
        del refs[:count]
        return taken

    tokens_ref, *ff_acts = take(7)
    norm_ref, staged, grad_ref, weight_ref = take(4)
    q_ref, pairs_ref, low_ref, end_ref, lse_ref, o_ref = take(6)
    ff_out, qkv_out, norm_out, back_out = take(4)
    qkv_acts = [tokens_ref] + take(3)
    ff_refs = take(8) + [ff_out] + take(7)
    qkv_refs = take(12) + [qkv_out] + take(7)
    norm_refs = take(2) + [norm_out] + take(2)
    heads_in, heads_out, tok_in, tok_ref, weight, weight_sem = take(6)
    swaps = [take(2), take(2)]
    attention_refs = refs
    sent = []

    def start(copy):
        copy.start()
        sent.append(copy)
        return copy

    greet_all(("core", "xa", "xb"))
    ff = Reducer(ff_acts, FF_DOTS, FF_WIDTHS, ff_refs, start)
    qkv = RingReducer(qkv_acts, QKV_DOTS, QKV_WIDTH, qkv_refs, start)
    upstream = Exchange(staged, heads_in, *swaps[0], start)
    upstream.begin()
    sums = NormSums(*norm_refs, start)
    sums.held[0] = norm_ref[...]
    sums.begin(0)
    for at in range(len(FF_DOTS)):
        ff.multiply(at)
    sums.step(0)
    upstream.finish()
    attention = AttendBack(
        [q_ref, heads_in, pairs_ref, low_ref, end_ref, lse_ref, o_ref],
        heads_out,
        attention_refs,
        start,
    )
    def ff_reduce(k):
        sums.step(k + 1)
        for p in ff.parts:
            ff.reduce_step(p, k)

    def ff_gather(k):
        for p in ff.parts:
            ff.gather_step(p, k)

    def qkv_reduce(k):
        for p in qkv.parts:
            qkv.reduce_step(p, k)

    def qkv_gather(k):
        for p in qkv.parts:
            qkv.gather_step(p, k)

    events = [(BACK_REDUCE[k], functools.partial(ff_reduce, k)) for k in range(2)]
    events += attention.events
    events.sort(key=lambda e: e[0])
    done = 0
    for at, act in events:
        if at > done:
            attention.run(done, at)
            done = at
        act()
    attention.run(done, 4 * SLOT_UNITS)
    attention.finish()
    downstream = Exchange(heads_out, tok_in, *swaps[1], start)
    downstream.begin()
    ff_reduce(2)
    ff_reduce(3)
    downstream.finish()

    def unpack(i, carry):
        both = [tok_in[i * 2], tok_in[i * 2 + 1]]
        query = [jnp.concatenate([t[128:192, :HEAD], t[128:192, HEAD:]], axis=0) for t in both]
        key = [t[0:128, :HEAD] for t in both]
        value = [t[0:128, HEAD:] for t in both]
        for which, piece in enumerate((query, key, value)):
            here = pl.ds(pl.multiple_of(which * 1024 + i * 128, 128), 128)
            tok_ref[:, here] = jnp.concatenate(piece, axis=1)
        return carry

    lax.fori_loop(0, 8, unpack, 0)
    pooled = [
        qkv.pool(1 + which, tok_ref.at[:, pl.ds(which * 1024, 1024)]) for which in range(3)
    ]
    ff_reduce(4)
    for near, far in pooled:
        near.wait()
        far.wait_recv()
    for at in range(len(QKV_DOTS)):
        qkv.multiply(at)
    project_back(tok_ref, weight_ref, weight, weight_sem, grad_ref, back_out)
    ff_reduce(5)
    ff_gather(4)
    ff_gather(3)
    qkv_reduce(0)
    ff_gather(2)
    qkv_reduce(1)
    ff_gather(1)
    qkv_reduce(2)
    qkv_reduce(3)
    qkv_gather(2)
    qkv_gather(1)
    ff_gather(0)
    qkv_gather(0)
    ff.finish()
    qkv.finish()
    for copy in sent:
        copy.wait_send()


FF_DOTS = tuple(
    [(0, 512, 0, 3, j * 512) for j in range(4)]
    + [(1, 2048, q * 512, 4, 0) for q in range(4)]
    + [(2, 512, 0, 5, 0)]
)
FF_WIDTHS = (1024, 896, 896, 896, 896)
QKV_DOTS = ((0, 512, 0, 1, 0), (0, 512, 0, 2, 0), (0, 512, 0, 3, 0))
QKV_WIDTH = 512


def reducer_scratch(widths):
    total, parts = (sum(widths), len(widths))
    bf16, dma = (jnp.bfloat16, pltpu.SemaphoreType.DMA)
    return [
        pltpu.VMEM((2, ROWS, total), bf16),
        *[pltpu.VMEM((2, ROWS >> (k + 1), total), bf16) for k in range(5)],
        pltpu.VMEM((16, total), bf16),
        pltpu.VMEM((16, total), bf16),
        dma((8,)),
        dma((8,)),
        dma((parts, 6)),
        dma((parts, 6)),
        dma((parts, 7)),
        dma((parts, 7)),
        dma((8 + parts,)),
    ]


def back(acts, norm_sums, staged, grad_one, full_qkv, attention):
    bf16, f32, dma = (jnp.bfloat16, jnp.float32, pltpu.SemaphoreType.DMA)
    whole, anywhere = (pl.BlockSpec(memory_space=pltpu.VMEM), pl.BlockSpec(memory_space=pl.ANY))
    ff_total, qkv_total = (sum(FF_WIDTHS), 3 * QKV_WIDTH)
    held = pltpu.VMEM((7, 2, 8, 512), f32)
    return pl.pallas_call(
        back_kernel,
        out_shape=[
            jax.ShapeDtypeStruct((2, ROWS, ff_total), bf16),
            jax.ShapeDtypeStruct((2, ROWS, qkv_total), bf16),
            jax.ShapeDtypeStruct((8, 512), f32),
            jax.ShapeDtypeStruct((128, 1024), bf16),
        ],
        in_specs=[whole] * 10 + [anywhere] + [whole] * 6,
        out_specs=[anywhere] * 2 + [whole] * 2,
        scratch_shapes=[
            *[pltpu.VMEM((256, 512), bf16)] * 3,
            *reducer_scratch(FF_WIDTHS),
            *ring_scratch(QKV_WIDTH),
            held,
            held,
            dma((7,)),
            dma((7,)),
            pltpu.VMEM((16, 64, 128), bf16),
            pltpu.VMEM((16, 192, 128), bf16),
            pltpu.VMEM((16, 192, 128), bf16),
            pltpu.VMEM((128, 3072), bf16),
            pltpu.VMEM((2, 1024, 256), bf16),
            dma((2,)),
            *[dma((16,))] * 4,
            *back_scratch(),
        ],
        compiler_params=pltpu.CompilerParams(
            collective_id=1, has_side_effects=True, vmem_limit_bytes=62 * 2**20
        ),
    )(*acts, norm_sums, staged, grad_one, full_qkv, *attention)


CHUNK = 512


def cast_kernel(ff_ref, qkv_ref, *refs):
    outs, (narrow, wide, in_sem, out_sem) = (refs[:6], refs[6:])
    grad_in, grad_down, grad_out, *grad_qkv = outs
    chunks = []
    for c in range(2):
        for j in range(9):
            src = ff_ref.at[c, :, pl.ds(j * CHUNK, CHUNK)]
            if j < 4:
                dst = grad_in.at[:, pl.ds((c * 4 + j) * CHUNK, CHUNK)]
            elif j < 8:
                dst = grad_down.at[pl.ds((j - 4) * ROWS, ROWS), pl.ds(c * CHUNK, CHUNK)]
            else:
                dst = grad_out.at[:, pl.ds(c * CHUNK, CHUNK)]
            chunks.append((src, dst))
        for j in range(3):
            src = qkv_ref.at[c, :, pl.ds(j * CHUNK, CHUNK)]
            chunks.append((src, grad_qkv[j].at[:, pl.ds(c * CHUNK, CHUNK)]))
    loads = [
        pltpu.make_async_copy(src, narrow.at[n], in_sem.at[n]) for n, (src, _) in enumerate(chunks)
    ]
    stores = [
        pltpu.make_async_copy(wide.at[n], dst, out_sem.at[n]) for n, (_, dst) in enumerate(chunks)
    ]
    for load in loads:
        load.start()
    for n in range(len(chunks)):
        loads[n].wait()

        def widen(i, carry):
            here = pl.ds(pl.multiple_of(i * 64, 64), 64)
            wide[n, here] = narrow[n, here].astype(jnp.float32)
            return carry

        lax.fori_loop(0, ROWS // 64, widen, 0)
        stores[n].start()
    for store in stores:
        store.wait()


def grads_out(ff_summed, qkv_summed):
    f32 = jnp.float32
    anywhere = pl.BlockSpec(memory_space=pl.ANY)
    square = jax.ShapeDtypeStruct((ROWS, 1024), f32)
    return pl.pallas_call(
        cast_kernel,
        out_shape=[
            jax.ShapeDtypeStruct((ROWS, 4096), f32),
            jax.ShapeDtypeStruct((2048, 1024), f32),
            square,
            square,
            square,
            square,
        ],
        in_specs=[anywhere] * 2,
        out_specs=[anywhere] * 6,
        scratch_shapes=[
            pltpu.VMEM((24, ROWS, CHUNK), jnp.bfloat16),
            pltpu.VMEM((24, ROWS, CHUNK), f32),
            pltpu.SemaphoreType.DMA((24,)),
            pltpu.SemaphoreType.DMA((24,)),
        ],
        compiler_params=pltpu.CompilerParams(vmem_limit_bytes=56 * 2**20),
    )(ff_summed, qkv_summed)


def shards(
    tokens,
    segments,
    valid,
    w_query,
    w_key,
    w_value,
    w_out,
    norm1_gain,
    norm1_bias,
    w_in,
    w_down,
    norm2_gain,
    norm2_bias,
    cotangent,
):
    packed = jnp.zeros((16, 512), jnp.bfloat16).at[:4].set(
        jnp.stack([norm1_gain, norm1_bias, norm2_gain, norm2_bias])
    )
    token_rows = tokens[0]
    (
        full_qkv,
        queries,
        pairs,
        summed,
        lse,
        low,
        end,
        tokens_all,
        first_low,
        hidden,
        mixed,
        pre_grad,
        ff_grad,
        attn_grad,
        staged,
        norm_sums,
        grad_one,
        result,
    ) = front(
        token_rows,
        [w_query, w_key, w_value, w_out, w_in, w_down],
        packed,
        cotangent[0],
        segments[0],
        valid[0],
    )
    ff_summed, qkv_summed, norm_total, input_grad = back(
        [tokens_all, first_low, hidden, mixed, pre_grad, ff_grad, attn_grad],
        norm_sums,
        staged,
        grad_one,
        full_qkv,
        [queries, pairs, low, end, lse, summed],
    )
    grad_in, grad_down, grad_out, *grad_qkv = grads_out(ff_summed, qkv_summed)
    return (
        result[None],
        input_grad[None],
        *grad_qkv,
        grad_out,
        norm_total[0],
        norm_total[1],
        grad_in,
        grad_down,
        norm_total[2],
        norm_total[3],
    )


def solution(mesh):
    return jax.shard_map(
        shards,
        mesh=mesh,
        in_specs=(
            P("shard", ("blk", "aa"), None),
            P("shard", None),
            P("shard", None),
            P("shard", None),
            P("shard", None),
            P("shard", None),
            P("shard", None),
            P("shard"),
            P("shard"),
            P("shard", None),
            P("shard", None),
            P("shard"),
            P("shard"),
            P("shard", ("blk", "aa"), None),
        ),
        out_specs=(
            P("shard", ("blk", "aa"), None),
            P("shard", ("blk", "aa"), None),
            P("shard", None),
            P("shard", None),
            P("shard", None),
            P("shard", None),
            P("shard"),
            P("shard"),
            P("shard", None),
            P("shard", None),
            P("shard"),
            P("shard"),
        ),
        check_vma=False,
    )
```

```python
import functools
import math

import jax
import jax.numpy as jnp
from jax import lax
from jax.experimental import pallas as pl
from jax.experimental.pallas import tpu as pltpu
from jax.sharding import PartitionSpec as P

HEADS = 16
HEAD = 64
MASKED_SCORE = -1e30
NORM_EPSILON = 1e-05
BLOCK_LEN = 2048


MESH = pl.DeviceIdType.MESH
ROWS = 512
REDUCE_DIMS = ("xa", "ya", "za", "yb", "zb")
GATHER_DIMS = ("ya", "za", "yb", "zb")


def place():
    shard = lax.axis_index("shard")
    blk = lax.axis_index("blk")
    aa = lax.axis_index("aa")
    return (shard, blk // 2, blk % 2, aa // 4, aa % 4)


def flipped(i):
    return i + 1 - 2 * (i % 2)


def partner(dim):
    shard, x_lo, core, z, y = place()
    if dim == "core":
        core = 1 - core
    elif dim == "xa":
        x_lo = 1 - x_lo
    elif dim == "xb":
        shard, x_lo = 1 - shard, 1 - x_lo
    elif dim == "ya":
        y = flipped(y)
    elif dim == "yb":
        y = 3 - y
    elif dim == "za":
        z = flipped(z)
    else:
        z = 3 - z
    return (shard, x_lo * 2 + core, z * 4 + y)


def ring_bit(dim):
    shard, x_lo, _, z, y = place()
    if dim == "xa":
        return (shard * 2 + x_lo + shard) % 2
    if dim == "ya":
        return (y + y // 2) % 2
    if dim == "yb":
        return y // 2
    if dim == "za":
        return (z + z // 2) % 2
    return z // 2


def remote(src, dst, send_sem, recv_sem, dim):
    return pltpu.make_async_remote_copy(
        src_ref=src,
        dst_ref=dst,
        send_sem=send_sem,
        recv_sem=recv_sem,
        device_id=partner(dim),
        device_id_type=MESH,
    )


def row_starts(dims, rows):
    starts, at, size = ([0], 0, rows)
    for dim in dims:
        size //= 2
        at = at + ring_bit(dim) * size
        starts.append(at)
    return starts


def rotated(dims, by):
    return dims[by:] + dims[:by]


class Gather:
    def __init__(self, sources, places, send, recv, start):
        self.sources, self.places = (sources, places)
        self.send, self.recv, self.start = (send, recv, start)
        self.shard, _, self.core, _, _ = place()
        self.orders = [rotated(GATHER_DIMS, part) for part in range(4)]
        self.moving, self.siblings = ({}, [])

    def columns(self, i, part, off):
        cols = self.sources[i].shape[1]
        col = pl.multiple_of(self.core * (cols // 2) + (off + part * (cols // 8)), 128)
        return pl.ds(col, cols // 8)

    def block(self, i, part, shard, at, size):
        target, off = self.places[i]
        rows = self.sources[i].shape[0]
        at = pl.multiple_of(shard * rows + at, 16)
        return target.at[pl.ds(at, size), self.columns(i, part, off)]

    def own(self, i):
        target, off = self.places[i]
        rows, cols = self.sources[i].shape
        return target.at[pl.ds(pl.multiple_of(self.shard * rows, rows), rows), pl.ds(off, cols)]

    def begin(self, i):
        rows = self.sources[i].shape[0]
        for part in range(4):
            at = row_starts(self.orders[part], rows)[4]
            mine = pl.ds(pl.multiple_of(at, 16), rows // 16)
            self.moving[i, part] = self.start(
                remote(
                    self.sources[i].at[mine, self.columns(i, part, 0)],
                    self.block(i, part, self.shard, at, rows // 16),
                    self.send.at[i, part, 0],
                    self.recv.at[i, part, 0],
                    "xb",
                )
            )

    def stage(self, i, stage):
        rows = self.sources[i].shape[0]
        for part in range(4):
            self.moving[i, part].wait_recv()
            starts = row_starts(self.orders[part], rows)
            if stage < 5:
                k = 4 - stage
                mine = self.block(i, part, 1 - self.shard, starts[k + 1], rows >> (k + 1))
                self.moving[i, part] = self.start(
                    remote(
                        mine,
                        mine,
                        self.send.at[i, part, stage],
                        self.recv.at[i, part, stage],
                        self.orders[part][k],
                    )
                )
            if stage >= 4:
                at = starts[1] if stage == 4 else rows // 2 - starts[1]
                mine = self.block(i, part, 1 - self.shard, at, rows // 2)
                self.siblings.append(
                    self.start(
                        remote(
                            mine,
                            mine,
                            self.send.at[i, part, stage + 1],
                            self.recv.at[i, part, stage + 1],
                            "core",
                        )
                    )
                )

    def finish(self):
        for copy in self.siblings:
            copy.wait_recv()
        self.siblings = []


def plane_peer(step):
    shard, x_lo, core, z, y = place()
    return (shard, x_lo * 2 + core, (z * 4 + y + step) % 16)


class Exchange:
    def __init__(self, outgoing, incoming, send, recv, start):
        self.outgoing, self.incoming = (outgoing, incoming)
        self.send, self.recv, self.start = (send, recv, start)
        self.copies = []

    def begin(self):
        me = lax.axis_index("aa")
        for step in (1, 3, 4, 12, 15, 13, 5, 11, 2, 8, 14, 6, 10, 7, 9):
            self.copies.append(
                self.start(
                    pltpu.make_async_remote_copy(
                        src_ref=self.outgoing.at[(me + step) % 16],
                        dst_ref=self.incoming.at[me],
                        send_sem=self.send.at[step],
                        recv_sem=self.recv.at[step],
                        device_id=plane_peer(step),
                        device_id_type=MESH,
                    )
                )
            )
        self.incoming[me] = self.outgoing[me]

    def finish(self):
        for copy in self.copies:
            copy.wait_recv()


def greet_all(dims):
    barrier = pltpu.get_barrier_semaphore()
    for dim in dims:
        pl.semaphore_signal(barrier, inc=1, device_id=partner(dim), device_id_type=MESH)
    for step in range(1, 16):
        pl.semaphore_signal(barrier, inc=1, device_id=plane_peer(step), device_id_type=MESH)
    pl.semaphore_wait(barrier, len(dims) + 15)


def unfolded(block, side):
    lane = lax.broadcasted_iota(jnp.int32, (64, 128), 1)
    keep = (lane >= HEAD) if side else (lane < HEAD)
    block = block.astype(jnp.float32)
    moved = jnp.concatenate([block[:, HEAD:], block[:, :HEAD]], axis=1)
    first, second = (moved, block) if side else (block, moved)
    both = jnp.concatenate([jnp.where(keep, first, 0.0), jnp.where(keep, second, 0.0)], axis=0)
    return both.astype(jnp.bfloat16)


LEAST = -(2**31)
FRONT_BLOCK = 512


def visible(place_k, low, end, start):
    size = jnp.maximum(end - low, 0) + LEAST
    return (place_k - (low - start - LEAST)) < size


def query_spans(segments_ref, valid_ref, low_ref, end_ref):
    _, x_lo, core, _, _ = place()
    segments = segments_ref[...]
    start = pl.multiple_of((x_lo * 2 + core) * 16, 16)
    mine = segments_ref[pl.ds(start, 16)]
    low, end = (jnp.zeros_like(mine), jnp.zeros_like(mine))
    before = jnp.zeros((1, 1), jnp.int32)
    for number in range(35):
        same = jnp.where(segments == number, 1, 0)
        count = jnp.sum(jnp.sum(same, axis=1, keepdims=True), axis=0, keepdims=True)
        picked = mine == number
        low = jnp.where(picked, before, low)
        before = before + count
        end = jnp.where(picked, before, end)
    live = jnp.sum(jnp.sum(valid_ref[...], axis=1, keepdims=True), axis=0, keepdims=True)
    end = jnp.minimum(end, live)
    for row in range(16):
        here = pl.ds(row * 128, 128)
        low_ref[:, here] = jnp.broadcast_to(low[row : row + 1], (8, 128))
        end_ref[:, here] = jnp.broadcast_to(end[row : row + 1], (8, 128))


def normalized(values):
    centred = values - jnp.mean(values, axis=1, keepdims=True)
    inverse = lax.rsqrt(jnp.mean(centred * centred, axis=1, keepdims=True) + NORM_EPSILON)
    return (centred * inverse, inverse)


def normalized_back(upstream, scaled, inverse, gain):
    weighted = upstream * gain
    centred = weighted - jnp.mean(weighted, axis=1, keepdims=True)
    return inverse * (centred - scaled * jnp.mean(weighted * scaled, axis=1, keepdims=True))


def summed_rows(values):
    return jnp.sum(values, axis=0, keepdims=True)


def dense(x_ref, cot_ref, mixed_in, norm_in, weights, scratch, outs, give):
    w_out, w_in, w_down = weights
    slope, low_ref, hidden_ref, mixed_ref, pre_ref, down_ref, attn_ref = scratch
    staged_ref, sums_ref, grad_ref, result_ref = outs
    f32, bf16 = (jnp.float32, jnp.bfloat16)
    gain_one, bias_one, gain_two, bias_two = [
        jnp.concatenate(
            [norm_in[half, i * 4 + j : i * 4 + j + 1] for half in range(2) for j in range(4)], axis=1
        ).astype(f32)
        for i in range(4)
    ]
    for pair in range(8):
        both = [mixed_in[pair * 2], mixed_in[pair * 2 + 1]]
        both = [jnp.concatenate([t[:, :HEAD], t[:, HEAD:]], axis=0) for t in both]
        mixed_ref[:, pair * 128 : (pair + 1) * 128] = jnp.concatenate(both, axis=1)
    give(3)
    attn = jnp.dot(mixed_ref[...], w_out[...], preferred_element_type=f32)
    scaled_one, inverse_one = normalized(x_ref[...].astype(f32) + attn)
    first = scaled_one * gain_one + bias_one
    low_ref[...] = first.astype(bf16)
    give(1)

    def up(c, total):
        here = pl.ds(pl.multiple_of(c * 1024, 1024), 1024)
        pre = jnp.dot(low_ref[...], w_in[:, here], preferred_element_type=f32)
        share = 0.5 + 0.5 * lax.erf(pre * 0.5**0.5)
        hidden = (pre * share).astype(bf16)
        hidden_ref[:, here] = hidden
        slope[:, here] = share + pre * jnp.exp(pre * pre * -0.5) * (2 * math.pi) ** -0.5
        return total + jnp.dot(hidden, w_down[here], preferred_element_type=f32)

    ff_out = lax.fori_loop(0, 4, up, jnp.zeros((128, 1024), f32), unroll=2)
    give(2)
    scaled_two, inverse_two = normalized(first + ff_out)
    result_ref[...] = (scaled_two * gain_two + bias_two).astype(bf16)
    upstream = cot_ref[...].astype(f32)
    grad_two = normalized_back(upstream, scaled_two, inverse_two, gain_two)
    down_ref[...] = grad_two.astype(bf16)
    give(5)

    def down(c, total):
        here = pl.ds(pl.multiple_of(c * 1024, 1024), 1024)
        grad = lax.dot_general(
            down_ref[...], w_down[here], (((1,), (1,)), ((), ())), preferred_element_type=f32
        )
        grad = (grad * slope[:, here]).astype(bf16)
        pre_ref[:, here] = grad
        return total + lax.dot_general(
            grad, w_in[:, here], (((1,), (1,)), ((), ())), preferred_element_type=f32
        )

    first_grad = lax.fori_loop(0, 4, down, grad_two, unroll=2)
    give(4)
    grad_one = normalized_back(first_grad, scaled_one, inverse_one, gain_one)
    grad_ref[...] = grad_one
    attn_ref[...] = grad_one.astype(bf16)
    give(6)
    mixed_grad = lax.dot_general(
        attn_ref[...], w_out[...], (((1,), (1,)), ((), ())), preferred_element_type=f32
    ).astype(bf16)
    for head in range(HEADS):
        part = mixed_grad[:, head * HEAD : (head + 1) * HEAD]
        staged_ref[head] = jnp.concatenate([part[0:64], part[64:128]], axis=1)
    sums = [
        summed_rows(first_grad * scaled_one),
        summed_rows(first_grad),
        summed_rows(upstream * scaled_two),
        summed_rows(upstream),
    ]
    for half in range(2):
        cols = slice(half * 512, (half + 1) * 512)
        sums_ref[half] = jnp.concatenate([v[:, cols] for v in sums] + [jnp.zeros((4, 512), f32)])


def front_kernel(
    x_ref,
    wq_ref,
    wk_ref,
    wv_ref,
    wo_ref,
    wi_ref,
    wd_ref,
    norm_ref,
    cot_ref,
    segments_ref,
    valid_ref,
    qkv_out,
    q_out,
    pairs_out,
    o_out,
    lse_out,
    low_ref,
    end_ref,
    *refs,
):
    dense_out, refs = (refs[:11], refs[11:])
    front_body(
        x_ref,
        (wq_ref, wk_ref, wv_ref, wo_ref, wi_ref, wd_ref),
        norm_ref,
        cot_ref,
        (segments_ref, valid_ref),
        qkv_out,
        (q_out, pairs_out, o_out, lse_out, low_ref, end_ref),
        dense_out,
        *refs,
    )


def front_body(
    x_ref,
    weights,
    norm_ref,
    cot_ref,
    documents,
    qkv_out,
    attention_out,
    dense_out,
    wqkv,
    w_out,
    w_in,
    w_down,
    norm_in,
    mixed_in,
    slope,
    pre_full,
    down_full,
    attn_full,
    low_full,
    hidden_full,
    mixed_full,
    pool_send,
    pool_recv,
    pool_own,
    save_sem,
    q_held,
    pairs_held,
    o_held,
    lse_held,
    low_held,
    end_held,
    staged,
    heads_in,
    folded,
    pairs_t,
    top_s,
    send,
    recv,
    own_in,
    own_out,
    hop_send,
    hop_recv,
    swap_send,
    swap_recv,
    back_send,
    back_recv,
):
    shard, _, _, _, _ = place()
    attention_held = (q_held, pairs_held, o_held, lse_held, low_held, end_held)
    q_out, pairs_out, o_out, lse_out, low_ref, end_ref = attention_held
    saves = []

    def save(i):
        copy = pltpu.make_async_copy(attention_held[i], attention_out[i], save_sem.at[i])
        copy.start()
        saves.append(copy)

    sent = []

    def start(copy):
        copy.start()
        sent.append(copy)
        return copy

    gather = Gather(
        weights,
        [(wqkv, 0), (wqkv, 1024), (wqkv, 2048), (w_out, 0), (w_in, 0), (w_down, 0)],
        send,
        recv,
        start,
    )
    inward = []
    for i in range(6):
        inward.append(pltpu.make_async_copy(weights[i], gather.own(i), own_in.at[i]))
        inward[i].start()
    greet_all(("core", "xa", "xb"))
    norms = start(
        remote(norm_ref, norm_in.at[shard], hop_send.at[3], hop_recv.at[3], "xb")
    )
    norm_in[shard] = norm_ref[...]
    for i in range(6):
        gather.begin(i)
    _, _, core, _, _ = place()
    pooled = []

    def give(i):
        src = (x_ref, low_full, hidden_full, mixed_full, pre_full, down_full, attn_full)[i]
        mine, theirs = (src, src)
        if i > 3:
            half = src.shape[1] // 2
            mine, theirs = [
                src.at[:, pl.ds(pl.multiple_of(c * half, half), half)] for c in (core, 1 - core)
            ]
        copy = pltpu.make_async_copy(mine, dense_out[i].at[pl.ds(0, 128)], pool_own.at[i])
        copy.start()
        saves.append(copy)
        sems = (pool_send.at[i], pool_recv.at[i])
        pooled.append(start(remote(theirs, dense_out[i].at[pl.ds(128, 128)], *sems, "core")))

    give(0)
    for i in range(3):
        gather.stage(i, 1)
    for stage in range(2, 6):
        for i in range(3):
            gather.stage(i, stage)
        if stage == 3:
            for i in range(3, 6):
                gather.stage(i, 1)
    for i in range(3):
        inward[i].wait()
    gather.finish()
    keep = pltpu.make_async_copy(wqkv, qkv_out, own_out.at[0])
    keep.start()

    def project(piece, carry):
        q, k, v = [
            jnp.dot(
                x_ref[...],
                wqkv[:, pl.ds(pl.multiple_of(which * 1024 + piece * 256, 256), 256)],
                preferred_element_type=jnp.float32,
            )
            for which in range(3)
        ]
        q = (q.astype(jnp.bfloat16).astype(jnp.float32) * HEAD ** (-0.5)).astype(jnp.bfloat16)
        k, v = (k.astype(jnp.bfloat16), v.astype(jnp.bfloat16))
        for h in range(4):
            at = slice(h * HEAD, (h + 1) * HEAD)
            staged[piece * 4 + h, 0:128] = jnp.concatenate([k[:, at], v[:, at]], axis=1)
            staged[piece * 4 + h, 128:192] = jnp.concatenate([q[0:64, at], q[64:128, at]], axis=1)
        return carry

    lax.fori_loop(0, 4, project, 0)
    heads = Exchange(staged, heads_in, swap_send, swap_recv, start)
    heads.begin()
    for i in range(3, 6):
        gather.stage(i, 2)
    query_spans(*documents, low_ref, end_ref)
    heads.finish()

    def spread(c, carry):
        here = pl.ds(pl.multiple_of(c * 128, 128), 128)
        pairs_out[here] = heads_in[c, 0:128]
        q_out[here] = unfolded(heads_in[c, 128:192], 0)
        return carry

    lax.fori_loop(0, 16, spread, 0)

    def slot_rows(slot):
        return pairs_out.at[pl.ds(slot * BLOCK_LEN, BLOCK_LEN)]

    def hop(index, source, target, dim):
        return start(
            remote(
                slot_rows(source), slot_rows(target), hop_send.at[index], hop_recv.at[index], dim
            )
        )

    hops = {1: hop(0, 0, 1, "core"), 2: hop(1, 0, 2, "xa")}
    for i in (0, 4, 5):
        save(i)
    top_s[...] = jnp.full_like(top_s, MASKED_SCORE)
    o_out[...] = jnp.zeros_like(o_out)
    first_row = lax.broadcasted_iota(jnp.int32, (128, 512), 0) == 0

    def turn(c, carry):
        here = pl.ds(pl.multiple_of(c * 512, 512), 512)
        turned = jnp.transpose(pairs_out[here].astype(jnp.float32))
        pairs_t[:, here] = jnp.where(first_row, 1.0, turned).astype(jnp.bfloat16)
        return carry

    def slot_step(slot, block):
        _, x_lo, core, _, _ = place()
        owner = (slot // 2 + x_lo) % 2 * 2 + (slot % 2 + core) % 2
        rows = pl.ds(slot * BLOCK_LEN, BLOCK_LEN)
        mine = pl.ds(pl.multiple_of(block * FRONT_BLOCK, FRONT_BLOCK), FRONT_BLOCK)
        scores = lax.dot_general(
            pairs_out[rows],
            q_out[mine],
            (((1,), (1,)), ((), ())),
            preferred_element_type=jnp.float32,
        )
        place_k = lax.broadcasted_iota(jnp.int32, scores.shape, 0)
        allowed = visible(place_k, low_ref[0:1, mine], end_ref[0:1, mine], owner * BLOCK_LEN)
        if slot == 0:
            place_q = lax.broadcasted_iota(jnp.int32, (1, FRONT_BLOCK), 1) + block * FRONT_BLOCK
            allowed = allowed | (place_k == place_q)
        scores = jnp.where(allowed, scores, MASKED_SCORE)
        top = top_s[0:1, mine]
        new_top = jnp.maximum(top, jnp.max(scores, axis=0, keepdims=True))
        weights = jnp.exp(scores - new_top)
        factor = jnp.exp(top - new_top)
        o_out[:, mine] = o_out[:, mine] * factor + jnp.dot(
            pairs_t[:, rows], weights.astype(jnp.bfloat16), preferred_element_type=jnp.float32
        )
        top_s[:, mine] = jnp.broadcast_to(new_top, (8, FRONT_BLOCK))

    events = {
        0: [(i, 3) for i in (3, 4, 5)],
        1: [(i, 4) for i in (3, 4, 5)],
        3: [(i, 5) for i in (3, 4, 5)],
    }
    for slot in range(4):
        if slot:
            hops[slot].wait_recv()
        if slot == 2:
            hops[3] = hop(2, 2, 3, "core")
        if slot == 3:
            save(1)
        lax.fori_loop(slot * 4, slot * 4 + 4, turn, 0)
        for half in range(2):

            def blocks(b, carry):
                slot_step(slot, b)
                return carry

            lax.fori_loop(half * 2, half * 2 + 2, blocks, 0)
            if half == 0:
                for i, stage in events.get(slot, ()):
                    gather.stage(i, stage)

    def close(c, carry):
        here = pl.ds(pl.multiple_of(c * 128, 128), 128)
        total = o_out[0:1, here]
        mixed = o_out[:, here] / total
        o_out[:, here] = mixed
        lse = top_s[0:1, here] + jnp.log(total)
        lse_out[:, here] = jnp.broadcast_to(lse, (8, 128))
        block = jnp.transpose(mixed)
        both = jnp.concatenate([block[0:64, HEAD:], block[64:128, HEAD:]], axis=1)
        folded[c] = both.astype(jnp.bfloat16)
        return carry

    lax.fori_loop(0, 16, close, 0)
    back = Exchange(folded, mixed_in, back_send, back_recv, start)
    back.begin()
    save(2)
    save(3)
    gather.finish()
    norms.wait_recv()
    for i in range(3, 6):
        inward[i].wait()
    back.finish()
    dense(
        x_ref,
        cot_ref,
        mixed_in,
        norm_in,
        (w_out, w_in, w_down),
        (slope, low_full, hidden_full, mixed_full, pre_full, down_full, attn_full),
        dense_out[7:],
        give,
    )
    for copy in pooled:
        copy.wait_recv()
    for copy in saves:
        copy.wait()
    keep.wait()
    for copy in sent:
        copy.wait_send()


def front(token_rows, weights, packed, cotangent, segments, valid):
    bf16, f32, i32, dma = (jnp.bfloat16, jnp.float32, jnp.int32, pltpu.SemaphoreType.DMA)
    n, shape = (len(weights), jax.ShapeDtypeStruct)
    whole, anywhere = (pl.BlockSpec(memory_space=pltpu.VMEM), pl.BlockSpec(memory_space=pl.ANY))
    return pl.pallas_call(
        front_kernel,
        out_shape=[
            shape((1024, 3072), bf16),
            shape((BLOCK_LEN, 128), bf16),
            shape((4 * BLOCK_LEN, 128), bf16),
            shape((128, BLOCK_LEN), f32),
            shape((8, BLOCK_LEN), f32),
            shape((8, BLOCK_LEN), i32),
            shape((8, BLOCK_LEN), i32),
            *[shape((256, width), bf16) for width in (1024, 1024, 4096, 1024, 2048, 512, 512)],
            shape((HEADS, 64, 128), bf16),
            shape((2, 8, 512), f32),
            shape((128, 1024), f32),
            shape((128, 1024), bf16),
        ],
        in_specs=[whole] + [anywhere] * n + [whole] * 4,
        out_specs=[anywhere] * 14 + [whole] * 4,
        scratch_shapes=[
            pltpu.VMEM((1024, 3072), bf16),
            pltpu.VMEM((1024, 1024), bf16),
            pltpu.VMEM((1024, 4096), bf16),
            pltpu.VMEM((4096, 1024), bf16),
            pltpu.VMEM((2, 16, 128), bf16),
            pltpu.VMEM((16, 64, 128), bf16),
            pltpu.VMEM((128, 4096), f32),
            pltpu.VMEM((128, 4096), bf16),
            pltpu.VMEM((128, 1024), bf16),
            pltpu.VMEM((128, 1024), bf16),
            pltpu.VMEM((128, 1024), bf16),
            pltpu.VMEM((128, 4096), bf16),
            pltpu.VMEM((128, 1024), bf16),
            dma((7,)),
            dma((7,)),
            dma((7,)),
            dma((6,)),
            pltpu.VMEM((BLOCK_LEN, 128), bf16),
            pltpu.VMEM((4 * BLOCK_LEN, 128), bf16),
            pltpu.VMEM((128, BLOCK_LEN), f32),
            pltpu.VMEM((8, BLOCK_LEN), f32),
            pltpu.VMEM((8, BLOCK_LEN), i32),
            pltpu.VMEM((8, BLOCK_LEN), i32),
            pltpu.VMEM((16, 192, 128), bf16),
            pltpu.VMEM((16, 192, 128), bf16),
            pltpu.VMEM((16, 64, 128), bf16),
            pltpu.VMEM((128, 4 * BLOCK_LEN), bf16),
            pltpu.VMEM((8, BLOCK_LEN), f32),
            dma((n, 4, 7)),
            dma((n, 4, 7)),
            dma((n,)),
            dma((1,)),
            dma((4,)),
            dma((4,)),
            *[dma((16,))] * 4,
        ],
        compiler_params=pltpu.CompilerParams(
            collective_id=0, has_side_effects=True, vmem_limit_bytes=62 * 2**20
        ),
    )(
        token_rows,
        *weights,
        packed,
        cotangent,
        segments.reshape(64, 128),
        valid.reshape(64, 128),
    )


BACK_REDUCE = (7, 12)
SLOT_UNITS = 4
BACK_BLOCK = 512


def back_scratch():
    return [
        pltpu.VMEM((BLOCK_LEN, 128), jnp.bfloat16),
        pltpu.VMEM((HEAD, 4 * BLOCK_LEN), jnp.bfloat16),
        pltpu.VMEM((8, BLOCK_LEN), jnp.float32),
        pltpu.VMEM((HEAD, BLOCK_LEN), jnp.float32),
        pltpu.VMEM((4 * BLOCK_LEN, 128), jnp.float32),
        pltpu.VMEM((3, BLOCK_LEN, 128), jnp.bfloat16),
        pltpu.VMEM((3, BLOCK_LEN, 128), jnp.bfloat16),
        pltpu.SemaphoreType.DMA((3,)),
        pltpu.SemaphoreType.DMA((3,)),
    ]


class AttendBack:
    def __init__(self, ins, out, scratch, start):
        self.q, self.packed, self.pairs, self.low, self.end, self.lse, self.o_t = ins
        self.out = out
        self.g, self.pairs_t, self.delta, self.dq, self.dkv = scratch[:5]
        self.away, self.landed, self.send, self.recv = scratch[5:9]
        self.start = start
        self.copies = {}
        self.events = [
            (0, self.begin),
            (SLOT_UNITS, lambda: self.give(3, 0, None, "core")),
            (2 * SLOT_UNITS + 1, lambda: self.give(2, 1, 0, "xa")),
            (3 * SLOT_UNITS, lambda: self.give(1, 2, None, "core")),
        ]

    def begin(self):
        self.delta[...] = jnp.zeros_like(self.delta)
        self.dq[...] = jnp.zeros_like(self.dq)
        self.dkv[...] = jnp.zeros_like(self.dkv)

        def chunk(c, carry):
            both = unfolded(self.packed[c], 1)
            here = pl.ds(pl.multiple_of(c * 128, 128), 128)
            self.g[here] = both
            products = jnp.transpose(both.astype(jnp.float32)) * self.o_t[:, here]
            total = jnp.sum(products, axis=0, keepdims=True)
            self.delta[:, here] = jnp.broadcast_to(total, (8, 128))
            return carry

        lax.fori_loop(0, 16, chunk, 0)

        def turn(c, carry):
            here = pl.ds(pl.multiple_of(c * 512, 512), 512)
            self.pairs_t[:, here] = jnp.transpose(self.pairs[here])[0:HEAD]
            return carry

        lax.fori_loop(0, 16, turn, 0)

    def run(self, first, last):
        edge = 3 * SLOT_UNITS
        if first < edge:
            lax.fori_loop(first, min(last, edge), functools.partial(self.unit, own=False), 0)
        if last > edge:
            lax.fori_loop(max(first, edge), last, functools.partial(self.unit, own=True), 0)

    def unit(self, n, carry, own):
        _, x_lo, core, _, _ = place()
        block = n % 4
        slot = 3 - n // 4
        owner = (slot // 2 + x_lo) % 2 * 2 + (slot % 2 + core) % 2
        key_start = owner * BLOCK_LEN
        here = pl.ds(pl.multiple_of(slot * BLOCK_LEN, BLOCK_LEN), BLOCK_LEN)
        mine = pl.ds(pl.multiple_of(block * BACK_BLOCK, BACK_BLOCK), BACK_BLOCK)
        keys = self.pairs[here]
        queries, upstream = (self.q[mine], self.g[mine])
        scores = lax.dot_general(
            keys, queries, (((1,), (1,)), ((), ())), preferred_element_type=jnp.float32
        )
        place_k = lax.broadcasted_iota(jnp.int32, scores.shape, 0)
        allowed = visible(place_k, self.low[0:1, mine], self.end[0:1, mine], key_start)
        if own:
            place_q = lax.broadcasted_iota(jnp.int32, (1, BACK_BLOCK), 1)
            place_q = place_q + block * BACK_BLOCK
            allowed = allowed | (place_k == place_q)
        scores = jnp.where(allowed, scores, MASKED_SCORE)
        probs = jnp.exp(scores - self.lse[0:1, mine])
        prob_grad = lax.dot_general(
            keys, upstream, (((1,), (1,)), ((), ())), preferred_element_type=jnp.float32
        )
        score_grad = (probs * (prob_grad - self.delta[0:1, mine])).astype(jnp.bfloat16)
        self.dkv[here] += jnp.dot(
            score_grad, queries, preferred_element_type=jnp.float32
        ) + jnp.dot(probs.astype(jnp.bfloat16), upstream, preferred_element_type=jnp.float32)
        self.dq[:, mine] += jnp.dot(
            self.pairs_t[:, here], score_grad, preferred_element_type=jnp.float32
        )
        return carry

    def give(self, slot, index, add, dim):
        if add is not None:
            self.copies[add].wait_recv()

        def chunk(c, carry):
            here = pl.ds(pl.multiple_of(c * 256, 256), 256)
            there = pl.ds(pl.multiple_of(slot * BLOCK_LEN + c * 256, 256), 256)
            total = self.dkv[there]
            if add is not None:
                total = total + self.landed[add, here].astype(jnp.float32)
            self.away[index, here] = total.astype(jnp.bfloat16)
            return carry

        lax.fori_loop(0, BLOCK_LEN // 256, chunk, 0)
        self.copies[index] = self.start(
            remote(
                self.away.at[index],
                self.landed.at[index],
                self.send.at[index],
                self.recv.at[index],
                dim,
            )
        )

    def finish(self):
        self.copies[1].wait_recv()
        self.copies[2].wait_recv()

        def chunk(c, carry):
            here = pl.ds(pl.multiple_of(c * 128, 128), 128)
            total = self.dkv[here] + self.landed[1, here].astype(jnp.float32)
            total = total + self.landed[2, here].astype(jnp.float32)
            self.out[c, 0:128] = total.astype(jnp.bfloat16)
            grad = jnp.transpose(self.dq[:, here]) * HEAD ** (-0.5)
            folded = jnp.concatenate([grad[0:64], grad[64:128]], axis=1)
            self.out[c, 128:192] = folded.astype(jnp.bfloat16)
            return carry

        lax.fori_loop(0, 16, chunk, 0)


class Reducer:
    def __init__(self, acts, dots, widths, refs, start):
        self.acts, self.dots, self.start = (acts, dots, start)
        self.partial, self.landed, self.last, self.out = (refs[0], refs[1:7], refs[7], refs[8])
        self.act_send, self.act_recv, self.red_send, self.red_recv = refs[9:13]
        self.gat_send, self.gat_recv, self.own = refs[13:16]
        self.shard, _, self.core, _, _ = place()
        self.parts = range(len(widths))
        self.edges = [sum(widths[:p]) for p in range(len(widths) + 1)]
        self.cols = [pl.ds(self.edges[p], widths[p]) for p in self.parts]
        self.orders = [rotated(REDUCE_DIMS, p) for p in self.parts]
        self.starts = [row_starts(self.orders[p], ROWS) for p in self.parts]
        self.moving, self.held, self.shared = ({}, {}, [])

    def pool(self, i, src):
        dst = self.acts[i]
        tokens = src.shape[0]
        half = src.shape[1] // 2
        mine, theirs = [
            src.at[:, pl.ds(pl.multiple_of(c * half, half), half)]
            for c in (self.core, 1 - self.core)
        ]
        near = pltpu.make_async_copy(mine, dst.at[pl.ds(0, tokens)], self.own.at[i])
        near.start()
        far = remote(
            theirs, dst.at[pl.ds(tokens, tokens)], self.act_send.at[i], self.act_recv.at[i], "core"
        )
        return (near, self.start(far))

    def multiply(self, at):
        left, left_step, left_off, right, right_off = self.dots[at]
        for s in range(2):
            product = lax.dot_general(
                self.acts[left][:, pl.ds(s * left_step + left_off, ROWS)],
                self.acts[right][:, pl.ds(right_off, 512)],
                (((0,), (0,)), ((), ())),
                preferred_element_type=jnp.float32,
            )
            self.partial[s, :, pl.ds(at * 512, 512)] = product.astype(jnp.bfloat16)
        for p in self.parts:
            if at * 512 < self.edges[p + 1] <= (at + 1) * 512:
                self.reduce_start(p, 0)

    def reduce_start(self, p, k):
        starts, cols = (self.starts[p], self.cols[p])
        if k < 5:
            half = ROWS >> (k + 1)
            away = pl.multiple_of(starts[k] + (half - (starts[k + 1] - starts[k])), 16)
            src = self.partial.at[:, pl.ds(away, half), cols]
            dst = self.landed[k].at[:, :, cols]
            dim = self.orders[p][k]
        else:
            src = self.partial.at[1 - self.shard, pl.ds(pl.multiple_of(starts[5], 16), 16), cols]
            dst = self.landed[5].at[:, cols]
            dim = "xb"
        self.moving[p] = self.start(
            remote(src, dst, self.red_send.at[p, k], self.red_recv.at[p, k], dim)
        )

    def reduce_step(self, p, k):
        self.moving[p].wait_recv()
        starts, cols = (self.starts[p], self.cols[p])
        if k < 5:
            half = ROWS >> (k + 1)
            step = min(half, 32)

            def add(i, carry):
                here = pl.ds(pl.multiple_of(i * step, step), step)
                there = pl.ds(pl.multiple_of(starts[k + 1] + i * step, 16), step)
                self.partial[:, there, cols] += self.landed[k][:, here, cols]
                return carry

            lax.fori_loop(0, half // step, add, 0)
            self.reduce_start(p, k + 1)
        else:
            here = pl.ds(pl.multiple_of(starts[5], 16), 16)
            self.last[:, cols] = self.partial[self.shard, here, cols] + self.landed[5][:, cols]
            self.held[p] = pltpu.make_async_copy(
                self.last.at[:, cols], self.rows_out(p, starts[5], 16), self.own.at[8 + p]
            )
            self.held[p].start()
            self.gather_start(p, 4)

    def rows_out(self, p, at, size):
        return self.out.at[self.core, pl.ds(pl.multiple_of(at, 16), size), self.cols[p]]

    def gather_start(self, p, k):
        mine = self.rows_out(p, self.starts[p][k + 1], ROWS >> (k + 1))
        src = self.last.at[:, self.cols[p]] if k == 4 else mine
        self.moving[p] = self.start(
            remote(src, mine, self.gat_send.at[p, k], self.gat_recv.at[p, k], self.orders[p][k])
        )

    def gather_step(self, p, k):
        self.moving[p].wait_recv()
        if k == 4:
            self.held[p].wait()
        if k > 0:
            self.gather_start(p, k - 1)
        if k == 1:
            self.share(p, 0, self.starts[p][1])
        if k == 0:
            self.share(p, 1, ROWS // 2 - self.starts[p][1])

    def share(self, p, slot, at):
        mine = self.rows_out(p, at, ROWS // 2)
        sems = (self.gat_send.at[p, 5 + slot], self.gat_recv.at[p, 5 + slot])
        self.shared.append(self.start(remote(mine, mine, *sems, "core")))

    def finish(self):
        for copy in self.shared:
            copy.wait_recv()


RINGS = {"y": 4, "z": 4, "xa": 2}
RING_ORDERS = (("y", "z", "xa"), ("z", "y", "xa"), ("xa", "y", "z"))


def ring_position(dim):
    _, _, _, z, y = place()
    return {"y": y, "z": z, "xa": ring_bit("xa")}[dim]


def ring_member(dim, step):
    shard, x_lo, core, z, y = place()
    if dim == "xa":
        return partner("xa")
    if dim == "y":
        y = (y + step) % 4
    else:
        z = (z + step) % 4
    return (shard, x_lo * 2 + core, z * 4 + y)


def copy_to(device, src, dst, send_sem, recv_sem):
    return pltpu.make_async_remote_copy(
        src_ref=src,
        dst_ref=dst,
        send_sem=send_sem,
        recv_sem=recv_sem,
        device_id=device,
        device_id_type=MESH,
    )


class RingReducer(Reducer):
    def __init__(self, acts, dots, width, refs, start):
        self.acts, self.dots, self.start, self.width = (acts, dots, start, width)
        self.partial, self.landed, self.crossed, self.last, self.out = (
            refs[0],
            [refs[1 + p * 3 : 4 + p * 3] for p in range(3)],
            refs[10],
            refs[11],
            refs[12],
        )
        self.act_send, self.act_recv, self.red_send, self.red_recv = refs[13:17]
        self.gat_send, self.gat_recv, self.own = refs[17:20]
        self.shard, _, self.core, _, _ = place()
        self.parts = range(3)
        self.edges = [width * p for p in range(4)]
        self.cols = [pl.ds(width * p, width) for p in self.parts]
        self.sizes, self.starts = ([], [])
        for order in RING_ORDERS:
            sizes, starts = ([ROWS], [0])
            for dim in order:
                sizes.append(sizes[-1] // RINGS[dim])
                starts.append(starts[-1] + ring_position(dim) * sizes[-1])
            self.sizes.append(sizes)
            self.starts.append(starts)
        self.moving, self.held, self.shared = ({}, {}, [])

    def others(self, p, k):
        dim = RING_ORDERS[p][k]
        n, at, size = (RINGS[dim], self.starts[p][k], self.sizes[p][k + 1])
        return [
            (ring_member(dim, d), at + (ring_position(dim) + d) % n * size) for d in range(1, n)
        ]

    def reduce_start(self, p, k):
        if k < 3:
            self.moving[p] = []
            for d, (device, at) in enumerate(self.others(p, k)):
                rows = pl.ds(pl.multiple_of(at, 16), self.sizes[p][k + 1])
                self.moving[p].append(
                    self.start(
                        copy_to(
                            device,
                            self.partial.at[:, rows, self.cols[p]],
                            self.landed[p][k].at[d],
                            self.red_send.at[p, k, d],
                            self.red_recv.at[p, k, d],
                        )
                    )
                )
        else:
            rows = pl.ds(pl.multiple_of(self.starts[p][3], 16), 16)
            sems = (self.red_send.at[p, 3, 0], self.red_recv.at[p, 3, 0])
            src = self.partial.at[1 - self.shard, rows, self.cols[p]]
            dst = self.crossed.at[:, self.cols[p]]
            self.moving[p] = [self.start(remote(src, dst, *sems, "xb"))]

    def reduce_step(self, p, k):
        for copy in self.moving[p]:
            copy.wait_recv()
        cols = self.cols[p]
        if k < 3:
            count, size = (len(self.moving[p]), self.sizes[p][k + 1])

            def add(i, carry):
                here = pl.ds(pl.multiple_of(i * 16, 16), 16)
                there = pl.ds(pl.multiple_of(self.starts[p][k + 1] + i * 16, 16), 16)
                total = self.partial[:, there, cols].astype(jnp.float32)
                for d in range(count):
                    total = total + self.landed[p][k][d, :, here].astype(jnp.float32)
                self.partial[:, there, cols] = total.astype(jnp.bfloat16)
                return carry

            lax.fori_loop(0, size // 16, add, 0)
            self.reduce_start(p, k + 1)
        else:
            here = pl.ds(pl.multiple_of(self.starts[p][3], 16), 16)
            self.last[:, cols] = self.partial[self.shard, here, cols] + self.crossed[:, cols]
            self.held[p] = pltpu.make_async_copy(
                self.last.at[:, cols], self.rows_out(p, self.starts[p][3], 16), self.own.at[8 + p]
            )
            self.held[p].start()
            self.gather_start(p, 2)

    def gather_start(self, p, k):
        mine = self.rows_out(p, self.starts[p][k + 1], self.sizes[p][k + 1])
        src = self.last.at[:, self.cols[p]] if k == 2 else mine
        self.moving[p] = [
            self.start(
                copy_to(device, src, mine, self.gat_send.at[p, k, d], self.gat_recv.at[p, k, d])
            )
            for d, (device, _) in enumerate(self.others(p, k))
        ]

    def gather_step(self, p, k):
        if k == 2:
            self.held[p].wait()
        if k > 0:
            for copy in self.moving[p]:
                copy.wait_recv()
            self.gather_start(p, k - 1)
            if k == 1:
                self.share(p, 0, self.starts[p][1])
        else:
            dim = RING_ORDERS[p][0]
            n, size = (RINGS[dim], self.sizes[p][1])
            for d, copy in enumerate(self.moving[p], 1):
                copy.wait_recv()
                self.share(p, d, (ring_position(dim) + n - d) % n * size)

    def share(self, p, slot, at):
        mine = self.rows_out(p, at, self.sizes[p][1])
        sems = (self.gat_send.at[p, 3, slot], self.gat_recv.at[p, 3, slot])
        self.shared.append(self.start(remote(mine, mine, *sems, "core")))


def ring_scratch(width):
    bf16, dma = (jnp.bfloat16, pltpu.SemaphoreType.DMA)
    landed = []
    for order in RING_ORDERS:
        rows = ROWS
        for dim in order:
            rows //= RINGS[dim]
            landed.append(pltpu.VMEM((RINGS[dim] - 1, 2, rows, width), bf16))
    return [
        pltpu.VMEM((2, ROWS, 3 * width), bf16),
        *landed,
        pltpu.VMEM((16, 3 * width), bf16),
        pltpu.VMEM((16, 3 * width), bf16),
        dma((8,)),
        dma((8,)),
        dma((3, 4, 3)),
        dma((3, 4, 3)),
        dma((3, 4, 4)),
        dma((3, 4, 4)),
        dma((11,)),
    ]


class NormSums:
    def __init__(self, held, landed, out, send, recv, start):
        self.held, self.landed, self.out = (held, landed, out)
        self.send, self.recv, self.start = (send, recv, start)
        self.dims = ("core",) + REDUCE_DIMS + ("xb",)

    def begin(self, k):
        shard, _, _, _, _ = place()
        if k < 6:
            src, dst = (self.held.at[k], self.landed.at[k])
        else:
            src, dst = (self.held.at[6, pl.ds(1 - shard, 1)], self.landed.at[6, pl.ds(0, 1)])
        self.copy = self.start(remote(src, dst, self.send.at[k], self.recv.at[k], self.dims[k]))

    def step(self, k):
        shard, _, _, _, _ = place()
        self.copy.wait_recv()
        if k < 6:
            self.held[k + 1] = self.held[k] + self.landed[k]
            self.begin(k + 1)
        else:
            self.out[...] = self.held[6, shard] + self.landed[6, 0]


def project_back(tok_ref, weight_ref, weight, sem, grad_ref, back_out):
    def fetch(c):
        cols = pl.ds(c * 256, 256)
        return pltpu.make_async_copy(weight_ref.at[:, cols], weight.at[c % 2], sem.at[c % 2])

    fetch(0).start()
    total = grad_ref[...]
    for c in range(12):
        if c < 11:
            fetch(c + 1).start()
        fetch(c).wait()
        total = total + lax.dot_general(
            tok_ref[:, c * 256 : (c + 1) * 256],
            weight[c % 2],
            (((1,), (1,)), ((), ())),
            preferred_element_type=jnp.float32,
        )
    back_out[...] = total.astype(jnp.bfloat16)


def back_kernel(*refs):
    refs = list(refs)

    def take(count):
        taken = refs[:count]
        del refs[:count]
        return taken

    act_refs = take(7)
    norm_ref, staged, grad_ref, weight_ref = take(4)
    attention_in = take(6)
    ff_out, qkv_out, norm_out, back_out = take(4)
    loads, held = ([], take(13))
    load_sem = take(1)[0]
    for i, (src, dst) in enumerate(zip(act_refs + attention_in, held)):
        loads.append(pltpu.make_async_copy(src, dst, load_sem.at[i]))
        loads[i].start()
    ff_acts, qkv_acts = (held[1:7], [held[0]] + take(3))
    q_ref, pairs_ref, low_ref, end_ref, lse_ref, o_ref = held[7:]
    ff_refs = take(8) + [ff_out] + take(7)
    qkv_refs = take(12) + [qkv_out] + take(7)
    norm_refs = take(2) + [norm_out] + take(2)
    heads_in, heads_out, tok_in, tok_ref, weight, weight_sem = take(6)
    swaps = [take(2), take(2)]
    attention_refs = refs
    sent = []

    def start(copy):
        copy.start()
        sent.append(copy)
        return copy

    greet_all(("core", "xa", "xb"))
    ff = Reducer(ff_acts, FF_DOTS, FF_WIDTHS, ff_refs, start)
    qkv = RingReducer(qkv_acts, QKV_DOTS, QKV_WIDTH, qkv_refs, start)
    upstream = Exchange(staged, heads_in, *swaps[0], start)
    upstream.begin()
    sums = NormSums(*norm_refs, start)
    sums.held[0] = norm_ref[...]
    sums.begin(0)
    for load in loads[1:7]:
        load.wait()
    for at in range(len(FF_DOTS)):
        ff.multiply(at)
    sums.step(0)
    for load in loads[7:]:
        load.wait()
    upstream.finish()
    attention = AttendBack(
        [q_ref, heads_in, pairs_ref, low_ref, end_ref, lse_ref, o_ref],
        heads_out,
        attention_refs,
        start,
    )
    def ff_reduce(k):
        sums.step(k + 1)
        for p in ff.parts:
            ff.reduce_step(p, k)

    def ff_gather(k):
        for p in ff.parts:
            ff.gather_step(p, k)

    def qkv_reduce(k):
        for p in qkv.parts:
            qkv.reduce_step(p, k)

    def qkv_gather(k):
        for p in qkv.parts:
            qkv.gather_step(p, k)

    events = [(BACK_REDUCE[k], functools.partial(ff_reduce, k)) for k in range(2)]
    events += attention.events
    events.sort(key=lambda e: e[0])
    done = 0
    for at, act in events:
        if at > done:
            attention.run(done, at)
            done = at
        act()
    attention.run(done, 4 * SLOT_UNITS)
    attention.finish()
    downstream = Exchange(heads_out, tok_in, *swaps[1], start)
    downstream.begin()
    ff_reduce(2)
    ff_reduce(3)
    downstream.finish()

    def unpack(i, carry):
        both = [tok_in[i * 2], tok_in[i * 2 + 1]]
        query = [jnp.concatenate([t[128:192, :HEAD], t[128:192, HEAD:]], axis=0) for t in both]
        key = [t[0:128, :HEAD] for t in both]
        value = [t[0:128, HEAD:] for t in both]
        for which, piece in enumerate((query, key, value)):
            here = pl.ds(pl.multiple_of(which * 1024 + i * 128, 128), 128)
            tok_ref[:, here] = jnp.concatenate(piece, axis=1)
        return carry

    lax.fori_loop(0, 8, unpack, 0)
    pooled = [
        qkv.pool(1 + which, tok_ref.at[:, pl.ds(which * 1024, 1024)]) for which in range(3)
    ]
    ff_reduce(4)
    for near, far in pooled:
        near.wait()
        far.wait_recv()
    loads[0].wait()
    for at in range(len(QKV_DOTS)):
        qkv.multiply(at)
    project_back(tok_ref, weight_ref, weight, weight_sem, grad_ref, back_out)
    ff_reduce(5)
    ff_gather(4)
    ff_gather(3)
    qkv_reduce(0)
    ff_gather(2)
    qkv_reduce(1)
    ff_gather(1)
    qkv_reduce(2)
    qkv_reduce(3)
    qkv_gather(2)
    qkv_gather(1)
    ff_gather(0)
    qkv_gather(0)
    ff.finish()
    qkv.finish()
    for copy in sent:
        copy.wait_send()


FF_DOTS = tuple(
    [(0, 512, 0, 3, j * 512) for j in range(4)]
    + [(1, 2048, q * 512, 4, 0) for q in range(4)]
    + [(2, 512, 0, 5, 0)]
)
FF_WIDTHS = (1024, 896, 896, 896, 896)
QKV_DOTS = ((0, 512, 0, 1, 0), (0, 512, 0, 2, 0), (0, 512, 0, 3, 0))
QKV_WIDTH = 512


def reducer_scratch(widths):
    total, parts = (sum(widths), len(widths))
    bf16, dma = (jnp.bfloat16, pltpu.SemaphoreType.DMA)
    return [
        pltpu.VMEM((2, ROWS, total), bf16),
        *[pltpu.VMEM((2, ROWS >> (k + 1), total), bf16) for k in range(5)],
        pltpu.VMEM((16, total), bf16),
        pltpu.VMEM((16, total), bf16),
        dma((8,)),
        dma((8,)),
        dma((parts, 6)),
        dma((parts, 6)),
        dma((parts, 7)),
        dma((parts, 7)),
        dma((8 + parts,)),
    ]


def back(acts, norm_sums, staged, grad_one, full_qkv, attention):
    bf16, f32, dma = (jnp.bfloat16, jnp.float32, pltpu.SemaphoreType.DMA)
    whole, anywhere = (pl.BlockSpec(memory_space=pltpu.VMEM), pl.BlockSpec(memory_space=pl.ANY))
    ff_total, qkv_total = (sum(FF_WIDTHS), 3 * QKV_WIDTH)
    held = pltpu.VMEM((7, 2, 8, 512), f32)
    return pl.pallas_call(
        back_kernel,
        out_shape=[
            jax.ShapeDtypeStruct((2, ROWS, ff_total), bf16),
            jax.ShapeDtypeStruct((2, ROWS, qkv_total), bf16),
            jax.ShapeDtypeStruct((8, 512), f32),
            jax.ShapeDtypeStruct((128, 1024), bf16),
        ],
        in_specs=[anywhere] * 7 + [whole] * 3 + [anywhere] * 7,
        out_specs=[anywhere] * 2 + [whole] * 2,
        scratch_shapes=[
            *[pltpu.VMEM(a.shape, a.dtype) for a in (*acts, *attention)],
            dma((13,)),
            *[pltpu.VMEM((256, 512), bf16)] * 3,
            *reducer_scratch(FF_WIDTHS),
            *ring_scratch(QKV_WIDTH),
            held,
            held,
            dma((7,)),
            dma((7,)),
            pltpu.VMEM((16, 64, 128), bf16),
            pltpu.VMEM((16, 192, 128), bf16),
            pltpu.VMEM((16, 192, 128), bf16),
            pltpu.VMEM((128, 3072), bf16),
            pltpu.VMEM((2, 1024, 256), bf16),
            dma((2,)),
            *[dma((16,))] * 4,
            *back_scratch(),
        ],
        compiler_params=pltpu.CompilerParams(
            collective_id=1, has_side_effects=True, vmem_limit_bytes=62 * 2**20
        ),
    )(*acts, norm_sums, staged, grad_one, full_qkv, *attention)


CHUNK = 512


def cast_kernel(ff_ref, qkv_ref, *refs):
    plain, refs = (list(zip(refs[:2], refs[8:10])), refs[2:8] + refs[10:])
    outs, (narrow, wide, in_sem, out_sem, bounce) = (refs[:6], refs[6:])
    grad_in, grad_down, grad_out, *grad_qkv = outs
    chunks = []
    for c in range(2):
        for j in range(9):
            src = ff_ref.at[c, :, pl.ds(j * CHUNK, CHUNK)]
            if j < 4:
                dst = grad_in.at[:, pl.ds((c * 4 + j) * CHUNK, CHUNK)]
            elif j < 8:
                dst = grad_down.at[pl.ds((j - 4) * ROWS, ROWS), pl.ds(c * CHUNK, CHUNK)]
            else:
                dst = grad_out.at[:, pl.ds(c * CHUNK, CHUNK)]
            chunks.append((src, dst))
        for j in range(3):
            src = qkv_ref.at[c, :, pl.ds(j * CHUNK, CHUNK)]
            chunks.append((src, grad_qkv[j].at[:, pl.ds(c * CHUNK, CHUNK)]))
    loads = [
        pltpu.make_async_copy(src, narrow.at[n], in_sem.at[n]) for n, (src, _) in enumerate(chunks)
    ]
    stores = [
        pltpu.make_async_copy(wide.at[n], dst, out_sem.at[n]) for n, (_, dst) in enumerate(chunks)
    ]
    for load in loads:
        load.start()
    n = len(chunks)
    for i, (src, dst) in enumerate(plain):
        loads.append(pltpu.make_async_copy(src, bounce.at[i], in_sem.at[n + i]))
        loads[-1].start()
        stores.append(pltpu.make_async_copy(bounce.at[i], dst, out_sem.at[n + i]))
    for n in range(len(chunks)):
        loads[n].wait()

        def widen(i, carry):
            here = pl.ds(pl.multiple_of(i * 64, 64), 64)
            wide[n, here] = narrow[n, here].astype(jnp.float32)
            return carry

        lax.fori_loop(0, ROWS // 64, widen, 0)
        stores[n].start()
    for n in range(len(chunks), len(stores)):
        loads[n].wait()
        stores[n].start()
    for store in stores:
        store.wait()


def results(ff_summed, qkv_summed, result, input_grad):
    f32 = jnp.float32
    anywhere = pl.BlockSpec(memory_space=pl.ANY)
    square = jax.ShapeDtypeStruct((ROWS, 1024), f32)
    return pl.pallas_call(
        cast_kernel,
        out_shape=[
            jax.ShapeDtypeStruct((ROWS, 4096), f32),
            jax.ShapeDtypeStruct((2048, 1024), f32),
            square,
            square,
            square,
            square,
            jax.ShapeDtypeStruct(result.shape, result.dtype),
            jax.ShapeDtypeStruct(input_grad.shape, input_grad.dtype),
        ],
        in_specs=[anywhere] * 4,
        out_specs=[anywhere] * 8,
        scratch_shapes=[
            pltpu.VMEM((24, ROWS, CHUNK), jnp.bfloat16),
            pltpu.VMEM((24, ROWS, CHUNK), f32),
            pltpu.SemaphoreType.DMA((26,)),
            pltpu.SemaphoreType.DMA((26,)),
            pltpu.VMEM((2, *result.shape), result.dtype),
        ],
        compiler_params=pltpu.CompilerParams(vmem_limit_bytes=56 * 2**20),
    )(ff_summed, qkv_summed, result, input_grad)


def shards(
    tokens,
    segments,
    valid,
    w_query,
    w_key,
    w_value,
    w_out,
    norm1_gain,
    norm1_bias,
    w_in,
    w_down,
    norm2_gain,
    norm2_bias,
    cotangent,
):
    packed = jnp.concatenate([norm1_gain, norm1_bias, norm2_gain, norm2_bias]).reshape(16, 128)
    token_rows = tokens[0]
    (
        full_qkv,
        queries,
        pairs,
        summed,
        lse,
        low,
        end,
        tokens_all,
        first_low,
        hidden,
        mixed,
        pre_grad,
        ff_grad,
        attn_grad,
        staged,
        norm_sums,
        grad_one,
        result,
    ) = front(
        token_rows,
        [w_query, w_key, w_value, w_out, w_in, w_down],
        packed,
        cotangent[0],
        segments[0],
        valid[0],
    )
    ff_summed, qkv_summed, norm_total, input_grad = back(
        [tokens_all, first_low, hidden, mixed, pre_grad, ff_grad, attn_grad],
        norm_sums,
        staged,
        grad_one,
        full_qkv,
        [queries, pairs, low, end, lse, summed],
    )
    grad_in, grad_down, grad_out, *grad_qkv, result, input_grad = results(
        ff_summed, qkv_summed, result, input_grad
    )
    return (
        result[None],
        input_grad[None],
        *grad_qkv,
        grad_out,
        norm_total[0],
        norm_total[1],
        grad_in,
        grad_down,
        norm_total[2],
        norm_total[3],
    )


def solution(mesh):
    return jax.shard_map(
        shards,
        mesh=mesh,
        in_specs=(
            P("shard", ("blk", "aa"), None),
            P("shard", None),
            P("shard", None),
            P("shard", None),
            P("shard", None),
            P("shard", None),
            P("shard", None),
            P("shard"),
            P("shard"),
            P("shard", None),
            P("shard", None),
            P("shard"),
            P("shard"),
            P("shard", ("blk", "aa"), None),
        ),
        out_specs=(
            P("shard", ("blk", "aa"), None),
            P("shard", ("blk", "aa"), None),
            P("shard", None),
            P("shard", None),
            P("shard", None),
            P("shard", None),
            P("shard"),
            P("shard"),
            P("shard", None),
            P("shard", None),
            P("shard"),
            P("shard"),
        ),
        check_vma=False,
    )
```

```python
import functools
import math

import jax
import jax.numpy as jnp
from jax import lax
from jax.experimental import pallas as pl
from jax.experimental.pallas import tpu as pltpu
from jax.sharding import PartitionSpec as P

HEADS = 16
HEAD = 64
MASKED_SCORE = -1e30
NORM_EPSILON = 1e-05
BLOCK_LEN = 2048


MESH = pl.DeviceIdType.MESH
ROWS = 512
REDUCE_DIMS = ("xa", "ya", "za", "yb", "zb")
GATHER_DIMS = ("ya", "za", "yb", "zb")


def place():
    shard = lax.axis_index("shard")
    blk = lax.axis_index("blk")
    aa = lax.axis_index("aa")
    return (shard, blk // 2, blk % 2, aa // 4, aa % 4)


def flipped(i):
    return i + 1 - 2 * (i % 2)


def partner(dim):
    shard, x_lo, core, z, y = place()
    if dim == "core":
        core = 1 - core
    elif dim == "xa":
        x_lo = 1 - x_lo
    elif dim == "xb":
        shard, x_lo = 1 - shard, 1 - x_lo
    elif dim == "ya":
        y = flipped(y)
    elif dim == "yb":
        y = 3 - y
    elif dim == "za":
        z = flipped(z)
    else:
        z = 3 - z
    return (shard, x_lo * 2 + core, z * 4 + y)


def ring_bit(dim):
    shard, x_lo, _, z, y = place()
    if dim == "xa":
        return (shard * 2 + x_lo + shard) % 2
    if dim == "ya":
        return (y + y // 2) % 2
    if dim == "yb":
        return y // 2
    if dim == "za":
        return (z + z // 2) % 2
    return z // 2


def remote(src, dst, send_sem, recv_sem, dim):
    return pltpu.make_async_remote_copy(
        src_ref=src,
        dst_ref=dst,
        send_sem=send_sem,
        recv_sem=recv_sem,
        device_id=partner(dim),
        device_id_type=MESH,
    )


def row_starts(dims, rows):
    starts, at, size = ([0], 0, rows)
    for dim in dims:
        size //= 2
        at = at + ring_bit(dim) * size
        starts.append(at)
    return starts


def rotated(dims, by):
    return dims[by:] + dims[:by]


DIRECT = ((4, 0), (5, 1), (4, 2), (5, 3))


class Gather:
    def __init__(self, sources, places, send, recv, start):
        self.sources, self.places = (sources, places)
        self.send, self.recv, self.start = (send, recv, start)
        self.shard, _, self.core, _, _ = place()
        self.orders = [rotated(GATHER_DIMS, part) for part in range(4)]
        self.moving, self.siblings = ({}, [])

    def columns(self, i, part, off):
        cols = self.sources[i].shape[1]
        col = pl.multiple_of(self.core * (cols // 2) + (off + part * (cols // 8)), 128)
        return pl.ds(col, cols // 8)

    def block(self, i, part, shard, at, size):
        target, off = self.places[i]
        rows = self.sources[i].shape[0]
        at = pl.multiple_of(shard * rows + at, 16)
        return target.at[pl.ds(at, size), self.columns(i, part, off)]

    def own(self, i):
        target, off = self.places[i]
        rows, cols = self.sources[i].shape
        return target.at[pl.ds(pl.multiple_of(self.shard * rows, rows), rows), pl.ds(off, cols)]

    def begin_direct(self):
        for i, part in DIRECT:
            rows = self.sources[i].shape[0]
            self.moving[i, part] = self.start(
                remote(
                    self.sources[i].at[:, self.columns(i, part, 0)],
                    self.block(i, part, self.shard, 0, rows),
                    self.send.at[i, part, 0],
                    self.recv.at[i, part, 0],
                    "xb",
                )
            )

    def finish_direct(self):
        for i, part in DIRECT:
            self.moving[i, part].wait_recv()
            mine = self.block(i, part, 1 - self.shard, 0, self.sources[i].shape[0])
            sems = (self.send.at[i, part, 5], self.recv.at[i, part, 5])
            self.siblings.append(self.start(remote(mine, mine, *sems, "core")))

    def parts(self, i):
        return [part for part in range(4) if (i, part) not in DIRECT]

    def begin(self, i):
        rows = self.sources[i].shape[0]
        for part in self.parts(i):
            at = row_starts(self.orders[part], rows)[4]
            mine = pl.ds(pl.multiple_of(at, 16), rows // 16)
            self.moving[i, part] = self.start(
                remote(
                    self.sources[i].at[mine, self.columns(i, part, 0)],
                    self.block(i, part, self.shard, at, rows // 16),
                    self.send.at[i, part, 0],
                    self.recv.at[i, part, 0],
                    "xb",
                )
            )

    def stage(self, i, stage):
        rows = self.sources[i].shape[0]
        for part in self.parts(i):
            self.moving[i, part].wait_recv()
            starts = row_starts(self.orders[part], rows)
            if stage < 5:
                k = 4 - stage
                mine = self.block(i, part, 1 - self.shard, starts[k + 1], rows >> (k + 1))
                self.moving[i, part] = self.start(
                    remote(
                        mine,
                        mine,
                        self.send.at[i, part, stage],
                        self.recv.at[i, part, stage],
                        self.orders[part][k],
                    )
                )
            if stage >= 4:
                at = starts[1] if stage == 4 else rows // 2 - starts[1]
                mine = self.block(i, part, 1 - self.shard, at, rows // 2)
                self.siblings.append(
                    self.start(
                        remote(
                            mine,
                            mine,
                            self.send.at[i, part, stage + 1],
                            self.recv.at[i, part, stage + 1],
                            "core",
                        )
                    )
                )

    def finish(self):
        for copy in self.siblings:
            copy.wait_recv()
        self.siblings = []


def plane_peer(step):
    shard, x_lo, core, z, y = place()
    return (shard, x_lo * 2 + core, (z * 4 + y + step) % 16)


class Exchange:
    def __init__(self, outgoing, incoming, send, recv, start):
        self.outgoing, self.incoming = (outgoing, incoming)
        self.send, self.recv, self.start = (send, recv, start)
        self.copies = []

    def begin(self):
        me = lax.axis_index("aa")
        for step in (1, 3, 4, 12, 15, 13, 5, 11, 2, 8, 14, 6, 10, 7, 9):
            self.copies.append(
                self.start(
                    pltpu.make_async_remote_copy(
                        src_ref=self.outgoing.at[(me + step) % 16],
                        dst_ref=self.incoming.at[me],
                        send_sem=self.send.at[step],
                        recv_sem=self.recv.at[step],
                        device_id=plane_peer(step),
                        device_id_type=MESH,
                    )
                )
            )
        self.incoming[me] = self.outgoing[me]

    def finish(self):
        for copy in self.copies:
            copy.wait_recv()


def greet_all(dims):
    barrier = pltpu.get_barrier_semaphore()
    for dim in dims:
        pl.semaphore_signal(barrier, inc=1, device_id=partner(dim), device_id_type=MESH)
    for step in range(1, 16):
        pl.semaphore_signal(barrier, inc=1, device_id=plane_peer(step), device_id_type=MESH)
    pl.semaphore_wait(barrier, len(dims) + 15)


def unfolded(block, side):
    lane = lax.broadcasted_iota(jnp.int32, (64, 128), 1)
    keep = (lane >= HEAD) if side else (lane < HEAD)
    block = block.astype(jnp.float32)
    moved = jnp.concatenate([block[:, HEAD:], block[:, :HEAD]], axis=1)
    first, second = (moved, block) if side else (block, moved)
    both = jnp.concatenate([jnp.where(keep, first, 0.0), jnp.where(keep, second, 0.0)], axis=0)
    return both.astype(jnp.bfloat16)


LEAST = -(2**31)
FRONT_BLOCK = 512
TOKENS_AT = 1


def visible(place_k, low, end, start):
    size = jnp.maximum(end - low, 0) + LEAST
    return (place_k - (low - start - LEAST)) < size


def query_spans(segments_ref, valid_ref, low_ref, end_ref):
    _, x_lo, core, _, _ = place()
    segments = segments_ref[...]
    start = pl.multiple_of((x_lo * 2 + core) * 16, 16)
    mine = segments_ref[pl.ds(start, 16)]
    low, end = (jnp.zeros_like(mine), jnp.zeros_like(mine))
    before = jnp.zeros((1, 1), jnp.int32)
    for number in range(35):
        same = jnp.where(segments == number, 1, 0)
        count = jnp.sum(jnp.sum(same, axis=1, keepdims=True), axis=0, keepdims=True)
        picked = mine == number
        low = jnp.where(picked, before, low)
        before = before + count
        end = jnp.where(picked, before, end)
    live = jnp.sum(jnp.sum(valid_ref[...], axis=1, keepdims=True), axis=0, keepdims=True)
    end = jnp.minimum(end, live)
    for row in range(16):
        here = pl.ds(row * 128, 128)
        low_ref[:, here] = jnp.broadcast_to(low[row : row + 1], (8, 128))
        end_ref[:, here] = jnp.broadcast_to(end[row : row + 1], (8, 128))


def normalized(values):
    centred = values - jnp.mean(values, axis=1, keepdims=True)
    inverse = lax.rsqrt(jnp.mean(centred * centred, axis=1, keepdims=True) + NORM_EPSILON)
    return (centred * inverse, inverse)


def normalized_back(upstream, scaled, inverse, gain):
    weighted = upstream * gain
    centred = weighted - jnp.mean(weighted, axis=1, keepdims=True)
    return inverse * (centred - scaled * jnp.mean(weighted * scaled, axis=1, keepdims=True))


def summed_rows(values):
    return jnp.sum(values, axis=0, keepdims=True)


def dense(x_ref, cot_ref, mixed_in, norm_in, weights, scratch, outs, give):
    w_out, w_in, w_down = weights
    slope, low_ref, hidden_ref, mixed_ref, pre_ref, down_ref, attn_ref = scratch
    staged_ref, sums_ref, grad_ref, result_ref = outs
    f32, bf16 = (jnp.float32, jnp.bfloat16)
    gain_one, bias_one, gain_two, bias_two = [
        jnp.concatenate(
            [norm_in[half, i * 4 + j : i * 4 + j + 1] for half in range(2) for j in range(4)], axis=1
        ).astype(f32)
        for i in range(4)
    ]
    for pair in range(8):
        both = [mixed_in[pair * 2], mixed_in[pair * 2 + 1]]
        both = [jnp.concatenate([t[:, :HEAD], t[:, HEAD:]], axis=0) for t in both]
        mixed_ref[:, pair * 128 : (pair + 1) * 128] = jnp.concatenate(both, axis=1)
    give(3)
    attn = jnp.dot(mixed_ref[...], w_out[...], preferred_element_type=f32)
    scaled_one, inverse_one = normalized(x_ref[...].astype(f32) + attn)
    first = scaled_one * gain_one + bias_one
    low_ref[...] = first.astype(bf16)
    give(1)

    def up(c, total):
        here = pl.ds(pl.multiple_of(c * 1024, 1024), 1024)
        pre = jnp.dot(low_ref[...], w_in[:, here], preferred_element_type=f32)
        share = 0.5 + 0.5 * lax.erf(pre * 0.5**0.5)
        hidden = (pre * share).astype(bf16)
        hidden_ref[:, here] = hidden
        slope[:, here] = share + pre * jnp.exp(pre * pre * -0.5) * (2 * math.pi) ** -0.5
        return total + jnp.dot(hidden, w_down[here], preferred_element_type=f32)

    ff_out = lax.fori_loop(0, 4, up, jnp.zeros((128, 1024), f32), unroll=2)
    give(2)
    scaled_two, inverse_two = normalized(first + ff_out)
    result_ref[...] = (scaled_two * gain_two + bias_two).astype(bf16)
    upstream = cot_ref[...].astype(f32)
    grad_two = normalized_back(upstream, scaled_two, inverse_two, gain_two)
    down_ref[...] = grad_two.astype(bf16)
    give(5)

    def down(c, total):
        here = pl.ds(pl.multiple_of(c * 1024, 1024), 1024)
        grad = lax.dot_general(
            down_ref[...], w_down[here], (((1,), (1,)), ((), ())), preferred_element_type=f32
        )
        grad = (grad * slope[:, here]).astype(bf16)
        pre_ref[:, here] = grad
        return total + lax.dot_general(
            grad, w_in[:, here], (((1,), (1,)), ((), ())), preferred_element_type=f32
        )

    first_grad = lax.fori_loop(0, 4, down, grad_two, unroll=2)
    give(4)
    grad_one = normalized_back(first_grad, scaled_one, inverse_one, gain_one)
    grad_ref[...] = grad_one
    attn_ref[...] = grad_one.astype(bf16)
    give(6)
    mixed_grad = lax.dot_general(
        attn_ref[...], w_out[...], (((1,), (1,)), ((), ())), preferred_element_type=f32
    ).astype(bf16)
    for head in range(HEADS):
        part = mixed_grad[:, head * HEAD : (head + 1) * HEAD]
        staged_ref[head] = jnp.concatenate([part[0:64], part[64:128]], axis=1)
    sums = [
        summed_rows(first_grad * scaled_one),
        summed_rows(first_grad),
        summed_rows(upstream * scaled_two),
        summed_rows(upstream),
    ]
    for half in range(2):
        cols = slice(half * 512, (half + 1) * 512)
        sums_ref[half] = jnp.concatenate([v[:, cols] for v in sums] + [jnp.zeros((4, 512), f32)])


def front_kernel(
    x_ref,
    wq_ref,
    wk_ref,
    wv_ref,
    wo_ref,
    wi_ref,
    wd_ref,
    norm_ref,
    cot_ref,
    segments_ref,
    valid_ref,
    qkv_out,
    q_out,
    pairs_out,
    o_out,
    lse_out,
    low_ref,
    end_ref,
    *refs,
):
    dense_out, refs = (refs[:11], refs[11:])
    front_body(
        x_ref,
        (wq_ref, wk_ref, wv_ref, wo_ref, wi_ref, wd_ref),
        norm_ref,
        cot_ref,
        (segments_ref, valid_ref),
        qkv_out,
        (q_out, pairs_out, o_out, lse_out, low_ref, end_ref),
        dense_out,
        *refs,
    )


def front_body(
    x_ref,
    weights,
    norm_ref,
    cot_ref,
    documents,
    qkv_out,
    attention_out,
    dense_out,
    wqkv,
    w_out,
    w_in,
    w_down,
    norm_in,
    mixed_in,
    slope,
    pre_full,
    down_full,
    attn_full,
    low_full,
    hidden_full,
    mixed_full,
    pool_send,
    pool_recv,
    pool_own,
    save_sem,
    q_held,
    pairs_held,
    o_held,
    lse_held,
    low_held,
    end_held,
    staged,
    heads_in,
    folded,
    pairs_t,
    top_s,
    send,
    recv,
    own_in,
    own_out,
    hop_send,
    hop_recv,
    swap_send,
    swap_recv,
    back_send,
    back_recv,
    tok_send,
    tok_recv,
    tok_own,
):
    shard, _, _, z, y = place()
    attention_held = (q_held, pairs_held, o_held, lse_held, low_held, end_held)
    q_out, pairs_out, o_out, lse_out, low_ref, end_ref = attention_held
    saves = []

    def save(i):
        copy = pltpu.make_async_copy(attention_held[i], attention_out[i], save_sem.at[i])
        copy.start()
        saves.append(copy)

    sent = []

    def start(copy):
        copy.start()
        sent.append(copy)
        return copy

    gather = Gather(
        weights,
        [(wqkv, 0), (wqkv, 1024), (wqkv, 2048), (w_out, 0), (w_in, 0), (w_down, 0)],
        send,
        recv,
        start,
    )
    inward = []
    for i in range(6):
        inward.append(pltpu.make_async_copy(weights[i], gather.own(i), own_in.at[i]))
        inward[i].start()
    greet_all(("core", "xa", "xb"))
    norms = start(
        remote(norm_ref, norm_in.at[shard], hop_send.at[3], hop_recv.at[3], "xb")
    )
    norm_in[shard] = norm_ref[...]
    for i in range(6):
        gather.begin(i)
    _, _, core, _, _ = place()
    pooled = []

    def give(i):
        src = (x_ref, low_full, hidden_full, mixed_full, pre_full, down_full, attn_full)[i]
        mine, theirs = (src, src)
        if i > 3:
            half = src.shape[1] // 2
            mine, theirs = [
                src.at[:, pl.ds(pl.multiple_of(c * half, half), half)] for c in (core, 1 - core)
            ]
        copy = pltpu.make_async_copy(mine, dense_out[i].at[pl.ds(0, 128)], pool_own.at[i])
        copy.start()
        saves.append(copy)
        sems = (pool_send.at[i], pool_recv.at[i])
        pooled.append(start(remote(theirs, dense_out[i].at[pl.ds(128, 128)], *sems, "core")))

    for i in range(3):
        gather.stage(i, 1)
    for stage in range(2, 6):
        for i in range(3):
            gather.stage(i, stage)
        if stage == 3:
            for i in range(3, 6):
                gather.stage(i, 1)
            gather.begin_direct()
    for i in range(3):
        inward[i].wait()
    gather.finish()
    keep = pltpu.make_async_copy(wqkv, qkv_out, own_out.at[0])
    keep.start()

    def project(piece, carry):
        q, k, v = [
            jnp.dot(
                x_ref[...],
                wqkv[:, pl.ds(pl.multiple_of(which * 1024 + piece * 256, 256), 256)],
                preferred_element_type=jnp.float32,
            )
            for which in range(3)
        ]
        q = (q.astype(jnp.bfloat16).astype(jnp.float32) * HEAD ** (-0.5)).astype(jnp.bfloat16)
        k, v = (k.astype(jnp.bfloat16), v.astype(jnp.bfloat16))
        for h in range(4):
            at = slice(h * HEAD, (h + 1) * HEAD)
            staged[piece * 4 + h, 0:128] = jnp.concatenate([k[:, at], v[:, at]], axis=1)
            staged[piece * 4 + h, 128:192] = jnp.concatenate([q[0:64, at], q[64:128, at]], axis=1)
        return carry

    lax.fori_loop(0, 4, project, 0)
    heads = Exchange(staged, heads_in, swap_send, swap_recv, start)
    heads.begin()
    for i in range(3, 6):
        gather.stage(i, 2)
    query_spans(*documents, low_ref, end_ref)
    heads.finish()

    def spread(c, carry):
        here = pl.ds(pl.multiple_of(c * 128, 128), 128)
        pairs_out[here] = heads_in[c, 0:128]
        q_out[here] = unfolded(heads_in[c, 128:192], 0)
        return carry

    lax.fori_loop(0, 16, spread, 0)

    def slot_rows(slot):
        return pairs_out.at[pl.ds(slot * BLOCK_LEN, BLOCK_LEN)]

    def hop(index, source, target, dim):
        return start(
            remote(
                slot_rows(source), slot_rows(target), hop_send.at[index], hop_recv.at[index], dim
            )
        )

    hops = {1: hop(0, 0, 1, "core"), 2: hop(1, 0, 2, "xa")}
    columns = [(slice(None), pl.ds(half * 512, 512)) for half in range(2)]
    lines = Lines(dense_out[0], columns, tok_send, tok_recv, start)
    lines.scatter(0, [x_ref.at[cols] for cols in columns])
    own_tokens = pltpu.make_async_copy(x_ref, dense_out[0].at[z, y], tok_own.at[0])
    own_tokens.start()
    for i in (0, 4, 5):
        save(i)
    top_s[...] = jnp.full_like(top_s, MASKED_SCORE)
    o_out[...] = jnp.zeros_like(o_out)
    first_row = lax.broadcasted_iota(jnp.int32, (128, 512), 0) == 0

    def turn(c, carry):
        here = pl.ds(pl.multiple_of(c * 512, 512), 512)
        turned = jnp.transpose(pairs_out[here].astype(jnp.float32))
        pairs_t[:, here] = jnp.where(first_row, 1.0, turned).astype(jnp.bfloat16)
        return carry

    def slot_step(slot, block):
        _, x_lo, core, _, _ = place()
        owner = (slot // 2 + x_lo) % 2 * 2 + (slot % 2 + core) % 2
        rows = pl.ds(slot * BLOCK_LEN, BLOCK_LEN)
        mine = pl.ds(pl.multiple_of(block * FRONT_BLOCK, FRONT_BLOCK), FRONT_BLOCK)
        scores = lax.dot_general(
            pairs_out[rows],
            q_out[mine],
            (((1,), (1,)), ((), ())),
            preferred_element_type=jnp.float32,
        )
        place_k = lax.broadcasted_iota(jnp.int32, scores.shape, 0)
        allowed = visible(place_k, low_ref[0:1, mine], end_ref[0:1, mine], owner * BLOCK_LEN)
        if slot == 0:
            place_q = lax.broadcasted_iota(jnp.int32, (1, FRONT_BLOCK), 1) + block * FRONT_BLOCK
            allowed = allowed | (place_k == place_q)
        scores = jnp.where(allowed, scores, MASKED_SCORE)
        top = top_s[0:1, mine]
        new_top = jnp.maximum(top, jnp.max(scores, axis=0, keepdims=True))
        weights = jnp.exp(scores - new_top)
        factor = jnp.exp(top - new_top)
        o_out[:, mine] = o_out[:, mine] * factor + jnp.dot(
            pairs_t[:, rows], weights.astype(jnp.bfloat16), preferred_element_type=jnp.float32
        )
        top_s[:, mine] = jnp.broadcast_to(new_top, (8, FRONT_BLOCK))

    events = {
        0: [(i, 3) for i in (3, 4, 5)],
        1: [(i, 4) for i in (3, 4, 5)],
        3: [(i, 5) for i in (3, 4, 5)],
    }
    for slot in range(4):
        if slot:
            hops[slot].wait_recv()
        if slot == 2:
            hops[3] = hop(2, 2, 3, "core")
        if slot == 3:
            save(1)
        lax.fori_loop(slot * 4, slot * 4 + 4, turn, 0)
        for half in range(2):

            def blocks(b, carry):
                slot_step(slot, b)
                return carry

            lax.fori_loop(half * 2, half * 2 + 2, blocks, 0)
            if half == 0:
                for i, stage in events.get(slot, ()):
                    gather.stage(i, stage)
                if slot == 3:
                    gather.finish_direct()
                if slot == TOKENS_AT:
                    own_tokens.wait()
                    lines.arrive()
                    lines.scatter(1, [lines.line(half) for half in range(2)])

    def close(c, carry):
        here = pl.ds(pl.multiple_of(c * 128, 128), 128)
        total = o_out[0:1, here]
        mixed = o_out[:, here] / total
        o_out[:, here] = mixed
        lse = top_s[0:1, here] + jnp.log(total)
        lse_out[:, here] = jnp.broadcast_to(lse, (8, 128))
        block = jnp.transpose(mixed)
        both = jnp.concatenate([block[0:64, HEAD:], block[64:128, HEAD:]], axis=1)
        folded[c] = both.astype(jnp.bfloat16)
        return carry

    lax.fori_loop(0, 16, close, 0)
    back = Exchange(folded, mixed_in, back_send, back_recv, start)
    back.begin()
    save(2)
    save(3)
    gather.finish()
    norms.wait_recv()
    for i in range(3, 6):
        inward[i].wait()
    back.finish()
    dense(
        x_ref,
        cot_ref,
        mixed_in,
        norm_in,
        (w_out, w_in, w_down),
        (slope, low_full, hidden_full, mixed_full, pre_full, down_full, attn_full),
        dense_out[7:],
        give,
    )
    lines.arrive()
    for copy in pooled:
        copy.wait_recv()
    for copy in saves:
        copy.wait()
    keep.wait()
    for copy in sent:
        copy.wait_send()


def front(token_rows, weights, packed, cotangent, segments, valid):
    bf16, f32, i32, dma = (jnp.bfloat16, jnp.float32, jnp.int32, pltpu.SemaphoreType.DMA)
    n, shape = (len(weights), jax.ShapeDtypeStruct)
    whole, anywhere = (pl.BlockSpec(memory_space=pltpu.VMEM), pl.BlockSpec(memory_space=pl.ANY))
    return pl.pallas_call(
        front_kernel,
        out_shape=[
            shape((1024, 3072), bf16),
            shape((BLOCK_LEN, 128), bf16),
            shape((4 * BLOCK_LEN, 128), bf16),
            shape((128, BLOCK_LEN), f32),
            shape((8, BLOCK_LEN), f32),
            shape((8, BLOCK_LEN), i32),
            shape((8, BLOCK_LEN), i32),
            shape((4, 4, 128, 1024), bf16),
            *[shape((256, width), bf16) for width in (1024, 4096, 1024, 2048, 512, 512)],
            shape((HEADS, 64, 128), bf16),
            shape((2, 8, 512), f32),
            shape((128, 1024), f32),
            shape((128, 1024), bf16),
        ],
        in_specs=[whole] + [anywhere] * n + [whole] * 4,
        out_specs=[anywhere] * 14 + [whole] * 4,
        scratch_shapes=[
            pltpu.VMEM((1024, 3072), bf16),
            pltpu.VMEM((1024, 1024), bf16),
            pltpu.VMEM((1024, 4096), bf16),
            pltpu.VMEM((4096, 1024), bf16),
            pltpu.VMEM((2, 16, 128), bf16),
            pltpu.VMEM((16, 64, 128), bf16),
            pltpu.VMEM((128, 4096), f32),
            pltpu.VMEM((128, 4096), bf16),
            pltpu.VMEM((128, 1024), bf16),
            pltpu.VMEM((128, 1024), bf16),
            pltpu.VMEM((128, 1024), bf16),
            pltpu.VMEM((128, 4096), bf16),
            pltpu.VMEM((128, 1024), bf16),
            dma((7,)),
            dma((7,)),
            dma((7,)),
            dma((6,)),
            pltpu.VMEM((BLOCK_LEN, 128), bf16),
            pltpu.VMEM((4 * BLOCK_LEN, 128), bf16),
            pltpu.VMEM((128, BLOCK_LEN), f32),
            pltpu.VMEM((8, BLOCK_LEN), f32),
            pltpu.VMEM((8, BLOCK_LEN), i32),
            pltpu.VMEM((8, BLOCK_LEN), i32),
            pltpu.VMEM((16, 192, 128), bf16),
            pltpu.VMEM((16, 192, 128), bf16),
            pltpu.VMEM((16, 64, 128), bf16),
            pltpu.VMEM((128, 4 * BLOCK_LEN), bf16),
            pltpu.VMEM((8, BLOCK_LEN), f32),
            dma((n, 4, 7)),
            dma((n, 4, 7)),
            dma((n,)),
            dma((1,)),
            dma((4,)),
            dma((4,)),
            *[dma((16,))] * 4,
            dma((2, 2, 4)),
            dma((2, 2, 4)),
            dma((1,)),
        ],
        compiler_params=pltpu.CompilerParams(
            collective_id=0, has_side_effects=True, vmem_limit_bytes=62 * 2**20
        ),
    )(
        token_rows,
        *weights,
        packed,
        cotangent,
        segments.reshape(64, 128),
        valid.reshape(64, 128),
    )


BACK_REDUCE = (7, 12)
SLOT_UNITS = 4
BACK_BLOCK = 512


def back_scratch():
    return [
        pltpu.VMEM((BLOCK_LEN, 128), jnp.bfloat16),
        pltpu.VMEM((HEAD, 4 * BLOCK_LEN), jnp.bfloat16),
        pltpu.VMEM((8, BLOCK_LEN), jnp.float32),
        pltpu.VMEM((HEAD, BLOCK_LEN), jnp.float32),
        pltpu.VMEM((4 * BLOCK_LEN, 128), jnp.float32),
        pltpu.VMEM((3, BLOCK_LEN, 128), jnp.bfloat16),
        pltpu.VMEM((3, BLOCK_LEN, 128), jnp.bfloat16),
        pltpu.SemaphoreType.DMA((3,)),
        pltpu.SemaphoreType.DMA((3,)),
        pltpu.VMEM((192, BLOCK_LEN), jnp.bfloat16),
    ]


class AttendBack:
    def __init__(self, ins, out, scratch, start):
        self.q, self.packed, self.pairs, self.low, self.end, self.lse, self.o_t = ins
        self.out = out
        self.g, self.pairs_t, self.delta, self.dq, self.dkv = scratch[:5]
        self.away, self.landed, self.send, self.recv, self.grads_t = scratch[5:10]
        self.start = start
        self.copies = {}
        self.events = [
            (0, self.begin),
            (SLOT_UNITS, lambda: self.give(3, 0, None, "core")),
            (2 * SLOT_UNITS + 1, lambda: self.give(2, 1, 0, "xa")),
            (3 * SLOT_UNITS, lambda: self.give(1, 2, None, "core")),
        ]

    def begin(self):
        self.delta[...] = jnp.zeros_like(self.delta)
        self.dq[...] = jnp.zeros_like(self.dq)
        self.dkv[...] = jnp.zeros_like(self.dkv)

        def chunk(c, carry):
            both = unfolded(self.packed[c], 1)
            here = pl.ds(pl.multiple_of(c * 128, 128), 128)
            self.g[here] = both
            products = jnp.transpose(both.astype(jnp.float32)) * self.o_t[:, here]
            total = jnp.sum(products, axis=0, keepdims=True)
            self.delta[:, here] = jnp.broadcast_to(total, (8, 128))
            return carry

        lax.fori_loop(0, 16, chunk, 0)

        def turn(c, carry):
            here = pl.ds(pl.multiple_of(c * 512, 512), 512)
            self.pairs_t[:, here] = jnp.transpose(self.pairs[here])[0:HEAD]
            return carry

        lax.fori_loop(0, 16, turn, 0)

    def run(self, first, last):
        edge = 3 * SLOT_UNITS
        if first < edge:
            lax.fori_loop(first, min(last, edge), functools.partial(self.unit, own=False), 0)
        if last > edge:
            lax.fori_loop(max(first, edge), last, functools.partial(self.unit, own=True), 0)

    def unit(self, n, carry, own):
        _, x_lo, core, _, _ = place()
        block = n % 4
        slot = 3 - n // 4
        owner = (slot // 2 + x_lo) % 2 * 2 + (slot % 2 + core) % 2
        key_start = owner * BLOCK_LEN
        here = pl.ds(pl.multiple_of(slot * BLOCK_LEN, BLOCK_LEN), BLOCK_LEN)
        mine = pl.ds(pl.multiple_of(block * BACK_BLOCK, BACK_BLOCK), BACK_BLOCK)
        keys = self.pairs[here]
        queries, upstream = (self.q[mine], self.g[mine])
        scores = lax.dot_general(
            keys, queries, (((1,), (1,)), ((), ())), preferred_element_type=jnp.float32
        )
        place_k = lax.broadcasted_iota(jnp.int32, scores.shape, 0)
        allowed = visible(place_k, self.low[0:1, mine], self.end[0:1, mine], key_start)
        if own:
            place_q = lax.broadcasted_iota(jnp.int32, (1, BACK_BLOCK), 1)
            place_q = place_q + block * BACK_BLOCK
            allowed = allowed | (place_k == place_q)
        scores = jnp.where(allowed, scores, MASKED_SCORE)
        probs = jnp.exp(scores - self.lse[0:1, mine])
        prob_grad = lax.dot_general(
            keys, upstream, (((1,), (1,)), ((), ())), preferred_element_type=jnp.float32
        )
        score_grad = (probs * (prob_grad - self.delta[0:1, mine])).astype(jnp.bfloat16)
        self.dkv[here] += jnp.dot(
            score_grad, queries, preferred_element_type=jnp.float32
        ) + jnp.dot(probs.astype(jnp.bfloat16), upstream, preferred_element_type=jnp.float32)
        self.dq[:, mine] += jnp.dot(
            self.pairs_t[:, here], score_grad, preferred_element_type=jnp.float32
        )
        return carry

    def give(self, slot, index, add, dim):
        if add is not None:
            self.copies[add].wait_recv()

        def chunk(c, carry):
            here = pl.ds(pl.multiple_of(c * 256, 256), 256)
            there = pl.ds(pl.multiple_of(slot * BLOCK_LEN + c * 256, 256), 256)
            total = self.dkv[there]
            if add is not None:
                total = total + self.landed[add, here].astype(jnp.float32)
            self.away[index, here] = total.astype(jnp.bfloat16)
            return carry

        lax.fori_loop(0, BLOCK_LEN // 256, chunk, 0)
        self.copies[index] = self.start(
            remote(
                self.away.at[index],
                self.landed.at[index],
                self.send.at[index],
                self.recv.at[index],
                dim,
            )
        )

    def finish(self):
        self.copies[1].wait_recv()
        self.copies[2].wait_recv()

        def chunk(c, carry):
            here = pl.ds(pl.multiple_of(c * 128, 128), 128)
            total = self.dkv[here] + self.landed[1, here].astype(jnp.float32)
            total = total + self.landed[2, here].astype(jnp.float32)
            self.out[c, 0:128] = total.astype(jnp.bfloat16)
            self.grads_t[HEAD:, here] = jnp.transpose(total).astype(jnp.bfloat16)
            grad = self.dq[:, here] * HEAD ** (-0.5)
            self.grads_t[0:HEAD, here] = grad.astype(jnp.bfloat16)
            grad = jnp.transpose(grad)
            folded = jnp.concatenate([grad[0:64], grad[64:128]], axis=1)
            self.out[c, 128:192] = folded.astype(jnp.bfloat16)
            return carry

        lax.fori_loop(0, 16, chunk, 0)


class Reducer:
    def __init__(self, acts, dots, widths, refs, start):
        self.acts, self.dots, self.start = (acts, dots, start)
        self.partial, self.landed, self.last, self.out = (refs[0], refs[1:7], refs[7], refs[8])
        self.act_send, self.act_recv, self.red_send, self.red_recv = refs[9:13]
        self.gat_send, self.gat_recv, self.own = refs[13:16]
        self.shard, _, self.core, _, _ = place()
        self.parts = range(len(widths))
        self.edges = [sum(widths[:p]) for p in range(len(widths) + 1)]
        self.cols = [pl.ds(self.edges[p], widths[p]) for p in self.parts]
        self.orders = [rotated(REDUCE_DIMS, p) for p in self.parts]
        self.starts = [row_starts(self.orders[p], ROWS) for p in self.parts]
        self.moving, self.held, self.shared = ({}, {}, [])

    def multiply(self, at):
        left, left_step, left_off, right, right_off = self.dots[at]
        for s in range(2):
            product = lax.dot_general(
                self.acts[left][:, pl.ds(s * left_step + left_off, ROWS)],
                self.acts[right][:, pl.ds(right_off, 512)],
                (((0,), (0,)), ((), ())),
                preferred_element_type=jnp.float32,
            )
            self.partial[s, :, pl.ds(at * 512, 512)] = product.astype(jnp.bfloat16)
        for p in self.parts:
            if at * 512 < self.edges[p + 1] <= (at + 1) * 512:
                self.reduce_start(p, 0)

    def reduce_start(self, p, k):
        starts, cols = (self.starts[p], self.cols[p])
        if k < 5:
            half = ROWS >> (k + 1)
            away = pl.multiple_of(starts[k] + (half - (starts[k + 1] - starts[k])), 16)
            src = self.partial.at[:, pl.ds(away, half), cols]
            dst = self.landed[k].at[:, :, cols]
            dim = self.orders[p][k]
        else:
            src = self.partial.at[1 - self.shard, pl.ds(pl.multiple_of(starts[5], 16), 16), cols]
            dst = self.landed[5].at[:, cols]
            dim = "xb"
        self.moving[p] = self.start(
            remote(src, dst, self.red_send.at[p, k], self.red_recv.at[p, k], dim)
        )

    def reduce_step(self, p, k):
        self.moving[p].wait_recv()
        starts, cols = (self.starts[p], self.cols[p])
        if k < 5:
            half = ROWS >> (k + 1)
            step = min(half, 32)

            def add(i, carry):
                here = pl.ds(pl.multiple_of(i * step, step), step)
                there = pl.ds(pl.multiple_of(starts[k + 1] + i * step, 16), step)
                self.partial[:, there, cols] += self.landed[k][:, here, cols]
                return carry

            lax.fori_loop(0, half // step, add, 0)
            self.reduce_start(p, k + 1)
        else:
            here = pl.ds(pl.multiple_of(starts[5], 16), 16)
            self.last[:, cols] = self.partial[self.shard, here, cols] + self.landed[5][:, cols]
            self.held[p] = pltpu.make_async_copy(
                self.last.at[:, cols], self.rows_out(p, starts[5], 16), self.own.at[8 + p]
            )
            self.held[p].start()
            self.gather_start(p, 4)

    def rows_out(self, p, at, size):
        return self.out.at[self.core, pl.ds(pl.multiple_of(at, 16), size), self.cols[p]]

    def gather_start(self, p, k):
        mine = self.rows_out(p, self.starts[p][k + 1], ROWS >> (k + 1))
        src = self.last.at[:, self.cols[p]] if k == 4 else mine
        self.moving[p] = self.start(
            remote(src, mine, self.gat_send.at[p, k], self.gat_recv.at[p, k], self.orders[p][k])
        )

    def gather_step(self, p, k):
        self.moving[p].wait_recv()
        if k == 4:
            self.held[p].wait()
        if k > 0:
            self.gather_start(p, k - 1)
        if k == 1:
            self.share(p, 0, self.starts[p][1])
        if k == 0:
            self.share(p, 1, ROWS // 2 - self.starts[p][1])

    def share(self, p, slot, at):
        mine = self.rows_out(p, at, ROWS // 2)
        sems = (self.gat_send.at[p, 5 + slot], self.gat_recv.at[p, 5 + slot])
        self.shared.append(self.start(remote(mine, mine, *sems, "core")))

    def finish(self):
        for copy in self.shared:
            copy.wait_recv()


def ring_member(dim, step):
    shard, x_lo, core, z, y = place()
    if dim == "y":
        y = (y + step) % 4
    else:
        z = (z + step) % 4
    return (shard, x_lo * 2 + core, z * 4 + y)


def copy_to(device, src, dst, send_sem, recv_sem):
    return pltpu.make_async_remote_copy(
        src_ref=src,
        dst_ref=dst,
        send_sem=send_sem,
        recv_sem=recv_sem,
        device_id=device,
        device_id_type=MESH,
    )


class Lines:
    def __init__(self, blocks, halves, send, recv, start):
        self.blocks, self.halves, self.start = (blocks, halves, start)
        self.send, self.recv = (send, recv)
        _, _, _, self.z, self.y = place()
        self.dims = (("y", "z"), ("z", "y"))

    def one(self, half):
        return self.blocks.at[(self.z, self.y, *self.halves[half])]

    def line(self, half, back=0):
        if half == 0:
            return self.blocks.at[((self.z + 4 - back) % 4, slice(None), *self.halves[0])]
        return self.blocks.at[(slice(None), (self.y + 4 - back) % 4, *self.halves[1])]

    def scatter(self, stage, sources):
        self.moving = []
        for half in range(2):
            dst = self.one(half) if stage == 0 else self.line(half)
            self.moving.append(
                [
                    self.start(
                        copy_to(
                            ring_member(self.dims[half][stage], d),
                            sources[half],
                            dst,
                            self.send.at[half, stage, d],
                            self.recv.at[half, stage, d],
                        )
                    )
                    for d in range(1, 4)
                ]
            )

    def arrive(self):
        for copies in self.moving:
            for copy in copies:
                copy.wait_recv()


class HeadGradients:
    def __init__(self, refs, out, start):
        self.partial, self.half, self.quarter, self.last = refs[:4]
        self.landed, (self.send, self.recv, self.own) = (refs[4:7], refs[7:10])
        self.share_send, self.share_recv = refs[12:14]
        self.out, self.start = (out, start)
        self.shard, _, self.core, self.z, self.y = place()
        self.bit = ring_bit("xa")
        pieces = pl.ds(self.core * 2, 2)
        halves = [(pieces, pl.ds(0, 96)), (pieces, pl.ds(96, 96))]
        self.lines = Lines(out, halves, refs[10], refs[11], start)
        self.shared = []

    def pass_on(self, k, src, dst, dim):
        self.moving = self.start(remote(src, dst, self.send.at[k], self.recv.at[k], dim))

    def multiply(self, grads_t, tokens):
        for s in range(2):
            product = jnp.dot(
                grads_t[...], tokens[:, pl.ds(s * ROWS, ROWS)], preferred_element_type=jnp.float32
            )
            self.partial[s] = product.astype(jnp.bfloat16)
        away = pl.ds(pl.multiple_of((1 - self.core) * 256, 256), 256)
        self.pass_on(0, self.partial.at[:, :, away], self.landed[0], "core")

    def step(self, k):
        self.moving.wait_recv()
        if k == 0:
            mine = pl.ds(pl.multiple_of(self.core * 256, 256), 256)
            self.half[...] = self.partial[:, :, mine] + self.landed[0][...]
            away = pl.ds(pl.multiple_of((1 - self.bit) * 128, 128), 128)
            self.pass_on(1, self.half.at[:, :, away], self.landed[1], "xa")
        elif k == 1:
            mine = pl.ds(pl.multiple_of(self.bit * 128, 128), 128)
            self.quarter[...] = self.half[:, :, mine] + self.landed[1][...]
            self.pass_on(2, self.quarter.at[1 - self.shard], self.landed[2], "xb")
        elif k == 2:
            self.last[...] = self.quarter[self.shard] + self.landed[2][...]
            mine = self.out.at[self.z, self.y, self.core * 2 + self.bit]
            self.held = pltpu.make_async_copy(self.last, mine, self.own.at[0])
            self.held.start()
            self.pass_on(3, self.last, mine, "xa")
        else:
            self.held.wait()
            self.lines.scatter(0, [self.lines.one(half) for half in range(2)])

    def share(self, half, back):
        mine = self.lines.line(half, back)
        sems = (self.share_send.at[half, back], self.share_recv.at[half, back])
        self.shared.append(self.start(remote(mine, mine, *sems, "core")))

    def spread(self):
        self.lines.arrive()
        self.lines.scatter(1, [self.lines.line(half) for half in range(2)])
        for half in range(2):
            self.share(half, 0)

    def finish(self):
        for half, copies in enumerate(self.lines.moving):
            for back, copy in enumerate(copies, 1):
                copy.wait_recv()
                self.share(half, back)
        for copy in self.shared:
            copy.wait_recv()


def head_scratch():
    bf16, dma = (jnp.bfloat16, pltpu.SemaphoreType.DMA)
    shapes = [(2, 192, 512), (2, 192, 256), (2, 192, 128), (192, 128)]
    shapes += [(2, 192, 256), (2, 192, 128), (192, 128)]
    return [
        *[pltpu.VMEM(shape, bf16) for shape in shapes],
        dma((4,)),
        dma((4,)),
        dma((1,)),
        dma((2, 2, 4)),
        dma((2, 2, 4)),
        dma((2, 4)),
        dma((2, 4)),
    ]


class NormSums:
    def __init__(self, held, landed, out, send, recv, start):
        self.held, self.landed, self.out = (held, landed, out)
        self.send, self.recv, self.start = (send, recv, start)
        self.dims = ("core",) + REDUCE_DIMS + ("xb",)

    def begin(self, k):
        shard, _, _, _, _ = place()
        if k < 6:
            src, dst = (self.held.at[k], self.landed.at[k])
        else:
            src, dst = (self.held.at[6, pl.ds(1 - shard, 1)], self.landed.at[6, pl.ds(0, 1)])
        self.copy = self.start(remote(src, dst, self.send.at[k], self.recv.at[k], self.dims[k]))

    def step(self, k):
        shard, _, _, _, _ = place()
        self.copy.wait_recv()
        if k < 6:
            self.held[k + 1] = self.held[k] + self.landed[k]
            self.begin(k + 1)
        else:
            self.out[...] = self.held[6, shard] + self.landed[6, 0]


def project_back(tok_ref, weight_ref, weight, sem, grad_ref, back_out):
    def fetch(c):
        cols = pl.ds(c * 256, 256)
        return pltpu.make_async_copy(weight_ref.at[:, cols], weight.at[c % 2], sem.at[c % 2])

    fetch(0).start()
    total = grad_ref[...]
    for c in range(12):
        if c < 11:
            fetch(c + 1).start()
        fetch(c).wait()
        total = total + lax.dot_general(
            tok_ref[:, c * 256 : (c + 1) * 256],
            weight[c % 2],
            (((1,), (1,)), ((), ())),
            preferred_element_type=jnp.float32,
        )
    back_out[...] = total.astype(jnp.bfloat16)


def back_kernel(*refs):
    refs = list(refs)

    def take(count):
        taken = refs[:count]
        del refs[:count]
        return taken

    act_refs = take(7)
    norm_ref, staged, grad_ref, weight_ref = take(4)
    attention_in = take(6)
    ff_out, qkv_out, norm_out, back_out = take(4)
    loads, held = ([], take(13))
    load_sem = take(1)[0]
    for i, (src, dst) in enumerate(zip(act_refs + attention_in, held)):
        loads.append(pltpu.make_async_copy(src, dst, load_sem.at[i]))
        loads[i].start()
    block_tokens, ff_acts = (held[0], held[1:7])
    q_ref, pairs_ref, low_ref, end_ref, lse_ref, o_ref = held[7:]
    ff_refs = take(8) + [ff_out] + take(7)
    head_refs = take(14)
    norm_refs = take(2) + [norm_out] + take(2)
    heads_in, heads_out, tok_in, tok_ref, weight, weight_sem = take(6)
    swaps = [take(2), take(2)]
    attention_refs = refs
    sent = []

    def start(copy):
        copy.start()
        sent.append(copy)
        return copy

    greet_all(("core", "xa", "xb"))
    ff = Reducer(ff_acts, FF_DOTS, FF_WIDTHS, ff_refs, start)
    heads = HeadGradients(head_refs, qkv_out, start)
    upstream = Exchange(staged, heads_in, *swaps[0], start)
    upstream.begin()
    sums = NormSums(*norm_refs, start)
    sums.held[0] = norm_ref[...]
    sums.begin(0)
    for load in loads[1:7]:
        load.wait()
    for at in range(len(FF_DOTS)):
        ff.multiply(at)
    sums.step(0)
    for load in loads[7:]:
        load.wait()
    upstream.finish()
    attention = AttendBack(
        [q_ref, heads_in, pairs_ref, low_ref, end_ref, lse_ref, o_ref],
        heads_out,
        attention_refs,
        start,
    )
    def ff_reduce(k):
        sums.step(k + 1)
        for p in ff.parts:
            ff.reduce_step(p, k)

    def ff_gather(k):
        for p in ff.parts:
            ff.gather_step(p, k)

    events = [(BACK_REDUCE[k], functools.partial(ff_reduce, k)) for k in range(2)]
    events += attention.events
    events.sort(key=lambda e: e[0])
    done = 0
    for at, act in events:
        if at > done:
            attention.run(done, at)
            done = at
        act()
    attention.run(done, 4 * SLOT_UNITS)
    attention.finish()
    downstream = Exchange(heads_out, tok_in, *swaps[1], start)
    downstream.begin()
    loads[0].wait()
    heads.multiply(attention.grads_t, block_tokens)
    ff_reduce(2)
    heads.step(0)
    ff_reduce(3)
    heads.step(1)
    ff_reduce(4)
    heads.step(2)
    ff_reduce(5)
    heads.step(3)
    ff_gather(4)
    ff_gather(3)
    heads.spread()
    downstream.finish()

    def unpack(i, carry):
        both = [tok_in[i * 2], tok_in[i * 2 + 1]]
        query = [jnp.concatenate([t[128:192, :HEAD], t[128:192, HEAD:]], axis=0) for t in both]
        key = [t[0:128, :HEAD] for t in both]
        value = [t[0:128, HEAD:] for t in both]
        for which, piece in enumerate((query, key, value)):
            here = pl.ds(pl.multiple_of(which * 1024 + i * 128, 128), 128)
            tok_ref[:, here] = jnp.concatenate(piece, axis=1)
        return carry

    lax.fori_loop(0, 8, unpack, 0)
    project_back(tok_ref, weight_ref, weight, weight_sem, grad_ref, back_out)
    ff_gather(2)
    ff_gather(1)
    heads.finish()
    ff_gather(0)
    ff.finish()
    for copy in sent:
        copy.wait_send()


FF_DOTS = tuple(
    [(0, 512, 0, 3, j * 512) for j in range(4)]
    + [(1, 2048, q * 512, 4, 0) for q in range(4)]
    + [(2, 512, 0, 5, 0)]
)
FF_WIDTHS = (1024, 896, 896, 896, 896)
def reducer_scratch(widths):
    total, parts = (sum(widths), len(widths))
    bf16, dma = (jnp.bfloat16, pltpu.SemaphoreType.DMA)
    return [
        pltpu.VMEM((2, ROWS, total), bf16),
        *[pltpu.VMEM((2, ROWS >> (k + 1), total), bf16) for k in range(5)],
        pltpu.VMEM((16, total), bf16),
        pltpu.VMEM((16, total), bf16),
        dma((8,)),
        dma((8,)),
        dma((parts, 6)),
        dma((parts, 6)),
        dma((parts, 7)),
        dma((parts, 7)),
        dma((8 + parts,)),
    ]


def back(acts, norm_sums, staged, grad_one, full_qkv, attention):
    bf16, f32, dma = (jnp.bfloat16, jnp.float32, pltpu.SemaphoreType.DMA)
    whole, anywhere = (pl.BlockSpec(memory_space=pltpu.VMEM), pl.BlockSpec(memory_space=pl.ANY))
    ff_total = sum(FF_WIDTHS)
    held = pltpu.VMEM((7, 2, 8, 512), f32)
    return pl.pallas_call(
        back_kernel,
        out_shape=[
            jax.ShapeDtypeStruct((2, ROWS, ff_total), bf16),
            jax.ShapeDtypeStruct((4, 4, 4, 192, 128), bf16),
            jax.ShapeDtypeStruct((8, 512), f32),
            jax.ShapeDtypeStruct((128, 1024), bf16),
        ],
        in_specs=[anywhere] * 7 + [whole] * 3 + [anywhere] * 7,
        out_specs=[anywhere] * 2 + [whole] * 2,
        scratch_shapes=[
            *[pltpu.VMEM(a.shape, a.dtype) for a in (*acts, *attention)],
            dma((13,)),
            *reducer_scratch(FF_WIDTHS),
            *head_scratch(),
            held,
            held,
            dma((7,)),
            dma((7,)),
            pltpu.VMEM((16, 64, 128), bf16),
            pltpu.VMEM((16, 192, 128), bf16),
            pltpu.VMEM((16, 192, 128), bf16),
            pltpu.VMEM((128, 3072), bf16),
            pltpu.VMEM((2, 1024, 256), bf16),
            dma((2,)),
            *[dma((16,))] * 4,
            *back_scratch(),
        ],
        compiler_params=pltpu.CompilerParams(
            collective_id=1, has_side_effects=True, vmem_limit_bytes=62 * 2**20
        ),
    )(*acts, norm_sums, staged, grad_one, full_qkv, *attention)


CHUNK = 512


def cast_kernel(ff_ref, qkv_ref, *refs):
    plain, refs = (list(zip(refs[:2], refs[8:10])), refs[2:8] + refs[10:])
    outs, (narrow, heads, wide, in_sem, out_sem, bounce) = (refs[:6], refs[6:])
    grad_in, grad_down, grad_out, *grad_qkv = outs
    chunks = []
    for c in range(2):
        for j in range(9):
            src = ff_ref.at[c, :, pl.ds(j * CHUNK, CHUNK)]
            if j < 4:
                dst = grad_in.at[:, pl.ds((c * 4 + j) * CHUNK, CHUNK)]
            elif j < 8:
                dst = grad_down.at[pl.ds((j - 4) * ROWS, ROWS), pl.ds(c * CHUNK, CHUNK)]
            else:
                dst = grad_out.at[:, pl.ds(c * CHUNK, CHUNK)]
            chunks.append((src, dst))
    loads = [
        pltpu.make_async_copy(src, narrow.at[n], in_sem.at[n]) for n, (src, _) in enumerate(chunks)
    ]
    turned = pltpu.make_async_copy(qkv_ref, heads, in_sem.at[18])
    turned.start()
    for c in range(2):
        for j in range(3):
            chunks.append((None, grad_qkv[j].at[:, pl.ds(c * CHUNK, CHUNK)]))
    stores = [
        pltpu.make_async_copy(wide.at[n], dst, out_sem.at[n]) for n, (_, dst) in enumerate(chunks)
    ]
    for load in loads:
        load.start()
    n = len(chunks)
    for i, (src, dst) in enumerate(plain):
        loads.append(pltpu.make_async_copy(src, bounce.at[i], in_sem.at[n + i]))
        loads[-1].start()
        stores.append(pltpu.make_async_copy(bounce.at[i], dst, out_sem.at[n + i]))
    for n in range(18):
        loads[n].wait()

        def widen(i, carry):
            here = pl.ds(pl.multiple_of(i * 64, 64), 64)
            wide[n, here] = narrow[n, here].astype(jnp.float32)
            return carry

        lax.fori_loop(0, ROWS // 64, widen, 0)
        stores[n].start()
    turned.wait()
    for n in range(18, 24):
        c, which = ((n - 18) // 3, (n - 18) % 3)

        def turn(p, carry):
            rows = pl.ds(pl.multiple_of(p * 128, 128), 128)
            for pair in range(4):
                both = []
                for head in (c * 8 + pair * 2, c * 8 + pair * 2 + 1):
                    both.append(heads[head // 4, head % 4, p, which * HEAD : (which + 1) * HEAD])
                block = jnp.concatenate(both, axis=0).astype(jnp.float32)
                wide[n, rows, pair * 128 : (pair + 1) * 128] = jnp.transpose(block)
            return carry

        lax.fori_loop(0, 4, turn, 0)
        stores[n].start()
    for i in range(2):
        loads[18 + i].wait()
        stores[24 + i].start()
    for store in stores:
        store.wait()


def results(ff_summed, qkv_summed, result, input_grad):
    f32 = jnp.float32
    anywhere = pl.BlockSpec(memory_space=pl.ANY)
    square = jax.ShapeDtypeStruct((ROWS, 1024), f32)
    return pl.pallas_call(
        cast_kernel,
        out_shape=[
            jax.ShapeDtypeStruct((ROWS, 4096), f32),
            jax.ShapeDtypeStruct((2048, 1024), f32),
            square,
            square,
            square,
            square,
            jax.ShapeDtypeStruct(result.shape, result.dtype),
            jax.ShapeDtypeStruct(input_grad.shape, input_grad.dtype),
        ],
        in_specs=[anywhere] * 4,
        out_specs=[anywhere] * 8,
        scratch_shapes=[
            pltpu.VMEM((18, ROWS, CHUNK), jnp.bfloat16),
            pltpu.VMEM(qkv_summed.shape, jnp.bfloat16),
            pltpu.VMEM((24, ROWS, CHUNK), f32),
            pltpu.SemaphoreType.DMA((26,)),
            pltpu.SemaphoreType.DMA((26,)),
            pltpu.VMEM((2, *result.shape), result.dtype),
        ],
        compiler_params=pltpu.CompilerParams(vmem_limit_bytes=56 * 2**20),
    )(ff_summed, qkv_summed, result, input_grad)


def shards(
    tokens,
    segments,
    valid,
    w_query,
    w_key,
    w_value,
    w_out,
    norm1_gain,
    norm1_bias,
    w_in,
    w_down,
    norm2_gain,
    norm2_bias,
    cotangent,
):
    packed = jnp.concatenate([norm1_gain, norm1_bias, norm2_gain, norm2_bias]).reshape(16, 128)
    token_rows = tokens[0]
    (
        full_qkv,
        queries,
        pairs,
        summed,
        lse,
        low,
        end,
        tokens_all,
        first_low,
        hidden,
        mixed,
        pre_grad,
        ff_grad,
        attn_grad,
        staged,
        norm_sums,
        grad_one,
        result,
    ) = front(
        token_rows,
        [w_query, w_key, w_value, w_out, w_in, w_down],
        packed,
        cotangent[0],
        segments[0],
        valid[0],
    )
    ff_summed, qkv_summed, norm_total, input_grad = back(
        [tokens_all.reshape(BLOCK_LEN, 1024), first_low, hidden, mixed, pre_grad, ff_grad, attn_grad],
        norm_sums,
        staged,
        grad_one,
        full_qkv,
        [queries, pairs, low, end, lse, summed],
    )
    grad_in, grad_down, grad_out, *grad_qkv, result, input_grad = results(
        ff_summed, qkv_summed, result, input_grad
    )
    return (
        result[None],
        input_grad[None],
        *grad_qkv,
        grad_out,
        norm_total[0],
        norm_total[1],
        grad_in,
        grad_down,
        norm_total[2],
        norm_total[3],
    )


def solution(mesh):
    return jax.shard_map(
        shards,
        mesh=mesh,
        in_specs=(
            P("shard", ("blk", "aa"), None),
            P("shard", None),
            P("shard", None),
            P("shard", None),
            P("shard", None),
            P("shard", None),
            P("shard", None),
            P("shard"),
            P("shard"),
            P("shard", None),
            P("shard", None),
            P("shard"),
            P("shard"),
            P("shard", ("blk", "aa"), None),
        ),
        out_specs=(
            P("shard", ("blk", "aa"), None),
            P("shard", ("blk", "aa"), None),
            P("shard", None),
            P("shard", None),
            P("shard", None),
            P("shard", None),
            P("shard"),
            P("shard"),
            P("shard", None),
            P("shard", None),
            P("shard"),
            P("shard"),
        ),
        check_vma=False,
    )
```

```python
import functools
import math

import jax
import jax.numpy as jnp
from jax import lax
from jax.experimental import pallas as pl
from jax.experimental.pallas import tpu as pltpu
from jax.sharding import PartitionSpec as P

HEADS = 16
HEAD = 64
MASKED_SCORE = -1e30
NORM_EPSILON = 1e-05
BLOCK_LEN = 2048


MESH = pl.DeviceIdType.MESH
ROWS = 512
REDUCE_DIMS = ("xa", "ya", "za", "yb", "zb")
GATHER_DIMS = ("ya", "za", "yb", "zb")


def place():
    shard = lax.axis_index("shard")
    blk = lax.axis_index("blk")
    aa = lax.axis_index("aa")
    return (shard, blk // 2, blk % 2, aa // 4, aa % 4)


def flipped(i):
    return i + 1 - 2 * (i % 2)


def partner(dim):
    shard, x_lo, core, z, y = place()
    if dim == "core":
        core = 1 - core
    elif dim == "xa":
        x_lo = 1 - x_lo
    elif dim == "xb":
        shard, x_lo = 1 - shard, 1 - x_lo
    elif dim == "ya":
        y = flipped(y)
    elif dim == "yb":
        y = 3 - y
    elif dim == "za":
        z = flipped(z)
    else:
        z = 3 - z
    return (shard, x_lo * 2 + core, z * 4 + y)


def ring_bit(dim):
    shard, x_lo, _, z, y = place()
    if dim == "xa":
        return (shard * 2 + x_lo + shard) % 2
    if dim == "ya":
        return (y + y // 2) % 2
    if dim == "yb":
        return y // 2
    if dim == "za":
        return (z + z // 2) % 2
    return z // 2


def remote(src, dst, send_sem, recv_sem, dim):
    return pltpu.make_async_remote_copy(
        src_ref=src,
        dst_ref=dst,
        send_sem=send_sem,
        recv_sem=recv_sem,
        device_id=partner(dim),
        device_id_type=MESH,
    )


def row_starts(dims, rows):
    starts, at, size = ([0], 0, rows)
    for dim in dims:
        size //= 2
        at = at + ring_bit(dim) * size
        starts.append(at)
    return starts


def rotated(dims, by):
    return dims[by:] + dims[:by]


DIRECT = ((4, 0), (5, 1), (4, 2), (5, 3))


class Gather:
    def __init__(self, sources, places, send, recv, start):
        self.sources, self.places = (sources, places)
        self.send, self.recv, self.start = (send, recv, start)
        self.shard, _, self.core, _, _ = place()
        self.orders = [rotated(GATHER_DIMS, part) for part in range(4)]
        self.moving, self.siblings = ({}, [])

    def columns(self, i, part, off):
        cols = self.sources[i].shape[1]
        col = pl.multiple_of(self.core * (cols // 2) + (off + part * (cols // 8)), 128)
        return pl.ds(col, cols // 8)

    def block(self, i, part, shard, at, size):
        target, off = self.places[i]
        rows = self.sources[i].shape[0]
        at = pl.multiple_of(shard * rows + at, 16)
        return target.at[pl.ds(at, size), self.columns(i, part, off)]

    def own(self, i):
        target, off = self.places[i]
        rows, cols = self.sources[i].shape
        return target.at[pl.ds(pl.multiple_of(self.shard * rows, rows), rows), pl.ds(off, cols)]

    def begin_direct(self):
        for i, part in DIRECT:
            rows = self.sources[i].shape[0]
            self.moving[i, part] = self.start(
                remote(
                    self.sources[i].at[:, self.columns(i, part, 0)],
                    self.block(i, part, self.shard, 0, rows),
                    self.send.at[i, part, 0],
                    self.recv.at[i, part, 0],
                    "xb",
                )
            )

    def finish_direct(self):
        for i, part in DIRECT:
            self.moving[i, part].wait_recv()
            mine = self.block(i, part, 1 - self.shard, 0, self.sources[i].shape[0])
            sems = (self.send.at[i, part, 5], self.recv.at[i, part, 5])
            self.siblings.append(self.start(remote(mine, mine, *sems, "core")))

    def parts(self, i):
        return [part for part in range(4) if (i, part) not in DIRECT]

    def begin(self, i):
        rows = self.sources[i].shape[0]
        for part in self.parts(i):
            at = row_starts(self.orders[part], rows)[4]
            mine = pl.ds(pl.multiple_of(at, 16), rows // 16)
            self.moving[i, part] = self.start(
                remote(
                    self.sources[i].at[mine, self.columns(i, part, 0)],
                    self.block(i, part, self.shard, at, rows // 16),
                    self.send.at[i, part, 0],
                    self.recv.at[i, part, 0],
                    "xb",
                )
            )

    def stage(self, i, stage):
        rows = self.sources[i].shape[0]
        for part in self.parts(i):
            self.moving[i, part].wait_recv()
            starts = row_starts(self.orders[part], rows)
            if stage < 5:
                k = 4 - stage
                mine = self.block(i, part, 1 - self.shard, starts[k + 1], rows >> (k + 1))
                self.moving[i, part] = self.start(
                    remote(
                        mine,
                        mine,
                        self.send.at[i, part, stage],
                        self.recv.at[i, part, stage],
                        self.orders[part][k],
                    )
                )
            if stage >= 4:
                at = starts[1] if stage == 4 else rows // 2 - starts[1]
                mine = self.block(i, part, 1 - self.shard, at, rows // 2)
                self.siblings.append(
                    self.start(
                        remote(
                            mine,
                            mine,
                            self.send.at[i, part, stage + 1],
                            self.recv.at[i, part, stage + 1],
                            "core",
                        )
                    )
                )

    def finish(self):
        for copy in self.siblings:
            copy.wait_recv()
        self.siblings = []


def plane_peer(step):
    shard, x_lo, core, z, y = place()
    return (shard, x_lo * 2 + core, (z * 4 + y + step) % 16)


class Exchange:
    def __init__(self, outgoing, incoming, send, recv, start):
        self.outgoing, self.incoming = (outgoing, incoming)
        self.send, self.recv, self.start = (send, recv, start)
        self.copies = []

    def begin(self):
        me = lax.axis_index("aa")
        for step in (1, 3, 4, 12, 15, 13, 5, 11, 2, 8, 14, 6, 10, 7, 9):
            self.copies.append(
                self.start(
                    pltpu.make_async_remote_copy(
                        src_ref=self.outgoing.at[(me + step) % 16],
                        dst_ref=self.incoming.at[me],
                        send_sem=self.send.at[step],
                        recv_sem=self.recv.at[step],
                        device_id=plane_peer(step),
                        device_id_type=MESH,
                    )
                )
            )
        self.incoming[me] = self.outgoing[me]

    def finish(self):
        for copy in self.copies:
            copy.wait_recv()


def greet_all(dims):
    barrier = pltpu.get_barrier_semaphore()
    for dim in dims:
        pl.semaphore_signal(barrier, inc=1, device_id=partner(dim), device_id_type=MESH)
    for step in range(1, 16):
        pl.semaphore_signal(barrier, inc=1, device_id=plane_peer(step), device_id_type=MESH)
    pl.semaphore_wait(barrier, len(dims) + 15)


def unfolded(block, side):
    lane = lax.broadcasted_iota(jnp.int32, (64, 128), 1)
    keep = (lane >= HEAD) if side else (lane < HEAD)
    block = block.astype(jnp.float32)
    moved = jnp.concatenate([block[:, HEAD:], block[:, :HEAD]], axis=1)
    first, second = (moved, block) if side else (block, moved)
    both = jnp.concatenate([jnp.where(keep, first, 0.0), jnp.where(keep, second, 0.0)], axis=0)
    return both.astype(jnp.bfloat16)


LEAST = -(2**31)
FRONT_BLOCK = 512
TOKENS_AT = 1


def visible(place_k, low, end, start):
    size = jnp.maximum(end - low, 0) + LEAST
    return (place_k - (low - start - LEAST)) < size


def query_spans(segments_ref, valid_ref, low_ref, end_ref):
    _, x_lo, core, _, _ = place()
    segments = segments_ref[...]
    start = pl.multiple_of((x_lo * 2 + core) * 16, 16)
    mine = segments_ref[pl.ds(start, 16)]
    low, end = (jnp.zeros_like(mine), jnp.zeros_like(mine))
    before = jnp.zeros((1, 1), jnp.int32)
    for number in range(35):
        same = jnp.where(segments == number, 1, 0)
        count = jnp.sum(jnp.sum(same, axis=1, keepdims=True), axis=0, keepdims=True)
        picked = mine == number
        low = jnp.where(picked, before, low)
        before = before + count
        end = jnp.where(picked, before, end)
    live = jnp.sum(jnp.sum(valid_ref[...], axis=1, keepdims=True), axis=0, keepdims=True)
    end = jnp.minimum(end, live)
    for row in range(16):
        here = pl.ds(row * 128, 128)
        low_ref[:, here] = jnp.broadcast_to(low[row : row + 1], (8, 128))
        end_ref[:, here] = jnp.broadcast_to(end[row : row + 1], (8, 128))


def normalized(values):
    centred = values - jnp.mean(values, axis=1, keepdims=True)
    inverse = lax.rsqrt(jnp.mean(centred * centred, axis=1, keepdims=True) + NORM_EPSILON)
    return (centred * inverse, inverse)


def normalized_back(upstream, scaled, inverse, gain):
    weighted = upstream * gain
    centred = weighted - jnp.mean(weighted, axis=1, keepdims=True)
    return inverse * (centred - scaled * jnp.mean(weighted * scaled, axis=1, keepdims=True))


def summed_rows(values):
    return jnp.sum(values, axis=0, keepdims=True)


def dense(x_ref, cot_ref, mixed_in, norm_in, weights, scratch, outs, give):
    w_out, w_in, w_down = weights
    slope, low_ref, hidden_ref, mixed_ref, pre_ref, down_ref, attn_ref = scratch
    staged_ref, sums_ref, grad_ref, result_ref = outs
    f32, bf16 = (jnp.float32, jnp.bfloat16)
    gain_one, bias_one, gain_two, bias_two = [
        jnp.concatenate(
            [norm_in[half, i * 4 + j : i * 4 + j + 1] for half in range(2) for j in range(4)], axis=1
        ).astype(f32)
        for i in range(4)
    ]
    for pair in range(8):
        both = [mixed_in[pair * 2], mixed_in[pair * 2 + 1]]
        both = [jnp.concatenate([t[:, :HEAD], t[:, HEAD:]], axis=0) for t in both]
        mixed_ref[:, pair * 128 : (pair + 1) * 128] = jnp.concatenate(both, axis=1)
    give(3)
    attn = jnp.dot(mixed_ref[...], w_out[...], preferred_element_type=f32)
    scaled_one, inverse_one = normalized(x_ref[...].astype(f32) + attn)
    first = scaled_one * gain_one + bias_one
    low_ref[...] = first.astype(bf16)
    give(1)

    def up(c, total):
        here = pl.ds(pl.multiple_of(c * 1024, 1024), 1024)
        pre = jnp.dot(low_ref[...], w_in[:, here], preferred_element_type=f32)
        share = 0.5 + 0.5 * lax.erf(pre * 0.5**0.5)
        hidden = (pre * share).astype(bf16)
        hidden_ref[:, here] = hidden
        slope[:, here] = share + pre * jnp.exp(pre * pre * -0.5) * (2 * math.pi) ** -0.5
        return total + jnp.dot(hidden, w_down[here], preferred_element_type=f32)

    ff_out = lax.fori_loop(0, 4, up, jnp.zeros((128, 1024), f32), unroll=2)
    give(2)
    scaled_two, inverse_two = normalized(first + ff_out)
    result_ref[...] = (scaled_two * gain_two + bias_two).astype(bf16)
    upstream = cot_ref[...].astype(f32)
    grad_two = normalized_back(upstream, scaled_two, inverse_two, gain_two)
    down_ref[...] = grad_two.astype(bf16)
    give(5)

    def down(c, total):
        here = pl.ds(pl.multiple_of(c * 1024, 1024), 1024)
        grad = lax.dot_general(
            down_ref[...], w_down[here], (((1,), (1,)), ((), ())), preferred_element_type=f32
        )
        grad = (grad * slope[:, here]).astype(bf16)
        pre_ref[:, here] = grad
        return total + lax.dot_general(
            grad, w_in[:, here], (((1,), (1,)), ((), ())), preferred_element_type=f32
        )

    first_grad = lax.fori_loop(0, 4, down, grad_two, unroll=2)
    give(4)
    grad_one = normalized_back(first_grad, scaled_one, inverse_one, gain_one)
    grad_ref[...] = grad_one
    attn_ref[...] = grad_one.astype(bf16)
    give(6)
    mixed_grad = lax.dot_general(
        attn_ref[...], w_out[...], (((1,), (1,)), ((), ())), preferred_element_type=f32
    ).astype(bf16)
    for head in range(HEADS):
        part = mixed_grad[:, head * HEAD : (head + 1) * HEAD]
        staged_ref[head] = jnp.concatenate([part[0:64], part[64:128]], axis=1)
    sums = [
        summed_rows(first_grad * scaled_one),
        summed_rows(first_grad),
        summed_rows(upstream * scaled_two),
        summed_rows(upstream),
    ]
    for half in range(2):
        cols = slice(half * 512, (half + 1) * 512)
        sums_ref[half] = jnp.concatenate([v[:, cols] for v in sums] + [jnp.zeros((4, 512), f32)])


def front_kernel(
    x_ref,
    wq_ref,
    wk_ref,
    wv_ref,
    wo_ref,
    wi_ref,
    wd_ref,
    norm_ref,
    cot_ref,
    segments_ref,
    valid_ref,
    qkv_out,
    q_out,
    pairs_out,
    o_out,
    lse_out,
    low_ref,
    end_ref,
    *refs,
):
    dense_out, refs = (refs[:11], refs[11:])
    front_body(
        x_ref,
        (wq_ref, wk_ref, wv_ref, wo_ref, wi_ref, wd_ref),
        norm_ref,
        cot_ref,
        (segments_ref, valid_ref),
        qkv_out,
        (q_out, pairs_out, o_out, lse_out, low_ref, end_ref),
        dense_out,
        *refs,
    )


def front_body(
    x_ref,
    weights,
    norm_ref,
    cot_ref,
    documents,
    qkv_out,
    attention_out,
    dense_out,
    wqkv,
    w_out,
    w_in,
    w_down,
    norm_in,
    mixed_in,
    slope,
    pre_full,
    down_full,
    attn_full,
    low_full,
    hidden_full,
    mixed_full,
    pool_send,
    pool_recv,
    pool_own,
    save_sem,
    q_held,
    pairs_held,
    o_held,
    lse_held,
    low_held,
    end_held,
    staged,
    heads_in,
    folded,
    pairs_t,
    top_s,
    send,
    recv,
    own_in,
    own_out,
    hop_send,
    hop_recv,
    swap_send,
    swap_recv,
    back_send,
    back_recv,
    tok_send,
    tok_recv,
    tok_own,
):
    shard, _, _, z, y = place()
    attention_held = (q_held, pairs_held, o_held, lse_held, low_held, end_held)
    q_out, pairs_out, o_out, lse_out, low_ref, end_ref = attention_held
    saves = []

    def save(i):
        copy = pltpu.make_async_copy(attention_held[i], attention_out[i], save_sem.at[i])
        copy.start()
        saves.append(copy)

    sent = []

    def start(copy):
        copy.start()
        sent.append(copy)
        return copy

    gather = Gather(
        weights,
        [(wqkv, 0), (wqkv, 1024), (wqkv, 2048), (w_out, 0), (w_in, 0), (w_down, 0)],
        send,
        recv,
        start,
    )
    inward = []
    for i in range(6):
        inward.append(pltpu.make_async_copy(weights[i], gather.own(i), own_in.at[i]))
        inward[i].start()
    greet_all(("core", "xa", "xb"))
    norms = start(
        remote(norm_ref, norm_in.at[shard], hop_send.at[3], hop_recv.at[3], "xb")
    )
    norm_in[shard] = norm_ref[...]
    for i in range(6):
        gather.begin(i)
    _, _, core, _, _ = place()
    pooled = []

    def give(i):
        src = (x_ref, low_full, hidden_full, mixed_full, pre_full, down_full, attn_full)[i]
        mine, theirs = (src, src)
        if i > 3:
            half = src.shape[1] // 2
            mine, theirs = [
                src.at[:, pl.ds(pl.multiple_of(c * half, half), half)] for c in (core, 1 - core)
            ]
        copy = pltpu.make_async_copy(mine, dense_out[i].at[pl.ds(0, 128)], pool_own.at[i])
        copy.start()
        saves.append(copy)
        sems = (pool_send.at[i], pool_recv.at[i])
        pooled.append(start(remote(theirs, dense_out[i].at[pl.ds(128, 128)], *sems, "core")))

    for i in range(3):
        gather.stage(i, 1)
    for stage in range(2, 6):
        for i in range(3):
            gather.stage(i, stage)
        if stage == 3:
            for i in range(3, 6):
                gather.stage(i, 1)
            gather.begin_direct()
    for i in range(3):
        inward[i].wait()
    gather.finish()
    keep = pltpu.make_async_copy(wqkv, qkv_out, own_out.at[0])
    keep.start()

    def project(piece, carry):
        q, k, v = [
            jnp.dot(
                x_ref[...],
                wqkv[:, pl.ds(pl.multiple_of(which * 1024 + piece * 256, 256), 256)],
                preferred_element_type=jnp.float32,
            )
            for which in range(3)
        ]
        q = (q.astype(jnp.bfloat16).astype(jnp.float32) * HEAD ** (-0.5)).astype(jnp.bfloat16)
        k, v = (k.astype(jnp.bfloat16), v.astype(jnp.bfloat16))
        for h in range(4):
            at = slice(h * HEAD, (h + 1) * HEAD)
            staged[piece * 4 + h, 0:128] = jnp.concatenate([k[:, at], v[:, at]], axis=1)
            staged[piece * 4 + h, 128:192] = jnp.concatenate([q[0:64, at], q[64:128, at]], axis=1)
        return carry

    lax.fori_loop(0, 4, project, 0)
    heads = Exchange(staged, heads_in, swap_send, swap_recv, start)
    heads.begin()
    for i in range(3, 6):
        gather.stage(i, 2)
    query_spans(*documents, low_ref, end_ref)
    heads.finish()

    def spread(c, carry):
        here = pl.ds(pl.multiple_of(c * 128, 128), 128)
        pairs_out[here] = heads_in[c, 0:128]
        q_out[here] = unfolded(heads_in[c, 128:192], 0)
        return carry

    lax.fori_loop(0, 16, spread, 0)

    def slot_rows(slot):
        return pairs_out.at[pl.ds(slot * BLOCK_LEN, BLOCK_LEN)]

    def hop(index, source, target, dim):
        return start(
            remote(
                slot_rows(source), slot_rows(target), hop_send.at[index], hop_recv.at[index], dim
            )
        )

    hops = {1: hop(0, 0, 1, "core"), 2: hop(1, 0, 2, "xa")}
    columns = [(slice(None), pl.ds(half * 512, 512)) for half in range(2)]
    lines = Lines(dense_out[0], columns, tok_send, tok_recv, start)
    lines.scatter(0, [x_ref.at[cols] for cols in columns])
    own_tokens = pltpu.make_async_copy(x_ref, dense_out[0].at[z, y], tok_own.at[0])
    own_tokens.start()
    for i in (0, 4, 5):
        save(i)
    top_s[...] = jnp.full_like(top_s, MASKED_SCORE)
    o_out[...] = jnp.zeros_like(o_out)
    first_row = lax.broadcasted_iota(jnp.int32, (128, 512), 0) == 0

    def turn(c, carry):
        here = pl.ds(pl.multiple_of(c * 512, 512), 512)
        turned = jnp.transpose(pairs_out[here].astype(jnp.float32))
        pairs_t[:, here] = jnp.where(first_row, 1.0, turned).astype(jnp.bfloat16)
        return carry

    def slot_step(slot, block):
        _, x_lo, core, _, _ = place()
        owner = (slot // 2 + x_lo) % 2 * 2 + (slot % 2 + core) % 2
        rows = pl.ds(slot * BLOCK_LEN, BLOCK_LEN)
        mine = pl.ds(pl.multiple_of(block * FRONT_BLOCK, FRONT_BLOCK), FRONT_BLOCK)
        scores = lax.dot_general(
            pairs_out[rows],
            q_out[mine],
            (((1,), (1,)), ((), ())),
            preferred_element_type=jnp.float32,
        )
        place_k = lax.broadcasted_iota(jnp.int32, scores.shape, 0)
        allowed = visible(place_k, low_ref[0:1, mine], end_ref[0:1, mine], owner * BLOCK_LEN)
        if slot == 0:
            place_q = lax.broadcasted_iota(jnp.int32, (1, FRONT_BLOCK), 1) + block * FRONT_BLOCK
            allowed = allowed | (place_k == place_q)
        scores = jnp.where(allowed, scores, MASKED_SCORE)
        top = top_s[0:1, mine]
        new_top = jnp.maximum(top, jnp.max(scores, axis=0, keepdims=True))
        weights = jnp.exp(scores - new_top)
        factor = jnp.exp(top - new_top)
        o_out[:, mine] = o_out[:, mine] * factor + jnp.dot(
            pairs_t[:, rows], weights.astype(jnp.bfloat16), preferred_element_type=jnp.float32
        )
        top_s[:, mine] = jnp.broadcast_to(new_top, (8, FRONT_BLOCK))

    events = {
        0: [(i, 3) for i in (3, 4, 5)],
        1: [(i, 4) for i in (3, 4, 5)],
        3: [(i, 5) for i in (3, 4, 5)],
    }
    for slot in range(4):
        if slot:
            hops[slot].wait_recv()
        if slot == 2:
            hops[3] = hop(2, 2, 3, "core")
        if slot == 3:
            save(1)
        lax.fori_loop(slot * 4, slot * 4 + 4, turn, 0)
        for half in range(2):

            def blocks(b, carry):
                slot_step(slot, b)
                return carry

            lax.fori_loop(half * 2, half * 2 + 2, blocks, 0)
            if half == 0:
                for i, stage in events.get(slot, ()):
                    gather.stage(i, stage)
                if slot == 3:
                    gather.finish_direct()
                if slot == TOKENS_AT:
                    own_tokens.wait()
                    lines.arrive()
                    lines.scatter(1, [lines.line(half) for half in range(2)])

    def close(c, carry):
        here = pl.ds(pl.multiple_of(c * 128, 128), 128)
        total = o_out[0:1, here]
        mixed = o_out[:, here] / total
        o_out[:, here] = mixed
        lse = top_s[0:1, here] + jnp.log(total)
        lse_out[:, here] = jnp.broadcast_to(lse, (8, 128))
        block = jnp.transpose(mixed)
        both = jnp.concatenate([block[0:64, HEAD:], block[64:128, HEAD:]], axis=1)
        folded[c] = both.astype(jnp.bfloat16)
        return carry

    lax.fori_loop(0, 16, close, 0)
    back = Exchange(folded, mixed_in, back_send, back_recv, start)
    back.begin()
    save(2)
    save(3)
    gather.finish()
    norms.wait_recv()
    for i in range(3, 6):
        inward[i].wait()
    back.finish()
    dense(
        x_ref,
        cot_ref,
        mixed_in,
        norm_in,
        (w_out, w_in, w_down),
        (slope, low_full, hidden_full, mixed_full, pre_full, down_full, attn_full),
        dense_out[7:],
        give,
    )
    lines.arrive()
    for copy in pooled:
        copy.wait_recv()
    for copy in saves:
        copy.wait()
    keep.wait()
    for copy in sent:
        copy.wait_send()


def front(token_rows, weights, packed, cotangent, segments, valid):
    bf16, f32, i32, dma = (jnp.bfloat16, jnp.float32, jnp.int32, pltpu.SemaphoreType.DMA)
    n, shape = (len(weights), jax.ShapeDtypeStruct)
    whole, anywhere = (pl.BlockSpec(memory_space=pltpu.VMEM), pl.BlockSpec(memory_space=pl.ANY))
    return pl.pallas_call(
        front_kernel,
        out_shape=[
            shape((1024, 3072), bf16),
            shape((BLOCK_LEN, 128), bf16),
            shape((4 * BLOCK_LEN, 128), bf16),
            shape((128, BLOCK_LEN), f32),
            shape((8, BLOCK_LEN), f32),
            shape((8, BLOCK_LEN), i32),
            shape((8, BLOCK_LEN), i32),
            shape((4, 4, 128, 1024), bf16),
            *[shape((256, width), bf16) for width in (1024, 4096, 1024, 2048, 512, 512)],
            shape((HEADS, 64, 128), bf16),
            shape((2, 8, 512), f32),
            shape((128, 1024), f32),
            shape((128, 1024), bf16),
        ],
        in_specs=[whole] + [anywhere] * n + [whole] * 4,
        out_specs=[anywhere] * 14 + [whole] * 4,
        scratch_shapes=[
            pltpu.VMEM((1024, 3072), bf16),
            pltpu.VMEM((1024, 1024), bf16),
            pltpu.VMEM((1024, 4096), bf16),
            pltpu.VMEM((4096, 1024), bf16),
            pltpu.VMEM((2, 16, 128), bf16),
            pltpu.VMEM((16, 64, 128), bf16),
            pltpu.VMEM((128, 4096), f32),
            pltpu.VMEM((128, 4096), bf16),
            pltpu.VMEM((128, 1024), bf16),
            pltpu.VMEM((128, 1024), bf16),
            pltpu.VMEM((128, 1024), bf16),
            pltpu.VMEM((128, 4096), bf16),
            pltpu.VMEM((128, 1024), bf16),
            dma((7,)),
            dma((7,)),
            dma((7,)),
            dma((6,)),
            pltpu.VMEM((BLOCK_LEN, 128), bf16),
            pltpu.VMEM((4 * BLOCK_LEN, 128), bf16),
            pltpu.VMEM((128, BLOCK_LEN), f32),
            pltpu.VMEM((8, BLOCK_LEN), f32),
            pltpu.VMEM((8, BLOCK_LEN), i32),
            pltpu.VMEM((8, BLOCK_LEN), i32),
            pltpu.VMEM((16, 192, 128), bf16),
            pltpu.VMEM((16, 192, 128), bf16),
            pltpu.VMEM((16, 64, 128), bf16),
            pltpu.VMEM((128, 4 * BLOCK_LEN), bf16),
            pltpu.VMEM((8, BLOCK_LEN), f32),
            dma((n, 4, 7)),
            dma((n, 4, 7)),
            dma((n,)),
            dma((1,)),
            dma((4,)),
            dma((4,)),
            *[dma((16,))] * 4,
            dma((2, 2, 4)),
            dma((2, 2, 4)),
            dma((1,)),
        ],
        compiler_params=pltpu.CompilerParams(
            collective_id=0, has_side_effects=True, vmem_limit_bytes=62 * 2**20
        ),
    )(
        token_rows,
        *weights,
        packed,
        cotangent,
        segments.reshape(64, 128),
        valid.reshape(64, 128),
    )


BACK_REDUCE = (7, 12)
SLOT_UNITS = 4
BACK_BLOCK = 512


def back_scratch():
    return [
        pltpu.VMEM((BLOCK_LEN, 128), jnp.bfloat16),
        pltpu.VMEM((HEAD, 4 * BLOCK_LEN), jnp.bfloat16),
        pltpu.VMEM((8, BLOCK_LEN), jnp.float32),
        pltpu.VMEM((HEAD, BLOCK_LEN), jnp.float32),
        pltpu.VMEM((4 * BLOCK_LEN, 128), jnp.float32),
        pltpu.VMEM((3, BLOCK_LEN, 128), jnp.bfloat16),
        pltpu.VMEM((3, BLOCK_LEN, 128), jnp.bfloat16),
        pltpu.SemaphoreType.DMA((3,)),
        pltpu.SemaphoreType.DMA((3,)),
        pltpu.VMEM((192, BLOCK_LEN), jnp.bfloat16),
    ]


class AttendBack:
    def __init__(self, ins, out, scratch, start):
        self.q, self.packed, self.pairs, self.low, self.end, self.lse, self.o_t = ins
        self.out = out
        self.g, self.pairs_t, self.delta, self.dq, self.dkv = scratch[:5]
        self.away, self.landed, self.send, self.recv, self.grads_t = scratch[5:10]
        self.start = start
        self.copies = {}
        self.events = [
            (0, self.begin),
            (SLOT_UNITS, lambda: self.give(3, 0, None, "core")),
            (2 * SLOT_UNITS + 1, lambda: self.give(2, 1, 0, "xa")),
            (3 * SLOT_UNITS, lambda: self.give(1, 2, None, "core")),
        ]

    def begin(self):
        self.delta[...] = jnp.zeros_like(self.delta)
        self.dq[...] = jnp.zeros_like(self.dq)
        self.dkv[...] = jnp.zeros_like(self.dkv)

        def chunk(c, carry):
            both = unfolded(self.packed[c], 1)
            here = pl.ds(pl.multiple_of(c * 128, 128), 128)
            self.g[here] = both
            products = jnp.transpose(both.astype(jnp.float32)) * self.o_t[:, here]
            total = jnp.sum(products, axis=0, keepdims=True)
            self.delta[:, here] = jnp.broadcast_to(total, (8, 128))
            return carry

        lax.fori_loop(0, 16, chunk, 0)

        def turn(c, carry):
            here = pl.ds(pl.multiple_of(c * 512, 512), 512)
            self.pairs_t[:, here] = jnp.transpose(self.pairs[here])[0:HEAD]
            return carry

        lax.fori_loop(0, 16, turn, 0)

    def run(self, first, last):
        edge = 3 * SLOT_UNITS
        if first < edge:
            lax.fori_loop(first, min(last, edge), functools.partial(self.unit, own=False), 0)
        if last > edge:
            lax.fori_loop(max(first, edge), last, functools.partial(self.unit, own=True), 0)

    def unit(self, n, carry, own):
        _, x_lo, core, _, _ = place()
        block = n % 4
        slot = 3 - n // 4
        owner = (slot // 2 + x_lo) % 2 * 2 + (slot % 2 + core) % 2
        key_start = owner * BLOCK_LEN
        here = pl.ds(pl.multiple_of(slot * BLOCK_LEN, BLOCK_LEN), BLOCK_LEN)
        mine = pl.ds(pl.multiple_of(block * BACK_BLOCK, BACK_BLOCK), BACK_BLOCK)
        keys = self.pairs[here]
        queries, upstream = (self.q[mine], self.g[mine])
        scores = lax.dot_general(
            keys, queries, (((1,), (1,)), ((), ())), preferred_element_type=jnp.float32
        )
        place_k = lax.broadcasted_iota(jnp.int32, scores.shape, 0)
        allowed = visible(place_k, self.low[0:1, mine], self.end[0:1, mine], key_start)
        if own:
            place_q = lax.broadcasted_iota(jnp.int32, (1, BACK_BLOCK), 1)
            place_q = place_q + block * BACK_BLOCK
            allowed = allowed | (place_k == place_q)
        scores = jnp.where(allowed, scores, MASKED_SCORE)
        probs = jnp.exp(scores - self.lse[0:1, mine])
        prob_grad = lax.dot_general(
            keys, upstream, (((1,), (1,)), ((), ())), preferred_element_type=jnp.float32
        )
        score_grad = (probs * (prob_grad - self.delta[0:1, mine])).astype(jnp.bfloat16)
        self.dkv[here] += jnp.dot(
            score_grad, queries, preferred_element_type=jnp.float32
        ) + jnp.dot(probs.astype(jnp.bfloat16), upstream, preferred_element_type=jnp.float32)
        self.dq[:, mine] += jnp.dot(
            self.pairs_t[:, here], score_grad, preferred_element_type=jnp.float32
        )
        return carry

    def give(self, slot, index, add, dim):
        if add is not None:
            self.copies[add].wait_recv()

        def chunk(c, carry):
            here = pl.ds(pl.multiple_of(c * 256, 256), 256)
            there = pl.ds(pl.multiple_of(slot * BLOCK_LEN + c * 256, 256), 256)
            total = self.dkv[there]
            if add is not None:
                total = total + self.landed[add, here].astype(jnp.float32)
            self.away[index, here] = total.astype(jnp.bfloat16)
            return carry

        lax.fori_loop(0, BLOCK_LEN // 256, chunk, 0)
        self.copies[index] = self.start(
            remote(
                self.away.at[index],
                self.landed.at[index],
                self.send.at[index],
                self.recv.at[index],
                dim,
            )
        )

    def finish(self):
        self.copies[1].wait_recv()
        self.copies[2].wait_recv()

        def chunk(c, carry):
            here = pl.ds(pl.multiple_of(c * 128, 128), 128)
            total = self.dkv[here] + self.landed[1, here].astype(jnp.float32)
            total = total + self.landed[2, here].astype(jnp.float32)
            self.out[c, 0:128] = total.astype(jnp.bfloat16)
            self.grads_t[HEAD:, here] = jnp.transpose(total).astype(jnp.bfloat16)
            grad = self.dq[:, here] * HEAD ** (-0.5)
            self.grads_t[0:HEAD, here] = grad.astype(jnp.bfloat16)
            grad = jnp.transpose(grad)
            folded = jnp.concatenate([grad[0:64], grad[64:128]], axis=1)
            self.out[c, 128:192] = folded.astype(jnp.bfloat16)
            return carry

        lax.fori_loop(0, 16, chunk, 0)


class Reducer:
    def __init__(self, acts, dots, widths, refs, start):
        self.acts, self.dots, self.start = (acts, dots, start)
        self.partial, self.landed, self.last, self.out = (refs[0], refs[1:7], refs[7], refs[8])
        self.act_send, self.act_recv, self.red_send, self.red_recv = refs[9:13]
        self.gat_send, self.gat_recv, self.own = refs[13:16]
        self.shard, _, self.core, _, _ = place()
        self.parts = range(len(widths))
        self.edges = [sum(widths[:p]) for p in range(len(widths) + 1)]
        self.cols = [pl.ds(self.edges[p], widths[p]) for p in self.parts]
        self.orders = [rotated(REDUCE_DIMS, p) for p in self.parts]
        self.starts = [row_starts(self.orders[p], ROWS) for p in self.parts]
        self.moving, self.held, self.shared = ({}, {}, [])

    def multiply(self, at):
        left, left_step, left_off, right, right_off = self.dots[at]
        for s in range(2):
            product = lax.dot_general(
                self.acts[left][:, pl.ds(s * left_step + left_off, ROWS)],
                self.acts[right][:, pl.ds(right_off, 512)],
                (((0,), (0,)), ((), ())),
                preferred_element_type=jnp.float32,
            )
            self.partial[s, :, pl.ds(at * 512, 512)] = product.astype(jnp.bfloat16)
        for p in self.parts:
            if at * 512 < self.edges[p + 1] <= (at + 1) * 512:
                self.reduce_start(p, 0)

    def reduce_start(self, p, k):
        starts, cols = (self.starts[p], self.cols[p])
        if k < 5:
            half = ROWS >> (k + 1)
            away = pl.multiple_of(starts[k] + (half - (starts[k + 1] - starts[k])), 16)
            src = self.partial.at[:, pl.ds(away, half), cols]
            dst = self.landed[k].at[:, :, cols]
            dim = self.orders[p][k]
        else:
            src = self.partial.at[1 - self.shard, pl.ds(pl.multiple_of(starts[5], 16), 16), cols]
            dst = self.landed[5].at[:, cols]
            dim = "xb"
        self.moving[p] = self.start(
            remote(src, dst, self.red_send.at[p, k], self.red_recv.at[p, k], dim)
        )

    def reduce_step(self, p, k):
        self.moving[p].wait_recv()
        starts, cols = (self.starts[p], self.cols[p])
        if k < 5:
            half = ROWS >> (k + 1)
            step = min(half, 32)

            def add(i, carry):
                here = pl.ds(pl.multiple_of(i * step, step), step)
                there = pl.ds(pl.multiple_of(starts[k + 1] + i * step, 16), step)
                self.partial[:, there, cols] += self.landed[k][:, here, cols]
                return carry

            lax.fori_loop(0, half // step, add, 0)
            self.reduce_start(p, k + 1)
        else:
            here = pl.ds(pl.multiple_of(starts[5], 16), 16)
            self.last[:, cols] = self.partial[self.shard, here, cols] + self.landed[5][:, cols]
            self.held[p] = pltpu.make_async_copy(
                self.last.at[:, cols], self.rows_out(p, starts[5], 16), self.own.at[8 + p]
            )
            self.held[p].start()
            self.gather_start(p, 4)

    def rows_out(self, p, at, size):
        return self.out.at[self.core, pl.ds(pl.multiple_of(at, 16), size), self.cols[p]]

    def gather_start(self, p, k):
        mine = self.rows_out(p, self.starts[p][k + 1], ROWS >> (k + 1))
        src = self.last.at[:, self.cols[p]] if k == 4 else mine
        self.moving[p] = self.start(
            remote(src, mine, self.gat_send.at[p, k], self.gat_recv.at[p, k], self.orders[p][k])
        )

    def gather_step(self, p, k):
        self.moving[p].wait_recv()
        if k == 4:
            self.held[p].wait()
        if k > 0:
            self.gather_start(p, k - 1)
        if k == 1:
            self.share(p, 0, self.starts[p][1])
        if k == 0:
            self.share(p, 1, ROWS // 2 - self.starts[p][1])

    def share(self, p, slot, at):
        mine = self.rows_out(p, at, ROWS // 2)
        sems = (self.gat_send.at[p, 5 + slot], self.gat_recv.at[p, 5 + slot])
        self.shared.append(self.start(remote(mine, mine, *sems, "core")))

    def finish(self):
        for copy in self.shared:
            copy.wait_recv()


def ring_member(dim, step):
    shard, x_lo, core, z, y = place()
    if dim == "y":
        y = (y + step) % 4
    else:
        z = (z + step) % 4
    return (shard, x_lo * 2 + core, z * 4 + y)


def copy_to(device, src, dst, send_sem, recv_sem):
    return pltpu.make_async_remote_copy(
        src_ref=src,
        dst_ref=dst,
        send_sem=send_sem,
        recv_sem=recv_sem,
        device_id=device,
        device_id_type=MESH,
    )


class Lines:
    def __init__(self, blocks, halves, send, recv, start):
        self.blocks, self.halves, self.start = (blocks, halves, start)
        self.send, self.recv = (send, recv)
        _, _, _, self.z, self.y = place()
        self.dims = (("y", "z"), ("z", "y"))

    def one(self, half):
        return self.blocks.at[(self.z, self.y, *self.halves[half])]

    def line(self, half, back=0):
        if half == 0:
            return self.blocks.at[((self.z + 4 - back) % 4, slice(None), *self.halves[0])]
        return self.blocks.at[(slice(None), (self.y + 4 - back) % 4, *self.halves[1])]

    def scatter(self, stage, sources):
        self.moving = []
        for half in range(2):
            dst = self.one(half) if stage == 0 else self.line(half)
            self.moving.append(
                [
                    self.start(
                        copy_to(
                            ring_member(self.dims[half][stage], d),
                            sources[half],
                            dst,
                            self.send.at[half, stage, d],
                            self.recv.at[half, stage, d],
                        )
                    )
                    for d in range(1, 4)
                ]
            )

    def arrive(self):
        for copies in self.moving:
            for copy in copies:
                copy.wait_recv()


class HeadGradients:
    def __init__(self, refs, out, start):
        self.partial, self.half, self.quarter, self.last = refs[:4]
        self.landed, (self.send, self.recv, self.own) = (refs[4:7], refs[7:10])
        self.share_send, self.share_recv = refs[12:14]
        self.out, self.start = (out, start)
        self.shard, _, self.core, self.z, self.y = place()
        self.bit = ring_bit("xa")
        pieces = pl.ds(self.core * 2, 2)
        halves = [(pieces, pl.ds(0, 96)), (pieces, pl.ds(96, 96))]
        self.lines = Lines(out, halves, refs[10], refs[11], start)
        self.shared = []

    def pass_on(self, k, src, dst, dim):
        self.moving = self.start(remote(src, dst, self.send.at[k], self.recv.at[k], dim))

    def multiply(self, grads_t, tokens):
        for s in range(2):
            product = jnp.dot(
                grads_t[...], tokens[:, pl.ds(s * ROWS, ROWS)], preferred_element_type=jnp.float32
            )
            self.partial[s] = product.astype(jnp.bfloat16)
        away = pl.ds(pl.multiple_of((1 - self.core) * 256, 256), 256)
        self.pass_on(0, self.partial.at[:, :, away], self.landed[0], "core")

    def step(self, k):
        self.moving.wait_recv()
        if k == 0:
            mine = pl.ds(pl.multiple_of(self.core * 256, 256), 256)
            self.half[...] = self.partial[:, :, mine] + self.landed[0][...]
            away = pl.ds(pl.multiple_of((1 - self.bit) * 128, 128), 128)
            self.pass_on(1, self.half.at[:, :, away], self.landed[1], "xa")
        elif k == 1:
            mine = pl.ds(pl.multiple_of(self.bit * 128, 128), 128)
            self.quarter[...] = self.half[:, :, mine] + self.landed[1][...]
            self.pass_on(2, self.quarter.at[1 - self.shard], self.landed[2], "xb")
        elif k == 2:
            self.last[...] = self.quarter[self.shard] + self.landed[2][...]
            mine = self.out.at[self.z, self.y, self.core * 2 + self.bit]
            self.held = pltpu.make_async_copy(self.last, mine, self.own.at[0])
            self.held.start()
            self.pass_on(3, self.last, mine, "xa")
        else:
            self.held.wait()
            self.lines.scatter(0, [self.lines.one(half) for half in range(2)])

    def share(self, half, back):
        mine = self.lines.line(half, back)
        sems = (self.share_send.at[half, back], self.share_recv.at[half, back])
        self.shared.append(self.start(remote(mine, mine, *sems, "core")))

    def spread(self):
        self.lines.arrive()
        self.lines.scatter(1, [self.lines.line(half) for half in range(2)])
        for half in range(2):
            self.share(half, 0)

    def finish(self):
        for half, copies in enumerate(self.lines.moving):
            for back, copy in enumerate(copies, 1):
                copy.wait_recv()
                self.share(half, back)
        for copy in self.shared:
            copy.wait_recv()


def head_scratch():
    bf16, dma = (jnp.bfloat16, pltpu.SemaphoreType.DMA)
    shapes = [(2, 192, 512), (2, 192, 256), (2, 192, 128), (192, 128)]
    shapes += [(2, 192, 256), (2, 192, 128), (192, 128)]
    return [
        *[pltpu.VMEM(shape, bf16) for shape in shapes],
        dma((4,)),
        dma((4,)),
        dma((1,)),
        dma((2, 2, 4)),
        dma((2, 2, 4)),
        dma((2, 4)),
        dma((2, 4)),
    ]


class NormSums:
    def __init__(self, held, landed, out, send, recv, start):
        self.held, self.landed, self.out = (held, landed, out)
        self.send, self.recv, self.start = (send, recv, start)
        self.dims = ("core",) + REDUCE_DIMS + ("xb",)

    def begin(self, k):
        shard, _, _, _, _ = place()
        if k < 6:
            src, dst = (self.held.at[k], self.landed.at[k])
        else:
            src, dst = (self.held.at[6, pl.ds(1 - shard, 1)], self.landed.at[6, pl.ds(0, 1)])
        self.copy = self.start(remote(src, dst, self.send.at[k], self.recv.at[k], self.dims[k]))

    def step(self, k):
        shard, _, _, _, _ = place()
        self.copy.wait_recv()
        if k < 6:
            self.held[k + 1] = self.held[k] + self.landed[k]
            self.begin(k + 1)
        else:
            self.out[...] = self.held[6, shard] + self.landed[6, 0]


def project_back(tok_ref, weight_ref, weight, sem, grad_ref, back_out):
    def fetch(c):
        cols = pl.ds(c * 256, 256)
        return pltpu.make_async_copy(weight_ref.at[:, cols], weight.at[c % 2], sem.at[c % 2])

    fetch(0).start()
    total = grad_ref[...]
    for c in range(12):
        if c < 11:
            fetch(c + 1).start()
        fetch(c).wait()
        total = total + lax.dot_general(
            tok_ref[:, c * 256 : (c + 1) * 256],
            weight[c % 2],
            (((1,), (1,)), ((), ())),
            preferred_element_type=jnp.float32,
        )
    back_out[...] = total.astype(jnp.bfloat16)


def back_kernel(*refs):
    refs = list(refs)

    def take(count):
        taken = refs[:count]
        del refs[:count]
        return taken

    act_refs = take(7)
    norm_ref, staged, grad_ref, weight_ref = take(4)
    attention_in = take(6)
    ff_out, qkv_out, norm_out, back_out = take(4)
    loads, held = ([], take(13))
    load_sem = take(1)[0]
    for i, (src, dst) in enumerate(zip(act_refs + attention_in, held)):
        loads.append(pltpu.make_async_copy(src, dst, load_sem.at[i]))
        loads[i].start()
    block_tokens, ff_acts = (held[0], held[1:7])
    q_ref, pairs_ref, low_ref, end_ref, lse_ref, o_ref = held[7:]
    ff_refs = take(8) + [ff_out] + take(7)
    head_refs = take(14)
    norm_refs = take(2) + [norm_out] + take(2)
    heads_in, heads_out, tok_in, tok_ref, weight, weight_sem = take(6)
    swaps = [take(2), take(2)]
    attention_refs = refs
    sent = []

    def start(copy):
        copy.start()
        sent.append(copy)
        return copy

    greet_all(("core", "xa", "xb"))
    ff = Reducer(ff_acts, FF_DOTS, FF_WIDTHS, ff_refs, start)
    heads = HeadGradients(head_refs, qkv_out, start)
    upstream = Exchange(staged, heads_in, *swaps[0], start)
    upstream.begin()
    sums = NormSums(*norm_refs, start)
    sums.held[0] = norm_ref[...]
    sums.begin(0)
    for load in loads[1:7]:
        load.wait()
    for at in range(len(FF_DOTS)):
        ff.multiply(at)
    sums.step(0)
    for load in loads[7:]:
        load.wait()
    upstream.finish()
    attention = AttendBack(
        [q_ref, heads_in, pairs_ref, low_ref, end_ref, lse_ref, o_ref],
        heads_out,
        attention_refs,
        start,
    )
    def ff_reduce(k):
        sums.step(k + 1)
        for p in ff.parts:
            ff.reduce_step(p, k)

    def ff_gather(k):
        for p in ff.parts:
            ff.gather_step(p, k)

    events = [(BACK_REDUCE[k], functools.partial(ff_reduce, k)) for k in range(2)]
    events += attention.events
    events.sort(key=lambda e: e[0])
    done = 0
    for at, act in events:
        if at > done:
            attention.run(done, at)
            done = at
        act()
    attention.run(done, 4 * SLOT_UNITS)
    attention.finish()
    downstream = Exchange(heads_out, tok_in, *swaps[1], start)
    downstream.begin()
    loads[0].wait()
    heads.multiply(attention.grads_t, block_tokens)
    ff_reduce(2)
    heads.step(0)
    ff_reduce(3)
    heads.step(1)
    ff_reduce(4)
    heads.step(2)
    ff_reduce(5)
    heads.step(3)
    ff_gather(4)
    ff_gather(3)
    heads.spread()
    ff_gather(2)
    ff_gather(1)
    downstream.finish()

    def unpack(i, carry):
        both = [tok_in[i * 2], tok_in[i * 2 + 1]]
        query = [jnp.concatenate([t[128:192, :HEAD], t[128:192, HEAD:]], axis=0) for t in both]
        key = [t[0:128, :HEAD] for t in both]
        value = [t[0:128, HEAD:] for t in both]
        for which, piece in enumerate((query, key, value)):
            here = pl.ds(pl.multiple_of(which * 1024 + i * 128, 128), 128)
            tok_ref[:, here] = jnp.concatenate(piece, axis=1)
        return carry

    lax.fori_loop(0, 8, unpack, 0)
    project_back(tok_ref, weight_ref, weight, weight_sem, grad_ref, back_out)
    heads.finish()
    ff_gather(0)
    ff.finish()
    for copy in sent:
        copy.wait_send()


FF_DOTS = tuple(
    [(0, 512, 0, 3, j * 512) for j in range(4)]
    + [(1, 2048, q * 512, 4, 0) for q in range(4)]
    + [(2, 512, 0, 5, 0)]
)
FF_WIDTHS = (1024, 896, 896, 896, 896)
def reducer_scratch(widths):
    total, parts = (sum(widths), len(widths))
    bf16, dma = (jnp.bfloat16, pltpu.SemaphoreType.DMA)
    return [
        pltpu.VMEM((2, ROWS, total), bf16),
        *[pltpu.VMEM((2, ROWS >> (k + 1), total), bf16) for k in range(5)],
        pltpu.VMEM((16, total), bf16),
        pltpu.VMEM((16, total), bf16),
        dma((8,)),
        dma((8,)),
        dma((parts, 6)),
        dma((parts, 6)),
        dma((parts, 7)),
        dma((parts, 7)),
        dma((8 + parts,)),
    ]


def back(acts, norm_sums, staged, grad_one, full_qkv, attention):
    bf16, f32, dma = (jnp.bfloat16, jnp.float32, pltpu.SemaphoreType.DMA)
    whole, anywhere = (pl.BlockSpec(memory_space=pltpu.VMEM), pl.BlockSpec(memory_space=pl.ANY))
    ff_total = sum(FF_WIDTHS)
    held = pltpu.VMEM((7, 2, 8, 512), f32)
    return pl.pallas_call(
        back_kernel,
        out_shape=[
            jax.ShapeDtypeStruct((2, ROWS, ff_total), bf16),
            jax.ShapeDtypeStruct((4, 4, 4, 192, 128), bf16),
            jax.ShapeDtypeStruct((8, 512), f32),
            jax.ShapeDtypeStruct((128, 1024), bf16),
        ],
        in_specs=[anywhere] * 7 + [whole] * 3 + [anywhere] * 7,
        out_specs=[anywhere] * 2 + [whole] * 2,
        scratch_shapes=[
            *[pltpu.VMEM(a.shape, a.dtype) for a in (*acts, *attention)],
            dma((13,)),
            *reducer_scratch(FF_WIDTHS),
            *head_scratch(),
            held,
            held,
            dma((7,)),
            dma((7,)),
            pltpu.VMEM((16, 64, 128), bf16),
            pltpu.VMEM((16, 192, 128), bf16),
            pltpu.VMEM((16, 192, 128), bf16),
            pltpu.VMEM((128, 3072), bf16),
            pltpu.VMEM((2, 1024, 256), bf16),
            dma((2,)),
            *[dma((16,))] * 4,
            *back_scratch(),
        ],
        compiler_params=pltpu.CompilerParams(
            collective_id=1, has_side_effects=True, vmem_limit_bytes=62 * 2**20
        ),
    )(*acts, norm_sums, staged, grad_one, full_qkv, *attention)


CHUNK = 512


def cast_kernel(ff_ref, qkv_ref, *refs):
    plain, refs = (list(zip(refs[:2], refs[8:10])), refs[2:8] + refs[10:])
    outs, (narrow, heads, wide, in_sem, out_sem, bounce) = (refs[:6], refs[6:])
    grad_in, grad_down, grad_out, *grad_qkv = outs
    chunks = []
    for c in range(2):
        for j in range(9):
            src = ff_ref.at[c, :, pl.ds(j * CHUNK, CHUNK)]
            if j < 4:
                dst = grad_in.at[:, pl.ds((c * 4 + j) * CHUNK, CHUNK)]
            elif j < 8:
                dst = grad_down.at[pl.ds((j - 4) * ROWS, ROWS), pl.ds(c * CHUNK, CHUNK)]
            else:
                dst = grad_out.at[:, pl.ds(c * CHUNK, CHUNK)]
            chunks.append((src, dst))
    loads = [
        pltpu.make_async_copy(src, narrow.at[n], in_sem.at[n]) for n, (src, _) in enumerate(chunks)
    ]
    turned = pltpu.make_async_copy(qkv_ref, heads, in_sem.at[18])
    turned.start()
    for c in range(2):
        for j in range(3):
            chunks.append((None, grad_qkv[j].at[:, pl.ds(c * CHUNK, CHUNK)]))
    stores = [
        pltpu.make_async_copy(wide.at[n], dst, out_sem.at[n]) for n, (_, dst) in enumerate(chunks)
    ]
    for load in loads:
        load.start()
    n = len(chunks)
    for i, (src, dst) in enumerate(plain):
        loads.append(pltpu.make_async_copy(src, bounce.at[i], in_sem.at[n + i]))
        loads[-1].start()
        stores.append(pltpu.make_async_copy(bounce.at[i], dst, out_sem.at[n + i]))
    for n in range(18):
        loads[n].wait()

        def widen(i, carry):
            here = pl.ds(pl.multiple_of(i * 64, 64), 64)
            wide[n, here] = narrow[n, here].astype(jnp.float32)
            return carry

        lax.fori_loop(0, ROWS // 64, widen, 0)
        stores[n].start()
    turned.wait()
    for n in range(18, 24):
        c, which = ((n - 18) // 3, (n - 18) % 3)

        def turn(p, carry):
            rows = pl.ds(pl.multiple_of(p * 128, 128), 128)
            for pair in range(4):
                both = []
                for head in (c * 8 + pair * 2, c * 8 + pair * 2 + 1):
                    both.append(heads[head // 4, head % 4, p, which * HEAD : (which + 1) * HEAD])
                block = jnp.concatenate(both, axis=0).astype(jnp.float32)
                wide[n, rows, pair * 128 : (pair + 1) * 128] = jnp.transpose(block)
            return carry

        lax.fori_loop(0, 4, turn, 0)
        stores[n].start()
    for i in range(2):
        loads[18 + i].wait()
        stores[24 + i].start()
    for store in stores:
        store.wait()


def results(ff_summed, qkv_summed, result, input_grad):
    f32 = jnp.float32
    anywhere = pl.BlockSpec(memory_space=pl.ANY)
    square = jax.ShapeDtypeStruct((ROWS, 1024), f32)
    return pl.pallas_call(
        cast_kernel,
        out_shape=[
            jax.ShapeDtypeStruct((ROWS, 4096), f32),
            jax.ShapeDtypeStruct((2048, 1024), f32),
            square,
            square,
            square,
            square,
            jax.ShapeDtypeStruct(result.shape, result.dtype),
            jax.ShapeDtypeStruct(input_grad.shape, input_grad.dtype),
        ],
        in_specs=[anywhere] * 4,
        out_specs=[anywhere] * 8,
        scratch_shapes=[
            pltpu.VMEM((18, ROWS, CHUNK), jnp.bfloat16),
            pltpu.VMEM(qkv_summed.shape, jnp.bfloat16),
            pltpu.VMEM((24, ROWS, CHUNK), f32),
            pltpu.SemaphoreType.DMA((26,)),
            pltpu.SemaphoreType.DMA((26,)),
            pltpu.VMEM((2, *result.shape), result.dtype),
        ],
        compiler_params=pltpu.CompilerParams(vmem_limit_bytes=56 * 2**20),
    )(ff_summed, qkv_summed, result, input_grad)


def shards(
    tokens,
    segments,
    valid,
    w_query,
    w_key,
    w_value,
    w_out,
    norm1_gain,
    norm1_bias,
    w_in,
    w_down,
    norm2_gain,
    norm2_bias,
    cotangent,
):
    packed = jnp.concatenate([norm1_gain, norm1_bias, norm2_gain, norm2_bias]).reshape(16, 128)
    token_rows = tokens[0]
    (
        full_qkv,
        queries,
        pairs,
        summed,
        lse,
        low,
        end,
        tokens_all,
        first_low,
        hidden,
        mixed,
        pre_grad,
        ff_grad,
        attn_grad,
        staged,
        norm_sums,
        grad_one,
        result,
    ) = front(
        token_rows,
        [w_query, w_key, w_value, w_out, w_in, w_down],
        packed,
        cotangent[0],
        segments[0],
        valid[0],
    )
    ff_summed, qkv_summed, norm_total, input_grad = back(
        [tokens_all.reshape(BLOCK_LEN, 1024), first_low, hidden, mixed, pre_grad, ff_grad, attn_grad],
        norm_sums,
        staged,
        grad_one,
        full_qkv,
        [queries, pairs, low, end, lse, summed],
    )
    grad_in, grad_down, grad_out, *grad_qkv, result, input_grad = results(
        ff_summed, qkv_summed, result, input_grad
    )
    return (
        result[None],
        input_grad[None],
        *grad_qkv,
        grad_out,
        norm_total[0],
        norm_total[1],
        grad_in,
        grad_down,
        norm_total[2],
        norm_total[3],
    )


def solution(mesh):
    return jax.shard_map(
        shards,
        mesh=mesh,
        in_specs=(
            P("shard", ("blk", "aa"), None),
            P("shard", None),
            P("shard", None),
            P("shard", None),
            P("shard", None),
            P("shard", None),
            P("shard", None),
            P("shard"),
            P("shard"),
            P("shard", None),
            P("shard", None),
            P("shard"),
            P("shard"),
            P("shard", ("blk", "aa"), None),
        ),
        out_specs=(
            P("shard", ("blk", "aa"), None),
            P("shard", ("blk", "aa"), None),
            P("shard", None),
            P("shard", None),
            P("shard", None),
            P("shard", None),
            P("shard"),
            P("shard"),
            P("shard", None),
            P("shard", None),
            P("shard"),
            P("shard"),
        ),
        check_vma=False,
    )
```
